32 devices in a mesh: dp: 16 (over z, y, core), tp: 2 (over x).
Axes of the slice: x: 2, y: 2, z: 4, core: 2. Of those that a mesh axis runs over, the one named last changes fastest.
Arguments:
- layer_input: bfloat16 [16, 256, 2048], P('dp', 'tp'), may hold values from -6 to 6
- grad_out: bfloat16 [16, 256, 2048], P('dp', 'tp'), may hold values from -6 to 6
- lengths: int32 [16], P('dp'), may hold values from 1 to 256, 3072 in all
- resets: int32 [16, 256], P('dp', 'tp'), may hold values 0 or 1
- norm_gain: bfloat16 [2048], P(('dp', 'tp')), may hold values from 0.099609375 to 1.8984375
- w_x: bfloat16 [2048, 2560], P(('dp', 'tp')), may hold values from -0.125 to 0.125
- w_y: bfloat16 [2048, 2560], P(('dp', 'tp')), may hold values from -0.125 to 0.125
- conv_w: bfloat16 [4, 2560], P(None, ('dp', 'tp')), may hold values from -3 to 3
- conv_b: bfloat16 [2560], P(('dp', 'tp')), may hold values from -3 to 3
- gate_a_w: bfloat16 [2560, 256], P(('dp', 'tp')), may hold values from -0.375 to 0.375
- gate_a_b: bfloat16 [2560], P(('dp', 'tp')), may hold values from -3 to 3
- gate_i_w: bfloat16 [2560, 256], P(('dp', 'tp')), may hold values from -0.375 to 0.375
- gate_i_b: bfloat16 [2560], P(('dp', 'tp')), may hold values from -3 to 3
- decay_param: bfloat16 [2560], P(('dp', 'tp')), may hold values from 4.5 to 8
- w_out: bfloat16 [2560, 2048], P(('dp', 'tp')), may hold values from -0.5 to 0.5
- mlp_gain: bfloat16 [2048], P(('dp', 'tp')), may hold values from 0.099609375 to 1.8984375
- w_gate: bfloat16 [2048, 6144], P('dp', 'tp'), may hold values from -0.125 to 0.125
- w_up: bfloat16 [2048, 6144], P('dp', 'tp'), may hold values from -0.125 to 0.125
- w_down: bfloat16 [6144, 2048], P('tp', 'dp'), may hold values from -0.15625 to 0.15625
Outputs:
- layer_output: bfloat16 [16, 256, 2048], P('dp', 'tp')
- grad_x: float32 [16, 256, 2048], P('dp', 'tp')
- grad_norm_gain: float32 [2048], P(('dp', 'tp'))
- grad_w_x: float32 [2048, 2560], P(('dp', 'tp'))
- grad_w_y: float32 [2048, 2560], P(('dp', 'tp'))
- grad_conv_w: float32 [4, 2560], P(None, ('dp', 'tp'))
- grad_conv_b: float32 [2560], P(('dp', 'tp'))
- grad_gate_a_w: float32 [2560, 256], P(('dp', 'tp'))
- grad_gate_a_b: float32 [2560], P(('dp', 'tp'))
- grad_gate_i_w: float32 [2560, 256], P(('dp', 'tp'))
- grad_gate_i_b: float32 [2560], P(('dp', 'tp'))
- grad_decay: float32 [2560], P(('dp', 'tp'))
- grad_w_out: float32 [2560, 2048], P(('dp', 'tp'))
- grad_mlp_gain: float32 [2048], P(('dp', 'tp'))
- grad_w_gate: float32 [2048, 6144], P('dp', 'tp')
- grad_w_up: float32 [2048, 6144], P('dp', 'tp')
- grad_w_down: float32 [6144, 2048], P('tp', 'dp')
The draws below stay inside these ranges and needn't reach their ends.
Inputs may be any that keep to these rules, and one draw needn't show every extreme that they name: `lengths`: some row has exactly 256. `resets`: position 0 of every row starts a segment in any case.
All inputs are finite; a program needn't handle non-finite values. No bound on the sum of `lengths` or of `resets` on one device may be relied on, other than what follows from the above.
Results may differ from the reference program's by a relative error of at most 0.017.
Values may be sent and summed in bfloat16 or wider, within the bound.
A program may use at most 384 MiB of HBM per device.

```python
import math
import jax
import jax.numpy as jnp
import numpy as np
from jax import lax

D = 2048
HEADS = 10
BLK = 256
R = 2560
FF = 6144
CONV = 4
SEQ = 256
BATCH = 16


def touch_ends(drawn, rng, least, largest):
    index_at = [jax.random.randint(jax.random.fold_in(rng, axis), (), 0, length) for axis, length in enumerate(drawn.shape)]
    main_axis = drawn.shape.index(max(drawn.shape))
    beside = index_at[:main_axis] + [(index_at[main_axis] + 1) % drawn.shape[main_axis]] + index_at[main_axis + 1:]
    return drawn.at[tuple(index_at)].set(least).at[tuple(beside)].set(largest)


def block_scale(rng, extent, split, low, largest):
    factor_of = 1.0
    for position, parts in split:
        heights = jax.random.uniform(jax.random.fold_in(jax.random.fold_in(rng, 6), position), (parts,), jnp.float32, low / len(split), largest / len(split))
        factor_of = factor_of * jnp.repeat(jnp.exp(heights), extent[position] // parts).reshape((-1,) + (1,) * (len(extent) - 1 - position))
    return factor_of


def split_up(number_of, total, most, skew):
    portions = [(1 << 20) // math.isqrt(rank ** skew) + 1 for rank in range(2, number_of + 1)]
    rest, given = total - most - (number_of - 1), [1] * (number_of - 1)
    while rest > 0:
        candidates = [i for i in range(number_of - 1) if given[i] < most]
        mass, remaining = sum([portions[i] for i in candidates]), rest
        for i in candidates:
            addition = min(most - given[i], max(1, remaining * portions[i] // mass), rest)
            given[i] = given[i] + addition
            rest = rest - addition
    return np.array([most] + given)


def ragged_sizes(own_key, count, total, limit, skew):
    if count == 2:
        one = jax.random.randint(own_key, (), max(1, total - limit), min(limit, total - 1) + 1)
        return jnp.stack([one, total - one])
    sizes = jnp.asarray(split_up(count, total, limit, skew), jnp.int32)
    twos = (count - 1) // 2
    source_of, taker = sizes[1:1 + 2 * twos:2], sizes[2:2 + 2 * twos:2]
    margin = jnp.minimum(source_of - 1, limit - taker)
    moved = jax.random.randint(jax.random.fold_in(own_key, 1), (twos,), 0, 1 << 20) % (margin + 1)
    sizes = sizes.at[1:1 + 2 * twos:2].set(source_of - moved).at[2:2 + 2 * twos:2].set(taker + moved)
    return sizes[jax.random.permutation(jax.random.fold_in(own_key, 2), count)]


def normal_values(key, dims, deviation, bound, cuts=(), kind=jnp.bfloat16):
    loudness = block_scale(key, dims, cuts, -0.22, 0.18) if cuts else 1.0
    result = jax.random.normal(key, dims, jnp.float32) * deviation * loudness
    return jnp.minimum(jnp.maximum(result, -bound), bound).astype(kind)


def setup_inputs(seed: int = 0) -> dict:
    streams_of = jax.random.split(jax.random.key(seed), 20)
    return {
        "layer_input": normal_values(streams_of[0], (BATCH, SEQ, D), 1.0, 6.0, ((0, 16), (1, 2))),
        "grad_out": normal_values(streams_of[1], (BATCH, SEQ, D), 1.0, 6.0, ((0, 16), (1, 2))),
        "lengths": ragged_sizes(streams_of[2], BATCH, BATCH * SEQ * 3 // 4, SEQ, 2).astype(jnp.int32),
        "resets": touch_ends((jax.random.randint(streams_of[3], (BATCH, SEQ), 0, 64) < 1).astype(jnp.int32), jax.random.fold_in(streams_of[3], 1), 0, 1),
        "norm_gain": jnp.clip(1.0 + 0.18 * jax.random.normal(streams_of[4], (D,), jnp.float32), 0.099609375, 1.8984375).astype(jnp.bfloat16),
        "w_x": normal_values(streams_of[5], (D, R), D ** -0.5, 0.125, ((0, 32),)),
        "w_y": normal_values(streams_of[6], (D, R), D ** -0.5, 0.125, ((0, 32),)),
        "conv_w": normal_values(streams_of[7], (CONV, R), 0.5, 3.0, ((1, 32),)),
        "conv_b": normal_values(streams_of[8], (R,), 0.5, 3.0, ((0, 32),)),
        "gate_a_w": normal_values(streams_of[9], (R, BLK), BLK ** -0.5, 0.375, ((0, 32),)),
        "gate_a_b": normal_values(streams_of[10], (R,), 0.5, 3.0, ((0, 32),)),
        "gate_i_w": normal_values(streams_of[11], (R, BLK), BLK ** -0.5, 0.375, ((0, 32),)),
        "gate_i_b": normal_values(streams_of[12], (R,), 0.5, 3.0, ((0, 32),)),
        "decay_param": jnp.clip(4.5 + 3.5 * jax.random.uniform(streams_of[13], (R,), jnp.float32) ** block_scale(streams_of[13], (R,), ((0, 32),), -0.2, 0.2), 4.5, 8.0).astype(jnp.bfloat16),
        "w_out": normal_values(streams_of[14], (R, D), (R // 16) ** -0.5, 0.5, ((0, 32),)),
        "mlp_gain": jnp.clip(1.0 + 0.18 * jax.random.normal(streams_of[15], (D,), jnp.float32), 0.099609375, 1.8984375).astype(jnp.bfloat16),
        "w_gate": normal_values(streams_of[16], (D, FF), D ** -0.5, 0.125, ((0, 16), (1, 2))),
        "w_up": normal_values(streams_of[17], (D, FF), D ** -0.5, 0.125, ((0, 16), (1, 2))),
        "w_down": normal_values(streams_of[18], (FF, D), (FF // 4) ** -0.5, 0.15625, ((0, 2), (1, 16))),
    }


@jax.custom_vjp
def low(v):
    return lax.optimization_barrier(v.astype(jnp.bfloat16)).astype(jnp.float32)

@jax.custom_vjp
def low_back(v):
    return v

def low_keep(v):
    return (low(v), None)

def low_pass(kept, grad):
    return (grad,)

def back_keep(v):
    return (v, None)

def back_low(kept, grad):
    return (low(grad),)
low.defvjp(low_keep, low_pass)
low_back.defvjp(back_keep, back_low)
epsilon = 1e-06
highest = lax.Precision.HIGHEST

def affine_pair(earlier, later):
    return (later[0] * earlier[0], later[0] * earlier[1] + later[1])

def rms_apply(values, gain):
    scaled = lax.rsqrt(lax.optimization_barrier(jnp.mean(values * values, axis=-1, keepdims=True)) + epsilon)
    return values * scaled * gain

def gate_section(pre_rate, pre_input, inputs, decay, bias_rate, bias_input, starts):
    rate = jax.nn.sigmoid(pre_rate + bias_rate)
    inject = jax.nn.sigmoid(pre_input + bias_input)
    log_decay = -8.0 * rate * jax.nn.softplus(-decay)
    factor = jnp.exp(log_decay) * (1.0 - starts)
    scale_in = jnp.where(starts > 0.5, 1.0, jnp.sqrt(-jnp.expm1(2.0 * log_decay)))
    return (factor, scale_in * inject * inputs)

def row_layer(rows_in, starts, params):
    gain_one, proj_x, proj_y, conv_taps, conv_bias, rate_w, rate_b, input_w, input_b, decay, proj_out, gain_two, ff_gate, ff_up, ff_down = params
    groups, length, width = rows_in.shape
    normed = low(rms_apply(rows_in, gain_one))
    branch_x = low(low_back(jnp.einsum('gtd,dr->gtr', normed, proj_x, precision=highest)))
    pre_y = low_back(jnp.einsum('gtd,dr->gtr', normed, proj_y, precision=highest))
    branch_y = jax.nn.gelu(pre_y, approximate=True)
    padded = jnp.pad(branch_x, ((0, 0), (CONV - 1, 0), (0, 0)))
    conv_sum = conv_bias + jnp.zeros_like(branch_x)
    for tap_index in range(CONV):
        conv_sum = conv_sum + conv_taps[tap_index] * padded[:, CONV - 1 - tap_index:CONV - 1 - tap_index + length]
    mixed = low(low_back(conv_sum))
    mixed4 = mixed.reshape(groups, length, HEADS, BLK)
    pre_rate = low_back(jnp.einsum('gthi,hij->gthj', mixed4, rate_w.reshape(HEADS, BLK, BLK), precision=highest).reshape(groups, length, HEADS * BLK))
    pre_input = low_back(jnp.einsum('gthi,hij->gthj', mixed4, input_w.reshape(HEADS, BLK, BLK), precision=highest).reshape(groups, length, HEADS * BLK))
    factor, inject = gate_section(pre_rate, pre_input, mixed, decay, rate_b, input_b, starts)
    coefs, states = lax.associative_scan(affine_pair, (factor, inject), axis=1)
    gated = low(states * branch_y)
    first_sum = rows_in + low_back(jnp.einsum('gtr,rd->gtd', gated, proj_out, precision=highest))
    normed_two = low(rms_apply(first_sum, gain_two))
    pre_gate = low_back(jnp.einsum('gtd,df->gtf', normed_two, ff_gate, precision=highest))
    pre_up = low_back(jnp.einsum('gtd,df->gtf', normed_two, ff_up, precision=highest))
    hidden = low(jax.nn.gelu(pre_gate, approximate=True) * pre_up)
    return first_sum + low_back(jnp.einsum('gtf,fd->gtd', hidden, ff_down, precision=highest))

def reference(layer_input, grad_out, lengths, resets, norm_gain, w_x, w_y, conv_w, conv_b, gate_a_w, gate_a_b, gate_i_w, gate_i_b, decay_param, w_out, mlp_gain, w_gate, w_up, w_down):
    params = tuple((p.astype(jnp.float32) for p in (norm_gain, w_x, w_y, conv_w, conv_b, gate_a_w, gate_a_b, gate_i_w, gate_i_b, decay_param, w_out, mlp_gain, w_gate, w_up, w_down)))
    group = math.gcd(BATCH, max(1, 4096 // SEQ))
    steps_count = BATCH // group
    place = jnp.arange(SEQ, dtype=jnp.int32)
    starts_all = jnp.where((resets > 0) | (place[None, :] == 0), 1.0, 0.0).astype(jnp.float32)[..., None]
    valid = (place[None, :] < lengths[:, None]).astype(jnp.float32)[..., None]
    inputs = layer_input.astype(jnp.float32).reshape(steps_count, group, SEQ, D)
    cotangent = (grad_out.astype(jnp.float32) * valid).reshape(steps_count, group, SEQ, D)
    starts = starts_all.reshape(steps_count, group, SEQ, 1)

    def one_group(total, item):
        rows_in, cot_rows, start_rows = item
        value, pull = jax.vjp(lambda values, weights: row_layer(values, start_rows, weights), rows_in, params)
        grad_rows, grad_params = pull(cot_rows)
        total = jax.tree.map(lambda a, b: a + b, total, grad_params)
        return (total, (value.astype(jnp.bfloat16), grad_rows))
    zeros = tuple((jnp.zeros_like(p) for p in params))
    total, (outputs, grads) = lax.scan(one_group, zeros, (inputs, cotangent, starts))
    return (outputs.reshape(BATCH, SEQ, D), grads.reshape(BATCH, SEQ, D), total[0], total[1], total[2], total[3], total[4], total[5], total[6], total[7], total[8], total[9], total[10], total[11], total[12], total[13], total[14])
```

```python
import functools

import jax
import jax.numpy as jnp
from jax import lax
from jax.experimental import pallas as pl
from jax.experimental.pallas import tpu as pltpu
from jax.sharding import PartitionSpec as P

BLK = 256
PAD = 16
WIDE = 512
EPS = 1e-06
MESH = pl.DeviceIdType.MESH
F32 = jnp.float32
BF16 = jnp.bfloat16


def chip_at(pos, n):
    back = pos // (n // 2)
    return (1 - back) * (2 * pos) + back * (2 * (n - 1 - pos) + 1)


def place_of(chip, n):
    odd = chip % 2
    return (1 - odd) * (chip // 2) + odd * (n - 1 - chip // 2)


def gather_kernel(
    n,
    wx, wy, wo, gs, wg, wu, wd, rows_in, cot, starts,
    o_xy, o_out, o_gs, o_gu, o_d, o_rows, o_cot, o_starts,
    local_sem, pair_send, pair_recv, ring_send, ring_recv, x_send, x_recv,
):
    dp, x = lax.axis_index("dp"), lax.axis_index("tp")
    chip, core = dp // 2, dp % 2
    other = 1 - core
    pos = place_of(chip, n)
    half = n // 2
    nxt = (chip_at((pos + 1) % n, n) * 2 + core, x)
    prv = (chip_at((pos + n - 1) % n, n) * 2 + core, x)
    sib = (chip * 2 + other, x)
    across = (dp, 1 - x)
    barrier = pltpu.get_barrier_semaphore()
    for device in (nxt, prv, sib, across):
        pl.semaphore_signal(barrier, inc=1, device_id=device, device_id_type=MESH)
    pl.semaphore_wait(barrier, 4)

    def cols(width, which):
        return pl.ds(pl.multiple_of(which * width, 128), width)

    taken = {"l": 0, "p": 0, "r": 0, "x": 0}

    def local(src, dst):
        copy = pltpu.make_async_copy(src, dst, local_sem.at[taken["l"]])
        taken["l"] += 1
        copy.start()
        return copy

    def remote(kind, src, dst, device):
        sends, recvs = {"p": (pair_send, pair_recv), "r": (ring_send, ring_recv), "x": (x_send, x_recv)}[kind]
        i = taken[kind]
        taken[kind] += 1
        copy = pltpu.make_async_remote_copy(
            src_ref=src, dst_ref=dst, send_sem=sends.at[i], recv_sem=recvs.at[i],
            device_id=device, device_id_type=MESH,
        )
        copy.start()
        return copy

    rhalf = wx.shape[1] // 2
    dhalf = wo.shape[1] // 2
    fhalf = wg.shape[1] // 2
    parts = [
        (wx, rhalf, lambda: o_xy.at[chip, core, x, :, pl.ds(0, rhalf)]),
        (wy, rhalf, lambda: o_xy.at[chip, core, x, :, pl.ds(rhalf, rhalf)]),
        (wo, dhalf, lambda: o_out.at[chip, core, x]),
        (wg, fhalf, lambda: o_gu.at[chip, core, :, pl.ds(0, fhalf)]),
        (wu, fhalf, lambda: o_gu.at[chip, core, :, pl.ds(fhalf, fhalf)]),
        (wd, fhalf, lambda: o_d.at[chip, core]),
    ]
    pair, mine = [], []
    for src, width, slot in parts[:3]:
        pair.append(remote("p", src.at[:, cols(width, other)], slot(), sib))
    for src, width, slot in parts[:3]:
        mine.append(local(src.at[:, cols(width, core)], slot()))
    mine.append(local(gs, o_gs.at[core, chip, x]))
    for src, width, slot in parts[3:]:
        pair.append(remote("p", src.at[:, cols(width, other)], slot(), sib))
    for src, width, slot in parts[3:]:
        mine.append(local(src.at[:, cols(width, core)], slot()))
    late = [
        remote("p", rows_in, o_rows.at[1], sib),
        remote("p", starts, o_starts.at[1], sib),
        remote("p", cot, o_cot.at[2], sib),
    ]
    plain = [local(rows_in, o_rows.at[0]), local(starts, o_starts.at[0]), local(cot, o_cot.at[0])]
    cot_x = remote("x", cot, o_cot.at[1], across)

    def rec_block(chip_id):
        return [o_xy.at[chip_id, :, x], o_out.at[chip_id, :, x], o_gs.at[core, chip_id, x]]

    def rec_half(chip_id, which):
        piece = [o_xy.at[chip_id, which, x], o_out.at[chip_id, which, x]]
        return piece + ([o_gs.at[core, chip_id, x]] if which == 0 else [])

    def ff_block(chip_id):
        return [o_gu.at[chip_id], o_d.at[chip_id]]

    def ff_half(chip_id, which):
        return [o_gu.at[chip_id, which], o_d.at[chip_id, which]]

    def send_all(kind, refs, device):
        return [remote(kind, ref, ref, device) for ref in refs]

    for copy in pair[:3]:
        copy.wait_recv()
    for copy in mine[:4]:
        copy.wait()
    sends, arrivals_x = [], []

    def step(block, piece, s, first):
        ahead = chip_at((pos + n - (s - 1)) % n, n)
        behind = chip_at((pos + s - 1) % n, n)
        if s < half:
            f = send_all("r", block(ahead), nxt)
            b = send_all("r", block(behind), prv)
        else:
            f = send_all("r", piece(ahead, 0), nxt)
            b = send_all("r", piece(behind, 1), prv)
        if first:
            arrivals_x.extend(send_all("x", block(ahead), across))
        return f, b

    f, b = step(rec_block, rec_half, 1, True)
    for s in range(2, half + 1):
        for copy in f + b:
            copy.wait_recv()
        sends.extend(f + b)
        ahead = chip_at((pos + n - (s - 1)) % n, n)
        behind = chip_at((pos + s - 1) % n, n)
        f, b = step(rec_block, rec_half, s, False)
        arrivals_x.extend(send_all("x", rec_block(ahead), across))
        arrivals_x.extend(send_all("x", rec_block(behind), across))
    rec_last = f + b
    for copy in pair[3:]:
        copy.wait_recv()
    for copy in mine[4:]:
        copy.wait()
    f, b = step(ff_block, ff_half, 1, False)
    for copy in rec_last:
        copy.wait_recv()
    sends.extend(rec_last)
    arrivals_x.extend(send_all("x", rec_block(chip_at((pos + half) % n, n)), across))
    cot_x.wait_recv()
    last_cot = remote("p", o_cot.at[1], o_cot.at[3], sib)
    for s in range(2, half + 1):
        for copy in f + b:
            copy.wait_recv()
        sends.extend(f + b)
        f, b = step(ff_block, ff_half, s, False)
    for copy in arrivals_x:
        copy.wait_recv()
    swap = remote("p", o_gs.at[core], o_gs.at[core], sib)
    for copy in f + b:
        copy.wait_recv()
    sends.extend(f + b)
    swap.wait_recv()
    last_cot.wait_recv()
    for copy in late:
        copy.wait_recv()
    for copy in plain:
        copy.wait()
    for copy in pair + late + [cot_x, last_cot, swap] + sends + arrivals_x:
        copy.wait_send()


def gather_weights(n, wx, wy, wo, gs, wg, wu, wd, rows_in, cot, starts):
    r, d, f = wx.shape[1], wo.shape[1], wg.shape[1]
    half = n // 2
    tokens = rows_in.shape[0]
    shapes = [
        jax.ShapeDtypeStruct((n, 2, 2, wx.shape[0], r), BF16),
        jax.ShapeDtypeStruct((n, 2, 2, wo.shape[0], d // 2), BF16),
        jax.ShapeDtypeStruct((2, n, 2) + gs.shape, BF16),
        jax.ShapeDtypeStruct((n, 2, wg.shape[0], f), BF16),
        jax.ShapeDtypeStruct((n, 2, wg.shape[0], f // 2), BF16),
        jax.ShapeDtypeStruct((2, tokens, d), BF16),
        jax.ShapeDtypeStruct((4, tokens, d), BF16),
        jax.ShapeDtypeStruct((2,) + starts.shape, F32),
    ]
    pairs, ring, over = 11, half * 10 - 1, 3 * n + 1
    dma = pltpu.SemaphoreType.DMA
    result = pl.pallas_call(
        functools.partial(gather_kernel, n),
        out_shape=shapes,
        in_specs=[pl.BlockSpec(memory_space=pl.ANY)] * 10,
        out_specs=[pl.BlockSpec(memory_space=pl.ANY)] * 8,
        scratch_shapes=[
            dma((10,)), dma((pairs,)), dma((pairs,)), dma((ring,)), dma((ring,)), dma((over,)), dma((over,)),
        ],
        compiler_params=pltpu.CompilerParams(collective_id=0, has_side_effects=True),
        name="gather_weights",
    )(wx, wy, wo, gs, wg, wu, wd, rows_in, cot, starts)
    return result


def minus_expm1(v):
    series = jnp.ones_like(v)
    for k in range(9, 1, -1):
        series = 1.0 + series * v * (1.0 / k)
    return jnp.where(v > -0.5, -v * series, 1.0 - jnp.exp(v))


def gates_of(u, weights, cp, start):
    tokens = u.shape[0] * u.shape[1]
    flat = u.reshape(tokens, BLK)
    z = jnp.dot(flat, weights, preferred_element_type=F32)
    r = jax.nn.sigmoid(z[:, :BLK] + cp[5:6]).reshape(u.shape)
    ig = jax.nn.sigmoid(z[:, BLK:] + cp[6:7]).reshape(u.shape)
    la = -8.0 * r * cp[7:8][None]
    decayed = jnp.exp(la)
    rest = minus_expm1(2.0 * la)
    return r, ig, decayed, rest


def recurrence_kernel(xb, halo, weights, cp, starts, u_ref, a_ref, h_ref, c_ref, b_ref):
    rows, length = xb.shape[0], xb.shape[1]
    p = cp[...]
    us = []
    for row in range(rows):
        padded = jnp.concatenate([halo[row], xb[row].astype(F32)], axis=0)
        total = p[4:5] + p[0:1] * padded[8 : 8 + length]
        for k in range(1, 4):
            total = total + p[k : k + 1] * padded[8 - k : 8 - k + length]
        us.append(total.astype(BF16))
    u = jnp.stack(us)
    u_ref[...] = u
    start = starts[...]
    start = jnp.concatenate([start, start], axis=2)
    r, ig, decayed, rest = gates_of(u, weights[...], p, start)
    a_ref[...] = decayed * (1.0 - start)
    b_ref[...] = jnp.where(start > 0.5, 1.0, jnp.sqrt(rest)) * ig * u.astype(F32)

    def eight(i, carry):
        at = pl.ds(pl.multiple_of(i * 8, 8), 8)
        out = []
        for row in range(rows):
            h, c = carry[row]
            a, b = a_ref[row, at, :], b_ref[row, at, :]
            hs, cs = [], []
            for j in range(8):
                h = a[j : j + 1] * h + b[j : j + 1]
                c = a[j : j + 1] * c
                hs.append(h)
                cs.append(c)
            h_ref[row, at, :] = jnp.concatenate(hs, axis=0)
            c_ref[row, at, :] = jnp.concatenate(cs, axis=0)
            out.append((h, c))
        return tuple(out)

    zero, one = jnp.zeros((1, BLK), F32), jnp.ones((1, BLK), F32)
    lax.fori_loop(0, length // 8, eight, ((zero, one),) * rows)


def recurrence(xb, halo, weights, cp, starts):
    rows, length, channels = xb.shape
    wide = pl.BlockSpec((rows, length, BLK), lambda h: (0, 0, h))
    return pl.pallas_call(
        recurrence_kernel,
        grid=(channels // BLK,),
        in_specs=[
            wide,
            pl.BlockSpec((rows, 8, BLK), lambda h: (0, 0, h)),
            pl.BlockSpec((BLK, 2 * BLK), lambda h: (h, 0)),
            pl.BlockSpec((cp.shape[0], BLK), lambda h: (0, h)),
            pl.BlockSpec(starts.shape, lambda h: (0, 0, 0)),
        ],
        out_specs=[wide] * 4,
        out_shape=[jax.ShapeDtypeStruct(xb.shape, BF16)] + [jax.ShapeDtypeStruct(xb.shape, F32)] * 3,
        scratch_shapes=[pltpu.VMEM((rows, length, BLK), F32)],
        compiler_params=pltpu.CompilerParams(vmem_limit_bytes=40 << 20),
        cost_estimate=pl.CostEstimate(flops=4 * 10**8, bytes_accessed=6 * 10**6, transcendentals=2 * 10**6),
        name="recurrence",
    )(xb, halo, weights, cp, starts)


def gelu_parts(v):
    inner = 0.7978845608028654 * (v + 0.044715 * v * v * v)
    t = jnp.tanh(inner)
    value = 0.5 * v * (1.0 + t)
    slope = 0.5 * (1.0 + t) + 0.5 * v * (1.0 - t * t) * 0.7978845608028654 * (1.0 + 3.0 * 0.044715 * v * v)
    return value, slope


def adjoint_kernel(do, h_ref, y_ref, a_ref, dy_ref, lam_ref, c_ref, dh_ref):
    rows, length = do.shape[0], do.shape[1]
    value, slope = gelu_parts(y_ref[...])
    dy_ref[...] = (do[...] * h_ref[...] * slope).astype(BF16)
    dh_ref[...] = do[...] * value

    def eight(step, carry):
        i = length // 8 - 1 - step
        at = pl.ds(pl.multiple_of(i * 8, 8), 8)
        out = []
        for row in range(rows):
            ahead, c = carry[row]
            a, d = a_ref[row, at, :], dh_ref[row, at, :]
            ls, cs = [None] * 8, [None] * 8
            for j in range(7, -1, -1):
                lam = d[j : j + 1] + ahead
                ls[j], cs[j] = lam, c
                ahead = a[j : j + 1] * lam
                c = a[j : j + 1] * c
            lam_ref[row, at, :] = jnp.concatenate(ls, axis=0)
            c_ref[row, at, :] = jnp.concatenate(cs, axis=0)
            out.append((ahead, c))
        return tuple(out)

    zero, one = jnp.zeros((1, BLK), F32), jnp.ones((1, BLK), F32)
    lax.fori_loop(0, length // 8, eight, ((zero, one),) * rows)


def adjoint(do, h, ypre, a):
    rows, length, channels = do.shape
    wide = pl.BlockSpec((rows, length, BLK), lambda i: (0, 0, i))
    return pl.pallas_call(
        adjoint_kernel,
        grid=(channels // BLK,),
        in_specs=[wide] * 4,
        out_specs=[wide] * 3,
        out_shape=[jax.ShapeDtypeStruct(do.shape, BF16)] + [jax.ShapeDtypeStruct(do.shape, F32)] * 2,
        scratch_shapes=[pltpu.VMEM((rows, length, BLK), F32)],
        compiler_params=pltpu.CompilerParams(vmem_limit_bytes=40 << 20),
        cost_estimate=pl.CostEstimate(flops=10**7, bytes_accessed=9 * 10**6, transcendentals=10**6),
        name="adjoint",
    )(do, h, ypre, a)


def gates_back_kernel(lam_ref, c_ref, inc, h_ref, h_in, u_ref, weights, cp, starts, du_ref, dw_ref, sums_ref):
    rows, length = u_ref.shape[0], u_ref.shape[1]
    tokens = rows * length
    p = cp[...]
    u = u_ref[...]
    uf = u.astype(F32)
    start = starts[...]
    start = jnp.concatenate([start, start], axis=2)
    w = weights[...]
    r, ig, decayed, rest = gates_of(u, w, p, start)
    mult = jnp.where(start > 0.5, 1.0, jnp.sqrt(rest))
    lam = lam_ref[...] + c_ref[...] * inc[...]
    before = jnp.stack([jnp.concatenate([h_in[row], h_ref[row][: length - 1]], axis=0) for row in range(rows)])
    keep = 1.0 - start
    d_la = lam * before * decayed * keep - jnp.where(
        start > 0.5, 0.0, lam * ig * uf * decayed * decayed * lax.rsqrt(jnp.where(start > 0.5, 1.0, rest))
    )
    dpa = d_la * (-8.0 * p[7:8][None]) * r * (1.0 - r)
    direct = lam * mult
    dpi = direct * uf * ig * (1.0 - ig)
    d_decay = d_la * (8.0 * p[8:9][None]) * r
    dz = jnp.concatenate(
        [dpa.reshape(tokens, BLK).astype(BF16), dpi.reshape(tokens, BLK).astype(BF16)], axis=1
    )
    back = lax.dot_general(dz, w, (((1,), (1,)), ((), ())), preferred_element_type=F32)
    du_ref[...] = (direct * ig + back.reshape(u.shape)).astype(BF16)
    dw_ref[...] = lax.dot_general(
        u.reshape(tokens, BLK), dz, (((0,), (0,)), ((), ())), preferred_element_type=F32
    )
    zero = jnp.zeros((5, BLK), F32)
    sums_ref[...] = jnp.concatenate(
        [jnp.sum(v.reshape(tokens, BLK), axis=0, keepdims=True) for v in (dpa, dpi, d_decay)] + [zero], axis=0
    )


def gates_back(lam, coef, inc, h, h_in, u, weights, cp, starts):
    rows, length, channels = u.shape
    wide = pl.BlockSpec((rows, length, BLK), lambda i: (0, 0, i))
    line = pl.BlockSpec((rows, 1, BLK), lambda i: (0, 0, i))
    square = pl.BlockSpec((BLK, 2 * BLK), lambda i: (i, 0))
    return pl.pallas_call(
        gates_back_kernel,
        grid=(channels // BLK,),
        in_specs=[
            wide, wide, line, wide, line, wide, square,
            pl.BlockSpec((cp.shape[0], BLK), lambda i: (0, i)),
            pl.BlockSpec(starts.shape, lambda i: (0, 0, 0)),
        ],
        out_specs=[wide, square, pl.BlockSpec((8, BLK), lambda i: (0, i))],
        out_shape=[
            jax.ShapeDtypeStruct(u.shape, BF16),
            jax.ShapeDtypeStruct((channels, 2 * BLK), F32),
            jax.ShapeDtypeStruct((8, channels), F32),
        ],
        compiler_params=pltpu.CompilerParams(vmem_limit_bytes=40 << 20),
        cost_estimate=pl.CostEstimate(flops=12 * 10**8, bytes_accessed=9 * 10**6, transcendentals=2 * 10**6),
        name="gates_back",
    )(lam, coef, inc, h, h_in, u, weights, cp, starts)


def nt(left, right):
    return lax.dot_general(left, right, (((1,), (1,)), ((), ())), preferred_element_type=F32)


def nn(left, right):
    return jnp.dot(left, right, preferred_element_type=F32)


def body(
    dp_size,
    layer_input, grad_out, lengths, resets, norm_gain, w_x, w_y, conv_w, conv_b, gate_a_w, gate_a_b,
    gate_i_w, gate_i_b, decay_param, w_out, mlp_gain, w_gate, w_up, w_down,
):
    n = dp_size // 2
    half = n // 2
    dp, x = lax.axis_index("dp"), lax.axis_index("tp")
    chip, core = dp // 2, dp % 2
    pos = place_of(chip, n)
    tokens, width = layer_input.shape[1], layer_input.shape[2]
    rec = w_x.shape[1]
    rh = rec // 2
    taps = conv_w.shape[0]
    own = rec // (2 * dp_size)
    own_d = width // (2 * dp_size)

    ring = [chip_at(i, n) for i in range(n)]
    up = [(ring[i] * 2 + c, ring[(i + 1) % n] * 2 + c) for i in range(n) for c in range(2)]
    down = [(b, a) for a, b in up]
    pairs = [(d, d + 1 - 2 * (d % 2)) for d in range(dp_size)]

    def sibling(v):
        return lax.ppermute(v, "dp", pairs)

    def across(v):
        return lax.ppermute(v, "tp", [(0, 1), (1, 0)])

    def swapped(v):
        return jnp.concatenate([v[1:], v[:1]], axis=0)

    def by_core(mine, theirs, axis):
        return jnp.where(
            core == 0, jnp.concatenate([mine, theirs], axis), jnp.concatenate([theirs, mine], axis)
        )

    rows_own = layer_input.reshape(tokens, width)
    place = x * tokens + jnp.arange(tokens, dtype=jnp.int32)
    starts = jnp.where((resets.reshape(tokens) > 0) | (place == 0), 1.0, 0.0).astype(F32)
    starts = jnp.broadcast_to(starts[:, None], (tokens, 128))
    valid = (place < lengths[0]).astype(F32)[:, None]
    cot = grad_out.reshape(tokens, width).astype(F32) * valid

    small = jnp.concatenate(
        [norm_gain, mlp_gain, conv_w.reshape(-1), conv_b, gate_a_b, gate_i_b, decay_param]
    )
    small = jnp.pad(small, (0, PAD * WIDE - small.shape[0])).reshape(PAD, WIDE)
    gs = jnp.concatenate([jnp.concatenate([gate_a_w, gate_i_w], axis=1), small], axis=0)
    w_xy, w_o, all_gs, w_gu, w_d, rows_two, cot_all, starts_two = gather_weights(
        n, w_x, w_y, w_out, gs, w_gate, w_up, w_down.T, rows_own, cot.astype(BF16), starts
    )
    w_xy = w_xy.reshape(width, rec)
    w_o = w_o.reshape(rec, width // 2)
    w_gu = w_gu.reshape(width, w_gate.shape[1])
    w_d = w_d.reshape(width, w_gate.shape[1] // 2)
    cot_all = cot_all.reshape(4 * tokens, width)

    vectors = all_gs[:, :, :, own:].transpose(1, 0, 2, 3, 4).reshape(2 * dp_size, PAD * WIDE)
    gain_one = vectors[:, :own_d].reshape(width).astype(F32)
    gain_two = vectors[:, own_d : 2 * own_d].reshape(width).astype(F32)
    lines = vectors[:, 2 * own_d : 2 * own_d + (taps + 4) * own].reshape(2 * dp_size, taps + 4, own)
    lines = lax.dynamic_slice_in_dim(lines, core * dp_size, dp_size, 0)
    lines = lines.transpose(1, 0, 2).reshape(taps + 4, rh).astype(F32)
    decay = lines[taps + 3 :]
    cp = jnp.concatenate(
        [lines[: taps + 3], jax.nn.softplus(-decay), jax.nn.sigmoid(-decay), jnp.zeros((7, rh), F32)], axis=0
    )
    gates = lax.dynamic_slice_in_dim(all_gs[:, :, :, :own], core * half, half, 1)
    gates = gates.transpose(1, 0, 2, 3, 4).reshape(rh, WIDE)

    rows_f = rows_two.astype(F32)
    rs1 = lax.rsqrt(jnp.mean(rows_f * rows_f, axis=-1, keepdims=True) + EPS)
    n1 = (rows_f * rs1 * gain_one).astype(BF16).reshape(2 * tokens, width)
    xy = nn(n1, w_xy)
    xb = xy[:, :rh].astype(BF16).reshape(2, tokens, rh)
    ypre = xy[:, rh:].reshape(2, tokens, rh)
    before = lax.ppermute(xb[:, tokens - (taps - 1) :], "tp", [(0, 1)])
    halo = jnp.concatenate([jnp.zeros((2, 8 - (taps - 1), rh), F32), before.astype(F32)], axis=1)
    u, a, h_local, coef = recurrence(xb, halo, gates, cp, starts_two)
    h_in = lax.ppermute(h_local[:, tokens - 1 :], "tp", [(0, 1)])
    h = h_local + coef * h_in
    ybr, _ = gelu_parts(ypre)
    o = (h * ybr).astype(BF16)
    o_sib = swapped(sibling(o))
    o_full = by_core(o, o_sib, 2).reshape(2 * tokens, rec)
    part = nn(o_full, w_o).reshape(2, tokens, width // 2)
    x1 = rows_own.astype(F32) + by_core(part[0], sibling(part[1]), 1)
    rs2 = lax.rsqrt(jnp.mean(x1 * x1, axis=-1, keepdims=True) + EPS)
    n2 = (x1 * rs2 * gain_two).astype(BF16)
    two = jnp.concatenate([n2, across(n2)], axis=0)
    n2_all = jnp.concatenate([two, sibling(two)], axis=0)

    fh = w_d.shape[1]
    gu = nn(n2_all, w_gu)
    gate, upv = gu[:, :fh], gu[:, fh:]
    act, slope = gelu_parts(gate)
    hidden = (act * upv).astype(BF16)
    d_hidden = nn(cot_all, w_d)
    d_gu = jnp.concatenate([(d_hidden * upv * slope).astype(BF16), (d_hidden * act).astype(BF16)], axis=1)

    def gathered_sum(partial):
        partial = partial.astype(BF16)
        kept = partial[: 2 * tokens].astype(F32) + sibling(partial[2 * tokens :]).astype(F32)
        kept = kept.astype(BF16)
        return kept[:tokens].astype(F32) + across(kept[tokens:]).astype(F32)

    d_n2 = gathered_sum(nt(d_gu, w_gu))

    def chip_rel(k):
        return chip_at((pos + k) % n, n)

    def ring_sum(product):
        def way(perm, sign, far):
            out = {}
            for which in (0, 1):
                first = half if which == far else half - 1
                got = None
                for k in range(first, 0, -1):
                    term = product(chip_rel((sign * k) % n), which)
                    send = term if got is None else term + got.astype(F32)
                    got = lax.ppermute(send.astype(BF16), "dp", perm)
                out[which] = got
            return out

        f, b = way(up, 1, 0), way(down, -1, 1)
        return [product(chip, w) + f[w].astype(F32) + b[w].astype(F32) for w in (0, 1)]

    def pick(array, chip_id, which):
        other = core + which - 2 * core * which
        index = (chip_id, other) + (0,) * (array.ndim - 2)
        return lax.dynamic_slice(array, index, (1, 1) + array.shape[2:]).reshape(array.shape[2:])

    cot_t = cot_all.T.reshape(n, 2, width // dp_size, 4 * tokens)
    n2_t = n2_all.T.reshape(n, 2, width // dp_size, 4 * tokens)
    sum_d = ring_sum(lambda chip_id, which: nn(pick(cot_t, chip_id, which), hidden))
    sum_gu = ring_sum(lambda chip_id, which: nn(pick(n2_t, chip_id, which), d_gu))
    ff_out = gathered_sum(nt(hidden, w_d))
    result = (x1 + ff_out).astype(BF16).reshape(1, tokens, width)

    q2 = gain_two * d_n2
    d_gain_two = jnp.sum(d_n2 * x1 * rs2, axis=0)
    d_x1 = cot + rs2 * q2 - x1 * (rs2 * rs2 * rs2) * jnp.mean(x1 * q2, axis=-1, keepdims=True)
    dbr = d_x1.astype(BF16)
    dbr_mine = lax.dynamic_slice_in_dim(dbr, core * (width // 2), width // 2, 1)
    dbr_theirs = lax.dynamic_slice_in_dim(dbr, (1 - core) * (width // 2), width // 2, 1)
    dbr_half = jnp.concatenate([dbr_mine, sibling(dbr_theirs)], axis=0)
    do_part = nt(dbr_half, w_o)
    do_mine = lax.dynamic_slice_in_dim(do_part, core * rh, rh, 1).reshape(2, tokens, rh)
    do_theirs = lax.dynamic_slice_in_dim(do_part, (1 - core) * rh, rh, 1).reshape(2, tokens, rh)
    do = do_mine + swapped(sibling(do_theirs))

    d_ypre, lam_local, coef_back = adjoint(do, h, ypre, a)
    inc = lax.ppermute(a[:, :1] * lam_local[:, :1], "tp", [(1, 0)])
    du, d_gates, sums = gates_back(lam_local, coef_back, inc, h, h_in, u, gates, cp, starts_two)
    after = lax.ppermute(du[:, : taps - 1], "tp", [(1, 0)])
    du_pad = jnp.concatenate([du, after], axis=1).astype(F32)
    xb_pad = jnp.concatenate([before, xb], axis=1).astype(F32)
    d_taps = jnp.stack(
        [jnp.sum(du_pad[:, :tokens] * xb_pad[:, taps - 1 - k : taps - 1 - k + tokens], axis=(0, 1)) for k in range(taps)]
    )
    d_bias = jnp.sum(du_pad[:, :tokens], axis=(0, 1))[None]
    d_xb = sum(cp[k] * du_pad[:, k : k + tokens] for k in range(taps)).astype(BF16)
    d_xy = jnp.concatenate([d_xb, d_ypre], axis=2).reshape(2 * tokens, rec)
    d_n1_part = nt(d_xy, w_xy).reshape(2, tokens, width)
    d_n1 = d_n1_part[0] + sibling(d_n1_part[1])
    q1 = gain_one * d_n1
    own_f, own_rs = rows_f[0], rs1[0]
    d_gain_one = jnp.sum(d_n1 * own_f * own_rs, axis=0)
    grad_x = d_x1 + own_rs * q1 - own_f * (own_rs * own_rs * own_rs) * jnp.mean(own_f * q1, axis=-1, keepdims=True)

    def plane(array, which):
        return lax.dynamic_index_in_dim(array, which, 2, keepdims=False)

    def both(mine, axis):
        return jnp.concatenate([mine, across(mine)], axis)

    def plane_rows(values, rows):
        grouped = values.T.reshape(n, 2, 2, rows, 2 * tokens)
        return jnp.concatenate([plane(grouped, x), across(plane(grouped, 1 - x))], axis=3)

    o_t = plane_rows(o_full, own)
    dbr_x = both(dbr_half, 0)
    sum_out = ring_sum(lambda chip_id, which: nn(pick(o_t, chip_id, which), dbr_x))
    n1_t = plane_rows(n1, own_d)
    d_xy_x = both(d_xy, 0)
    sum_xy = ring_sum(lambda chip_id, which: nn(pick(n1_t, chip_id, which), d_xy_x))

    def placed(part):
        zero = jnp.zeros_like(part)
        return by_core_rows(part, zero)

    def by_core_rows(mine, theirs):
        return jnp.where(
            core == 0, jnp.concatenate([mine, theirs], 0), jnp.concatenate([theirs, mine], 0)
        )

    g = d_gates.reshape(half, 2, 2, own, WIDE)
    g = plane(g, x) + across(plane(g, 1 - x).astype(BF16)).astype(F32)
    g_mine = lax.dynamic_index_in_dim(g, core, 1, keepdims=False)
    g_theirs = lax.dynamic_index_in_dim(g, 1 - core, 1, keepdims=False)
    g_lane = by_core_rows(g_mine, sibling(g_theirs))

    lines_back = jnp.concatenate([d_taps, d_bias, sums[:3]], axis=0)
    lines_back = lines_back.reshape(taps + 4, half, 2, 2, own).transpose(1, 2, 3, 0, 4)
    lines_back = placed(lines_back.reshape(half, 2, 2, (taps + 4) * own))
    gains = jnp.concatenate([d_gain_one.reshape(n, 2, 2, own_d), d_gain_two.reshape(n, 2, 2, own_d)], axis=3)
    vec = jnp.concatenate([gains, lines_back], axis=3)
    vec = jnp.pad(vec, ((0, 0), (0, 0), (0, 0), (0, -vec.shape[3] % 128)))
    vec = plane(vec, x) + across(plane(vec, 1 - x))
    vec = lax.dynamic_index_in_dim(vec, core, 1, keepdims=False) + sibling(
        lax.dynamic_index_in_dim(vec, 1 - core, 1, keepdims=False)
    )

    def lane_sum(array):
        def at(chip_id):
            return lax.dynamic_index_in_dim(array, chip_id, 0, keepdims=False)

        total = at(chip)
        for perm, sign, first in ((up, 1, half), (down, -1, half - 1)):
            got = None
            for k in range(first, 0, -1):
                term = at(chip_rel((sign * k) % n))
                send = term if got is None else term + got.astype(F32)
                got = lax.ppermute(send, "dp", perm)
            total = total + got
        return total

    sum_gates = lane_sum(g_lane)
    sum_vec = lane_sum(vec)

    def whole(halves, axis):
        return by_core(halves[0], sibling(halves[1]), axis)

    gu0, gu1 = sum_gu
    grad_gate = whole((gu0[:, :fh], gu1[:, :fh]), 1)
    grad_up = whole((gu0[:, fh:], gu1[:, fh:]), 1)
    grad_down = whole(sum_d, 1).T
    grad_w_x = whole((sum_xy[0][:, :rh], sum_xy[1][:, :rh]), 1)
    grad_w_y = whole((sum_xy[0][:, rh:], sum_xy[1][:, rh:]), 1)
    grad_w_out = whole(sum_out, 1)
    tail = sum_vec[2 * own_d : 2 * own_d + (taps + 4) * own].reshape(taps + 4, own)
    return (
        result,
        grad_x.reshape(1, tokens, width),
        sum_vec[:own_d],
        grad_w_x,
        grad_w_y,
        tail[:taps],
        tail[taps],
        sum_gates[:, :BLK],
        tail[taps + 1],
        sum_gates[:, BLK:],
        tail[taps + 2],
        tail[taps + 3],
        grad_w_out,
        sum_vec[own_d : 2 * own_d],
        grad_gate,
        grad_up,
        grad_down,
    )


def solution(mesh):
    every = ("dp", "tp")
    return jax.shard_map(
        functools.partial(body, mesh.shape["dp"]),
        mesh=mesh,
        in_specs=(
            P("dp", "tp", None),
            P("dp", "tp", None),
            P("dp"),
            P("dp", "tp"),
            P(every),
            P(every, None),
            P(every, None),
            P(None, every),
            P(every),
            P(every, None),
            P(every),
            P(every, None),
            P(every),
            P(every),
            P(every, None),
            P(every),
            P("dp", "tp"),
            P("dp", "tp"),
            P("tp", "dp"),
        ),
        out_specs=(
            P("dp", "tp", None),
            P("dp", "tp", None),
            P(every),
            P(every, None),
            P(every, None),
            P(None, every),
            P(every),
            P(every, None),
            P(every),
            P(every, None),
            P(every),
            P(every),
            P(every, None),
            P(every),
            P("dp", "tp"),
            P("dp", "tp"),
            P("tp", "dp"),
        ),
        check_vma=False,
    )
```

```python
import functools

import jax
import jax.numpy as jnp
from jax import lax
from jax.experimental import pallas as pl
from jax.experimental.pallas import tpu as pltpu
from jax.sharding import PartitionSpec as P

BLK = 256
PAD = 16
WIDE = 512
EPS = 1e-06
MESH = pl.DeviceIdType.MESH
F32 = jnp.float32
BF16 = jnp.bfloat16


def chip_at(pos, n):
    back = pos // (n // 2)
    return (1 - back) * (2 * pos) + back * (2 * (n - 1 - pos) + 1)


def place_of(chip, n):
    odd = chip % 2
    return (1 - odd) * (chip // 2) + odd * (n - 1 - chip // 2)


def heads_first(chip, core, n):
    return (chip + n - core * (n // 2)) % n


class Copies:
    def __init__(self, local, sends, recvs):
        self.local, self.sends, self.recvs = local, sends, recvs
        self.locals_used = self.used = 0

    def stay(self, src, dst):
        copy = pltpu.make_async_copy(src, dst, self.local.at[self.locals_used])
        self.locals_used += 1
        copy.start()
        return copy

    def send(self, src, dst, device):
        copy = pltpu.make_async_remote_copy(
            src_ref=src, dst_ref=dst, send_sem=self.sends.at[self.used], recv_sem=self.recvs.at[self.used],
            device_id=device, device_id_type=MESH,
        )
        self.used += 1
        copy.start()
        return copy


def greet(devices):
    barrier = pltpu.get_barrier_semaphore()
    for device in devices:
        pl.semaphore_signal(barrier, inc=1, device_id=device, device_id_type=MESH)
    pl.semaphore_wait(barrier, len(devices))


def half_cols(ref, which):
    width = ref.shape[1] // 2
    return ref.at[:, pl.ds(pl.multiple_of(which * width, 128), width)]


def gather_kernel(
    n,
    wx, wy, wo, gs, wg, wu, wd, rows_in, cot, starts,
    o_xy, o_out, o_gs, o_gu, o_d, o_rows, o_cot, o_starts,
    local_sem, send_sem, recv_sem,
):
    dp, x = lax.axis_index("dp"), lax.axis_index("tp")
    chip, core = dp // 2, dp % 2
    other = 1 - core
    pos = place_of(chip, n)
    half = n // 2
    nxt = (chip_at((pos + 1) % n, n) * 2 + core, x)
    prv = (chip_at((pos + n - 1) % n, n) * 2 + core, x)
    sib = (chip * 2 + other, x)
    over = (dp, 1 - x)
    greet([nxt, prv, sib, over])
    copies = Copies(local_sem, send_sem, recv_sem)
    send, stay = copies.send, copies.stay

    def by_heads(chip_id, which):
        return heads_first(chip_id, which, n)

    rhalf = wx.shape[1] // 2
    fhalf = wg.shape[1] // 2
    rec_parts = [
        (wx, o_xy.at[chip, core, x, :, pl.ds(0, rhalf)]),
        (wy, o_xy.at[chip, core, x, :, pl.ds(rhalf, rhalf)]),
    ]
    ff_parts = [
        (wg, o_gu.at[chip, core, :, pl.ds(0, fhalf)]),
        (wu, o_gu.at[chip, core, :, pl.ds(fhalf, fhalf)]),
        (wd, o_d.at[core]),
    ]
    pair = [send(half_cols(src, other), slot, sib) for src, slot in rec_parts]
    pair.append(send(half_cols(wo, other), o_out.at[by_heads(chip, other), core, x], sib))
    mine = [stay(half_cols(src, core), slot) for src, slot in rec_parts] + [stay(gs, o_gs.at[core, chip, x])]
    mine.append(stay(half_cols(wo, core), o_out.at[by_heads(chip, core), core, x]))
    late = [send(half_cols(src, other), slot, sib) for src, slot in ff_parts]
    plain = [stay(half_cols(src, core), slot) for src, slot in ff_parts]
    late += [send(rows_in, o_rows.at[1], sib), send(starts, o_starts.at[1], sib), send(cot, o_cot.at[2], sib)]
    plain += [stay(rows_in, o_rows.at[0]), stay(starts, o_starts.at[0]), stay(cot, o_cot.at[0])]

    def rec_block(chip_id):
        return [o_xy.at[chip_id, :, x], o_out.at[by_heads(chip_id, core), :, x], o_gs.at[core, chip_id, x]]

    def rec_piece(chip_id, which):
        refs = [o_xy.at[chip_id, which, x], o_out.at[by_heads(chip_id, core), which, x]]
        return refs + ([o_gs.at[core, chip_id, x]] if which == 0 else [])

    def ff_block(chip_id):
        return [o_gu.at[chip_id]]

    def ff_piece(chip_id, which):
        return [o_gu.at[chip_id, which]]

    def send_all(refs, device):
        return [send(ref, ref, device) for ref in refs]

    def hop(s, block, piece):
        ahead = chip_at((pos + n - (s - 1)) % n, n)
        behind = chip_at((pos + s - 1) % n, n)
        if s < half:
            return send_all(block(ahead), nxt) + send_all(block(behind), prv)
        return send_all(piece(ahead, 0), nxt) + send_all(piece(behind, 1), prv)

    for copy in pair:
        copy.wait_recv()
    for copy in mine:
        copy.wait()
    done, crossed, moving = [], send_all(rec_block(chip), over), []
    for s in range(1, half + 1):
        for copy in moving:
            copy.wait_recv()
        done.extend(moving)
        moving = hop(s, rec_block, rec_piece)
        if s > 1:
            crossed.extend(send_all(rec_block(chip_at((pos + n - (s - 1)) % n, n)), over))
            crossed.extend(send_all(rec_block(chip_at((pos + s - 1) % n, n)), over))
    last_rec = moving
    for copy in late:
        copy.wait_recv()
    for copy in plain:
        copy.wait()
    moving = hop(1, ff_block, ff_piece)
    for copy in last_rec:
        copy.wait_recv()
    done.extend(last_rec)
    crossed.extend(send_all(rec_block(chip_at((pos + half) % n, n)), over))
    cot_over = send(cot, o_cot.at[1], over)
    for s in range(2, half + 1):
        for copy in moving:
            copy.wait_recv()
        done.extend(moving)
        moving = hop(s, ff_block, ff_piece)
    for copy in crossed:
        copy.wait_recv()
    swap = send(o_gs.at[core], o_gs.at[core], sib)
    cot_over.wait_recv()
    last = send(o_cot.at[1], o_cot.at[3], sib)
    for copy in moving:
        copy.wait_recv()
    done.extend(moving)
    swap.wait_recv()
    last.wait_recv()
    for copy in pair + late + done + crossed + [cot_over, swap, last]:
        copy.wait_send()


def gather_weights(n, wx, wy, wo, gs, wg, wu, wd, rows_in, cot, starts):
    r, d, (rows_f, f) = wx.shape[1], wo.shape[1], wg.shape
    tokens = rows_in.shape[0]
    shapes = [
        jax.ShapeDtypeStruct((n, 2, 2, wx.shape[0], r), BF16),
        jax.ShapeDtypeStruct((n, 2, 2, wo.shape[0], d // 2), BF16),
        jax.ShapeDtypeStruct((2, n, 2) + gs.shape, BF16),
        jax.ShapeDtypeStruct((n, 2, rows_f, f), BF16),
        jax.ShapeDtypeStruct((2, rows_f, f // 2), BF16),
        jax.ShapeDtypeStruct((2, tokens, d), BF16),
        jax.ShapeDtypeStruct((4, tokens, d), BF16),
        jax.ShapeDtypeStruct((2,) + starts.shape, F32),
    ]
    count = 9 + (3 * n - 1) + n + 3 * n + 3
    dma = pltpu.SemaphoreType.DMA
    return pl.pallas_call(
        functools.partial(gather_kernel, n),
        out_shape=shapes,
        in_specs=[pl.BlockSpec(memory_space=pltpu.VMEM)] * 10,
        out_specs=[pl.BlockSpec(memory_space=pl.ANY)] * 8,
        scratch_shapes=[dma((10,)), dma((count,)), dma((count,))],
        compiler_params=pltpu.CompilerParams(
            collective_id=0, has_side_effects=True, vmem_limit_bytes=24 << 20
        ),
        name="gather_weights",
    )(wx, wy, wo, gs, wg, wu, wd, rows_in, cot, starts)


def scatter_kernel(
    n,
    c_x, c_y, c_out, c_g, c_v,
    g_x, g_y, g_out, g_gates, g_vec,
    r_x, r_y, r_out, r_g, r_v, s_x, s_y, s_out,
    send_sem, recv_sem,
):
    dp, x = lax.axis_index("dp"), lax.axis_index("tp")
    chip, core = dp // 2, dp % 2
    pos = place_of(chip, n)
    half = n // 2
    nxt = (chip_at((pos + 1) % n, n) * 2 + core, x)
    prv = (chip_at((pos + n - 1) % n, n) * 2 + core, x)
    sib = (dp + 1 - 2 * core, x)
    greet([nxt, prv, sib])
    copies = Copies(None, send_sem, recv_sem)

    pieces = []
    for part in (0, 1):
        for terms, slots, first in ((c_out, r_out, core), (c_y, r_y, 0), (c_x, r_x, 0)):
            pieces.append((
                lambda c, terms=terms, part=part, first=first: terms.at[heads_first(c, first, n), part],
                lambda w, k, slots=slots, part=part: slots.at[part, w, k],
                part,
            ))
    pieces.append((lambda c: c_g.at[c], lambda w, k: r_g.at[w, k], 0))
    pieces.append((lambda c: c_v.at[c], lambda w, k: r_v.at[w, k], 1))

    def add(a, b):
        return a[...].astype(F32) + b[...].astype(F32)

    sent, coming = [], {}
    for k in range(half, -1, -1):
        for i, (term, slot, far) in enumerate(pieces):
            for way, (device, sign) in enumerate(((nxt, 1), (prv, n - 1))):
                first = half if way == far else half - 1
                if k > first or k == 0:
                    continue
                source = term(chip_at((pos + sign * k) % n, n))
                if k < first:
                    coming[i, way].wait_recv()
                    got = slot(way, k)
                    got[...] = add(got, source).astype(got.dtype)
                    source = got
                copy = copies.send(source, slot(way, k - 1), device)
                coming[i, way] = copy
                sent.append(copy)

    def total(i):
        term, slot, _ = pieces[i]
        for way in (0, 1):
            coming[i, way].wait_recv()
        return add(term(chip), slot(0, 0)) + slot(1, 0)[...].astype(F32)

    def cols(ref):
        width = ref.shape[1] // 2
        return pl.ds(pl.multiple_of(core * width, 128), width)

    results = ((g_out, s_out), (g_y, s_y), (g_x, s_x))
    for part in (0, 1):
        sums = [total(3 * part + i) for i in range(3)]

        @pl.when(core == part)
        def _():
            for value, (ref, _) in zip(sums, results):
                ref[:, cols(ref)] = value

        @pl.when(core != part)
        def _():
            for value, (_, ref) in zip(sums, results):
                ref[...] = value

    final = [copies.send(src, ref.at[:, cols(ref)], sib) for ref, src in results]
    g_gates[...] = total(6)
    g_vec[...] = total(7)
    for copy in final:
        copy.wait_recv()
    for copy in sent + final:
        copy.wait_send()


def scatter_sums(n, c_x, c_y, c_out, c_g, c_v):
    _, _, rows_d, rhalf = c_x.shape
    _, _, rows_r, dhalf = c_out.shape
    half = n // 2
    count = 8 * (2 * half - 1) + 3
    dma = pltpu.SemaphoreType.DMA
    vmem = pl.BlockSpec(memory_space=pltpu.VMEM)
    return pl.pallas_call(
        functools.partial(scatter_kernel, n),
        out_shape=[
            jax.ShapeDtypeStruct((rows_d, 2 * rhalf), F32),
            jax.ShapeDtypeStruct((rows_d, 2 * rhalf), F32),
            jax.ShapeDtypeStruct((rows_r, 2 * dhalf), F32),
            jax.ShapeDtypeStruct(c_g.shape[1:], F32),
            jax.ShapeDtypeStruct(c_v.shape[1:], F32),
        ],
        in_specs=[vmem] * 5,
        out_specs=[vmem] * 5,
        scratch_shapes=[
            pltpu.VMEM((2, 2, half, rows_d, rhalf), BF16),
            pltpu.VMEM((2, 2, half, rows_d, rhalf), BF16),
            pltpu.VMEM((2, 2, half, rows_r, dhalf), BF16),
            pltpu.VMEM((2, half) + c_g.shape[1:], BF16),
            pltpu.VMEM((2, half) + c_v.shape[1:], F32),
            pltpu.VMEM((rows_d, rhalf), F32),
            pltpu.VMEM((rows_d, rhalf), F32),
            pltpu.VMEM((rows_r, dhalf), F32),
            dma((count,)), dma((count,)),
        ],
        compiler_params=pltpu.CompilerParams(
            collective_id=1, has_side_effects=True, vmem_limit_bytes=56 << 20
        ),
        name="scatter_sums",
    )(c_x, c_y, c_out, c_g, c_v)


def project_kernel(steps, rows, gain, w, n1_ref, x_ref, y_ref):
    i = pl.program_id(0)

    @pl.when(i == 0)
    def _():
        values = rows[...].astype(F32)
        scale = lax.rsqrt(jnp.mean(values * values, axis=-1, keepdims=True) + EPS)
        n1_ref[...] = (values * scale * gain[...]).astype(BF16).reshape(n1_ref.shape)

    result = jnp.dot(n1_ref[...], w[...], preferred_element_type=F32).reshape(y_ref.shape)

    @pl.when(i < steps)
    def _():
        x_ref[...] = result.astype(BF16)

    @pl.when(i >= steps)
    def _():
        y_ref[...] = result


def project(rows, gain, w):
    _, tokens, width = rows.shape
    rh = w.shape[1] // 2
    steps = rh // BLK
    return pl.pallas_call(
        functools.partial(project_kernel, steps),
        grid=(2 * steps,),
        in_specs=[
            pl.BlockSpec(rows.shape, lambda i: (0, 0, 0)),
            pl.BlockSpec((1, width), lambda i: (0, 0)),
            pl.BlockSpec((width, BLK), lambda i: (0, i)),
        ],
        out_specs=[
            pl.BlockSpec((2 * tokens, width), lambda i: (0, 0)),
            pl.BlockSpec((2, tokens, BLK), lambda i: (0, 0, jnp.minimum(i, steps - 1))),
            pl.BlockSpec((2, tokens, BLK), lambda i: (0, 0, jnp.maximum(i - steps, 0))),
        ],
        out_shape=[
            jax.ShapeDtypeStruct((2 * tokens, width), BF16),
            jax.ShapeDtypeStruct((2, tokens, rh), BF16),
            jax.ShapeDtypeStruct((2, tokens, rh), F32),
        ],
        compiler_params=pltpu.CompilerParams(vmem_limit_bytes=40 << 20),
        cost_estimate=pl.CostEstimate(flops=27 * 10**8, bytes_accessed=15 * 10**6, transcendentals=0),
        name="project",
    )(rows, gain, w)


def project_out_kernel(o, o_sib, w, mine_ref, theirs_ref):
    rh = o.shape[2]
    for row, ref in ((0, mine_ref), (1, theirs_ref)):
        ref[...] = jnp.dot(o[row], w[:rh], preferred_element_type=F32) + jnp.dot(
            o_sib[1 - row], w[rh:], preferred_element_type=F32
        )


def project_out(o, o_sib, w):
    _, tokens, rh = o.shape
    cols = w.shape[1]
    tile = min(BLK, cols)
    whole = pl.BlockSpec(o.shape, lambda i: (0, 0, 0))
    part = pl.BlockSpec((tokens, tile), lambda i: (0, i))
    return pl.pallas_call(
        project_out_kernel,
        grid=(cols // tile,),
        in_specs=[whole, whole, pl.BlockSpec((2 * rh, tile), lambda i: (0, i))],
        out_specs=[part, part],
        out_shape=[jax.ShapeDtypeStruct((tokens, cols), F32)] * 2,
        compiler_params=pltpu.CompilerParams(vmem_limit_bytes=40 << 20),
        cost_estimate=pl.CostEstimate(flops=14 * 10**8, bytes_accessed=8 * 10**6, transcendentals=0),
        name="project_out",
    )(o, o_sib, w)


def minus_expm1(v):
    series = jnp.ones_like(v)
    for k in range(9, 1, -1):
        series = 1.0 + series * v * (1.0 / k)
    return jnp.where(v > -0.5, -v * series, 1.0 - jnp.exp(v))


def gates_of(u, weights, cp, start):
    tokens = u.shape[0] * u.shape[1]
    flat = u.reshape(tokens, BLK)
    z = jnp.dot(flat, weights, preferred_element_type=F32)
    r = jax.nn.sigmoid(z[:, :BLK] + cp[5:6]).reshape(u.shape)
    ig = jax.nn.sigmoid(z[:, BLK:] + cp[6:7]).reshape(u.shape)
    la = -8.0 * r * cp[7:8][None]
    decayed = jnp.exp(la)
    rest = minus_expm1(2.0 * la)
    return r, ig, decayed, rest


def recurrence_kernel(xb, halo, weights, cp, starts, u_ref, a_ref, h_ref, c_ref, b_ref):
    rows, length = xb.shape[0], xb.shape[1]
    p = cp[...]
    us = []
    for row in range(rows):
        padded = jnp.concatenate([halo[row], xb[row].astype(F32)], axis=0)
        total = p[4:5] + p[0:1] * padded[8 : 8 + length]
        for k in range(1, 4):
            total = total + p[k : k + 1] * padded[8 - k : 8 - k + length]
        us.append(total.astype(BF16))
    u = jnp.stack(us)
    u_ref[...] = u
    start = starts[...]
    start = jnp.concatenate([start, start], axis=2)
    r, ig, decayed, rest = gates_of(u, weights[...], p, start)
    a_ref[...] = decayed * (1.0 - start)
    b_ref[...] = jnp.where(start > 0.5, 1.0, jnp.sqrt(rest)) * ig * u.astype(F32)

    def eight(i, carry):
        at = pl.ds(pl.multiple_of(i * 8, 8), 8)
        out = []
        for row in range(rows):
            h, c = carry[row]
            a, b = a_ref[row, at, :], b_ref[row, at, :]
            hs, cs = [], []
            for j in range(8):
                h = a[j : j + 1] * h + b[j : j + 1]
                c = a[j : j + 1] * c
                hs.append(h)
                cs.append(c)
            h_ref[row, at, :] = jnp.concatenate(hs, axis=0)
            c_ref[row, at, :] = jnp.concatenate(cs, axis=0)
            out.append((h, c))
        return tuple(out)

    zero, one = jnp.zeros((1, BLK), F32), jnp.ones((1, BLK), F32)
    lax.fori_loop(0, length // 8, eight, ((zero, one),) * rows)


def recurrence(xb, halo, weights, cp, starts):
    rows, length, channels = xb.shape
    wide = pl.BlockSpec((rows, length, BLK), lambda h: (0, 0, h))
    return pl.pallas_call(
        recurrence_kernel,
        grid=(channels // BLK,),
        in_specs=[
            wide,
            pl.BlockSpec((rows, 8, BLK), lambda h: (0, 0, h)),
            pl.BlockSpec((BLK, 2 * BLK), lambda h: (h, 0)),
            pl.BlockSpec((cp.shape[0], BLK), lambda h: (0, h)),
            pl.BlockSpec(starts.shape, lambda h: (0, 0, 0)),
        ],
        out_specs=[wide] * 4,
        out_shape=[jax.ShapeDtypeStruct(xb.shape, BF16)] + [jax.ShapeDtypeStruct(xb.shape, F32)] * 3,
        scratch_shapes=[pltpu.VMEM((rows, length, BLK), F32)],
        compiler_params=pltpu.CompilerParams(vmem_limit_bytes=40 << 20),
        cost_estimate=pl.CostEstimate(flops=4 * 10**8, bytes_accessed=6 * 10**6, transcendentals=2 * 10**6),
        name="recurrence",
    )(xb, halo, weights, cp, starts)


def gelu_parts(v):
    inner = 0.7978845608028654 * (v + 0.044715 * v * v * v)
    t = jnp.tanh(inner)
    value = 0.5 * v * (1.0 + t)
    slope = 0.5 * (1.0 + t) + 0.5 * v * (1.0 - t * t) * 0.7978845608028654 * (1.0 + 3.0 * 0.044715 * v * v)
    return value, slope


def adjoint_kernel(do, h_ref, y_ref, a_ref, dy_ref, lam_ref, c_ref, dh_ref):
    rows, length = do.shape[0], do.shape[1]
    value, slope = gelu_parts(y_ref[...])
    dy_ref[...] = (do[...] * h_ref[...] * slope).astype(BF16)
    dh_ref[...] = do[...] * value

    def eight(step, carry):
        i = length // 8 - 1 - step
        at = pl.ds(pl.multiple_of(i * 8, 8), 8)
        out = []
        for row in range(rows):
            ahead, c = carry[row]
            a, d = a_ref[row, at, :], dh_ref[row, at, :]
            ls, cs = [None] * 8, [None] * 8
            for j in range(7, -1, -1):
                lam = d[j : j + 1] + ahead
                ls[j], cs[j] = lam, c
                ahead = a[j : j + 1] * lam
                c = a[j : j + 1] * c
            lam_ref[row, at, :] = jnp.concatenate(ls, axis=0)
            c_ref[row, at, :] = jnp.concatenate(cs, axis=0)
            out.append((ahead, c))
        return tuple(out)

    zero, one = jnp.zeros((1, BLK), F32), jnp.ones((1, BLK), F32)
    lax.fori_loop(0, length // 8, eight, ((zero, one),) * rows)


def adjoint(do, h, ypre, a):
    rows, length, channels = do.shape
    wide = pl.BlockSpec((rows, length, BLK), lambda i: (0, 0, i))
    return pl.pallas_call(
        adjoint_kernel,
        grid=(channels // BLK,),
        in_specs=[wide] * 4,
        out_specs=[wide] * 3,
        out_shape=[jax.ShapeDtypeStruct(do.shape, BF16)] + [jax.ShapeDtypeStruct(do.shape, F32)] * 2,
        scratch_shapes=[pltpu.VMEM((rows, length, BLK), F32)],
        compiler_params=pltpu.CompilerParams(vmem_limit_bytes=40 << 20),
        cost_estimate=pl.CostEstimate(flops=10**7, bytes_accessed=9 * 10**6, transcendentals=10**6),
        name="adjoint",
    )(do, h, ypre, a)


def gates_back_kernel(lam_ref, c_ref, inc, h_ref, h_in, u_ref, weights, cp, starts, du_ref, dw_ref, sums_ref):
    rows, length = u_ref.shape[0], u_ref.shape[1]
    tokens = rows * length
    p = cp[...]
    u = u_ref[...]
    uf = u.astype(F32)
    start = starts[...]
    start = jnp.concatenate([start, start], axis=2)
    w = weights[...]
    r, ig, decayed, rest = gates_of(u, w, p, start)
    mult = jnp.where(start > 0.5, 1.0, jnp.sqrt(rest))
    lam = lam_ref[...] + c_ref[...] * inc[...]
    before = jnp.stack([jnp.concatenate([h_in[row], h_ref[row][: length - 1]], axis=0) for row in range(rows)])
    keep = 1.0 - start
    d_la = lam * before * decayed * keep - jnp.where(
        start > 0.5, 0.0, lam * ig * uf * decayed * decayed * lax.rsqrt(jnp.where(start > 0.5, 1.0, rest))
    )
    dpa = d_la * (-8.0 * p[7:8][None]) * r * (1.0 - r)
    direct = lam * mult
    dpi = direct * uf * ig * (1.0 - ig)
    d_decay = d_la * (8.0 * p[8:9][None]) * r
    dz = jnp.concatenate(
        [dpa.reshape(tokens, BLK).astype(BF16), dpi.reshape(tokens, BLK).astype(BF16)], axis=1
    )
    back = lax.dot_general(dz, w, (((1,), (1,)), ((), ())), preferred_element_type=F32)
    du_ref[...] = (direct * ig + back.reshape(u.shape)).astype(BF16)
    dw_ref[...] = lax.dot_general(
        u.reshape(tokens, BLK), dz, (((0,), (0,)), ((), ())), preferred_element_type=F32
    )
    zero = jnp.zeros((5, BLK), F32)
    sums_ref[...] = jnp.concatenate(
        [jnp.sum(v.reshape(tokens, BLK), axis=0, keepdims=True) for v in (dpa, dpi, d_decay)] + [zero], axis=0
    )


def gates_back(lam, coef, inc, h, h_in, u, weights, cp, starts):
    rows, length, channels = u.shape
    wide = pl.BlockSpec((rows, length, BLK), lambda i: (0, 0, i))
    line = pl.BlockSpec((rows, 1, BLK), lambda i: (0, 0, i))
    square = pl.BlockSpec((BLK, 2 * BLK), lambda i: (i, 0))
    return pl.pallas_call(
        gates_back_kernel,
        grid=(channels // BLK,),
        in_specs=[
            wide, wide, line, wide, line, wide, square,
            pl.BlockSpec((cp.shape[0], BLK), lambda i: (0, i)),
            pl.BlockSpec(starts.shape, lambda i: (0, 0, 0)),
        ],
        out_specs=[wide, square, pl.BlockSpec((8, BLK), lambda i: (0, i))],
        out_shape=[
            jax.ShapeDtypeStruct(u.shape, BF16),
            jax.ShapeDtypeStruct((channels, 2 * BLK), F32),
            jax.ShapeDtypeStruct((8, channels), F32),
        ],
        compiler_params=pltpu.CompilerParams(vmem_limit_bytes=40 << 20),
        cost_estimate=pl.CostEstimate(flops=12 * 10**8, bytes_accessed=9 * 10**6, transcendentals=2 * 10**6),
        name="gates_back",
    )(lam, coef, inc, h, h_in, u, weights, cp, starts)


def nt(left, right):
    return lax.dot_general(left, right, (((1,), (1,)), ((), ())), preferred_element_type=F32)


def nn(left, right):
    return jnp.dot(left, right, preferred_element_type=F32)


def body(
    dp_size,
    layer_input, grad_out, lengths, resets, norm_gain, w_x, w_y, conv_w, conv_b, gate_a_w, gate_a_b,
    gate_i_w, gate_i_b, decay_param, w_out, mlp_gain, w_gate, w_up, w_down,
):
    n = dp_size // 2
    half = n // 2
    dp, x = lax.axis_index("dp"), lax.axis_index("tp")
    chip, core = dp // 2, dp % 2
    pos = place_of(chip, n)
    tokens, width = layer_input.shape[1], layer_input.shape[2]
    rec = w_x.shape[1]
    rh = rec // 2
    taps = conv_w.shape[0]
    own = rec // (2 * dp_size)
    own_d = width // (2 * dp_size)

    ring = [chip_at(i, n) for i in range(n)]
    up = [(ring[i] * 2 + c, ring[(i + 1) % n] * 2 + c) for i in range(n) for c in range(2)]
    down = [(b, a) for a, b in up]
    lanes = [[chip_id * 2 + c for chip_id in ring] for c in range(2)]
    pairs = [(d, d + 1 - 2 * (d % 2)) for d in range(dp_size)]

    def sibling(v):
        return lax.ppermute(v, "dp", pairs)

    def across(v):
        return lax.ppermute(v, "tp", [(0, 1), (1, 0)])

    def swapped(v):
        return jnp.concatenate([v[1:], v[:1]], axis=0)

    def by_core(mine, theirs, axis):
        return jnp.where(
            core == 0, jnp.concatenate([mine, theirs], axis), jnp.concatenate([theirs, mine], axis)
        )

    def ring_order(array, axis):
        size = array.shape[axis] // n
        return jnp.concatenate([lax.slice_in_dim(array, i * size, (i + 1) * size, axis=axis) for i in ring], axis)

    def chip_order(array, axis):
        size = array.shape[axis] // n
        return jnp.concatenate(
            [lax.slice_in_dim(array, ring.index(i) * size, (ring.index(i) + 1) * size, axis=axis) for i in range(n)],
            axis,
        )

    def after(value, *others):
        return lax.optimization_barrier((value,) + others)[0]

    rows_own = layer_input.reshape(tokens, width)
    place = x * tokens + jnp.arange(tokens, dtype=jnp.int32)
    starts = jnp.where((resets.reshape(tokens) > 0) | (place == 0), 1.0, 0.0).astype(F32)
    starts = jnp.broadcast_to(starts[:, None], (tokens, 128))
    valid = (place < lengths[0]).astype(F32)[:, None]
    cot = grad_out.reshape(tokens, width).astype(F32) * valid

    small = jnp.concatenate(
        [norm_gain, mlp_gain, conv_w.reshape(-1), conv_b, gate_a_b, gate_i_b, decay_param]
    )
    small = jnp.pad(small, (0, PAD * WIDE - small.shape[0])).reshape(PAD, WIDE)
    gs = jnp.concatenate([jnp.concatenate([gate_a_w, gate_i_w], axis=1), small], axis=0)
    w_xy, w_o, all_gs, w_gu, d_block, rows_two, cot_all, starts_two = gather_weights(
        n, w_x, w_y, w_out, gs, w_gate, w_up, w_down.T, rows_own, ring_order(cot.astype(BF16), 1), starts
    )
    w_d = lax.all_gather(
        d_block.reshape(-1, d_block.shape[2]), "dp", axis=0, tiled=True, axis_index_groups=lanes
    )
    w_gu = w_gu.reshape(width, w_gate.shape[1])
    w_xy = w_xy.reshape(width, rec)
    w_o = w_o.reshape(rec, width // 2)
    def lane_sum(array):
        return lax.psum_scatter(array, "dp", scatter_dimension=0, tiled=True, axis_index_groups=lanes)

    cot_all = cot_all.reshape(4 * tokens, width)

    vectors = all_gs[:, :, :, own:].transpose(1, 0, 2, 3, 4).reshape(2 * dp_size, PAD * WIDE)
    gain_one = vectors[:, :own_d].reshape(width).astype(F32)
    gain_two = vectors[:, own_d : 2 * own_d].reshape(width).astype(F32)
    lines = vectors[:, 2 * own_d : 2 * own_d + (taps + 4) * own].reshape(2 * dp_size, taps + 4, own)
    lines = lax.dynamic_slice_in_dim(lines, core * dp_size, dp_size, 0)
    lines = lines.transpose(1, 0, 2).reshape(taps + 4, rh).astype(F32)
    decay = lines[taps + 3 :]
    cp = jnp.concatenate(
        [lines[: taps + 3], jax.nn.softplus(-decay), jax.nn.sigmoid(-decay), jnp.zeros((7, rh), F32)], axis=0
    )
    gates = lax.dynamic_slice_in_dim(all_gs[:, :, :, :own], core * half, half, 1)
    gates = gates.transpose(1, 0, 2, 3, 4).reshape(rh, WIDE)

    n1, xb, ypre = project(rows_two, gain_one[None], w_xy)
    before = lax.ppermute(xb[:, tokens - (taps - 1) :], "tp", [(0, 1)])
    halo = jnp.concatenate([jnp.zeros((2, 8 - (taps - 1), rh), F32), before.astype(F32)], axis=1)
    u, a, h_local, coef = recurrence(xb, halo, gates, cp, starts_two)
    h_in = lax.ppermute(h_local[:, tokens - 1 :], "tp", [(0, 1)])
    h = h_local + coef * h_in
    ybr, _ = gelu_parts(ypre)
    o = (h * ybr).astype(BF16)
    o_sib = sibling(o)
    part_mine, part_theirs = project_out(o, o_sib, w_o)
    x1 = rows_own.astype(F32) + by_core(part_mine, sibling(part_theirs), 1)
    rs2 = lax.rsqrt(jnp.mean(x1 * x1, axis=-1, keepdims=True) + EPS)
    n2 = (x1 * rs2 * gain_two).astype(BF16)
    def plane(array, which):
        return lax.dynamic_index_in_dim(array, which, 2, keepdims=False)

    def both(mine, axis):
        return jnp.concatenate([mine, across(mine)], axis)

    n2_x = across(n2)

    def plane_rows(values, rows):
        grouped = after(values, n2_x).T.reshape(n, 2, 2, rows, 2 * tokens)
        return plane(grouped, x), plane(grouped, 1 - x)

    o_here, o_send = plane_rows(jnp.concatenate([o, swapped(o_sib)], axis=2).reshape(2 * tokens, rec), own)
    n1_here, n1_send = plane_rows(n1, own_d)
    two = jnp.concatenate([n2, n2_x], axis=0)
    n2_all = jnp.concatenate([two, sibling(two)], axis=0)
    o_t = jnp.concatenate([o_here, across(o_send)], axis=3).reshape(rh, 4 * tokens)
    n1_t = jnp.concatenate([n1_here, across(n1_send)], axis=3).reshape(width // 2, 4 * tokens)

    fh = w_d.shape[1]
    gu = nn(n2_all, w_gu)
    gate, upv = gu[:, :fh], gu[:, fh:]
    act, slope = gelu_parts(gate)
    hidden = (act * upv).astype(BF16)

    def tn(left, right):
        return lax.dot_general(left, right, (((0,), (0,)), ((), ())), preferred_element_type=F32)

    part_d = tn(cot_all, hidden).astype(BF16)
    sum_d = lane_sum(part_d)
    d_hidden = nn(after(cot_all, part_d), w_d)
    d_gu = jnp.concatenate([(d_hidden * upv * slope).astype(BF16), (d_hidden * act).astype(BF16)], axis=1)

    def pair_sum(partial):
        return (partial[: 2 * tokens].astype(F32) + sibling(partial[2 * tokens :]).astype(F32)).astype(BF16)

    d_n2_pair = pair_sum(nt(d_gu, w_gu).astype(BF16))
    d_n2_send = d_n2_pair[tokens:]
    d_n2 = d_n2_pair[:tokens].astype(F32) + across(d_n2_send).astype(F32)
    part_gu = tn(ring_order(n2_all, 1), after(d_gu, d_n2_send)).astype(BF16)
    sum_gu = lane_sum(part_gu)
    ff_pair = pair_sum(nt(after(hidden, part_gu), w_d).astype(BF16))
    ff_out = ff_pair[:tokens].astype(F32) + across(ff_pair[tokens:]).astype(F32)

    q2 = gain_two * d_n2
    d_gain_two = jnp.sum(d_n2 * x1 * rs2, axis=0)
    d_x1 = cot + rs2 * q2 - x1 * (rs2 * rs2 * rs2) * jnp.mean(x1 * q2, axis=-1, keepdims=True)
    dbr = d_x1.astype(BF16)
    dbr_mine = lax.dynamic_slice_in_dim(dbr, core * (width // 2), width // 2, 1)
    dbr_theirs = lax.dynamic_slice_in_dim(dbr, (1 - core) * (width // 2), width // 2, 1)
    dbr_half = jnp.concatenate([dbr_mine, sibling(dbr_theirs)], axis=0)
    do_part = nt(dbr_half, w_o)
    do = do_part[:, :rh].reshape(2, tokens, rh) + swapped(sibling(do_part[:, rh:].reshape(2, tokens, rh)))
    dbr_x = across(dbr_half)

    d_ypre, lam_local, coef_back = adjoint(do, h, ypre, a)
    d_ypre_x = both(d_ypre.reshape(2 * tokens, rh), 0)
    inc = lax.ppermute(a[:, :1] * lam_local[:, :1], "tp", [(1, 0)])
    du, d_gates, sums = gates_back(lam_local, coef_back, inc, h, h_in, u, gates, cp, starts_two)
    du_next = lax.ppermute(du[:, : taps - 1], "tp", [(1, 0)])
    du_pad = jnp.concatenate([du, du_next], axis=1).astype(F32)
    xb_pad = jnp.concatenate([before, xb], axis=1).astype(F32)
    d_taps = jnp.stack(
        [jnp.sum(du_pad[:, :tokens] * xb_pad[:, taps - 1 - k : taps - 1 - k + tokens], axis=(0, 1)) for k in range(taps)]
    )
    d_bias = jnp.sum(du_pad[:, :tokens], axis=(0, 1))[None]
    d_xb = sum(cp[k] * du_pad[:, k : k + tokens] for k in range(taps)).astype(BF16)
    d_xy = jnp.concatenate([d_xb, d_ypre], axis=2).reshape(2 * tokens, rec)
    result = (after(x1, d_xb) + chip_order(ff_out, 1)).astype(BF16).reshape(1, tokens, width)
    d_n1_part = nt(d_xy, w_xy).reshape(2, tokens, width)
    d_n1 = d_n1_part[0] + sibling(d_n1_part[1])
    q1 = gain_one * d_n1
    own_f = rows_own.astype(F32)
    own_rs = lax.rsqrt(jnp.mean(own_f * own_f, axis=-1, keepdims=True) + EPS)
    d_gain_one = jnp.sum(d_n1 * own_f * own_rs, axis=0)
    grad_x = d_x1 + own_rs * q1 - own_f * (own_rs * own_rs * own_rs) * jnp.mean(own_f * q1, axis=-1, keepdims=True)

    c_out = nn(after(o_t, d_xb), jnp.concatenate([dbr_half, dbr_x], axis=0)).astype(BF16).reshape(n, 2, own, width // 2)
    c_x = nn(n1_t, both(d_xb.reshape(2 * tokens, rh), 0)).astype(BF16).reshape(n, 2, own_d, rh)
    c_y = nn(n1_t, d_ypre_x).astype(BF16).reshape(n, 2, own_d, rh)

    def placed(part):
        zero = jnp.zeros_like(part)
        return by_core_rows(part, zero)

    def by_core_rows(mine, theirs):
        return jnp.where(
            core == 0, jnp.concatenate([mine, theirs], 0), jnp.concatenate([theirs, mine], 0)
        )

    g = d_gates.reshape(half, 2, 2, own, WIDE)
    g = plane(g, x) + across(plane(g, 1 - x).astype(BF16)).astype(F32)
    g_mine = lax.dynamic_index_in_dim(g, core, 1, keepdims=False)
    g_theirs = lax.dynamic_index_in_dim(g, 1 - core, 1, keepdims=False)
    g_lane = by_core_rows(g_mine, sibling(g_theirs))

    lines_back = jnp.concatenate([d_taps, d_bias, sums[:3]], axis=0)
    lines_back = lines_back.reshape(taps + 4, half, 2, 2, own).transpose(1, 2, 3, 0, 4)
    lines_back = placed(lines_back.reshape(half, 2, 2, (taps + 4) * own))
    gains = jnp.concatenate([d_gain_one.reshape(n, 2, 2, own_d), d_gain_two.reshape(n, 2, 2, own_d)], axis=3)
    vec = jnp.concatenate([gains, lines_back], axis=3)
    vec = jnp.pad(vec, ((0, 0), (0, 0), (0, 0), (0, -vec.shape[3] % 128)))
    vec = plane(vec, x) + across(plane(vec, 1 - x))
    vec = lax.dynamic_index_in_dim(vec, core, 1, keepdims=False) + sibling(
        lax.dynamic_index_in_dim(vec, 1 - core, 1, keepdims=False)
    )

    vec = jnp.pad(vec, ((0, 0), (0, -vec.shape[1] % 1024))).reshape(n, -1, 128)
    def whole(block):
        rows = block.shape[0] // 2
        block = block.reshape(2, rows, block.shape[1])
        mine = lax.dynamic_index_in_dim(block, core, 0, keepdims=False)
        theirs = lax.dynamic_index_in_dim(block, 1 - core, 0, keepdims=False)
        return mine, sibling(theirs)

    def halves(pair):
        return by_core(pair[0], pair[1], 1).astype(F32)

    grad_down = halves(whole(sum_d)).T
    grad_w_x, grad_w_y, grad_w_out, sum_gates, sum_vec = scatter_sums(
        n, after(c_x, grad_down, result, grad_x), c_y, c_out, g_lane.astype(BF16), vec
    )
    sum_vec = sum_vec.reshape(-1)
    gu_mine, gu_theirs = whole(sum_gu)
    grad_gate = halves((gu_mine[:, :fh], gu_theirs[:, :fh]))
    grad_up = halves((gu_mine[:, fh:], gu_theirs[:, fh:]))
    tail = sum_vec[2 * own_d : 2 * own_d + (taps + 4) * own].reshape(taps + 4, own)
    return (
        result,
        grad_x.reshape(1, tokens, width),
        sum_vec[:own_d],
        grad_w_x,
        grad_w_y,
        tail[:taps],
        tail[taps],
        sum_gates[:, :BLK],
        tail[taps + 1],
        sum_gates[:, BLK:],
        tail[taps + 2],
        tail[taps + 3],
        grad_w_out,
        sum_vec[own_d : 2 * own_d],
        grad_gate,
        grad_up,
        grad_down,
    )


def solution(mesh):
    every = ("dp", "tp")
    return jax.shard_map(
        functools.partial(body, mesh.shape["dp"]),
        mesh=mesh,
        in_specs=(
            P("dp", "tp", None),
            P("dp", "tp", None),
            P("dp"),
            P("dp", "tp"),
            P(every),
            P(every, None),
            P(every, None),
            P(None, every),
            P(every),
            P(every, None),
            P(every),
            P(every, None),
            P(every),
            P(every),
            P(every, None),
            P(every),
            P("dp", "tp"),
            P("dp", "tp"),
            P("tp", "dp"),
        ),
        out_specs=(
            P("dp", "tp", None),
            P("dp", "tp", None),
            P(every),
            P(every, None),
            P(every, None),
            P(None, every),
            P(every),
            P(every, None),
            P(every),
            P(every, None),
            P(every),
            P(every),
            P(every, None),
            P(every),
            P("dp", "tp"),
            P("dp", "tp"),
            P("tp", "dp"),
        ),
        check_vma=False,
    )
```

```python
import functools

import jax
import jax.numpy as jnp
from jax import lax
from jax.experimental import pallas as pl
from jax.experimental.pallas import tpu as pltpu
from jax.sharding import PartitionSpec as P

BLK = 256
PAD = 16
WIDE = 512
EPS = 1e-06
MESH = pl.DeviceIdType.MESH
F32 = jnp.float32
BF16 = jnp.bfloat16


def chip_at(pos, n):
    back = pos // (n // 2)
    return (1 - back) * (2 * pos) + back * (2 * (n - 1 - pos) + 1)


def place_of(chip, n):
    odd = chip % 2
    return (1 - odd) * (chip // 2) + odd * (n - 1 - chip // 2)


def heads_first(chip, core, n):
    return (chip + n - core * (n // 2)) % n


class Copies:
    def __init__(self, local, sends, recvs):
        self.local, self.sends, self.recvs = local, sends, recvs
        self.locals_used = self.used = 0

    def stay(self, src, dst):
        copy = pltpu.make_async_copy(src, dst, self.local.at[self.locals_used])
        self.locals_used += 1
        copy.start()
        return copy

    def send(self, src, dst, device):
        copy = pltpu.make_async_remote_copy(
            src_ref=src, dst_ref=dst, send_sem=self.sends.at[self.used], recv_sem=self.recvs.at[self.used],
            device_id=device, device_id_type=MESH,
        )
        self.used += 1
        copy.start()
        return copy


def greet(devices):
    barrier = pltpu.get_barrier_semaphore()
    for device in devices:
        pl.semaphore_signal(barrier, inc=1, device_id=device, device_id_type=MESH)
    pl.semaphore_wait(barrier, len(devices))


def half_cols(ref, which):
    width = ref.shape[1] // 2
    return ref.at[:, pl.ds(pl.multiple_of(which * width, 128), width)]


def gather_kernel(
    n,
    wx, wy, wo, gs, wg, wu, wd, rows_in, cot, starts,
    o_xy, o_out, o_gs, o_gu, o_d, o_rows, o_cot, o_starts,
    local_sem, send_sem, recv_sem,
):
    dp, x = lax.axis_index("dp"), lax.axis_index("tp")
    chip, core = dp // 2, dp % 2
    other = 1 - core
    pos = place_of(chip, n)
    half = n // 2
    nxt = (chip_at((pos + 1) % n, n) * 2 + core, x)
    prv = (chip_at((pos + n - 1) % n, n) * 2 + core, x)
    sib = (chip * 2 + other, x)
    over = (dp, 1 - x)
    greet([nxt, prv, sib, over])
    copies = Copies(local_sem, send_sem, recv_sem)
    send, stay = copies.send, copies.stay

    def by_heads(chip_id, which):
        return heads_first(chip_id, which, n)

    rhalf = wx.shape[1] // 2
    fhalf = wg.shape[1] // 2
    rec_parts = [
        (wx, o_xy.at[chip, core, x, :, pl.ds(0, rhalf)]),
        (wy, o_xy.at[chip, core, x, :, pl.ds(rhalf, rhalf)]),
    ]
    ff_parts = [
        (wg, o_gu.at[chip, core, :, pl.ds(0, fhalf)]),
        (wu, o_gu.at[chip, core, :, pl.ds(fhalf, fhalf)]),
        (wd, o_d.at[core]),
    ]
    pair = [send(half_cols(src, other), slot, sib) for src, slot in rec_parts]
    pair.append(send(half_cols(wo, other), o_out.at[by_heads(chip, other), core, x], sib))
    mine = [stay(half_cols(src, core), slot) for src, slot in rec_parts] + [stay(gs, o_gs.at[core, chip, x])]
    mine.append(stay(half_cols(wo, core), o_out.at[by_heads(chip, core), core, x]))
    late = [send(half_cols(src, other), slot, sib) for src, slot in ff_parts]
    plain = [stay(half_cols(src, core), slot) for src, slot in ff_parts]
    late += [send(rows_in, o_rows.at[1], sib), send(starts, o_starts.at[1], sib), send(cot, o_cot.at[2], sib)]
    plain += [stay(rows_in, o_rows.at[0]), stay(starts, o_starts.at[0]), stay(cot, o_cot.at[0])]

    def rec_block(chip_id):
        return [o_xy.at[chip_id, :, x], o_out.at[by_heads(chip_id, core), :, x], o_gs.at[core, chip_id, x]]

    def rec_piece(chip_id, which):
        refs = [o_xy.at[chip_id, which, x], o_out.at[by_heads(chip_id, core), which, x]]
        return refs + ([o_gs.at[core, chip_id, x]] if which == 0 else [])

    def ff_block(chip_id):
        return [o_gu.at[chip_id]]

    def ff_piece(chip_id, which):
        return [o_gu.at[chip_id, which]]

    def send_all(refs, device):
        return [send(ref, ref, device) for ref in refs]

    def hop(s, block, piece):
        ahead = chip_at((pos + n - (s - 1)) % n, n)
        behind = chip_at((pos + s - 1) % n, n)
        if s < half:
            return send_all(block(ahead), nxt) + send_all(block(behind), prv)
        return send_all(piece(ahead, 0), nxt) + send_all(piece(behind, 1), prv)

    for copy in pair:
        copy.wait_recv()
    for copy in mine:
        copy.wait()
    done, crossed, moving = [], send_all(rec_block(chip), over), []
    for s in range(1, half + 1):
        for copy in moving:
            copy.wait_recv()
        done.extend(moving)
        moving = hop(s, rec_block, rec_piece)
        if s > 1:
            crossed.extend(send_all(rec_block(chip_at((pos + n - (s - 1)) % n, n)), over))
            crossed.extend(send_all(rec_block(chip_at((pos + s - 1) % n, n)), over))
    last_rec = moving
    for copy in late:
        copy.wait_recv()
    for copy in plain:
        copy.wait()
    moving = hop(1, ff_block, ff_piece)
    for copy in last_rec:
        copy.wait_recv()
    done.extend(last_rec)
    crossed.extend(send_all(rec_block(chip_at((pos + half) % n, n)), over))
    cot_over = send(cot, o_cot.at[1], over)
    for s in range(2, half + 1):
        for copy in moving:
            copy.wait_recv()
        done.extend(moving)
        moving = hop(s, ff_block, ff_piece)
    for copy in crossed:
        copy.wait_recv()
    swap = send(o_gs.at[core], o_gs.at[core], sib)
    cot_over.wait_recv()
    last = send(o_cot.at[1], o_cot.at[3], sib)
    for copy in moving:
        copy.wait_recv()
    done.extend(moving)
    swap.wait_recv()
    last.wait_recv()
    for copy in pair + late + done + crossed + [cot_over, swap, last]:
        copy.wait_send()


def gather_weights(n, wx, wy, wo, gs, wg, wu, wd, rows_in, cot, starts):
    r, d, (rows_f, f) = wx.shape[1], wo.shape[1], wg.shape
    tokens = rows_in.shape[0]
    shapes = [
        jax.ShapeDtypeStruct((n, 2, 2, wx.shape[0], r), BF16),
        jax.ShapeDtypeStruct((n, 2, 2, wo.shape[0], d // 2), BF16),
        jax.ShapeDtypeStruct((2, n, 2) + gs.shape, BF16),
        jax.ShapeDtypeStruct((n, 2, rows_f, f), BF16),
        jax.ShapeDtypeStruct((2, rows_f, f // 2), BF16),
        jax.ShapeDtypeStruct((2, tokens, d), BF16),
        jax.ShapeDtypeStruct((4, tokens, d), BF16),
        jax.ShapeDtypeStruct((2,) + starts.shape, F32),
    ]
    count = 9 + (3 * n - 1) + n + 3 * n + 3
    dma = pltpu.SemaphoreType.DMA
    return pl.pallas_call(
        functools.partial(gather_kernel, n),
        out_shape=shapes,
        in_specs=[pl.BlockSpec(memory_space=pltpu.VMEM)] * 10,
        out_specs=[pl.BlockSpec(memory_space=pl.ANY)] * 8,
        scratch_shapes=[dma((10,)), dma((count,)), dma((count,))],
        compiler_params=pltpu.CompilerParams(
            collective_id=0, has_side_effects=True, vmem_limit_bytes=24 << 20
        ),
        name="gather_weights",
    )(wx, wy, wo, gs, wg, wu, wd, rows_in, cot, starts)


def scatter_kernel(
    n,
    c_x, c_y, c_out, c_g, c_v,
    g_x, g_y, g_out, g_gates, g_vec,
    r_x, r_y, r_out, r_g, r_v, s_x, s_y, s_out,
    send_sem, recv_sem,
):
    dp, x = lax.axis_index("dp"), lax.axis_index("tp")
    chip, core = dp // 2, dp % 2
    pos = place_of(chip, n)
    half = n // 2
    nxt = (chip_at((pos + 1) % n, n) * 2 + core, x)
    prv = (chip_at((pos + n - 1) % n, n) * 2 + core, x)
    sib = (dp + 1 - 2 * core, x)
    greet([nxt, prv, sib])
    copies = Copies(None, send_sem, recv_sem)

    pieces = []
    for part in (0, 1):
        for terms, slots, first in ((c_out, r_out, core), (c_y, r_y, 0), (c_x, r_x, 0)):
            pieces.append((
                lambda c, terms=terms, part=part, first=first: terms.at[heads_first(c, first, n), part],
                lambda w, k, slots=slots, part=part: slots.at[part, w, k],
                part,
            ))
    pieces.append((lambda c: c_g.at[c], lambda w, k: r_g.at[w, k], 0))
    pieces.append((lambda c: c_v.at[c], lambda w, k: r_v.at[w, k], 1))

    def add(a, b):
        return a[...].astype(F32) + b[...].astype(F32)

    sent, coming = [], {}
    for k in range(half, -1, -1):
        for i, (term, slot, far) in enumerate(pieces):
            for way, (device, sign) in enumerate(((nxt, 1), (prv, n - 1))):
                first = half if way == far else half - 1
                if k > first or k == 0:
                    continue
                source = term(chip_at((pos + sign * k) % n, n))
                if k < first:
                    coming[i, way].wait_recv()
                    got = slot(way, k)
                    got[...] = add(got, source).astype(got.dtype)
                    source = got
                copy = copies.send(source, slot(way, k - 1), device)
                coming[i, way] = copy
                sent.append(copy)

    def total(i):
        term, slot, _ = pieces[i]
        for way in (0, 1):
            coming[i, way].wait_recv()
        return add(term(chip), slot(0, 0)) + slot(1, 0)[...].astype(F32)

    def cols(ref):
        width = ref.shape[1] // 2
        return pl.ds(pl.multiple_of(core * width, 128), width)

    results = ((g_out, s_out), (g_y, s_y), (g_x, s_x))
    for part in (0, 1):
        sums = [total(3 * part + i) for i in range(3)]

        @pl.when(core == part)
        def _():
            for value, (ref, _) in zip(sums, results):
                ref[:, cols(ref)] = value

        @pl.when(core != part)
        def _():
            for value, (_, ref) in zip(sums, results):
                ref[...] = value

    final = [copies.send(src, ref.at[:, cols(ref)], sib) for ref, src in results]
    g_gates[...] = total(6)
    g_vec[...] = total(7)
    for copy in final:
        copy.wait_recv()
    for copy in sent + final:
        copy.wait_send()


def scatter_sums(n, c_x, c_y, c_out, c_g, c_v):
    _, _, rows_d, rhalf = c_x.shape
    _, _, rows_r, dhalf = c_out.shape
    half = n // 2
    count = 8 * (2 * half - 1) + 3
    dma = pltpu.SemaphoreType.DMA
    vmem = pl.BlockSpec(memory_space=pltpu.VMEM)
    return pl.pallas_call(
        functools.partial(scatter_kernel, n),
        out_shape=[
            jax.ShapeDtypeStruct((rows_d, 2 * rhalf), F32),
            jax.ShapeDtypeStruct((rows_d, 2 * rhalf), F32),
            jax.ShapeDtypeStruct((rows_r, 2 * dhalf), F32),
            jax.ShapeDtypeStruct(c_g.shape[1:], F32),
            jax.ShapeDtypeStruct(c_v.shape[1:], F32),
        ],
        in_specs=[vmem] * 5,
        out_specs=[vmem] * 5,
        scratch_shapes=[
            pltpu.VMEM((2, 2, half, rows_d, rhalf), BF16),
            pltpu.VMEM((2, 2, half, rows_d, rhalf), BF16),
            pltpu.VMEM((2, 2, half, rows_r, dhalf), BF16),
            pltpu.VMEM((2, half) + c_g.shape[1:], BF16),
            pltpu.VMEM((2, half) + c_v.shape[1:], F32),
            pltpu.VMEM((rows_d, rhalf), F32),
            pltpu.VMEM((rows_d, rhalf), F32),
            pltpu.VMEM((rows_r, dhalf), F32),
            dma((count,)), dma((count,)),
        ],
        compiler_params=pltpu.CompilerParams(
            collective_id=1, has_side_effects=True, vmem_limit_bytes=56 << 20
        ),
        name="scatter_sums",
    )(c_x, c_y, c_out, c_g, c_v)


def project_kernel(steps, rows, gain, w, n1_ref, x_ref, y_ref):
    i = pl.program_id(0)

    @pl.when(i == 0)
    def _():
        values = rows[...].astype(F32)
        scale = lax.rsqrt(jnp.mean(values * values, axis=-1, keepdims=True) + EPS)
        n1_ref[...] = (values * scale * gain[...]).astype(BF16).reshape(n1_ref.shape)

    result = jnp.dot(n1_ref[...], w[...], preferred_element_type=F32).reshape(y_ref.shape)

    @pl.when(i < steps)
    def _():
        x_ref[...] = result.astype(BF16)

    @pl.when(i >= steps)
    def _():
        y_ref[...] = result


def project(rows, gain, w):
    _, tokens, width = rows.shape
    rh = w.shape[1] // 2
    steps = rh // BLK
    return pl.pallas_call(
        functools.partial(project_kernel, steps),
        grid=(2 * steps,),
        in_specs=[
            pl.BlockSpec(rows.shape, lambda i: (0, 0, 0)),
            pl.BlockSpec((1, width), lambda i: (0, 0)),
            pl.BlockSpec((width, BLK), lambda i: (0, i)),
        ],
        out_specs=[
            pl.BlockSpec((2 * tokens, width), lambda i: (0, 0)),
            pl.BlockSpec((2, tokens, BLK), lambda i: (0, 0, jnp.minimum(i, steps - 1))),
            pl.BlockSpec((2, tokens, BLK), lambda i: (0, 0, jnp.maximum(i - steps, 0))),
        ],
        out_shape=[
            jax.ShapeDtypeStruct((2 * tokens, width), BF16),
            jax.ShapeDtypeStruct((2, tokens, rh), BF16),
            jax.ShapeDtypeStruct((2, tokens, rh), F32),
        ],
        compiler_params=pltpu.CompilerParams(vmem_limit_bytes=40 << 20),
        cost_estimate=pl.CostEstimate(flops=27 * 10**8, bytes_accessed=15 * 10**6, transcendentals=0),
        name="project",
    )(rows, gain, w)


def project_out_kernel(o, o_sib, w, mine_ref, theirs_ref):
    rh = o.shape[2]
    for row, ref in ((0, mine_ref), (1, theirs_ref)):
        ref[...] = jnp.dot(o[row], w[:rh], preferred_element_type=F32) + jnp.dot(
            o_sib[1 - row], w[rh:], preferred_element_type=F32
        )


def project_out(o, o_sib, w):
    _, tokens, rh = o.shape
    cols = w.shape[1]
    tile = min(BLK, cols)
    whole = pl.BlockSpec(o.shape, lambda i: (0, 0, 0))
    part = pl.BlockSpec((tokens, tile), lambda i: (0, i))
    return pl.pallas_call(
        project_out_kernel,
        grid=(cols // tile,),
        in_specs=[whole, whole, pl.BlockSpec((2 * rh, tile), lambda i: (0, i))],
        out_specs=[part, part],
        out_shape=[jax.ShapeDtypeStruct((tokens, cols), F32)] * 2,
        compiler_params=pltpu.CompilerParams(vmem_limit_bytes=40 << 20),
        cost_estimate=pl.CostEstimate(flops=14 * 10**8, bytes_accessed=8 * 10**6, transcendentals=0),
        name="project_out",
    )(o, o_sib, w)


def minus_expm1(v):
    series = jnp.ones_like(v)
    for k in range(9, 1, -1):
        series = 1.0 + series * v * (1.0 / k)
    return jnp.where(v > -0.5, -v * series, 1.0 - jnp.exp(v))


def gates_of(u, weights, cp, start):
    tokens = u.shape[0] * u.shape[1]
    flat = u.reshape(tokens, BLK)
    z = jnp.dot(flat, weights, preferred_element_type=F32)
    r = jax.nn.sigmoid(z[:, :BLK] + cp[5:6]).reshape(u.shape)
    ig = jax.nn.sigmoid(z[:, BLK:] + cp[6:7]).reshape(u.shape)
    la = -8.0 * r * cp[7:8][None]
    decayed = jnp.exp(la)
    rest = minus_expm1(2.0 * la)
    return r, ig, decayed, rest


def recurrence_kernel(xb, halo, weights, cp, starts, u_ref, a_ref, h_ref, c_ref, b_ref):
    rows, length = xb.shape[0], xb.shape[1]
    p = cp[...]
    us = []
    for row in range(rows):
        padded = jnp.concatenate([halo[row], xb[row].astype(F32)], axis=0)
        total = p[4:5] + p[0:1] * padded[8 : 8 + length]
        for k in range(1, 4):
            total = total + p[k : k + 1] * padded[8 - k : 8 - k + length]
        us.append(total.astype(BF16))
    u = jnp.stack(us)
    u_ref[...] = u
    start = starts[...]
    start = jnp.concatenate([start, start], axis=2)
    r, ig, decayed, rest = gates_of(u, weights[...], p, start)
    a_ref[...] = decayed * (1.0 - start)
    b_ref[...] = jnp.where(start > 0.5, 1.0, jnp.sqrt(rest)) * ig * u.astype(F32)

    def eight(i, carry):
        at = pl.ds(pl.multiple_of(i * 8, 8), 8)
        out = []
        for row in range(rows):
            h, c = carry[row]
            a, b = a_ref[row, at, :], b_ref[row, at, :]
            hs, cs = [], []
            for j in range(8):
                h = a[j : j + 1] * h + b[j : j + 1]
                c = a[j : j + 1] * c
                hs.append(h)
                cs.append(c)
            h_ref[row, at, :] = jnp.concatenate(hs, axis=0)
            c_ref[row, at, :] = jnp.concatenate(cs, axis=0)
            out.append((h, c))
        return tuple(out)

    zero, one = jnp.zeros((1, BLK), F32), jnp.ones((1, BLK), F32)
    lax.fori_loop(0, length // 8, eight, ((zero, one),) * rows)


def recurrence(xb, halo, weights, cp, starts):
    rows, length, channels = xb.shape
    wide = pl.BlockSpec((rows, length, BLK), lambda h: (0, 0, h))
    return pl.pallas_call(
        recurrence_kernel,
        grid=(channels // BLK,),
        in_specs=[
            wide,
            pl.BlockSpec((rows, 8, BLK), lambda h: (0, 0, h)),
            pl.BlockSpec((BLK, 2 * BLK), lambda h: (h, 0)),
            pl.BlockSpec((cp.shape[0], BLK), lambda h: (0, h)),
            pl.BlockSpec(starts.shape, lambda h: (0, 0, 0)),
        ],
        out_specs=[wide] * 4,
        out_shape=[jax.ShapeDtypeStruct(xb.shape, BF16)] + [jax.ShapeDtypeStruct(xb.shape, F32)] * 3,
        scratch_shapes=[pltpu.VMEM((rows, length, BLK), F32)],
        compiler_params=pltpu.CompilerParams(vmem_limit_bytes=40 << 20),
        cost_estimate=pl.CostEstimate(flops=4 * 10**8, bytes_accessed=6 * 10**6, transcendentals=2 * 10**6),
        name="recurrence",
    )(xb, halo, weights, cp, starts)


def gelu_parts(v):
    inner = 0.7978845608028654 * (v + 0.044715 * v * v * v)
    t = jnp.tanh(inner)
    value = 0.5 * v * (1.0 + t)
    slope = 0.5 * (1.0 + t) + 0.5 * v * (1.0 - t * t) * 0.7978845608028654 * (1.0 + 3.0 * 0.044715 * v * v)
    return value, slope


def adjoint_kernel(do, h_ref, y_ref, a_ref, dy_ref, lam_ref, c_ref, dh_ref):
    rows, length = do.shape[0], do.shape[1]
    value, slope = gelu_parts(y_ref[...])
    dy_ref[...] = (do[...] * h_ref[...] * slope).astype(BF16)
    dh_ref[...] = do[...] * value

    def eight(step, carry):
        i = length // 8 - 1 - step
        at = pl.ds(pl.multiple_of(i * 8, 8), 8)
        out = []
        for row in range(rows):
            ahead, c = carry[row]
            a, d = a_ref[row, at, :], dh_ref[row, at, :]
            ls, cs = [None] * 8, [None] * 8
            for j in range(7, -1, -1):
                lam = d[j : j + 1] + ahead
                ls[j], cs[j] = lam, c
                ahead = a[j : j + 1] * lam
                c = a[j : j + 1] * c
            lam_ref[row, at, :] = jnp.concatenate(ls, axis=0)
            c_ref[row, at, :] = jnp.concatenate(cs, axis=0)
            out.append((ahead, c))
        return tuple(out)

    zero, one = jnp.zeros((1, BLK), F32), jnp.ones((1, BLK), F32)
    lax.fori_loop(0, length // 8, eight, ((zero, one),) * rows)


def adjoint(do, h, ypre, a):
    rows, length, channels = do.shape
    wide = pl.BlockSpec((rows, length, BLK), lambda i: (0, 0, i))
    return pl.pallas_call(
        adjoint_kernel,
        grid=(channels // BLK,),
        in_specs=[wide] * 4,
        out_specs=[wide] * 3,
        out_shape=[jax.ShapeDtypeStruct(do.shape, BF16)] + [jax.ShapeDtypeStruct(do.shape, F32)] * 2,
        scratch_shapes=[pltpu.VMEM((rows, length, BLK), F32)],
        compiler_params=pltpu.CompilerParams(vmem_limit_bytes=40 << 20),
        cost_estimate=pl.CostEstimate(flops=10**7, bytes_accessed=9 * 10**6, transcendentals=10**6),
        name="adjoint",
    )(do, h, ypre, a)


def gates_back_kernel(lam_ref, c_ref, inc, h_ref, h_in, u_ref, weights, cp, starts, du_ref, dw_ref, sums_ref):
    rows, length = u_ref.shape[0], u_ref.shape[1]
    tokens = rows * length
    p = cp[...]
    u = u_ref[...]
    uf = u.astype(F32)
    start = starts[...]
    start = jnp.concatenate([start, start], axis=2)
    w = weights[...]
    r, ig, decayed, rest = gates_of(u, w, p, start)
    mult = jnp.where(start > 0.5, 1.0, jnp.sqrt(rest))
    lam = lam_ref[...] + c_ref[...] * inc[...]
    before = jnp.stack([jnp.concatenate([h_in[row], h_ref[row][: length - 1]], axis=0) for row in range(rows)])
    keep = 1.0 - start
    d_la = lam * before * decayed * keep - jnp.where(
        start > 0.5, 0.0, lam * ig * uf * decayed * decayed * lax.rsqrt(jnp.where(start > 0.5, 1.0, rest))
    )
    dpa = d_la * (-8.0 * p[7:8][None]) * r * (1.0 - r)
    direct = lam * mult
    dpi = direct * uf * ig * (1.0 - ig)
    d_decay = d_la * (8.0 * p[8:9][None]) * r
    dz = jnp.concatenate(
        [dpa.reshape(tokens, BLK).astype(BF16), dpi.reshape(tokens, BLK).astype(BF16)], axis=1
    )
    back = lax.dot_general(dz, w, (((1,), (1,)), ((), ())), preferred_element_type=F32)
    du_ref[...] = (direct * ig + back.reshape(u.shape)).astype(BF16)
    dw_ref[...] = lax.dot_general(
        u.reshape(tokens, BLK), dz, (((0,), (0,)), ((), ())), preferred_element_type=F32
    )
    zero = jnp.zeros((5, BLK), F32)
    sums_ref[...] = jnp.concatenate(
        [jnp.sum(v.reshape(tokens, BLK), axis=0, keepdims=True) for v in (dpa, dpi, d_decay)] + [zero], axis=0
    )


def gates_back(lam, coef, inc, h, h_in, u, weights, cp, starts):
    rows, length, channels = u.shape
    wide = pl.BlockSpec((rows, length, BLK), lambda i: (0, 0, i))
    line = pl.BlockSpec((rows, 1, BLK), lambda i: (0, 0, i))
    square = pl.BlockSpec((BLK, 2 * BLK), lambda i: (i, 0))
    return pl.pallas_call(
        gates_back_kernel,
        grid=(channels // BLK,),
        in_specs=[
            wide, wide, line, wide, line, wide, square,
            pl.BlockSpec((cp.shape[0], BLK), lambda i: (0, i)),
            pl.BlockSpec(starts.shape, lambda i: (0, 0, 0)),
        ],
        out_specs=[wide, square, pl.BlockSpec((8, BLK), lambda i: (0, i))],
        out_shape=[
            jax.ShapeDtypeStruct(u.shape, BF16),
            jax.ShapeDtypeStruct((channels, 2 * BLK), F32),
            jax.ShapeDtypeStruct((8, channels), F32),
        ],
        compiler_params=pltpu.CompilerParams(vmem_limit_bytes=40 << 20),
        cost_estimate=pl.CostEstimate(flops=12 * 10**8, bytes_accessed=9 * 10**6, transcendentals=2 * 10**6),
        name="gates_back",
    )(lam, coef, inc, h, h_in, u, weights, cp, starts)


def log1p_small(e):
    series = jnp.ones_like(e) * (1.0 / 14)
    for k in range(13, 0, -1):
        series = 1.0 / k - e * series
    return jnp.where(e < 0.25, e * series, jnp.log(1.0 + e))


def front_kernel(n, *refs):
    (
        wx, wy, wo, gs, wg, wu, wd, rows_in, cot, starts, spread_r, pick_r, spread_d, pick_d,
        o_xy, o_out, o_gates, o_cp, o_gains, o_gu, o_d, o_cot, o_starts, o_ypre, o_u, o_a, o_h, o_hin, o_xb, o_before,
        o_x1, o_n2, o_n1t, o_ot, o_hidden, o_gate, o_up, o_pd,
        v_xy, v_out, v_gs, v_gates, v_rows, v_cot, v_starts, v_cp, v_gains, v_n1, v_n1t, v_xb, v_ypre, v_halo, v_u, v_a,
        v_b, v_h, v_c, v_carry, v_o, v_osib, v_ot, v_part, v_theirs, v_psib, v_x1, v_n2, v_w, v_hidden, v_gu, v_pd,
        local_sem, send_sem, recv_sem, load_sem, store_sem, pd_sem,
    ) = refs
    dp, x = lax.axis_index("dp"), lax.axis_index("tp")
    chip, core = dp // 2, dp % 2
    other = 1 - core
    pos = place_of(chip, n)
    half = n // 2
    nxt = (chip_at((pos + 1) % n, n) * 2 + core, x)
    prv = (chip_at((pos + n - 1) % n, n) * 2 + core, x)
    sib = (chip * 2 + other, x)
    over = (dp, 1 - x)
    greet([nxt, prv, sib, over])
    copies = Copies(local_sem, send_sem, recv_sem)
    send, stay = copies.send, copies.stay
    tokens, width = rows_in.shape
    rec = wx.shape[1]
    rh = rec // 2
    own, own_d = wo.shape[0], wx.shape[0]
    fh = wg.shape[1] // 2
    kept, every = [], []

    def put(src, dst):
        kept.append(stay(src, dst))

    def give(src, dst, device):
        copy = send(src, dst, device)
        every.append(copy)
        return copy

    def land(group):
        for copy in group:
            copy.wait_recv()

    parts = [(wx, v_xy.at[chip, core, x, :, pl.ds(0, rh)]), (wy, v_xy.at[chip, core, x, :, pl.ds(rh, rh)])]
    pair = [give(half_cols(src, other), slot, sib) for src, slot in parts]
    pair.append(give(half_cols(wo, other), v_out.at[heads_first(chip, other, n), core, x], sib))
    mine = [stay(half_cols(src, core), slot) for src, slot in parts]
    mine.append(stay(half_cols(wo, core), v_out.at[heads_first(chip, core, n), core, x]))
    mine.append(stay(gs, v_gs.at[core, chip, x]))
    parts = [
        (wg, o_gu.at[chip, core, :, pl.ds(0, fh)]),
        (wu, o_gu.at[chip, core, :, pl.ds(fh, fh)]),
        (wd, o_d.at[pos, core]),
    ]
    late = [give(half_cols(src, other), slot, sib) for src, slot in parts]
    plain = [stay(half_cols(src, core), slot) for src, slot in parts]
    late += [give(rows_in, v_rows.at[1], sib), give(starts, v_starts.at[1], sib), give(cot, v_cot.at[2], sib)]
    plain += [stay(rows_in, v_rows.at[0]), stay(starts, v_starts.at[0]), stay(cot, v_cot.at[0])]

    def rec_block(place):
        c = chip_at(place, n)
        return [v_xy.at[c, :, x], v_out.at[heads_first(c, core, n), :, x], v_gs.at[core, c, x]]

    def rec_piece(place, which):
        c = chip_at(place, n)
        refs = [v_xy.at[c, which, x], v_out.at[heads_first(c, core, n), which, x]]
        return refs + ([v_gs.at[core, c, x]] if which == 0 else [])

    def gu_block(place):
        return [o_gu.at[chip_at(place, n)]]

    def gu_piece(place, which):
        return [o_gu.at[chip_at(place, n), which]]

    def d_block(place):
        return [o_d.at[place]]

    def d_piece(place, which):
        return [o_d.at[place, which]]

    def give_all(group, device):
        return [give(ref, ref, device) for ref in group]

    def hop(s, block, piece):
        ahead, behind = (pos + n - (s - 1)) % n, (pos + s - 1) % n
        if s < half:
            return give_all(block(ahead), nxt) + give_all(block(behind), prv)
        return give_all(piece(ahead, 0), nxt) + give_all(piece(behind, 1), prv)

    land(pair)
    for copy in mine:
        copy.wait()
    crossed, moving = give_all(rec_block(pos), over), []
    for s in range(1, half + 1):
        land(moving)
        moving = hop(s, rec_block, rec_piece)
        if s > 1:
            crossed += give_all(rec_block((pos + n - (s - 1)) % n), over)
            crossed += give_all(rec_block((pos + s - 1) % n), over)
    land(late)
    for copy in plain:
        copy.wait()
    gu = hop(1, gu_block, gu_piece)
    land(moving)
    crossed += give_all(rec_block((pos + half) % n), over)
    swap = [give(v_gs.at[core, :, x], v_gs.at[core, :, x], sib)]
    put(v_starts, o_starts)
    for s in range(2, half + 1):
        land(gu)
        gu = hop(s, gu_block, gu_piece)
    down = hop(1, d_block, d_piece)
    land(crossed)
    swap.append(give(v_gs.at[core, :, 1 - x], v_gs.at[core, :, 1 - x], sib))
    put(v_xy, o_xy)
    put(v_out, o_out)
    land(swap)

    small = v_gs[:, :, :, own : own + PAD, :128].reshape(4 * n * PAD, 128)
    spread = jnp.dot(small, spread_r[...], preferred_element_type=F32).reshape(4 * n, PAD, rh)
    lines = jnp.sum(spread[:, :8] * pick_r[...][:, None, :], axis=0)
    decay = lines[7:8]
    e = jnp.exp(-jnp.abs(decay))
    v_cp[0:8, :] = lines
    v_cp[7:8, :] = jnp.maximum(-decay, 0.0) + log1p_small(e)
    v_cp[8:16, :] = jnp.broadcast_to(jax.nn.sigmoid(-decay), (8, rh))
    for i in range(width // WIDE):
        at = pl.ds(i * WIDE, WIDE)
        wide = jnp.dot(small, spread_d[:, at], preferred_element_type=F32).reshape(4 * n, PAD, WIDE)
        v_gains[:, at] = jnp.sum(wide[:, 8:] * pick_d[:, at][:, None, :], axis=0)
    for i in range(2 * n):
        v_gates[i * own : (i + 1) * own, :] = v_gs[(i // 2) % 2, core * half + i // 4, i % 2, 0:own, :]
    put(v_cp, o_cp)
    put(v_gains, o_gains)
    put(v_gates, o_gates)

    values = v_rows[...].astype(F32)
    scale = lax.rsqrt(jnp.mean(values * values, axis=-1, keepdims=True) + EPS)
    v_n1[...] = (values * scale * v_gains[0:1, :]).astype(BF16).reshape(2 * tokens, width)

    def project_x(i, _):
        at = pl.ds(pl.multiple_of(i * BLK, BLK), BLK)
        w = v_xy[:, :, :, :, at].reshape(width, BLK)
        v_xb[:, :, at] = jnp.dot(v_n1[...], w, preferred_element_type=F32).astype(BF16).reshape(2, tokens, BLK)
        return 0

    def project_y(i, _):
        at = pl.ds(pl.multiple_of(i * BLK, BLK), BLK)
        w = v_xy[:, :, :, :, pl.ds(pl.multiple_of(rh + i * BLK, BLK), BLK)].reshape(width, BLK)
        v_ypre[:, :, at] = jnp.dot(v_n1[...], w, preferred_element_type=F32).reshape(2, tokens, BLK)
        return 0

    lax.fori_loop(0, rh // BLK, project_x, 0)
    halo = give(v_xb.at[:, pl.ds(tokens - 16, 16)], v_halo, over)
    put(v_xb, o_xb)
    lax.fori_loop(0, rh // BLK, project_y, 0)
    put(v_ypre, o_ypre)
    chips_n = BLK // (4 * own_d)

    def turn_n1(i, _):
        at = pl.ds(pl.multiple_of(i * BLK, BLK), BLK)
        turned = v_n1[:, at].astype(F32).T.astype(BF16)
        v_n1t[pl.ds(i * chips_n, chips_n)] = turned.reshape(chips_n, 2, 2, own_d, 2 * tokens)
        return 0

    lax.fori_loop(0, width // BLK, turn_n1, 0)
    halo.wait_recv()
    v_halo[...] = jnp.where(x == 0, jnp.zeros_like(v_halo), v_halo[...])
    put(v_halo, o_before)
    n1_over = give(v_n1t.at[:, :, 1 - x], o_n1t.at[:, :, :, pl.ds(2 * tokens, 2 * tokens)], over)
    put(v_n1t.at[:, :, x], o_n1t.at[:, :, :, pl.ds(0, 2 * tokens)])

    def head(i, _):
        at = pl.ds(pl.multiple_of(i * BLK, BLK), BLK)
        p = v_cp[:, at]
        us = []
        for row in range(2):
            padded = jnp.concatenate([v_halo[row, :, at].astype(F32)[8:], v_xb[row, :, at].astype(F32)], axis=0)
            total = p[4:5] + p[0:1] * padded[8 : 8 + tokens]
            for k in range(1, 4):
                total = total + p[k : k + 1] * padded[8 - k : 8 - k + tokens]
            us.append(total.astype(BF16))
        u = jnp.stack(us)
        v_u[:, :, at] = u
        start = v_starts[...]
        start = jnp.concatenate([start, start], axis=2)
        _, ig, decayed, rest = gates_of(u, v_gates[at, :], p, start)
        v_a[:, :, at] = decayed * (1.0 - start)
        v_b[...] = jnp.where(start > 0.5, 1.0, jnp.sqrt(rest)) * ig * u.astype(F32)

        def eight(j, carry):
            rows8 = pl.ds(pl.multiple_of(j * 8, 8), 8)
            out = []
            for row in range(2):
                h, c = carry[row]
                a, b = v_a[row, rows8, at], v_b[row, rows8, :]
                hs, cs = [], []
                for k in range(8):
                    h = a[k : k + 1] * h + b[k : k + 1]
                    c = a[k : k + 1] * c
                    hs.append(h)
                    cs.append(c)
                v_h[row, rows8, at] = jnp.concatenate(hs, axis=0)
                v_c[row, rows8, at] = jnp.concatenate(cs, axis=0)
                out.append((h, c))
            return tuple(out)

        zero, one = jnp.zeros((1, BLK), F32), jnp.ones((1, BLK), F32)
        lax.fori_loop(0, tokens // 8, eight, ((zero, one),) * 2)
        return 0

    lax.fori_loop(0, rh // BLK, head, 0)
    carry = give(v_h.at[:, pl.ds(tokens - 8, 8)], v_carry, over)
    put(v_u, o_u)
    put(v_a, o_a)
    carry.wait_recv()
    carry.wait_send()
    cot_over = give(v_cot.at[0], v_cot.at[1], over)
    v_carry[...] = jnp.where(x == 0, jnp.zeros_like(v_carry), v_carry[...])
    put(v_carry, o_hin)

    def output(i, _):
        at = pl.ds(pl.multiple_of(i * BLK, BLK), BLK)
        h = v_h[:, :, at] + v_c[:, :, at] * v_carry[:, 7:8, at]
        v_h[:, :, at] = h
        value, _ = gelu_parts(v_ypre[:, :, at])
        v_o[:, :, at] = (h * value).astype(BF16)
        return 0

    lax.fori_loop(0, rh // BLK, output, 0)
    o_pair = give(v_o, v_osib, sib)
    put(v_h, o_h)
    land(gu)
    land(down)
    down = hop(2, d_block, d_piece)
    o_pair.wait_recv()

    def project_row(row, ref):
        def tile(i, _):
            at = pl.ds(pl.multiple_of(i * BLK, BLK), BLK)
            w0 = v_out[0:half, :, :, :, at].reshape(rh, BLK)
            w1 = v_out[half:n, :, :, :, at].reshape(rh, BLK)
            ref[:, at] = jnp.dot(v_o[row], w0, preferred_element_type=F32) + jnp.dot(
                v_osib[1 - row], w1, preferred_element_type=F32
            )
            return 0

        lax.fori_loop(0, width // 2 // BLK, tile, 0)

    project_row(1, v_theirs)
    x1_pair = give(v_theirs, v_psib, sib)
    project_row(0, v_part)
    x1_pair.wait_recv()
    at_mine = pl.ds(pl.multiple_of(core * (width // 2), 128), width // 2)
    at_theirs = pl.ds(pl.multiple_of(other * (width // 2), 128), width // 2)
    v_x1[:, at_mine] = rows_in[:, at_mine].astype(F32) + v_part[...]
    v_x1[:, at_theirs] = rows_in[:, at_theirs].astype(F32) + v_psib[...]
    put(v_x1, o_x1)
    x1 = v_x1[...]
    scale = lax.rsqrt(jnp.mean(x1 * x1, axis=-1, keepdims=True) + EPS)
    v_n2[0] = (x1 * scale * v_gains[1:2, :]).astype(BF16)
    n2_over = give(v_n2.at[0], v_n2.at[1], over)
    n2_pair = give(v_n2.at[0], v_n2.at[2], sib)

    chips_o = 640 // (4 * own)

    def turn_o(i, _):
        at = pl.ds(pl.multiple_of(i * 640, 128), 640)
        here = v_o[:, :, at].astype(F32).reshape(2 * tokens, 640).T.astype(BF16)
        v_ot[pl.ds(i * chips_o, chips_o)] = here.reshape(chips_o, 2, 2, own, 2 * tokens)
        there = jnp.concatenate([v_osib[1, :, at], v_osib[0, :, at]], axis=0).astype(F32).T.astype(BF16)
        v_ot[pl.ds(half + i * chips_o, chips_o)] = there.reshape(chips_o, 2, 2, own, 2 * tokens)
        return 0

    lax.fori_loop(0, rh // 640, turn_o, 0)
    cot_over.wait_recv()
    cot_last = give(v_cot.at[1], v_cot.at[3], sib)
    o_over = give(v_ot.at[:, :, 1 - x], o_ot.at[:, :, :, pl.ds(2 * tokens, 2 * tokens)], over)
    put(v_ot.at[:, :, x], o_ot.at[:, :, :, pl.ds(0, 2 * tokens)])

    tile = 128
    steps = fh // tile

    def loads(t, slot):
        first = pl.ds(pl.multiple_of(t * tile, tile), tile)
        second = pl.ds(pl.multiple_of(fh + t * tile, tile), tile)
        return [
            pltpu.make_async_copy(o_gu.at[:, :, :, first], v_w.at[slot, :, :, :, pl.ds(0, tile)], load_sem.at[slot, 0]),
            pltpu.make_async_copy(
                o_gu.at[:, :, :, second], v_w.at[slot, :, :, :, pl.ds(tile, tile)], load_sem.at[slot, 1]
            ),
        ]

    def stores(t, slot):
        at = pl.ds(pl.multiple_of(t * tile, tile), tile)
        return [
            pltpu.make_async_copy(v_gu.at[slot, :, pl.ds(0, tile)], o_gate.at[:, at], store_sem.at[slot, 0]),
            pltpu.make_async_copy(v_gu.at[slot, :, pl.ds(tile, tile)], o_up.at[:, at], store_sem.at[slot, 1]),
        ]

    for copy in loads(0, 0):
        copy.start()
    n2_pair.wait_recv()
    land(down)
    down = hop(3, d_block, d_piece) if half > 3 else down
    n2_over.wait_recv()
    n2_last = give(v_n2.at[1], v_n2.at[3], sib)
    n2_last.wait_recv()
    put(v_n2, o_n2)

    def hidden_tile(t, _):
        slot = t % 2
        for copy in loads(t, slot):
            copy.wait()

        @pl.when(t + 1 < steps)
        def _():
            for copy in loads(t + 1, 1 - slot):
                copy.start()

        @pl.when(t >= 2)
        def _():
            for copy in stores(t - 2, slot):
                copy.wait()

        w = v_w[slot].reshape(width, 2 * tile)
        v_gu[slot] = jnp.dot(v_n2[...].reshape(4 * tokens, width), w, preferred_element_type=F32)
        for copy in stores(t, slot):
            copy.start()
        value, _ = gelu_parts(v_gu[slot, :, 0:tile])
        v_hidden[:, pl.ds(pl.multiple_of(t * tile, tile), tile)] = (value * v_gu[slot, :, tile:]).astype(BF16)
        return 0

    lax.fori_loop(0, steps, hidden_tile, 0)
    put(v_hidden, o_hidden)
    cot_last.wait_recv()
    put(v_cot, o_cot)
    if half > 3:
        land(down)
        down = hop(4, d_block, d_piece)

    def pd_store(t, slot):
        return pltpu.make_async_copy(v_pd.at[slot], o_pd.at[pl.ds(pl.multiple_of(t * BLK, BLK), BLK)], pd_sem.at[slot])

    def down_tile(t, _):
        slot = t % 2

        @pl.when(t >= 2)
        def _():
            pd_store(t - 2, slot).wait()

        left = v_cot[:, :, pl.ds(pl.multiple_of(t * BLK, BLK), BLK)].reshape(4 * tokens, BLK)
        v_pd[slot] = lax.dot_general(
            left, v_hidden[...], (((0,), (0,)), ((), ())), preferred_element_type=F32
        ).astype(BF16)
        pd_store(t, slot).start()
        return 0

    lax.fori_loop(0, width // BLK, down_tile, 0)
    for s in range(5, half + 1):
        land(down)
        down = hop(s, d_block, d_piece)
    for t in (steps - 2, steps - 1):
        for copy in stores(t, t % 2):
            copy.wait()
    for t in (width // BLK - 2, width // BLK - 1):
        pd_store(t, t % 2).wait()
    land(down)
    land([n1_over, o_over])
    for copy in kept:
        copy.wait()
    for copy in every:
        if copy is not carry:
            copy.wait_send()


def front(n, wx, wy, wo, gs, wg, wu, wd, rows_in, cot, starts):
    rec, f = wx.shape[1], wg.shape[1]
    own, own_d, rows_f = wo.shape[0], wx.shape[0], wg.shape[0]
    rh, fh = rec // 2, f // 2
    tokens, width = rows_in.shape
    half = n // 2
    core = lax.axis_index("dp") % 2
    row = jnp.arange(4 * n)
    index = (row // 2) % n * 4 + row // (2 * n) * 2 + row % 2
    lane_r, lane_d = jnp.arange(rh), jnp.arange(width)
    spread_r = (lane_r[None] % own == jnp.arange(128)[:, None]).astype(BF16)
    spread_d = (lane_d[None] % own_d == jnp.arange(128)[:, None]).astype(BF16)
    pick_r = (index[:, None] - core * 2 * n == lane_r[None] // own).astype(F32)
    pick_d = (index[:, None] == lane_d[None] // own_d).astype(F32)
    outs = dict(
        w_xy=((n, 2, 2, own_d, rec), BF16),
        w_o=((n, 2, 2, own, width // 2), BF16),
        gates=((rh, WIDE), BF16),
        cp=((16, rh), F32),
        gains=((8, width), F32),
        w_gu=((n, 2, rows_f, f), BF16),
        w_d=((n, 2, rows_f, fh), BF16),
        cot=((4, tokens, width), BF16),
        starts=((2, tokens, 128), F32),
        ypre=((2, tokens, rh), F32),
        u=((2, tokens, rh), BF16),
        a=((2, tokens, rh), F32),
        h=((2, tokens, rh), F32),
        h_in=((2, 8, rh), F32),
        xb=((2, tokens, rh), BF16),
        before=((2, 16, rh), BF16),
        x1=((tokens, width), F32),
        n2=((4, tokens, width), BF16),
        n1_t=((n, 2, own_d, 4 * tokens), BF16),
        o_t=((n, 2, own, 4 * tokens), BF16),
        hidden=((4 * tokens, fh), BF16),
        gate=((4 * tokens, fh), F32),
        up=((4 * tokens, fh), F32),
        part_d=((width, fh), BF16),
    )
    state = (2, tokens, rh)
    scratch = [
        ((n, 2, 2, own_d, rec), BF16), ((n, 2, 2, own, width // 2), BF16), ((2, n, 2) + gs.shape, BF16),
        ((rh, WIDE), BF16), ((2, tokens, width), BF16), ((4, tokens, width), BF16), ((2, tokens, 128), F32),
        ((16, rh), F32), ((8, width), F32), ((2 * tokens, width), BF16), ((n, 2, 2, own_d, 2 * tokens), BF16),
        (state, BF16), (state, F32), ((2, 16, rh), BF16), (state, BF16), (state, F32),
        ((2, tokens, BLK), F32), (state, F32), (state, F32), ((2, 8, rh), F32), (state, BF16), (state, BF16),
        ((n, 2, 2, own, 2 * tokens), BF16), ((tokens, width // 2), F32), ((tokens, width // 2), F32),
        ((tokens, width // 2), F32), ((tokens, width), F32), ((4, tokens, width), BF16),
        ((2, n, 2, rows_f, BLK), BF16), ((4 * tokens, fh), BF16), ((2, 4 * tokens, BLK), F32), ((2, BLK, fh), BF16),
    ]
    count = 9 + (3 * n - 1) + n + n + 3 * n + 2 + 12
    dma = pltpu.SemaphoreType.DMA
    result = pl.pallas_call(
        functools.partial(front_kernel, n),
        out_shape=[jax.ShapeDtypeStruct(shape, kind) for shape, kind in outs.values()],
        in_specs=[pl.BlockSpec(memory_space=pltpu.VMEM)] * 14,
        out_specs=[pl.BlockSpec(memory_space=pl.ANY)] * len(outs),
        scratch_shapes=[pltpu.VMEM(shape, kind) for shape, kind in scratch]
        + [dma((32,)), dma((count,)), dma((count,)), dma((2, 2)), dma((2, 2)), dma((2,))],
        compiler_params=pltpu.CompilerParams(
            collective_id=2, has_side_effects=True, vmem_limit_bytes=60 << 20
        ),
        name="front",
    )(wx, wy, wo, gs, wg, wu, wd, rows_in, cot, starts, spread_r, pick_r, spread_d, pick_d)
    return dict(zip(outs, result))


def nt(left, right):
    return lax.dot_general(left, right, (((1,), (1,)), ((), ())), preferred_element_type=F32)


def nn(left, right):
    return jnp.dot(left, right, preferred_element_type=F32)


def body(
    dp_size,
    layer_input, grad_out, lengths, resets, norm_gain, w_x, w_y, conv_w, conv_b, gate_a_w, gate_a_b,
    gate_i_w, gate_i_b, decay_param, w_out, mlp_gain, w_gate, w_up, w_down,
):
    n = dp_size // 2
    half = n // 2
    dp, x = lax.axis_index("dp"), lax.axis_index("tp")
    chip, core = dp // 2, dp % 2
    pos = place_of(chip, n)
    tokens, width = layer_input.shape[1], layer_input.shape[2]
    rec = w_x.shape[1]
    rh = rec // 2
    taps = conv_w.shape[0]
    own = rec // (2 * dp_size)
    own_d = width // (2 * dp_size)

    ring = [chip_at(i, n) for i in range(n)]
    up = [(ring[i] * 2 + c, ring[(i + 1) % n] * 2 + c) for i in range(n) for c in range(2)]
    down = [(b, a) for a, b in up]
    lanes = [[chip_id * 2 + c for chip_id in ring] for c in range(2)]
    pairs = [(d, d + 1 - 2 * (d % 2)) for d in range(dp_size)]

    def sibling(v):
        return lax.ppermute(v, "dp", pairs)

    def across(v):
        return lax.ppermute(v, "tp", [(0, 1), (1, 0)])

    def swapped(v):
        return jnp.concatenate([v[1:], v[:1]], axis=0)

    def by_core(mine, theirs, axis):
        return jnp.where(
            core == 0, jnp.concatenate([mine, theirs], axis), jnp.concatenate([theirs, mine], axis)
        )

    def ring_order(array, axis):
        size = array.shape[axis] // n
        return jnp.concatenate([lax.slice_in_dim(array, i * size, (i + 1) * size, axis=axis) for i in ring], axis)

    def chip_order(array, axis):
        size = array.shape[axis] // n
        return jnp.concatenate(
            [lax.slice_in_dim(array, ring.index(i) * size, (ring.index(i) + 1) * size, axis=axis) for i in range(n)],
            axis,
        )

    def after(value, *others):
        return lax.optimization_barrier((value,) + others)[0]

    rows_own = layer_input.reshape(tokens, width)
    place = x * tokens + jnp.arange(tokens, dtype=jnp.int32)
    starts = jnp.where((resets.reshape(tokens) > 0) | (place == 0), 1.0, 0.0).astype(F32)
    starts = jnp.broadcast_to(starts[:, None], (tokens, 128))
    valid = (place < lengths[0]).astype(F32)[:, None]
    cot = grad_out.reshape(tokens, width).astype(F32) * valid

    def lane_sum(array):
        return lax.psum_scatter(array, "dp", scatter_dimension=0, tiled=True, axis_index_groups=lanes)

    def plane(array, which):
        return lax.dynamic_index_in_dim(array, which, 2, keepdims=False)

    def both(mine, axis):
        return jnp.concatenate([mine, across(mine)], axis)

    def tn(left, right):
        return lax.dot_general(left, right, (((0,), (0,)), ((), ())), preferred_element_type=F32)

    fh = w_gate.shape[1] // 2
    cot_ring = ring_order(cot.astype(BF16), 1)
    if own % 16 == 0 and own_d % 16 == 0:
        vectors = jnp.concatenate([conv_w, jnp.stack([conv_b, gate_a_b, gate_i_b, decay_param])], axis=0)
        vectors = jnp.pad(vectors, ((0, 0), (0, WIDE - own)))
        gains = jnp.pad(jnp.stack([norm_gain, mlp_gain]), ((0, PAD - taps - 6), (0, WIDE - own_d)))
        gs = jnp.concatenate([jnp.concatenate([gate_a_w, gate_i_w], axis=1), vectors, gains], axis=0)
        got = front(n, w_x, w_y, w_out, gs, w_gate, w_up, w_down.T, rows_own, cot_ring, starts)
        w_xy, w_o = got["w_xy"].reshape(width, rec), got["w_o"].reshape(rec, width // 2)
        w_gu, w_d = got["w_gu"].reshape(width, 2 * fh), got["w_d"].reshape(width, fh)
        cot_all, n2_all = got["cot"].reshape(4 * tokens, width), got["n2"].reshape(4 * tokens, width)
        gain_one, gain_two, cp, gates = got["gains"][0], got["gains"][1], got["cp"], got["gates"]
        starts_two, ypre, u, a, h, xb, x1 = (got[key] for key in ("starts", "ypre", "u", "a", "h", "xb", "x1"))
        h_in, before = got["h_in"][:, 7:8], got["before"][:, PAD - taps + 1 :]
        n1_t, o_t = got["n1_t"].reshape(width // 2, 4 * tokens), got["o_t"].reshape(rh, 4 * tokens)
        hidden, gate, upv, part_d = got["hidden"], got["gate"], got["up"], got["part_d"]
        rs2 = lax.rsqrt(jnp.mean(x1 * x1, axis=-1, keepdims=True) + EPS)
    else:
        small = jnp.concatenate(
            [norm_gain, mlp_gain, conv_w.reshape(-1), conv_b, gate_a_b, gate_i_b, decay_param]
        )
        small = jnp.pad(small, (0, PAD * WIDE - small.shape[0])).reshape(PAD, WIDE)
        gs = jnp.concatenate([jnp.concatenate([gate_a_w, gate_i_w], axis=1), small], axis=0)
        w_xy, w_o, all_gs, w_gu, d_block, rows_two, cot_all, starts_two = gather_weights(
            n, w_x, w_y, w_out, gs, w_gate, w_up, w_down.T, rows_own, cot_ring, starts
        )
        w_d = lax.all_gather(
            d_block.reshape(-1, d_block.shape[2]), "dp", axis=0, tiled=True, axis_index_groups=lanes
        )
        w_gu = w_gu.reshape(width, w_gate.shape[1])
        w_xy = w_xy.reshape(width, rec)
        w_o = w_o.reshape(rec, width // 2)
        cot_all = cot_all.reshape(4 * tokens, width)

        vectors = all_gs[:, :, :, own:].transpose(1, 0, 2, 3, 4).reshape(2 * dp_size, PAD * WIDE)
        gain_one = vectors[:, :own_d].reshape(width).astype(F32)
        gain_two = vectors[:, own_d : 2 * own_d].reshape(width).astype(F32)
        lines = vectors[:, 2 * own_d : 2 * own_d + (taps + 4) * own].reshape(2 * dp_size, taps + 4, own)
        lines = lax.dynamic_slice_in_dim(lines, core * dp_size, dp_size, 0)
        lines = lines.transpose(1, 0, 2).reshape(taps + 4, rh).astype(F32)
        decay = lines[taps + 3 :]
        cp = jnp.concatenate(
            [lines[: taps + 3], jax.nn.softplus(-decay), jax.nn.sigmoid(-decay), jnp.zeros((7, rh), F32)], axis=0
        )
        gates = lax.dynamic_slice_in_dim(all_gs[:, :, :, :own], core * half, half, 1)
        gates = gates.transpose(1, 0, 2, 3, 4).reshape(rh, WIDE)

        n1, xb, ypre = project(rows_two, gain_one[None], w_xy)
        before = lax.ppermute(xb[:, tokens - (taps - 1) :], "tp", [(0, 1)])
        halo = jnp.concatenate([jnp.zeros((2, 8 - (taps - 1), rh), F32), before.astype(F32)], axis=1)
        u, a, h_local, coef = recurrence(xb, halo, gates, cp, starts_two)
        h_in = lax.ppermute(h_local[:, tokens - 1 :], "tp", [(0, 1)])
        h = h_local + coef * h_in
        ybr, _ = gelu_parts(ypre)
        o = (h * ybr).astype(BF16)
        o_sib = sibling(o)
        part_mine, part_theirs = project_out(o, o_sib, w_o)
        x1 = rows_own.astype(F32) + by_core(part_mine, sibling(part_theirs), 1)
        rs2 = lax.rsqrt(jnp.mean(x1 * x1, axis=-1, keepdims=True) + EPS)
        n2 = (x1 * rs2 * gain_two).astype(BF16)
        n2_x = across(n2)

        def plane_rows(values, rows):
            grouped = after(values, n2_x).T.reshape(n, 2, 2, rows, 2 * tokens)
            return plane(grouped, x), plane(grouped, 1 - x)

        o_here, o_send = plane_rows(jnp.concatenate([o, swapped(o_sib)], axis=2).reshape(2 * tokens, rec), own)
        n1_here, n1_send = plane_rows(n1, own_d)
        two = jnp.concatenate([n2, n2_x], axis=0)
        n2_all = jnp.concatenate([two, sibling(two)], axis=0)
        o_t = jnp.concatenate([o_here, across(o_send)], axis=3).reshape(rh, 4 * tokens)
        n1_t = jnp.concatenate([n1_here, across(n1_send)], axis=3).reshape(width // 2, 4 * tokens)

        gu = nn(n2_all, w_gu)
        gate, upv = gu[:, :fh], gu[:, fh:]
        act, _ = gelu_parts(gate)
        hidden = (act * upv).astype(BF16)

        part_d = tn(cot_all, hidden).astype(BF16)
    sum_d = lane_sum(part_d)
    act, slope = gelu_parts(gate)
    d_hidden = nn(after(cot_all, part_d), w_d)
    d_gu = jnp.concatenate([(d_hidden * upv * slope).astype(BF16), (d_hidden * act).astype(BF16)], axis=1)

    def pair_sum(partial):
        return (partial[: 2 * tokens].astype(F32) + sibling(partial[2 * tokens :]).astype(F32)).astype(BF16)

    d_n2_pair = pair_sum(nt(d_gu, w_gu).astype(BF16))
    d_n2_send = d_n2_pair[tokens:]
    d_n2 = d_n2_pair[:tokens].astype(F32) + across(d_n2_send).astype(F32)
    part_gu = tn(ring_order(n2_all, 1), after(d_gu, d_n2_send)).astype(BF16)
    sum_gu = lane_sum(part_gu)
    ff_pair = pair_sum(nt(after(hidden, part_gu), w_d).astype(BF16))
    ff_out = ff_pair[:tokens].astype(F32) + across(ff_pair[tokens:]).astype(F32)

    q2 = gain_two * d_n2
    d_gain_two = jnp.sum(d_n2 * x1 * rs2, axis=0)
    d_x1 = cot + rs2 * q2 - x1 * (rs2 * rs2 * rs2) * jnp.mean(x1 * q2, axis=-1, keepdims=True)
    dbr = d_x1.astype(BF16)
    dbr_mine = lax.dynamic_slice_in_dim(dbr, core * (width // 2), width // 2, 1)
    dbr_theirs = lax.dynamic_slice_in_dim(dbr, (1 - core) * (width // 2), width // 2, 1)
    dbr_half = jnp.concatenate([dbr_mine, sibling(dbr_theirs)], axis=0)
    do_part = nt(dbr_half, w_o)
    do = do_part[:, :rh].reshape(2, tokens, rh) + swapped(sibling(do_part[:, rh:].reshape(2, tokens, rh)))
    dbr_x = across(dbr_half)

    d_ypre, lam_local, coef_back = adjoint(do, h, ypre, a)
    d_ypre_x = both(d_ypre.reshape(2 * tokens, rh), 0)
    inc = lax.ppermute(a[:, :1] * lam_local[:, :1], "tp", [(1, 0)])
    du, d_gates, sums = gates_back(lam_local, coef_back, inc, h, h_in, u, gates, cp, starts_two)
    du_next = lax.ppermute(du[:, : taps - 1], "tp", [(1, 0)])
    du_pad = jnp.concatenate([du, du_next], axis=1).astype(F32)
    xb_pad = jnp.concatenate([before, xb], axis=1).astype(F32)
    d_taps = jnp.stack(
        [jnp.sum(du_pad[:, :tokens] * xb_pad[:, taps - 1 - k : taps - 1 - k + tokens], axis=(0, 1)) for k in range(taps)]
    )
    d_bias = jnp.sum(du_pad[:, :tokens], axis=(0, 1))[None]
    d_xb = sum(cp[k] * du_pad[:, k : k + tokens] for k in range(taps)).astype(BF16)
    d_xy = jnp.concatenate([d_xb, d_ypre], axis=2).reshape(2 * tokens, rec)
    result = (after(x1, d_xb) + chip_order(ff_out, 1)).astype(BF16).reshape(1, tokens, width)
    d_n1_part = nt(d_xy, w_xy).reshape(2, tokens, width)
    d_n1 = d_n1_part[0] + sibling(d_n1_part[1])
    q1 = gain_one * d_n1
    own_f = rows_own.astype(F32)
    own_rs = lax.rsqrt(jnp.mean(own_f * own_f, axis=-1, keepdims=True) + EPS)
    d_gain_one = jnp.sum(d_n1 * own_f * own_rs, axis=0)
    grad_x = d_x1 + own_rs * q1 - own_f * (own_rs * own_rs * own_rs) * jnp.mean(own_f * q1, axis=-1, keepdims=True)

    c_out = nn(after(o_t, d_xb), jnp.concatenate([dbr_half, dbr_x], axis=0)).astype(BF16).reshape(n, 2, own, width // 2)
    c_x = nn(n1_t, both(d_xb.reshape(2 * tokens, rh), 0)).astype(BF16).reshape(n, 2, own_d, rh)
    c_y = nn(n1_t, d_ypre_x).astype(BF16).reshape(n, 2, own_d, rh)

    def placed(part):
        zero = jnp.zeros_like(part)
        return by_core_rows(part, zero)

    def by_core_rows(mine, theirs):
        return jnp.where(
            core == 0, jnp.concatenate([mine, theirs], 0), jnp.concatenate([theirs, mine], 0)
        )

    g = d_gates.reshape(half, 2, 2, own, WIDE)
    g = plane(g, x) + across(plane(g, 1 - x).astype(BF16)).astype(F32)
    g_mine = lax.dynamic_index_in_dim(g, core, 1, keepdims=False)
    g_theirs = lax.dynamic_index_in_dim(g, 1 - core, 1, keepdims=False)
    g_lane = by_core_rows(g_mine, sibling(g_theirs))

    lines_back = jnp.concatenate([d_taps, d_bias, sums[:3]], axis=0)
    lines_back = lines_back.reshape(taps + 4, half, 2, 2, own).transpose(1, 2, 3, 0, 4)
    lines_back = placed(lines_back.reshape(half, 2, 2, (taps + 4) * own))
    gains = jnp.concatenate([d_gain_one.reshape(n, 2, 2, own_d), d_gain_two.reshape(n, 2, 2, own_d)], axis=3)
    vec = jnp.concatenate([gains, lines_back], axis=3)
    vec = jnp.pad(vec, ((0, 0), (0, 0), (0, 0), (0, -vec.shape[3] % 128)))
    vec = plane(vec, x) + across(plane(vec, 1 - x))
    vec = lax.dynamic_index_in_dim(vec, core, 1, keepdims=False) + sibling(
        lax.dynamic_index_in_dim(vec, 1 - core, 1, keepdims=False)
    )

    vec = jnp.pad(vec, ((0, 0), (0, -vec.shape[1] % 1024))).reshape(n, -1, 128)
    def whole(block):
        rows = block.shape[0] // 2
        block = block.reshape(2, rows, block.shape[1])
        mine = lax.dynamic_index_in_dim(block, core, 0, keepdims=False)
        theirs = lax.dynamic_index_in_dim(block, 1 - core, 0, keepdims=False)
        return mine, sibling(theirs)

    def halves(pair):
        return by_core(pair[0], pair[1], 1).astype(F32)

    grad_down = halves(whole(sum_d)).T
    grad_w_x, grad_w_y, grad_w_out, sum_gates, sum_vec = scatter_sums(
        n, after(c_x, grad_down, result, grad_x), c_y, c_out, g_lane.astype(BF16), vec
    )
    sum_vec = sum_vec.reshape(-1)
    gu_mine, gu_theirs = whole(sum_gu)
    grad_gate = halves((gu_mine[:, :fh], gu_theirs[:, :fh]))
    grad_up = halves((gu_mine[:, fh:], gu_theirs[:, fh:]))
    tail = sum_vec[2 * own_d : 2 * own_d + (taps + 4) * own].reshape(taps + 4, own)
    return (
        result,
        grad_x.reshape(1, tokens, width),
        sum_vec[:own_d],
        grad_w_x,
        grad_w_y,
        tail[:taps],
        tail[taps],
        sum_gates[:, :BLK],
        tail[taps + 1],
        sum_gates[:, BLK:],
        tail[taps + 2],
        tail[taps + 3],
        grad_w_out,
        sum_vec[own_d : 2 * own_d],
        grad_gate,
        grad_up,
        grad_down,
    )


def solution(mesh):
    every = ("dp", "tp")
    return jax.shard_map(
        functools.partial(body, mesh.shape["dp"]),
        mesh=mesh,
        in_specs=(
            P("dp", "tp", None),
            P("dp", "tp", None),
            P("dp"),
            P("dp", "tp"),
            P(every),
            P(every, None),
            P(every, None),
            P(None, every),
            P(every),
            P(every, None),
            P(every),
            P(every, None),
            P(every),
            P(every),
            P(every, None),
            P(every),
            P("dp", "tp"),
            P("dp", "tp"),
            P("tp", "dp"),
        ),
        out_specs=(
            P("dp", "tp", None),
            P("dp", "tp", None),
            P(every),
            P(every, None),
            P(every, None),
            P(None, every),
            P(every),
            P(every, None),
            P(every),
            P(every, None),
            P(every),
            P(every),
            P(every, None),
            P(every),
            P("dp", "tp"),
            P("dp", "tp"),
            P("tp", "dp"),
        ),
        check_vma=False,
    )
```

```python
import functools

import jax
import jax.numpy as jnp
import numpy as np
from jax import lax
from jax.experimental import pallas as pl
from jax.experimental.pallas import tpu as pltpu
from jax.sharding import PartitionSpec as P

BLK = 256
PAD = 16
WIDE = 512
EPS = 1e-06
MESH = pl.DeviceIdType.MESH
F32 = jnp.float32
BF16 = jnp.bfloat16


def chip_at(pos, n):
    back = pos // (n // 2)
    return (1 - back) * (2 * pos) + back * (2 * (n - 1 - pos) + 1)


def place_of(chip, n):
    odd = chip % 2
    return (1 - odd) * (chip // 2) + odd * (n - 1 - chip // 2)


def heads_first(chip, core, n):
    return (chip + n - core * (n // 2)) % n


class Copies:
    def __init__(self, local, sends, recvs):
        self.local, self.sends, self.recvs = local, sends, recvs
        self.locals_used = self.used = 0

    def stay(self, src, dst):
        copy = pltpu.make_async_copy(src, dst, self.local.at[self.locals_used])
        self.locals_used += 1
        copy.start()
        return copy

    def send(self, src, dst, device):
        copy = pltpu.make_async_remote_copy(
            src_ref=src, dst_ref=dst, send_sem=self.sends.at[self.used], recv_sem=self.recvs.at[self.used],
            device_id=device, device_id_type=MESH,
        )
        self.used += 1
        copy.start()
        return copy


def greet(devices):
    barrier = pltpu.get_barrier_semaphore()
    for device in devices:
        pl.semaphore_signal(barrier, inc=1, device_id=device, device_id_type=MESH)
    pl.semaphore_wait(barrier, len(devices))


def half_cols(ref, which):
    width = ref.shape[1] // 2
    return ref.at[:, pl.ds(pl.multiple_of(which * width, 128), width)]


def gather_kernel(
    n,
    wx, wy, wo, gs, wg, wu, wd, rows_in, cot, starts,
    o_xy, o_out, o_gs, o_gu, o_d, o_rows, o_cot, o_starts,
    local_sem, send_sem, recv_sem,
):
    dp, x = lax.axis_index("dp"), lax.axis_index("tp")
    chip, core = dp // 2, dp % 2
    other = 1 - core
    pos = place_of(chip, n)
    half = n // 2
    nxt = (chip_at((pos + 1) % n, n) * 2 + core, x)
    prv = (chip_at((pos + n - 1) % n, n) * 2 + core, x)
    sib = (chip * 2 + other, x)
    over = (dp, 1 - x)
    greet([nxt, prv, sib, over])
    copies = Copies(local_sem, send_sem, recv_sem)
    send, stay = copies.send, copies.stay

    def by_heads(chip_id, which):
        return heads_first(chip_id, which, n)

    rhalf = wx.shape[1] // 2
    fhalf = wg.shape[1] // 2
    rec_parts = [
        (wx, o_xy.at[chip, core, x, :, pl.ds(0, rhalf)]),
        (wy, o_xy.at[chip, core, x, :, pl.ds(rhalf, rhalf)]),
    ]
    ff_parts = [
        (wg, o_gu.at[chip, core, :, pl.ds(0, fhalf)]),
        (wu, o_gu.at[chip, core, :, pl.ds(fhalf, fhalf)]),
        (wd, o_d.at[core]),
    ]
    pair = [send(half_cols(src, other), slot, sib) for src, slot in rec_parts]
    pair.append(send(half_cols(wo, other), o_out.at[by_heads(chip, other), core, x], sib))
    mine = [stay(half_cols(src, core), slot) for src, slot in rec_parts] + [stay(gs, o_gs.at[core, chip, x])]
    mine.append(stay(half_cols(wo, core), o_out.at[by_heads(chip, core), core, x]))
    late = [send(half_cols(src, other), slot, sib) for src, slot in ff_parts]
    plain = [stay(half_cols(src, core), slot) for src, slot in ff_parts]
    late += [send(rows_in, o_rows.at[1], sib), send(starts, o_starts.at[1], sib), send(cot, o_cot.at[2], sib)]
    plain += [stay(rows_in, o_rows.at[0]), stay(starts, o_starts.at[0]), stay(cot, o_cot.at[0])]

    def rec_block(chip_id):
        return [o_xy.at[chip_id, :, x], o_out.at[by_heads(chip_id, core), :, x], o_gs.at[core, chip_id, x]]

    def rec_piece(chip_id, which):
        refs = [o_xy.at[chip_id, which, x], o_out.at[by_heads(chip_id, core), which, x]]
        return refs + ([o_gs.at[core, chip_id, x]] if which == 0 else [])

    def ff_block(chip_id):
        return [o_gu.at[chip_id]]

    def ff_piece(chip_id, which):
        return [o_gu.at[chip_id, which]]

    def send_all(refs, device):
        return [send(ref, ref, device) for ref in refs]

    def hop(s, block, piece):
        ahead = chip_at((pos + n - (s - 1)) % n, n)
        behind = chip_at((pos + s - 1) % n, n)
        if s < half:
            return send_all(block(ahead), nxt) + send_all(block(behind), prv)
        return send_all(piece(ahead, 0), nxt) + send_all(piece(behind, 1), prv)

    for copy in pair:
        copy.wait_recv()
    for copy in mine:
        copy.wait()
    done, crossed, moving = [], send_all(rec_block(chip), over), []
    for s in range(1, half + 1):
        for copy in moving:
            copy.wait_recv()
        done.extend(moving)
        moving = hop(s, rec_block, rec_piece)
        if s > 1:
            crossed.extend(send_all(rec_block(chip_at((pos + n - (s - 1)) % n, n)), over))
            crossed.extend(send_all(rec_block(chip_at((pos + s - 1) % n, n)), over))
    last_rec = moving
    for copy in late:
        copy.wait_recv()
    for copy in plain:
        copy.wait()
    moving = hop(1, ff_block, ff_piece)
    for copy in last_rec:
        copy.wait_recv()
    done.extend(last_rec)
    crossed.extend(send_all(rec_block(chip_at((pos + half) % n, n)), over))
    cot_over = send(cot, o_cot.at[1], over)
    for s in range(2, half + 1):
        for copy in moving:
            copy.wait_recv()
        done.extend(moving)
        moving = hop(s, ff_block, ff_piece)
    for copy in crossed:
        copy.wait_recv()
    swap = send(o_gs.at[core], o_gs.at[core], sib)
    cot_over.wait_recv()
    last = send(o_cot.at[1], o_cot.at[3], sib)
    for copy in moving:
        copy.wait_recv()
    done.extend(moving)
    swap.wait_recv()
    last.wait_recv()
    for copy in pair + late + done + crossed + [cot_over, swap, last]:
        copy.wait_send()


def gather_weights(n, wx, wy, wo, gs, wg, wu, wd, rows_in, cot, starts):
    r, d, (rows_f, f) = wx.shape[1], wo.shape[1], wg.shape
    tokens = rows_in.shape[0]
    shapes = [
        jax.ShapeDtypeStruct((n, 2, 2, wx.shape[0], r), BF16),
        jax.ShapeDtypeStruct((n, 2, 2, wo.shape[0], d // 2), BF16),
        jax.ShapeDtypeStruct((2, n, 2) + gs.shape, BF16),
        jax.ShapeDtypeStruct((n, 2, rows_f, f), BF16),
        jax.ShapeDtypeStruct((2, rows_f, f // 2), BF16),
        jax.ShapeDtypeStruct((2, tokens, d), BF16),
        jax.ShapeDtypeStruct((4, tokens, d), BF16),
        jax.ShapeDtypeStruct((2,) + starts.shape, F32),
    ]
    count = 9 + (3 * n - 1) + n + 3 * n + 3
    dma = pltpu.SemaphoreType.DMA
    return pl.pallas_call(
        functools.partial(gather_kernel, n),
        out_shape=shapes,
        in_specs=[pl.BlockSpec(memory_space=pltpu.VMEM)] * 10,
        out_specs=[pl.BlockSpec(memory_space=pl.ANY)] * 8,
        scratch_shapes=[dma((10,)), dma((count,)), dma((count,))],
        compiler_params=pltpu.CompilerParams(
            collective_id=0, has_side_effects=True, vmem_limit_bytes=24 << 20
        ),
        name="gather_weights",
    )(wx, wy, wo, gs, wg, wu, wd, rows_in, cot, starts)


def scatter_kernel(
    n,
    c_x, c_y, c_out, c_g, c_v,
    g_x, g_y, g_out, g_gates, g_vec,
    r_x, r_y, r_out, r_g, r_v, s_x, s_y, s_out,
    send_sem, recv_sem,
):
    dp, x = lax.axis_index("dp"), lax.axis_index("tp")
    chip, core = dp // 2, dp % 2
    pos = place_of(chip, n)
    half = n // 2
    nxt = (chip_at((pos + 1) % n, n) * 2 + core, x)
    prv = (chip_at((pos + n - 1) % n, n) * 2 + core, x)
    sib = (dp + 1 - 2 * core, x)
    greet([nxt, prv, sib])
    copies = Copies(None, send_sem, recv_sem)

    pieces = []
    for part in (0, 1):
        for terms, slots, first in ((c_out, r_out, core), (c_y, r_y, 0), (c_x, r_x, 0)):
            pieces.append((
                lambda c, terms=terms, part=part, first=first: terms.at[heads_first(c, first, n), part],
                lambda w, k, slots=slots, part=part: slots.at[part, w, k],
                part,
            ))
    pieces.append((lambda c: c_g.at[c], lambda w, k: r_g.at[w, k], 0))
    pieces.append((lambda c: c_v.at[c], lambda w, k: r_v.at[w, k], 1))

    def add(a, b):
        return a[...].astype(F32) + b[...].astype(F32)

    sent, coming = [], {}
    for k in range(half, -1, -1):
        for i, (term, slot, far) in enumerate(pieces):
            for way, (device, sign) in enumerate(((nxt, 1), (prv, n - 1))):
                first = half if way == far else half - 1
                if k > first or k == 0:
                    continue
                source = term(chip_at((pos + sign * k) % n, n))
                if k < first:
                    coming[i, way].wait_recv()
                    got = slot(way, k)
                    got[...] = add(got, source).astype(got.dtype)
                    source = got
                copy = copies.send(source, slot(way, k - 1), device)
                coming[i, way] = copy
                sent.append(copy)

    def total(i):
        term, slot, _ = pieces[i]
        for way in (0, 1):
            coming[i, way].wait_recv()
        return add(term(chip), slot(0, 0)) + slot(1, 0)[...].astype(F32)

    def cols(ref):
        width = ref.shape[1] // 2
        return pl.ds(pl.multiple_of(core * width, 128), width)

    results = ((g_out, s_out), (g_y, s_y), (g_x, s_x))
    for part in (0, 1):
        sums = [total(3 * part + i) for i in range(3)]

        @pl.when(core == part)
        def _():
            for value, (ref, _) in zip(sums, results):
                ref[:, cols(ref)] = value

        @pl.when(core != part)
        def _():
            for value, (_, ref) in zip(sums, results):
                ref[...] = value

    final = [copies.send(src, ref.at[:, cols(ref)], sib) for ref, src in results]
    g_gates[...] = total(6)
    g_vec[...] = total(7)
    for copy in final:
        copy.wait_recv()
    for copy in sent + final:
        copy.wait_send()


def scatter_sums(n, c_x, c_y, c_out, c_g, c_v):
    _, _, rows_d, rhalf = c_x.shape
    _, _, rows_r, dhalf = c_out.shape
    half = n // 2
    count = 8 * (2 * half - 1) + 3
    dma = pltpu.SemaphoreType.DMA
    vmem = pl.BlockSpec(memory_space=pltpu.VMEM)
    return pl.pallas_call(
        functools.partial(scatter_kernel, n),
        out_shape=[
            jax.ShapeDtypeStruct((rows_d, 2 * rhalf), F32),
            jax.ShapeDtypeStruct((rows_d, 2 * rhalf), F32),
            jax.ShapeDtypeStruct((rows_r, 2 * dhalf), F32),
            jax.ShapeDtypeStruct(c_g.shape[1:], F32),
            jax.ShapeDtypeStruct(c_v.shape[1:], F32),
        ],
        in_specs=[vmem] * 5,
        out_specs=[vmem] * 5,
        scratch_shapes=[
            pltpu.VMEM((2, 2, half, rows_d, rhalf), BF16),
            pltpu.VMEM((2, 2, half, rows_d, rhalf), BF16),
            pltpu.VMEM((2, 2, half, rows_r, dhalf), BF16),
            pltpu.VMEM((2, half) + c_g.shape[1:], BF16),
            pltpu.VMEM((2, half) + c_v.shape[1:], F32),
            pltpu.VMEM((rows_d, rhalf), F32),
            pltpu.VMEM((rows_d, rhalf), F32),
            pltpu.VMEM((rows_r, dhalf), F32),
            dma((count,)), dma((count,)),
        ],
        compiler_params=pltpu.CompilerParams(
            collective_id=1, has_side_effects=True, vmem_limit_bytes=56 << 20
        ),
        name="scatter_sums",
    )(c_x, c_y, c_out, c_g, c_v)


def project_kernel(steps, rows, gain, w, n1_ref, x_ref, y_ref):
    i = pl.program_id(0)

    @pl.when(i == 0)
    def _():
        values = rows[...].astype(F32)
        scale = lax.rsqrt(jnp.mean(values * values, axis=-1, keepdims=True) + EPS)
        n1_ref[...] = (values * scale * gain[...]).astype(BF16).reshape(n1_ref.shape)

    result = jnp.dot(n1_ref[...], w[...], preferred_element_type=F32).reshape(y_ref.shape)

    @pl.when(i < steps)
    def _():
        x_ref[...] = result.astype(BF16)

    @pl.when(i >= steps)
    def _():
        y_ref[...] = result


def project(rows, gain, w):
    _, tokens, width = rows.shape
    rh = w.shape[1] // 2
    steps = rh // BLK
    return pl.pallas_call(
        functools.partial(project_kernel, steps),
        grid=(2 * steps,),
        in_specs=[
            pl.BlockSpec(rows.shape, lambda i: (0, 0, 0)),
            pl.BlockSpec((1, width), lambda i: (0, 0)),
            pl.BlockSpec((width, BLK), lambda i: (0, i)),
        ],
        out_specs=[
            pl.BlockSpec((2 * tokens, width), lambda i: (0, 0)),
            pl.BlockSpec((2, tokens, BLK), lambda i: (0, 0, jnp.minimum(i, steps - 1))),
            pl.BlockSpec((2, tokens, BLK), lambda i: (0, 0, jnp.maximum(i - steps, 0))),
        ],
        out_shape=[
            jax.ShapeDtypeStruct((2 * tokens, width), BF16),
            jax.ShapeDtypeStruct((2, tokens, rh), BF16),
            jax.ShapeDtypeStruct((2, tokens, rh), F32),
        ],
        compiler_params=pltpu.CompilerParams(vmem_limit_bytes=40 << 20),
        cost_estimate=pl.CostEstimate(flops=27 * 10**8, bytes_accessed=15 * 10**6, transcendentals=0),
        name="project",
    )(rows, gain, w)


def project_out_kernel(o, o_sib, w, mine_ref, theirs_ref):
    rh = o.shape[2]
    for row, ref in ((0, mine_ref), (1, theirs_ref)):
        ref[...] = jnp.dot(o[row], w[:rh], preferred_element_type=F32) + jnp.dot(
            o_sib[1 - row], w[rh:], preferred_element_type=F32
        )


def project_out(o, o_sib, w):
    _, tokens, rh = o.shape
    cols = w.shape[1]
    tile = min(BLK, cols)
    whole = pl.BlockSpec(o.shape, lambda i: (0, 0, 0))
    part = pl.BlockSpec((tokens, tile), lambda i: (0, i))
    return pl.pallas_call(
        project_out_kernel,
        grid=(cols // tile,),
        in_specs=[whole, whole, pl.BlockSpec((2 * rh, tile), lambda i: (0, i))],
        out_specs=[part, part],
        out_shape=[jax.ShapeDtypeStruct((tokens, cols), F32)] * 2,
        compiler_params=pltpu.CompilerParams(vmem_limit_bytes=40 << 20),
        cost_estimate=pl.CostEstimate(flops=14 * 10**8, bytes_accessed=8 * 10**6, transcendentals=0),
        name="project_out",
    )(o, o_sib, w)


def minus_expm1(v):
    series = jnp.ones_like(v)
    for k in range(9, 1, -1):
        series = 1.0 + series * v * (1.0 / k)
    return jnp.where(v > -0.5, -v * series, 1.0 - jnp.exp(v))


def gates_of(u, weights, cp, start):
    tokens = u.shape[0] * u.shape[1]
    flat = u.reshape(tokens, BLK)
    z = jnp.dot(flat, weights, preferred_element_type=F32)
    r = jax.nn.sigmoid(z[:, :BLK] + cp[5:6]).reshape(u.shape)
    ig = jax.nn.sigmoid(z[:, BLK:] + cp[6:7]).reshape(u.shape)
    la = -8.0 * r * cp[7:8][None]
    decayed = jnp.exp(la)
    rest = minus_expm1(2.0 * la)
    return r, ig, decayed, rest


def recurrence_kernel(xb, halo, weights, cp, starts, u_ref, a_ref, h_ref, c_ref, b_ref):
    rows, length = xb.shape[0], xb.shape[1]
    p = cp[...]
    us = []
    for row in range(rows):
        padded = jnp.concatenate([halo[row], xb[row].astype(F32)], axis=0)
        total = p[4:5] + p[0:1] * padded[8 : 8 + length]
        for k in range(1, 4):
            total = total + p[k : k + 1] * padded[8 - k : 8 - k + length]
        us.append(total.astype(BF16))
    u = jnp.stack(us)
    u_ref[...] = u
    start = starts[...]
    start = jnp.concatenate([start, start], axis=2)
    r, ig, decayed, rest = gates_of(u, weights[...], p, start)
    a_ref[...] = decayed * (1.0 - start)
    b_ref[...] = jnp.where(start > 0.5, 1.0, jnp.sqrt(rest)) * ig * u.astype(F32)

    def eight(i, carry):
        at = pl.ds(pl.multiple_of(i * 8, 8), 8)
        out = []
        for row in range(rows):
            h, c = carry[row]
            a, b = a_ref[row, at, :], b_ref[row, at, :]
            hs, cs = [], []
            for j in range(8):
                h = a[j : j + 1] * h + b[j : j + 1]
                c = a[j : j + 1] * c
                hs.append(h)
                cs.append(c)
            h_ref[row, at, :] = jnp.concatenate(hs, axis=0)
            c_ref[row, at, :] = jnp.concatenate(cs, axis=0)
            out.append((h, c))
        return tuple(out)

    zero, one = jnp.zeros((1, BLK), F32), jnp.ones((1, BLK), F32)
    lax.fori_loop(0, length // 8, eight, ((zero, one),) * rows)


def recurrence(xb, halo, weights, cp, starts):
    rows, length, channels = xb.shape
    wide = pl.BlockSpec((rows, length, BLK), lambda h: (0, 0, h))
    return pl.pallas_call(
        recurrence_kernel,
        grid=(channels // BLK,),
        in_specs=[
            wide,
            pl.BlockSpec((rows, 8, BLK), lambda h: (0, 0, h)),
            pl.BlockSpec((BLK, 2 * BLK), lambda h: (h, 0)),
            pl.BlockSpec((cp.shape[0], BLK), lambda h: (0, h)),
            pl.BlockSpec(starts.shape, lambda h: (0, 0, 0)),
        ],
        out_specs=[wide] * 4,
        out_shape=[jax.ShapeDtypeStruct(xb.shape, BF16)] + [jax.ShapeDtypeStruct(xb.shape, F32)] * 3,
        scratch_shapes=[pltpu.VMEM((rows, length, BLK), F32)],
        compiler_params=pltpu.CompilerParams(vmem_limit_bytes=40 << 20),
        cost_estimate=pl.CostEstimate(flops=4 * 10**8, bytes_accessed=6 * 10**6, transcendentals=2 * 10**6),
        name="recurrence",
    )(xb, halo, weights, cp, starts)


def gelu_parts(v):
    inner = 0.7978845608028654 * (v + 0.044715 * v * v * v)
    t = jnp.tanh(inner)
    value = 0.5 * v * (1.0 + t)
    slope = 0.5 * (1.0 + t) + 0.5 * v * (1.0 - t * t) * 0.7978845608028654 * (1.0 + 3.0 * 0.044715 * v * v)
    return value, slope


def adjoint_kernel(do, h_ref, y_ref, a_ref, dy_ref, lam_ref, c_ref, dh_ref):
    rows, length = do.shape[0], do.shape[1]
    value, slope = gelu_parts(y_ref[...])
    dy_ref[...] = (do[...] * h_ref[...] * slope).astype(BF16)
    dh_ref[...] = do[...] * value

    def eight(step, carry):
        i = length // 8 - 1 - step
        at = pl.ds(pl.multiple_of(i * 8, 8), 8)
        out = []
        for row in range(rows):
            ahead, c = carry[row]
            a, d = a_ref[row, at, :], dh_ref[row, at, :]
            ls, cs = [None] * 8, [None] * 8
            for j in range(7, -1, -1):
                lam = d[j : j + 1] + ahead
                ls[j], cs[j] = lam, c
                ahead = a[j : j + 1] * lam
                c = a[j : j + 1] * c
            lam_ref[row, at, :] = jnp.concatenate(ls, axis=0)
            c_ref[row, at, :] = jnp.concatenate(cs, axis=0)
            out.append((ahead, c))
        return tuple(out)

    zero, one = jnp.zeros((1, BLK), F32), jnp.ones((1, BLK), F32)
    lax.fori_loop(0, length // 8, eight, ((zero, one),) * rows)


def adjoint(do, h, ypre, a):
    rows, length, channels = do.shape
    wide = pl.BlockSpec((rows, length, BLK), lambda i: (0, 0, i))
    return pl.pallas_call(
        adjoint_kernel,
        grid=(channels // BLK,),
        in_specs=[wide] * 4,
        out_specs=[wide] * 3,
        out_shape=[jax.ShapeDtypeStruct(do.shape, BF16)] + [jax.ShapeDtypeStruct(do.shape, F32)] * 2,
        scratch_shapes=[pltpu.VMEM((rows, length, BLK), F32)],
        compiler_params=pltpu.CompilerParams(vmem_limit_bytes=40 << 20),
        cost_estimate=pl.CostEstimate(flops=10**7, bytes_accessed=9 * 10**6, transcendentals=10**6),
        name="adjoint",
    )(do, h, ypre, a)


def gates_back_kernel(lam_ref, c_ref, inc, h_ref, h_in, u_ref, weights, cp, starts, du_ref, dw_ref, sums_ref):
    rows, length = u_ref.shape[0], u_ref.shape[1]
    tokens = rows * length
    p = cp[...]
    u = u_ref[...]
    uf = u.astype(F32)
    start = starts[...]
    start = jnp.concatenate([start, start], axis=2)
    w = weights[...]
    r, ig, decayed, rest = gates_of(u, w, p, start)
    mult = jnp.where(start > 0.5, 1.0, jnp.sqrt(rest))
    lam = lam_ref[...] + c_ref[...] * inc[...]
    before = jnp.stack([jnp.concatenate([h_in[row], h_ref[row][: length - 1]], axis=0) for row in range(rows)])
    keep = 1.0 - start
    d_la = lam * before * decayed * keep - jnp.where(
        start > 0.5, 0.0, lam * ig * uf * decayed * decayed * lax.rsqrt(jnp.where(start > 0.5, 1.0, rest))
    )
    dpa = d_la * (-8.0 * p[7:8][None]) * r * (1.0 - r)
    direct = lam * mult
    dpi = direct * uf * ig * (1.0 - ig)
    d_decay = d_la * (8.0 * p[8:9][None]) * r
    dz = jnp.concatenate(
        [dpa.reshape(tokens, BLK).astype(BF16), dpi.reshape(tokens, BLK).astype(BF16)], axis=1
    )
    back = lax.dot_general(dz, w, (((1,), (1,)), ((), ())), preferred_element_type=F32)
    du_ref[...] = (direct * ig + back.reshape(u.shape)).astype(BF16)
    dw_ref[...] = lax.dot_general(
        u.reshape(tokens, BLK), dz, (((0,), (0,)), ((), ())), preferred_element_type=F32
    )
    zero = jnp.zeros((5, BLK), F32)
    sums_ref[...] = jnp.concatenate(
        [jnp.sum(v.reshape(tokens, BLK), axis=0, keepdims=True) for v in (dpa, dpi, d_decay)] + [zero], axis=0
    )


def gates_back(lam, coef, inc, h, h_in, u, weights, cp, starts):
    rows, length, channels = u.shape
    wide = pl.BlockSpec((rows, length, BLK), lambda i: (0, 0, i))
    line = pl.BlockSpec((rows, 1, BLK), lambda i: (0, 0, i))
    square = pl.BlockSpec((BLK, 2 * BLK), lambda i: (i, 0))
    return pl.pallas_call(
        gates_back_kernel,
        grid=(channels // BLK,),
        in_specs=[
            wide, wide, line, wide, line, wide, square,
            pl.BlockSpec((cp.shape[0], BLK), lambda i: (0, i)),
            pl.BlockSpec(starts.shape, lambda i: (0, 0, 0)),
        ],
        out_specs=[wide, square, pl.BlockSpec((8, BLK), lambda i: (0, i))],
        out_shape=[
            jax.ShapeDtypeStruct(u.shape, BF16),
            jax.ShapeDtypeStruct((channels, 2 * BLK), F32),
            jax.ShapeDtypeStruct((8, channels), F32),
        ],
        compiler_params=pltpu.CompilerParams(vmem_limit_bytes=40 << 20),
        cost_estimate=pl.CostEstimate(flops=12 * 10**8, bytes_accessed=9 * 10**6, transcendentals=2 * 10**6),
        name="gates_back",
    )(lam, coef, inc, h, h_in, u, weights, cp, starts)


def log1p_small(e):
    series = jnp.ones_like(e) * (1.0 / 14)
    for k in range(13, 0, -1):
        series = 1.0 / k - e * series
    return jnp.where(e < 0.25, e * series, jnp.log(1.0 + e))


def front_kernel(n, *refs):
    (
        wx, wy, wo, gs, wg, wu, wd, rows_in, cot, starts, spread_r, pick_r, spread_d, pick_d,
        o_xy, o_out, o_gates, o_cp, o_gains, o_gu, o_d, o_cot, o_starts, o_ypre, o_u, o_a, o_h, o_hin, o_xb, o_before,
        o_x1, o_n2, o_n1t, o_ot, o_hidden, o_gate, o_up, o_pd,
        v_xy, v_out, v_gs, v_gates, v_rows, v_cot, v_starts, v_cp, v_gains, v_n1, v_n1t, v_xb, v_ypre, v_halo, v_u, v_a,
        v_b, v_h, v_c, v_carry, v_o, v_osib, v_ot, v_part, v_theirs, v_psib, v_x1, v_n2, v_w, v_hidden, v_gu, v_pd,
        local_sem, send_sem, recv_sem, load_sem, store_sem, pd_sem,
    ) = refs
    dp, x = lax.axis_index("dp"), lax.axis_index("tp")
    chip, core = dp // 2, dp % 2
    other = 1 - core
    pos = place_of(chip, n)
    half = n // 2
    nxt = (chip_at((pos + 1) % n, n) * 2 + core, x)
    prv = (chip_at((pos + n - 1) % n, n) * 2 + core, x)
    sib = (chip * 2 + other, x)
    over = (dp, 1 - x)
    greet([nxt, prv, sib, over])
    copies = Copies(local_sem, send_sem, recv_sem)
    send, stay = copies.send, copies.stay
    tokens, width = rows_in.shape
    rec = wx.shape[1]
    rh = rec // 2
    own, own_d = wo.shape[0], wx.shape[0]
    fh = wg.shape[1] // 2
    kept, every = [], []

    def put(src, dst):
        kept.append(stay(src, dst))

    def give(src, dst, device):
        copy = send(src, dst, device)
        every.append(copy)
        return copy

    def land(group):
        for copy in group:
            copy.wait_recv()

    class Chain:
        def __init__(self, pieces, arrived=None):
            self.pieces, self.arrived, self.hop = pieces, arrived, 0
            self.ways = ((nxt, n - 1), (prv, 1))
            self.moving = ([], [])

        def start(self, part):
            self.hop = 1
            for ref, own_core in self.pieces(pos):
                if own_core == part:
                    for way, (device, _) in enumerate(self.ways):
                        self.moving[way].append(give(ref, ref, device))
                    if self.arrived:
                        self.arrived(ref)

        def advance(self):
            self.hop += 1
            fresh = ([], [])
            blocks = [self.pieces((pos + back * (self.hop - 1)) % n) for _, back in self.ways]
            for i in range(len(blocks[0])):
                for way, (device, _) in enumerate(self.ways):
                    ref, own_core = blocks[way][i]
                    self.moving[way][i].wait_recv()
                    if self.hop < half or own_core == (way == 0):
                        fresh[way].append(give(ref, ref, device))
                    if self.arrived:
                        self.arrived(ref)
            self.moving = fresh

        def to_last(self):
            while self.hop < half:
                self.advance()

        def finish(self):
            block = self.pieces((pos + half) % n)
            for way in (0, 1):
                refs = [ref for ref, own_core in block if own_core == (way == 0)]
                for copy, ref in zip(self.moving[way], refs):
                    copy.wait_recv()
                    if self.arrived:
                        self.arrived(ref)

    parts = [(wx, v_xy.at[chip, core, x, :, pl.ds(0, rh)]), (wy, v_xy.at[chip, core, x, :, pl.ds(rh, rh)])]
    mine = [stay(half_cols(src, core), slot) for src, slot in parts]
    mine.append(stay(half_cols(wo, core), v_out.at[heads_first(chip, core, n), core, x]))
    mine.append(stay(gs, v_gs.at[core, chip, x]))
    pair = [give(half_cols(src, other), slot, sib) for src, slot in parts]
    pair.append(give(half_cols(wo, other), v_out.at[heads_first(chip, other, n), core, x], sib))

    crossed, held = [], []

    def rec_pieces(place):
        c = chip_at(place, n)
        at = heads_first(c, core, n)
        return [
            (v_xy.at[c, core, x], True), (v_gs.at[core, c, x], True), (v_out.at[at, core, x], True),
            (v_xy.at[c, other, x], False), (v_out.at[at, other, x], False),
        ]

    def rec_arrived(ref):
        if len(ref.shape) == 2 and ref.shape[1] == width // 2:
            held.append(ref)
        else:
            crossed.append(give(ref, ref, over))

    rec_chain = Chain(rec_pieces, rec_arrived)
    gu = Chain(lambda place: [
        (o_gu.at[chip_at(place, n), core], True), (o_gu.at[chip_at(place, n), other], False)
    ])
    down = Chain(lambda place: [(o_d.at[place, core], True), (o_d.at[place, other], False)])
    for copy in mine:
        copy.wait()
    rec_chain.start(True)
    land(pair)
    rec_chain.start(False)
    parts = [
        (wg, o_gu.at[chip, core, :, pl.ds(0, fh)]),
        (wu, o_gu.at[chip, core, :, pl.ds(fh, fh)]),
        (wd, o_d.at[pos, core]),
    ]
    late = [give(half_cols(src, other), slot, sib) for src, slot in parts]
    plain = [stay(half_cols(src, core), slot) for src, slot in parts]
    late += [give(rows_in, v_rows.at[1], sib), give(starts, v_starts.at[1], sib), give(cot, v_cot.at[2], sib)]
    plain += [stay(rows_in, v_rows.at[0]), stay(starts, v_starts.at[0]), stay(cot, v_cot.at[0])]
    rec_chain.to_last()
    land(late)
    for copy in plain:
        copy.wait()
    gu.start(True)
    gu.start(False)
    rec_chain.finish()
    swap = [give(v_gs.at[core, :, x], v_gs.at[core, :, x], sib)]
    put(v_starts, o_starts)
    if half > 3:
        gu.advance()
    land(crossed)
    swap.append(give(v_gs.at[core, :, 1 - x], v_gs.at[core, :, 1 - x], sib))
    outs = []

    def cross_held(count):
        for _ in range(min(count, len(held))):
            ref = held.pop(0)
            outs.append(give(ref, ref, over))

    cross_held(4)
    put(v_xy, o_xy)
    land(swap)

    small = v_gs[:, :, :, own : own + PAD, :128].reshape(4 * n * PAD, 128)
    spread = jnp.dot(small, spread_r[...], preferred_element_type=F32).reshape(4 * n, PAD, rh)
    heads = pick_r[:, pl.ds(pl.multiple_of(core * rh, 128), rh)]
    lines = jnp.sum(spread[:, :8] * heads[:, None, :], axis=0)
    decay = lines[7:8]
    e = jnp.exp(-jnp.abs(decay))
    v_cp[0:8, :] = lines
    v_cp[7:8, :] = jnp.maximum(-decay, 0.0) + log1p_small(e)
    v_cp[8:16, :] = jnp.broadcast_to(jax.nn.sigmoid(-decay), (8, rh))
    for i in range(width // WIDE):
        at = pl.ds(i * WIDE, WIDE)
        wide = jnp.dot(small, spread_d[:, at], preferred_element_type=F32).reshape(4 * n, PAD, WIDE)
        v_gains[:, at] = jnp.sum(wide[:, 8:] * pick_d[:, at][:, None, :], axis=0)
    for i in range(2 * n):
        v_gates[i * own : (i + 1) * own, :] = v_gs[(i // 2) % 2, core * half + i // 4, i % 2, 0:own, :]
    put(v_cp, o_cp)
    put(v_gains, o_gains)
    put(v_gates, o_gates)

    values = v_rows[...].astype(F32)
    scale = lax.rsqrt(jnp.mean(values * values, axis=-1, keepdims=True) + EPS)
    v_n1[...] = (values * scale * v_gains[0:1, :]).astype(BF16).reshape(2 * tokens, width)

    def project_x(i, _):
        at = pl.ds(pl.multiple_of(i * BLK, BLK), BLK)
        w = v_xy[:, :, :, :, at].reshape(width, BLK)
        v_xb[:, :, at] = jnp.dot(v_n1[...], w, preferred_element_type=F32).astype(BF16).reshape(2, tokens, BLK)
        return 0

    def project_y(i, _):
        at = pl.ds(pl.multiple_of(i * BLK, BLK), BLK)
        w = v_xy[:, :, :, :, pl.ds(pl.multiple_of(rh + i * BLK, BLK), BLK)].reshape(width, BLK)
        v_ypre[:, :, at] = jnp.dot(v_n1[...], w, preferred_element_type=F32).reshape(2, tokens, BLK)
        return 0

    lax.fori_loop(0, rh // BLK, project_x, 0)
    halo = give(v_xb.at[:, pl.ds(tokens - 16, 16)], v_halo, over)
    cross_held(4)
    put(v_xb, o_xb)
    if half > 3:
        gu.advance()
    lax.fori_loop(0, rh // BLK, project_y, 0)
    put(v_ypre, o_ypre)
    chips_n = BLK // (4 * own_d)

    def turn_n1(i, _):
        at = pl.ds(pl.multiple_of(i * BLK, BLK), BLK)
        turned = v_n1[:, at].astype(F32).T.astype(BF16)
        v_n1t[pl.ds(i * chips_n, chips_n)] = turned.reshape(chips_n, 2, 2, own_d, 2 * tokens)
        return 0

    lax.fori_loop(0, width // BLK, turn_n1, 0)
    halo.wait_recv()
    v_halo[...] = jnp.where(x == 0, jnp.zeros_like(v_halo), v_halo[...])
    put(v_halo, o_before)
    put(v_n1t.at[:, :, x], o_n1t.at[:, :, :, pl.ds(0, 2 * tokens)])

    def head(i, _):
        at = pl.ds(pl.multiple_of(i * BLK, BLK), BLK)
        p = v_cp[:, at]
        us = []
        for row in range(2):
            padded = jnp.concatenate([v_halo[row, :, at].astype(F32)[8:], v_xb[row, :, at].astype(F32)], axis=0)
            total = p[4:5] + p[0:1] * padded[8 : 8 + tokens]
            for k in range(1, 4):
                total = total + p[k : k + 1] * padded[8 - k : 8 - k + tokens]
            us.append(total.astype(BF16))
        u = jnp.stack(us)
        v_u[:, :, at] = u
        start = v_starts[...]
        start = jnp.concatenate([start, start], axis=2)
        _, ig, decayed, rest = gates_of(u, v_gates[at, :], p, start)
        v_a[:, :, at] = decayed * (1.0 - start)
        v_b[...] = jnp.where(start > 0.5, 1.0, jnp.sqrt(rest)) * ig * u.astype(F32)

        def eight(j, carry):
            rows8 = pl.ds(pl.multiple_of(j * 8, 8), 8)
            out = []
            for row in range(2):
                h, c = carry[row]
                a, b = v_a[row, rows8, at], v_b[row, rows8, :]
                hs, cs = [], []
                for k in range(8):
                    h = a[k : k + 1] * h + b[k : k + 1]
                    c = a[k : k + 1] * c
                    hs.append(h)
                    cs.append(c)
                v_h[row, rows8, at] = jnp.concatenate(hs, axis=0)
                v_c[row, rows8, at] = jnp.concatenate(cs, axis=0)
                out.append((h, c))
            return tuple(out)

        zero, one = jnp.zeros((1, BLK), F32), jnp.ones((1, BLK), F32)
        lax.fori_loop(0, tokens // 8, eight, ((zero, one),) * 2)
        return 0

    lax.fori_loop(0, rh // BLK, head, 0)
    carry = give(v_h.at[:, pl.ds(tokens - 8, 8)], v_carry, over)
    put(v_u, o_u)
    put(v_a, o_a)
    carry.wait_recv()
    carry.wait_send()
    cross_held(len(held))
    v_carry[...] = jnp.where(x == 0, jnp.zeros_like(v_carry), v_carry[...])
    put(v_carry, o_hin)

    def output(i, _):
        at = pl.ds(pl.multiple_of(i * BLK, BLK), BLK)
        h = v_h[:, :, at] + v_c[:, :, at] * v_carry[:, 7:8, at]
        v_h[:, :, at] = h
        value, _ = gelu_parts(v_ypre[:, :, at])
        v_o[:, :, at] = (h * value).astype(BF16)
        return 0

    lax.fori_loop(0, rh // BLK, output, 0)
    o_pair = give(v_o, v_osib, sib)
    put(v_h, o_h)
    gu.to_last()
    down.start(True)
    down.start(False)
    o_pair.wait_recv()
    land(outs)
    put(v_out, o_out)

    def project_row(row, ref):
        def tile(i, _):
            at = pl.ds(pl.multiple_of(i * BLK, BLK), BLK)
            w0 = v_out[0:half, :, :, :, at].reshape(rh, BLK)
            w1 = v_out[half:n, :, :, :, at].reshape(rh, BLK)
            ref[:, at] = jnp.dot(v_o[row], w0, preferred_element_type=F32) + jnp.dot(
                v_osib[1 - row], w1, preferred_element_type=F32
            )
            return 0

        lax.fori_loop(0, width // 2 // BLK, tile, 0)

    project_row(1, v_theirs)
    x1_pair = give(v_theirs, v_psib, sib)
    project_row(0, v_part)
    x1_pair.wait_recv()
    at_mine = pl.ds(pl.multiple_of(core * (width // 2), 128), width // 2)
    at_theirs = pl.ds(pl.multiple_of(other * (width // 2), 128), width // 2)
    v_x1[:, at_mine] = v_rows[0, :, at_mine].astype(F32) + v_part[...]
    v_x1[:, at_theirs] = v_rows[0, :, at_theirs].astype(F32) + v_psib[...]
    put(v_x1, o_x1)
    x1 = v_x1[...]
    scale = lax.rsqrt(jnp.mean(x1 * x1, axis=-1, keepdims=True) + EPS)
    v_n2[0] = (x1 * scale * v_gains[1:2, :]).astype(BF16)
    n2_over = give(v_n2.at[0], v_n2.at[1], over)
    n2_pair = give(v_n2.at[0], v_n2.at[2], sib)
    cot_over = give(v_cot.at[0], v_cot.at[1], over)
    n1_over = give(v_n1t.at[:, :, 1 - x], o_n1t.at[:, :, :, pl.ds(2 * tokens, 2 * tokens)], over)

    chips_o = 640 // (4 * own)

    def turn_o(i, _):
        at = pl.ds(pl.multiple_of(i * 640, 128), 640)
        here = v_o[:, :, at].astype(F32).reshape(2 * tokens, 640).T.astype(BF16)
        v_ot[pl.ds(i * chips_o, chips_o)] = here.reshape(chips_o, 2, 2, own, 2 * tokens)
        there = jnp.concatenate([v_osib[1, :, at], v_osib[0, :, at]], axis=0).astype(F32).T.astype(BF16)
        v_ot[pl.ds(half + i * chips_o, chips_o)] = there.reshape(chips_o, 2, 2, own, 2 * tokens)
        return 0

    lax.fori_loop(0, rh // 640, turn_o, 0)
    o_over = give(v_ot.at[:, :, 1 - x], o_ot.at[:, :, :, pl.ds(2 * tokens, 2 * tokens)], over)
    put(v_ot.at[:, :, x], o_ot.at[:, :, :, pl.ds(0, 2 * tokens)])

    tile = 128
    steps = fh // tile

    def loads(t, slot):
        first = pl.ds(pl.multiple_of(t * tile, tile), tile)
        second = pl.ds(pl.multiple_of(fh + t * tile, tile), tile)
        return [
            pltpu.make_async_copy(o_gu.at[:, :, :, first], v_w.at[slot, :, :, :, pl.ds(0, tile)], load_sem.at[slot, 0]),
            pltpu.make_async_copy(
                o_gu.at[:, :, :, second], v_w.at[slot, :, :, :, pl.ds(tile, tile)], load_sem.at[slot, 1]
            ),
        ]

    def stores(t, slot):
        at = pl.ds(pl.multiple_of(t * tile, tile), tile)
        return [
            pltpu.make_async_copy(v_gu.at[slot, :, pl.ds(0, tile)], o_gate.at[:, at], store_sem.at[slot, 0]),
            pltpu.make_async_copy(v_gu.at[slot, :, pl.ds(tile, tile)], o_up.at[:, at], store_sem.at[slot, 1]),
        ]

    gu.finish()
    for copy in loads(0, 0):
        copy.start()
    n2_pair.wait_recv()
    n2_over.wait_recv()
    n2_last = give(v_n2.at[1], v_n2.at[3], sib)
    n2_last.wait_recv()
    if half > 3:
        down.advance()
    put(v_n2, o_n2)

    def hidden_tile(t, _):
        slot = t % 2
        for copy in loads(t, slot):
            copy.wait()

        @pl.when(t + 1 < steps)
        def _():
            for copy in loads(t + 1, 1 - slot):
                copy.start()

        @pl.when(t >= 2)
        def _():
            for copy in stores(t - 2, slot):
                copy.wait()

        w = v_w[slot].reshape(width, 2 * tile)
        v_gu[slot] = jnp.dot(v_n2[...].reshape(4 * tokens, width), w, preferred_element_type=F32)
        for copy in stores(t, slot):
            copy.start()
        value, _ = gelu_parts(v_gu[slot, :, 0:tile])
        v_hidden[:, pl.ds(pl.multiple_of(t * tile, tile), tile)] = (value * v_gu[slot, :, tile:]).astype(BF16)
        return 0

    lax.fori_loop(0, steps, hidden_tile, 0)
    put(v_hidden, o_hidden)
    cot_over.wait_recv()
    cot_last = give(v_cot.at[1], v_cot.at[3], sib)
    if half > 3:
        down.advance()
    cot_last.wait_recv()
    put(v_cot, o_cot)

    def pd_store(t, slot):
        return pltpu.make_async_copy(v_pd.at[slot], o_pd.at[pl.ds(pl.multiple_of(t * BLK, BLK), BLK)], pd_sem.at[slot])

    def down_tile(t, _):
        slot = t % 2

        @pl.when(t >= 2)
        def _():
            pd_store(t - 2, slot).wait()

        left = v_cot[:, :, pl.ds(pl.multiple_of(t * BLK, BLK), BLK)].reshape(4 * tokens, BLK)
        v_pd[slot] = lax.dot_general(
            left, v_hidden[...], (((0,), (0,)), ((), ())), preferred_element_type=F32
        ).astype(BF16)
        pd_store(t, slot).start()
        return 0

    lax.fori_loop(0, width // BLK, down_tile, 0)
    down.to_last()
    for t in (steps - 2, steps - 1):
        for copy in stores(t, t % 2):
            copy.wait()
    for t in (width // BLK - 2, width // BLK - 1):
        pd_store(t, t % 2).wait()
    down.finish()
    land([n1_over, o_over])
    for copy in kept:
        copy.wait()
    for copy in every:
        if copy is not carry:
            copy.wait_send()


def front(n, wx, wy, wo, gs, wg, wu, wd, rows_in, cot, starts):
    rec, f = wx.shape[1], wg.shape[1]
    own, own_d, rows_f = wo.shape[0], wx.shape[0], wg.shape[0]
    rh, fh = rec // 2, f // 2
    tokens, width = rows_in.shape
    half = n // 2
    row = np.arange(4 * n)
    index = (row // 2) % n * 4 + row // (2 * n) * 2 + row % 2
    lane_r, lane_d, short = np.arange(rec), np.arange(width), np.arange(128)[:, None]
    spread_r = (lane_r[None, :rh] % own == short).astype(jnp.bfloat16)
    spread_d = (lane_d[None] % own_d == short).astype(jnp.bfloat16)
    pick_r = (index[:, None] == lane_r[None] // own).astype(np.float32)
    pick_d = (index[:, None] == lane_d[None] // own_d).astype(np.float32)
    outs = dict(
        w_xy=((n, 2, 2, own_d, rec), BF16),
        w_o=((n, 2, 2, own, width // 2), BF16),
        gates=((rh, WIDE), BF16),
        cp=((16, rh), F32),
        gains=((8, width), F32),
        w_gu=((n, 2, rows_f, f), BF16),
        w_d=((n, 2, rows_f, fh), BF16),
        cot=((4, tokens, width), BF16),
        starts=((2, tokens, 128), F32),
        ypre=((2, tokens, rh), F32),
        u=((2, tokens, rh), BF16),
        a=((2, tokens, rh), F32),
        h=((2, tokens, rh), F32),
        h_in=((2, 8, rh), F32),
        xb=((2, tokens, rh), BF16),
        before=((2, 16, rh), BF16),
        x1=((tokens, width), F32),
        n2=((4, tokens, width), BF16),
        n1_t=((n, 2, own_d, 4 * tokens), BF16),
        o_t=((n, 2, own, 4 * tokens), BF16),
        hidden=((4 * tokens, fh), BF16),
        gate=((4 * tokens, fh), F32),
        up=((4 * tokens, fh), F32),
        part_d=((width, fh), BF16),
    )
    state = (2, tokens, rh)
    scratch = [
        ((n, 2, 2, own_d, rec), BF16), ((n, 2, 2, own, width // 2), BF16), ((2, n, 2) + gs.shape, BF16),
        ((rh, WIDE), BF16), ((2, tokens, width), BF16), ((4, tokens, width), BF16), ((2, tokens, 128), F32),
        ((16, rh), F32), ((8, width), F32), ((2 * tokens, width), BF16), ((n, 2, 2, own_d, 2 * tokens), BF16),
        (state, BF16), (state, F32), ((2, 16, rh), BF16), (state, BF16), (state, F32),
        ((2, tokens, BLK), F32), (state, F32), (state, F32), ((2, 8, rh), F32), (state, BF16), (state, BF16),
        ((n, 2, 2, own, 2 * tokens), BF16), ((tokens, width // 2), F32), ((tokens, width // 2), F32),
        ((tokens, width // 2), F32), ((tokens, width), F32), ((4, tokens, width), BF16),
        ((2, n, 2, rows_f, BLK), BF16), ((4 * tokens, fh), BF16), ((2, 4 * tokens, BLK), F32), ((2, BLK, fh), BF16),
    ]
    count = 9 + (5 * n - 5) + 2 * (2 * n - 2) + 5 * n + 2 + 12
    dma = pltpu.SemaphoreType.DMA
    result = pl.pallas_call(
        functools.partial(front_kernel, n),
        out_shape=[jax.ShapeDtypeStruct(shape, kind) for shape, kind in outs.values()],
        in_specs=[pl.BlockSpec(memory_space=pl.ANY)] * 10 + [pl.BlockSpec(memory_space=pltpu.VMEM)] * 4,
        out_specs=[pl.BlockSpec(memory_space=pl.ANY)] * len(outs),
        scratch_shapes=[pltpu.VMEM(shape, kind) for shape, kind in scratch]
        + [dma((32,)), dma((count,)), dma((count,)), dma((2, 2)), dma((2, 2)), dma((2,))],
        compiler_params=pltpu.CompilerParams(
            collective_id=2, has_side_effects=True, vmem_limit_bytes=60 << 20
        ),
        name="front",
    )(wx, wy, wo, gs, wg, wu, wd, rows_in, cot, starts, spread_r, pick_r, spread_d, pick_d)
    return dict(zip(outs, result))


def finish_kernel(block, theirs, gate_ref, up_ref):
    core = lax.axis_index("dp") % 2
    half = gate_ref.shape[1] // 2

    def place(mine, other):
        for first, values in ((0, (mine, other)), (1, (other, mine))):

            @pl.when(core == first)
            def _():
                for i, value in enumerate(values):
                    at = pl.ds(i * half, half)
                    gate_ref[:, at] = value[:, :half].astype(F32)
                    up_ref[:, at] = value[:, half:].astype(F32)

    place(block[core], theirs[...])


def finish(block, theirs):
    _, rows, cols = block.shape
    tile = 32 if rows % 32 == 0 else rows
    out = pl.BlockSpec((tile, cols), lambda i: (i, 0))
    return pl.pallas_call(
        finish_kernel,
        grid=(rows // tile,),
        in_specs=[pl.BlockSpec((2, tile, cols), lambda i: (0, i, 0)), out],
        out_specs=[out, out],
        out_shape=[jax.ShapeDtypeStruct((rows, cols), F32)] * 2,
        compiler_params=pltpu.CompilerParams(vmem_limit_bytes=24 << 20),
        name="finish",
    )(block, theirs)


def nt(left, right):
    return lax.dot_general(left, right, (((1,), (1,)), ((), ())), preferred_element_type=F32)


def nn(left, right):
    return jnp.dot(left, right, preferred_element_type=F32)


def body(
    dp_size,
    layer_input, grad_out, lengths, resets, norm_gain, w_x, w_y, conv_w, conv_b, gate_a_w, gate_a_b,
    gate_i_w, gate_i_b, decay_param, w_out, mlp_gain, w_gate, w_up, w_down,
):
    n = dp_size // 2
    half = n // 2
    dp, x = lax.axis_index("dp"), lax.axis_index("tp")
    chip, core = dp // 2, dp % 2
    pos = place_of(chip, n)
    tokens, width = layer_input.shape[1], layer_input.shape[2]
    rec = w_x.shape[1]
    rh = rec // 2
    taps = conv_w.shape[0]
    own = rec // (2 * dp_size)
    own_d = width // (2 * dp_size)

    ring = [chip_at(i, n) for i in range(n)]
    up = [(ring[i] * 2 + c, ring[(i + 1) % n] * 2 + c) for i in range(n) for c in range(2)]
    down = [(b, a) for a, b in up]
    lanes = [[chip_id * 2 + c for chip_id in ring] for c in range(2)]
    pairs = [(d, d + 1 - 2 * (d % 2)) for d in range(dp_size)]

    def sibling(v):
        return lax.ppermute(v, "dp", pairs)

    def across(v):
        return lax.ppermute(v, "tp", [(0, 1), (1, 0)])

    def swapped(v):
        return jnp.concatenate([v[1:], v[:1]], axis=0)

    def by_core(mine, theirs, axis):
        return jnp.where(
            core == 0, jnp.concatenate([mine, theirs], axis), jnp.concatenate([theirs, mine], axis)
        )

    def ring_order(array, axis):
        size = array.shape[axis] // n
        return jnp.concatenate([lax.slice_in_dim(array, i * size, (i + 1) * size, axis=axis) for i in ring], axis)

    def chip_order(array, axis):
        size = array.shape[axis] // n
        return jnp.concatenate(
            [lax.slice_in_dim(array, ring.index(i) * size, (ring.index(i) + 1) * size, axis=axis) for i in range(n)],
            axis,
        )

    def after(value, *others):
        return lax.optimization_barrier((value,) + others)[0]

    rows_own = layer_input.reshape(tokens, width)
    place = x * tokens + jnp.arange(tokens, dtype=jnp.int32)
    starts = jnp.where((resets.reshape(tokens) > 0) | (place == 0), 1.0, 0.0).astype(F32)
    starts = jnp.broadcast_to(starts[:, None], (tokens, 128))
    valid = (place < lengths[0]).astype(F32)[:, None]
    cot = grad_out.reshape(tokens, width).astype(F32) * valid

    def lane_sum(array):
        return lax.psum_scatter(array, "dp", scatter_dimension=0, tiled=True, axis_index_groups=lanes)

    def plane(array, which):
        return lax.dynamic_index_in_dim(array, which, 2, keepdims=False)

    def both(mine, axis):
        return jnp.concatenate([mine, across(mine)], axis)

    def tn(left, right):
        return lax.dot_general(left, right, (((0,), (0,)), ((), ())), preferred_element_type=F32)

    fh = w_gate.shape[1] // 2
    cot_ring = ring_order(cot.astype(BF16), 1)
    if own % 16 == 0 and own_d % 16 == 0:
        vectors = jnp.concatenate([conv_w, jnp.stack([conv_b, gate_a_b, gate_i_b, decay_param])], axis=0)
        vectors = jnp.pad(vectors, ((0, 0), (0, WIDE - own)))
        gains = jnp.pad(jnp.stack([norm_gain, mlp_gain]), ((0, PAD - taps - 6), (0, WIDE - own_d)))
        gs = jnp.concatenate([jnp.concatenate([gate_a_w, gate_i_w], axis=1), vectors, gains], axis=0)
        got = front(n, w_x, w_y, w_out, gs, w_gate, w_up, w_down.T, rows_own, cot_ring, starts)
        w_xy, w_o = got["w_xy"].reshape(width, rec), got["w_o"].reshape(rec, width // 2)
        w_gu, w_d = got["w_gu"].reshape(width, 2 * fh), got["w_d"].reshape(width, fh)
        cot_all, n2_all = got["cot"].reshape(4 * tokens, width), got["n2"].reshape(4 * tokens, width)
        gain_one, gain_two, cp, gates = got["gains"][0], got["gains"][1], got["cp"], got["gates"]
        starts_two, ypre, u, a, h, xb, x1 = (got[key] for key in ("starts", "ypre", "u", "a", "h", "xb", "x1"))
        h_in, before = got["h_in"][:, 7:8], got["before"][:, PAD - taps + 1 :]
        n1_t, o_t = got["n1_t"].reshape(width // 2, 4 * tokens), got["o_t"].reshape(rh, 4 * tokens)
        hidden, gate, upv, part_d = got["hidden"], got["gate"], got["up"], got["part_d"]
        rs2 = lax.rsqrt(jnp.mean(x1 * x1, axis=-1, keepdims=True) + EPS)
    else:
        small = jnp.concatenate(
            [norm_gain, mlp_gain, conv_w.reshape(-1), conv_b, gate_a_b, gate_i_b, decay_param]
        )
        small = jnp.pad(small, (0, PAD * WIDE - small.shape[0])).reshape(PAD, WIDE)
        gs = jnp.concatenate([jnp.concatenate([gate_a_w, gate_i_w], axis=1), small], axis=0)
        w_xy, w_o, all_gs, w_gu, d_block, rows_two, cot_all, starts_two = gather_weights(
            n, w_x, w_y, w_out, gs, w_gate, w_up, w_down.T, rows_own, cot_ring, starts
        )
        w_d = lax.all_gather(
            d_block.reshape(-1, d_block.shape[2]), "dp", axis=0, tiled=True, axis_index_groups=lanes
        )
        w_gu = w_gu.reshape(width, w_gate.shape[1])
        w_xy = w_xy.reshape(width, rec)
        w_o = w_o.reshape(rec, width // 2)
        cot_all = cot_all.reshape(4 * tokens, width)

        vectors = all_gs[:, :, :, own:].transpose(1, 0, 2, 3, 4).reshape(2 * dp_size, PAD * WIDE)
        gain_one = vectors[:, :own_d].reshape(width).astype(F32)
        gain_two = vectors[:, own_d : 2 * own_d].reshape(width).astype(F32)
        lines = vectors[:, 2 * own_d : 2 * own_d + (taps + 4) * own].reshape(2 * dp_size, taps + 4, own)
        lines = lax.dynamic_slice_in_dim(lines, core * dp_size, dp_size, 0)
        lines = lines.transpose(1, 0, 2).reshape(taps + 4, rh).astype(F32)
        decay = lines[taps + 3 :]
        cp = jnp.concatenate(
            [lines[: taps + 3], jax.nn.softplus(-decay), jax.nn.sigmoid(-decay), jnp.zeros((7, rh), F32)], axis=0
        )
        gates = lax.dynamic_slice_in_dim(all_gs[:, :, :, :own], core * half, half, 1)
        gates = gates.transpose(1, 0, 2, 3, 4).reshape(rh, WIDE)

        n1, xb, ypre = project(rows_two, gain_one[None], w_xy)
        before = lax.ppermute(xb[:, tokens - (taps - 1) :], "tp", [(0, 1)])
        halo = jnp.concatenate([jnp.zeros((2, 8 - (taps - 1), rh), F32), before.astype(F32)], axis=1)
        u, a, h_local, coef = recurrence(xb, halo, gates, cp, starts_two)
        h_in = lax.ppermute(h_local[:, tokens - 1 :], "tp", [(0, 1)])
        h = h_local + coef * h_in
        ybr, _ = gelu_parts(ypre)
        o = (h * ybr).astype(BF16)
        o_sib = sibling(o)
        part_mine, part_theirs = project_out(o, o_sib, w_o)
        x1 = rows_own.astype(F32) + by_core(part_mine, sibling(part_theirs), 1)
        rs2 = lax.rsqrt(jnp.mean(x1 * x1, axis=-1, keepdims=True) + EPS)
        n2 = (x1 * rs2 * gain_two).astype(BF16)
        n2_x = across(n2)

        def plane_rows(values, rows):
            grouped = after(values, n2_x).T.reshape(n, 2, 2, rows, 2 * tokens)
            return plane(grouped, x), plane(grouped, 1 - x)

        o_here, o_send = plane_rows(jnp.concatenate([o, swapped(o_sib)], axis=2).reshape(2 * tokens, rec), own)
        n1_here, n1_send = plane_rows(n1, own_d)
        two = jnp.concatenate([n2, n2_x], axis=0)
        n2_all = jnp.concatenate([two, sibling(two)], axis=0)
        o_t = jnp.concatenate([o_here, across(o_send)], axis=3).reshape(rh, 4 * tokens)
        n1_t = jnp.concatenate([n1_here, across(n1_send)], axis=3).reshape(width // 2, 4 * tokens)

        gu = nn(n2_all, w_gu)
        gate, upv = gu[:, :fh], gu[:, fh:]
        act, _ = gelu_parts(gate)
        hidden = (act * upv).astype(BF16)

        part_d = tn(cot_all, hidden).astype(BF16)
    sum_d = lane_sum(part_d)
    act, slope = gelu_parts(gate)
    d_hidden = nn(after(cot_all, part_d), w_d)
    d_gu = jnp.concatenate([(d_hidden * upv * slope).astype(BF16), (d_hidden * act).astype(BF16)], axis=1)

    def pair_sum(partial):
        return (partial[: 2 * tokens].astype(F32) + sibling(partial[2 * tokens :]).astype(F32)).astype(BF16)

    d_n2_pair = pair_sum(nt(d_gu, w_gu).astype(BF16))
    d_n2_send = d_n2_pair[tokens:]
    d_n2 = d_n2_pair[:tokens].astype(F32) + across(d_n2_send).astype(F32)
    part_gu = tn(ring_order(n2_all, 1), after(d_gu, d_n2_send)).astype(BF16)
    sum_gu = lane_sum(part_gu)
    ff_pair = pair_sum(nt(after(hidden, part_gu), w_d).astype(BF16))
    ff_out = ff_pair[:tokens].astype(F32) + across(ff_pair[tokens:]).astype(F32)

    q2 = gain_two * d_n2
    d_gain_two = jnp.sum(d_n2 * x1 * rs2, axis=0)
    d_x1 = cot + rs2 * q2 - x1 * (rs2 * rs2 * rs2) * jnp.mean(x1 * q2, axis=-1, keepdims=True)
    dbr = d_x1.astype(BF16)
    dbr_mine = lax.dynamic_slice_in_dim(dbr, core * (width // 2), width // 2, 1)
    dbr_theirs = lax.dynamic_slice_in_dim(dbr, (1 - core) * (width // 2), width // 2, 1)
    dbr_half = jnp.concatenate([dbr_mine, sibling(dbr_theirs)], axis=0)
    do_part = nt(dbr_half, w_o)
    do = do_part[:, :rh].reshape(2, tokens, rh) + swapped(sibling(do_part[:, rh:].reshape(2, tokens, rh)))
    dbr_x = across(dbr_half)

    d_ypre, lam_local, coef_back = adjoint(do, h, ypre, a)
    d_ypre_x = both(d_ypre.reshape(2 * tokens, rh), 0)
    inc = lax.ppermute(a[:, :1] * lam_local[:, :1], "tp", [(1, 0)])
    du, d_gates, sums = gates_back(lam_local, coef_back, inc, h, h_in, u, gates, cp, starts_two)
    du_next = lax.ppermute(du[:, : taps - 1], "tp", [(1, 0)])
    du_pad = jnp.concatenate([du, du_next], axis=1).astype(F32)
    xb_pad = jnp.concatenate([before, xb], axis=1).astype(F32)
    d_taps = jnp.stack(
        [jnp.sum(du_pad[:, :tokens] * xb_pad[:, taps - 1 - k : taps - 1 - k + tokens], axis=(0, 1)) for k in range(taps)]
    )
    d_bias = jnp.sum(du_pad[:, :tokens], axis=(0, 1))[None]
    d_xb = sum(cp[k] * du_pad[:, k : k + tokens] for k in range(taps)).astype(BF16)
    d_xy = jnp.concatenate([d_xb, d_ypre], axis=2).reshape(2 * tokens, rec)
    result = (after(x1, d_xb) + chip_order(ff_out, 1)).astype(BF16).reshape(1, tokens, width)
    d_n1_part = nt(d_xy, w_xy).reshape(2, tokens, width)
    d_n1 = d_n1_part[0] + sibling(d_n1_part[1])
    q1 = gain_one * d_n1
    own_f = rows_own.astype(F32)
    own_rs = lax.rsqrt(jnp.mean(own_f * own_f, axis=-1, keepdims=True) + EPS)
    d_gain_one = jnp.sum(d_n1 * own_f * own_rs, axis=0)
    grad_x = d_x1 + own_rs * q1 - own_f * (own_rs * own_rs * own_rs) * jnp.mean(own_f * q1, axis=-1, keepdims=True)

    c_out = nn(after(o_t, d_xb), jnp.concatenate([dbr_half, dbr_x], axis=0)).astype(BF16).reshape(n, 2, own, width // 2)
    c_x = nn(n1_t, both(d_xb.reshape(2 * tokens, rh), 0)).astype(BF16).reshape(n, 2, own_d, rh)
    c_y = nn(n1_t, d_ypre_x).astype(BF16).reshape(n, 2, own_d, rh)

    def placed(part):
        zero = jnp.zeros_like(part)
        return by_core_rows(part, zero)

    def by_core_rows(mine, theirs):
        return jnp.where(
            core == 0, jnp.concatenate([mine, theirs], 0), jnp.concatenate([theirs, mine], 0)
        )

    g = d_gates.reshape(half, 2, 2, own, WIDE)
    g = plane(g, x) + across(plane(g, 1 - x).astype(BF16)).astype(F32)
    g_mine = lax.dynamic_index_in_dim(g, core, 1, keepdims=False)
    g_theirs = lax.dynamic_index_in_dim(g, 1 - core, 1, keepdims=False)
    g_lane = by_core_rows(g_mine, sibling(g_theirs))

    lines_back = jnp.concatenate([d_taps, d_bias, sums[:3]], axis=0)
    lines_back = lines_back.reshape(taps + 4, half, 2, 2, own).transpose(1, 2, 3, 0, 4)
    lines_back = placed(lines_back.reshape(half, 2, 2, (taps + 4) * own))
    gains = jnp.concatenate([d_gain_one.reshape(n, 2, 2, own_d), d_gain_two.reshape(n, 2, 2, own_d)], axis=3)
    vec = jnp.concatenate([gains, lines_back], axis=3)
    vec = jnp.pad(vec, ((0, 0), (0, 0), (0, 0), (0, -vec.shape[3] % 128)))
    vec = plane(vec, x) + across(plane(vec, 1 - x))
    vec = lax.dynamic_index_in_dim(vec, core, 1, keepdims=False) + sibling(
        lax.dynamic_index_in_dim(vec, 1 - core, 1, keepdims=False)
    )

    vec = jnp.pad(vec, ((0, 0), (0, -vec.shape[1] % 1024))).reshape(n, -1, 128)
    def whole(block):
        rows = block.shape[0] // 2
        block = block.reshape(2, rows, block.shape[1])
        mine = lax.dynamic_index_in_dim(block, core, 0, keepdims=False)
        theirs = lax.dynamic_index_in_dim(block, 1 - core, 0, keepdims=False)
        return mine, sibling(theirs)

    def halves(pair):
        return by_core(pair[0], pair[1], 1).astype(F32)

    grad_down = halves(whole(sum_d)).T
    grad_w_x, grad_w_y, grad_w_out, sum_gates, sum_vec = scatter_sums(
        n, after(c_x, grad_down, result, grad_x), c_y, c_out, g_lane.astype(BF16), vec
    )
    sum_vec = sum_vec.reshape(-1)
    sum_gu = after(sum_gu, sum_vec).reshape(2, -1, 2 * fh)
    theirs = lax.dynamic_index_in_dim(sum_gu, 1 - core, 0, keepdims=False)
    grad_gate, grad_up = finish(sum_gu, sibling(theirs))
    tail = sum_vec[2 * own_d : 2 * own_d + (taps + 4) * own].reshape(taps + 4, own)
    return (
        result,
        grad_x.reshape(1, tokens, width),
        sum_vec[:own_d],
        grad_w_x,
        grad_w_y,
        tail[:taps],
        tail[taps],
        sum_gates[:, :BLK],
        tail[taps + 1],
        sum_gates[:, BLK:],
        tail[taps + 2],
        tail[taps + 3],
        grad_w_out,
        sum_vec[own_d : 2 * own_d],
        grad_gate,
        grad_up,
        grad_down,
    )


def solution(mesh):
    every = ("dp", "tp")
    return jax.shard_map(
        functools.partial(body, mesh.shape["dp"]),
        mesh=mesh,
        in_specs=(
            P("dp", "tp", None),
            P("dp", "tp", None),
            P("dp"),
            P("dp", "tp"),
            P(every),
            P(every, None),
            P(every, None),
            P(None, every),
            P(every),
            P(every, None),
            P(every),
            P(every, None),
            P(every),
            P(every),
            P(every, None),
            P(every),
            P("dp", "tp"),
            P("dp", "tp"),
            P("tp", "dp"),
        ),
        out_specs=(
            P("dp", "tp", None),
            P("dp", "tp", None),
            P(every),
            P(every, None),
            P(every, None),
            P(None, every),
            P(every),
            P(every, None),
            P(every),
            P(every, None),
            P(every),
            P(every),
            P(every, None),
            P(every),
            P("dp", "tp"),
            P("dp", "tp"),
            P("tp", "dp"),
        ),
        check_vma=False,
    )
```

```python
import functools

import jax
import jax.numpy as jnp
import numpy as np
from jax import lax
from jax.experimental import pallas as pl
from jax.experimental.pallas import tpu as pltpu
from jax.sharding import PartitionSpec as P

BLK = 256
PAD = 16
WIDE = 512
EPS = 1e-06
MESH = pl.DeviceIdType.MESH
F32 = jnp.float32
BF16 = jnp.bfloat16


def chip_at(pos, n):
    back = pos // (n // 2)
    return (1 - back) * (2 * pos) + back * (2 * (n - 1 - pos) + 1)


def place_of(chip, n):
    odd = chip % 2
    return (1 - odd) * (chip // 2) + odd * (n - 1 - chip // 2)


def heads_first(chip, core, n):
    return (chip + n - core * (n // 2)) % n


class Copies:
    def __init__(self, local, sends, recvs):
        self.local, self.sends, self.recvs = local, sends, recvs
        self.locals_used = self.used = 0

    def stay(self, src, dst):
        copy = pltpu.make_async_copy(src, dst, self.local.at[self.locals_used])
        self.locals_used += 1
        copy.start()
        return copy

    def send(self, src, dst, device):
        copy = pltpu.make_async_remote_copy(
            src_ref=src, dst_ref=dst, send_sem=self.sends.at[self.used], recv_sem=self.recvs.at[self.used],
            device_id=device, device_id_type=MESH,
        )
        self.used += 1
        copy.start()
        return copy


def greet(devices):
    barrier = pltpu.get_barrier_semaphore()
    for device in devices:
        pl.semaphore_signal(barrier, inc=1, device_id=device, device_id_type=MESH)
    pl.semaphore_wait(barrier, len(devices))


def half_cols(ref, which):
    width = ref.shape[1] // 2
    return ref.at[:, pl.ds(pl.multiple_of(which * width, 128), width)]


def gather_kernel(
    n,
    wx, wy, wo, gs, wg, wu, wd, rows_in, cot, starts,
    o_xy, o_out, o_gs, o_gu, o_d, o_rows, o_cot, o_starts,
    local_sem, send_sem, recv_sem,
):
    dp, x = lax.axis_index("dp"), lax.axis_index("tp")
    chip, core = dp // 2, dp % 2
    other = 1 - core
    pos = place_of(chip, n)
    half = n // 2
    nxt = (chip_at((pos + 1) % n, n) * 2 + core, x)
    prv = (chip_at((pos + n - 1) % n, n) * 2 + core, x)
    sib = (chip * 2 + other, x)
    over = (dp, 1 - x)
    greet([nxt, prv, sib, over])
    copies = Copies(local_sem, send_sem, recv_sem)
    send, stay = copies.send, copies.stay

    def by_heads(chip_id, which):
        return heads_first(chip_id, which, n)

    rhalf = wx.shape[1] // 2
    fhalf = wg.shape[1] // 2
    rec_parts = [
        (wx, o_xy.at[chip, core, x, :, pl.ds(0, rhalf)]),
        (wy, o_xy.at[chip, core, x, :, pl.ds(rhalf, rhalf)]),
    ]
    ff_parts = [
        (wg, o_gu.at[chip, core, :, pl.ds(0, fhalf)]),
        (wu, o_gu.at[chip, core, :, pl.ds(fhalf, fhalf)]),
        (wd, o_d.at[core]),
    ]
    pair = [send(half_cols(src, other), slot, sib) for src, slot in rec_parts]
    pair.append(send(half_cols(wo, other), o_out.at[by_heads(chip, other), core, x], sib))
    mine = [stay(half_cols(src, core), slot) for src, slot in rec_parts] + [stay(gs, o_gs.at[core, chip, x])]
    mine.append(stay(half_cols(wo, core), o_out.at[by_heads(chip, core), core, x]))
    late = [send(half_cols(src, other), slot, sib) for src, slot in ff_parts]
    plain = [stay(half_cols(src, core), slot) for src, slot in ff_parts]
    late += [send(rows_in, o_rows.at[1], sib), send(starts, o_starts.at[1], sib), send(cot, o_cot.at[2], sib)]
    plain += [stay(rows_in, o_rows.at[0]), stay(starts, o_starts.at[0]), stay(cot, o_cot.at[0])]

    def rec_block(chip_id):
        return [o_xy.at[chip_id, :, x], o_out.at[by_heads(chip_id, core), :, x], o_gs.at[core, chip_id, x]]

    def rec_piece(chip_id, which):
        refs = [o_xy.at[chip_id, which, x], o_out.at[by_heads(chip_id, core), which, x]]
        return refs + ([o_gs.at[core, chip_id, x]] if which == 0 else [])

    def ff_block(chip_id):
        return [o_gu.at[chip_id]]

    def ff_piece(chip_id, which):
        return [o_gu.at[chip_id, which]]

    def send_all(refs, device):
        return [send(ref, ref, device) for ref in refs]

    def hop(s, block, piece):
        ahead = chip_at((pos + n - (s - 1)) % n, n)
        behind = chip_at((pos + s - 1) % n, n)
        if s < half:
            return send_all(block(ahead), nxt) + send_all(block(behind), prv)
        return send_all(piece(ahead, 0), nxt) + send_all(piece(behind, 1), prv)

    for copy in pair:
        copy.wait_recv()
    for copy in mine:
        copy.wait()
    done, crossed, moving = [], send_all(rec_block(chip), over), []
    for s in range(1, half + 1):
        for copy in moving:
            copy.wait_recv()
        done.extend(moving)
        moving = hop(s, rec_block, rec_piece)
        if s > 1:
            crossed.extend(send_all(rec_block(chip_at((pos + n - (s - 1)) % n, n)), over))
            crossed.extend(send_all(rec_block(chip_at((pos + s - 1) % n, n)), over))
    last_rec = moving
    for copy in late:
        copy.wait_recv()
    for copy in plain:
        copy.wait()
    moving = hop(1, ff_block, ff_piece)
    for copy in last_rec:
        copy.wait_recv()
    done.extend(last_rec)
    crossed.extend(send_all(rec_block(chip_at((pos + half) % n, n)), over))
    cot_over = send(cot, o_cot.at[1], over)
    for s in range(2, half + 1):
        for copy in moving:
            copy.wait_recv()
        done.extend(moving)
        moving = hop(s, ff_block, ff_piece)
    for copy in crossed:
        copy.wait_recv()
    swap = send(o_gs.at[core], o_gs.at[core], sib)
    cot_over.wait_recv()
    last = send(o_cot.at[1], o_cot.at[3], sib)
    for copy in moving:
        copy.wait_recv()
    done.extend(moving)
    swap.wait_recv()
    last.wait_recv()
    for copy in pair + late + done + crossed + [cot_over, swap, last]:
        copy.wait_send()


def gather_weights(n, wx, wy, wo, gs, wg, wu, wd, rows_in, cot, starts):
    r, d, (rows_f, f) = wx.shape[1], wo.shape[1], wg.shape
    tokens = rows_in.shape[0]
    shapes = [
        jax.ShapeDtypeStruct((n, 2, 2, wx.shape[0], r), BF16),
        jax.ShapeDtypeStruct((n, 2, 2, wo.shape[0], d // 2), BF16),
        jax.ShapeDtypeStruct((2, n, 2) + gs.shape, BF16),
        jax.ShapeDtypeStruct((n, 2, rows_f, f), BF16),
        jax.ShapeDtypeStruct((2, rows_f, f // 2), BF16),
        jax.ShapeDtypeStruct((2, tokens, d), BF16),
        jax.ShapeDtypeStruct((4, tokens, d), BF16),
        jax.ShapeDtypeStruct((2,) + starts.shape, F32),
    ]
    count = 9 + (3 * n - 1) + n + 3 * n + 3
    dma = pltpu.SemaphoreType.DMA
    return pl.pallas_call(
        functools.partial(gather_kernel, n),
        out_shape=shapes,
        in_specs=[pl.BlockSpec(memory_space=pltpu.VMEM)] * 10,
        out_specs=[pl.BlockSpec(memory_space=pl.ANY)] * 8,
        scratch_shapes=[dma((10,)), dma((count,)), dma((count,))],
        compiler_params=pltpu.CompilerParams(
            collective_id=0, has_side_effects=True, vmem_limit_bytes=24 << 20
        ),
        name="gather_weights",
    )(wx, wy, wo, gs, wg, wu, wd, rows_in, cot, starts)


def scatter_kernel(
    n,
    c_x, c_y, c_out, c_g, c_v,
    g_x, g_y, g_out, g_gates, g_vec,
    r_x, r_y, r_out, r_g, r_v, s_x, s_y, s_out,
    send_sem, recv_sem,
):
    dp, x = lax.axis_index("dp"), lax.axis_index("tp")
    chip, core = dp // 2, dp % 2
    pos = place_of(chip, n)
    half = n // 2
    nxt = (chip_at((pos + 1) % n, n) * 2 + core, x)
    prv = (chip_at((pos + n - 1) % n, n) * 2 + core, x)
    sib = (dp + 1 - 2 * core, x)
    greet([nxt, prv, sib])
    copies = Copies(None, send_sem, recv_sem)

    pieces = []
    for part in (0, 1):
        for terms, slots, first in ((c_out, r_out, core), (c_y, r_y, 0), (c_x, r_x, 0)):
            pieces.append((
                lambda c, terms=terms, part=part, first=first: terms.at[heads_first(c, first, n), part],
                lambda w, k, slots=slots, part=part: slots.at[part, w, k],
                part,
            ))
    pieces.append((lambda c: c_g.at[c], lambda w, k: r_g.at[w, k], 0))
    pieces.append((lambda c: c_v.at[c], lambda w, k: r_v.at[w, k], 1))

    def add(a, b):
        return a[...].astype(F32) + b[...].astype(F32)

    sent, coming = [], {}
    for k in range(half, -1, -1):
        for i, (term, slot, far) in enumerate(pieces):
            for way, (device, sign) in enumerate(((nxt, 1), (prv, n - 1))):
                first = half if way == far else half - 1
                if k > first or k == 0:
                    continue
                source = term(chip_at((pos + sign * k) % n, n))
                if k < first:
                    coming[i, way].wait_recv()
                    got = slot(way, k)
                    got[...] = add(got, source).astype(got.dtype)
                    source = got
                copy = copies.send(source, slot(way, k - 1), device)
                coming[i, way] = copy
                sent.append(copy)

    def total(i):
        term, slot, _ = pieces[i]
        for way in (0, 1):
            coming[i, way].wait_recv()
        return add(term(chip), slot(0, 0)) + slot(1, 0)[...].astype(F32)

    def cols(ref):
        width = ref.shape[1] // 2
        return pl.ds(pl.multiple_of(core * width, 128), width)

    results = ((g_out, s_out), (g_y, s_y), (g_x, s_x))
    for part in (0, 1):
        sums = [total(3 * part + i) for i in range(3)]

        @pl.when(core == part)
        def _():
            for value, (ref, _) in zip(sums, results):
                ref[:, cols(ref)] = value

        @pl.when(core != part)
        def _():
            for value, (_, ref) in zip(sums, results):
                ref[...] = value

    final = [copies.send(src, ref.at[:, cols(ref)], sib) for ref, src in results]
    g_gates[...] = total(6)
    g_vec[...] = total(7)
    for copy in final:
        copy.wait_recv()
    for copy in sent + final:
        copy.wait_send()


def scatter_sums(n, c_x, c_y, c_out, c_g, c_v):
    _, _, rows_d, rhalf = c_x.shape
    _, _, rows_r, dhalf = c_out.shape
    half = n // 2
    count = 8 * (2 * half - 1) + 3
    dma = pltpu.SemaphoreType.DMA
    vmem = pl.BlockSpec(memory_space=pltpu.VMEM)
    return pl.pallas_call(
        functools.partial(scatter_kernel, n),
        out_shape=[
            jax.ShapeDtypeStruct((rows_d, 2 * rhalf), F32),
            jax.ShapeDtypeStruct((rows_d, 2 * rhalf), F32),
            jax.ShapeDtypeStruct((rows_r, 2 * dhalf), F32),
            jax.ShapeDtypeStruct(c_g.shape[1:], F32),
            jax.ShapeDtypeStruct(c_v.shape[1:], F32),
        ],
        in_specs=[vmem] * 5,
        out_specs=[vmem] * 5,
        scratch_shapes=[
            pltpu.VMEM((2, 2, half, rows_d, rhalf), BF16),
            pltpu.VMEM((2, 2, half, rows_d, rhalf), BF16),
            pltpu.VMEM((2, 2, half, rows_r, dhalf), BF16),
            pltpu.VMEM((2, half) + c_g.shape[1:], BF16),
            pltpu.VMEM((2, half) + c_v.shape[1:], F32),
            pltpu.VMEM((rows_d, rhalf), F32),
            pltpu.VMEM((rows_d, rhalf), F32),
            pltpu.VMEM((rows_r, dhalf), F32),
            dma((count,)), dma((count,)),
        ],
        compiler_params=pltpu.CompilerParams(
            collective_id=1, has_side_effects=True, vmem_limit_bytes=56 << 20
        ),
        name="scatter_sums",
    )(c_x, c_y, c_out, c_g, c_v)


def project_kernel(steps, rows, gain, w, n1_ref, x_ref, y_ref):
    i = pl.program_id(0)

    @pl.when(i == 0)
    def _():
        values = rows[...].astype(F32)
        scale = lax.rsqrt(jnp.mean(values * values, axis=-1, keepdims=True) + EPS)
        n1_ref[...] = (values * scale * gain[...]).astype(BF16).reshape(n1_ref.shape)

    result = jnp.dot(n1_ref[...], w[...], preferred_element_type=F32).reshape(y_ref.shape)

    @pl.when(i < steps)
    def _():
        x_ref[...] = result.astype(BF16)

    @pl.when(i >= steps)
    def _():
        y_ref[...] = result


def project(rows, gain, w):
    _, tokens, width = rows.shape
    rh = w.shape[1] // 2
    steps = rh // BLK
    return pl.pallas_call(
        functools.partial(project_kernel, steps),
        grid=(2 * steps,),
        in_specs=[
            pl.BlockSpec(rows.shape, lambda i: (0, 0, 0)),
            pl.BlockSpec((1, width), lambda i: (0, 0)),
            pl.BlockSpec((width, BLK), lambda i: (0, i)),
        ],
        out_specs=[
            pl.BlockSpec((2 * tokens, width), lambda i: (0, 0)),
            pl.BlockSpec((2, tokens, BLK), lambda i: (0, 0, jnp.minimum(i, steps - 1))),
            pl.BlockSpec((2, tokens, BLK), lambda i: (0, 0, jnp.maximum(i - steps, 0))),
        ],
        out_shape=[
            jax.ShapeDtypeStruct((2 * tokens, width), BF16),
            jax.ShapeDtypeStruct((2, tokens, rh), BF16),
            jax.ShapeDtypeStruct((2, tokens, rh), F32),
        ],
        compiler_params=pltpu.CompilerParams(vmem_limit_bytes=40 << 20),
        cost_estimate=pl.CostEstimate(flops=27 * 10**8, bytes_accessed=15 * 10**6, transcendentals=0),
        name="project",
    )(rows, gain, w)


def project_out_kernel(o, o_sib, w, mine_ref, theirs_ref):
    rh = o.shape[2]
    for row, ref in ((0, mine_ref), (1, theirs_ref)):
        ref[...] = jnp.dot(o[row], w[:rh], preferred_element_type=F32) + jnp.dot(
            o_sib[1 - row], w[rh:], preferred_element_type=F32
        )


def project_out(o, o_sib, w):
    _, tokens, rh = o.shape
    cols = w.shape[1]
    tile = min(BLK, cols)
    whole = pl.BlockSpec(o.shape, lambda i: (0, 0, 0))
    part = pl.BlockSpec((tokens, tile), lambda i: (0, i))
    return pl.pallas_call(
        project_out_kernel,
        grid=(cols // tile,),
        in_specs=[whole, whole, pl.BlockSpec((2 * rh, tile), lambda i: (0, i))],
        out_specs=[part, part],
        out_shape=[jax.ShapeDtypeStruct((tokens, cols), F32)] * 2,
        compiler_params=pltpu.CompilerParams(vmem_limit_bytes=40 << 20),
        cost_estimate=pl.CostEstimate(flops=14 * 10**8, bytes_accessed=8 * 10**6, transcendentals=0),
        name="project_out",
    )(o, o_sib, w)


def minus_expm1(v):
    series = jnp.ones_like(v)
    for k in range(9, 1, -1):
        series = 1.0 + series * v * (1.0 / k)
    return jnp.where(v > -0.5, -v * series, 1.0 - jnp.exp(v))


def gates_of(u, weights, cp, start):
    tokens = u.shape[0] * u.shape[1]
    flat = u.reshape(tokens, BLK)
    z = jnp.dot(flat, weights, preferred_element_type=F32)
    r = jax.nn.sigmoid(z[:, :BLK] + cp[5:6]).reshape(u.shape)
    ig = jax.nn.sigmoid(z[:, BLK:] + cp[6:7]).reshape(u.shape)
    la = -8.0 * r * cp[7:8][None]
    decayed = jnp.exp(la)
    rest = minus_expm1(2.0 * la)
    return r, ig, decayed, rest


def recurrence_kernel(xb, halo, weights, cp, starts, u_ref, a_ref, h_ref, c_ref, b_ref):
    rows, length = xb.shape[0], xb.shape[1]
    p = cp[...]
    us = []
    for row in range(rows):
        padded = jnp.concatenate([halo[row], xb[row].astype(F32)], axis=0)
        total = p[4:5] + p[0:1] * padded[8 : 8 + length]
        for k in range(1, 4):
            total = total + p[k : k + 1] * padded[8 - k : 8 - k + length]
        us.append(total.astype(BF16))
    u = jnp.stack(us)
    u_ref[...] = u
    start = starts[...]
    start = jnp.concatenate([start, start], axis=2)
    r, ig, decayed, rest = gates_of(u, weights[...], p, start)
    a_ref[...] = decayed * (1.0 - start)
    b_ref[...] = jnp.where(start > 0.5, 1.0, jnp.sqrt(rest)) * ig * u.astype(F32)

    def eight(i, carry):
        at = pl.ds(pl.multiple_of(i * 8, 8), 8)
        out = []
        for row in range(rows):
            h, c = carry[row]
            a, b = a_ref[row, at, :], b_ref[row, at, :]
            hs, cs = [], []
            for j in range(8):
                h = a[j : j + 1] * h + b[j : j + 1]
                c = a[j : j + 1] * c
                hs.append(h)
                cs.append(c)
            h_ref[row, at, :] = jnp.concatenate(hs, axis=0)
            c_ref[row, at, :] = jnp.concatenate(cs, axis=0)
            out.append((h, c))
        return tuple(out)

    zero, one = jnp.zeros((1, BLK), F32), jnp.ones((1, BLK), F32)
    lax.fori_loop(0, length // 8, eight, ((zero, one),) * rows)


def recurrence(xb, halo, weights, cp, starts):
    rows, length, channels = xb.shape
    wide = pl.BlockSpec((rows, length, BLK), lambda h: (0, 0, h))
    return pl.pallas_call(
        recurrence_kernel,
        grid=(channels // BLK,),
        in_specs=[
            wide,
            pl.BlockSpec((rows, 8, BLK), lambda h: (0, 0, h)),
            pl.BlockSpec((BLK, 2 * BLK), lambda h: (h, 0)),
            pl.BlockSpec((cp.shape[0], BLK), lambda h: (0, h)),
            pl.BlockSpec(starts.shape, lambda h: (0, 0, 0)),
        ],
        out_specs=[wide] * 4,
        out_shape=[jax.ShapeDtypeStruct(xb.shape, BF16)] + [jax.ShapeDtypeStruct(xb.shape, F32)] * 3,
        scratch_shapes=[pltpu.VMEM((rows, length, BLK), F32)],
        compiler_params=pltpu.CompilerParams(vmem_limit_bytes=40 << 20),
        cost_estimate=pl.CostEstimate(flops=4 * 10**8, bytes_accessed=6 * 10**6, transcendentals=2 * 10**6),
        name="recurrence",
    )(xb, halo, weights, cp, starts)


def gelu_parts(v):
    inner = 0.7978845608028654 * (v + 0.044715 * v * v * v)
    t = jnp.tanh(inner)
    value = 0.5 * v * (1.0 + t)
    slope = 0.5 * (1.0 + t) + 0.5 * v * (1.0 - t * t) * 0.7978845608028654 * (1.0 + 3.0 * 0.044715 * v * v)
    return value, slope


def adjoint_kernel(do, h_ref, y_ref, a_ref, dy_ref, lam_ref, c_ref, dh_ref):
    rows, length = do.shape[0], do.shape[1]
    value, slope = gelu_parts(y_ref[...])
    dy_ref[...] = (do[...] * h_ref[...] * slope).astype(BF16)
    dh_ref[...] = do[...] * value

    def eight(step, carry):
        i = length // 8 - 1 - step
        at = pl.ds(pl.multiple_of(i * 8, 8), 8)
        out = []
        for row in range(rows):
            ahead, c = carry[row]
            a, d = a_ref[row, at, :], dh_ref[row, at, :]
            ls, cs = [None] * 8, [None] * 8
            for j in range(7, -1, -1):
                lam = d[j : j + 1] + ahead
                ls[j], cs[j] = lam, c
                ahead = a[j : j + 1] * lam
                c = a[j : j + 1] * c
            lam_ref[row, at, :] = jnp.concatenate(ls, axis=0)
            c_ref[row, at, :] = jnp.concatenate(cs, axis=0)
            out.append((ahead, c))
        return tuple(out)

    zero, one = jnp.zeros((1, BLK), F32), jnp.ones((1, BLK), F32)
    lax.fori_loop(0, length // 8, eight, ((zero, one),) * rows)


def adjoint(do, h, ypre, a):
    rows, length, channels = do.shape
    wide = pl.BlockSpec((rows, length, BLK), lambda i: (0, 0, i))
    return pl.pallas_call(
        adjoint_kernel,
        grid=(channels // BLK,),
        in_specs=[wide] * 4,
        out_specs=[wide] * 3,
        out_shape=[jax.ShapeDtypeStruct(do.shape, BF16)] + [jax.ShapeDtypeStruct(do.shape, F32)] * 2,
        scratch_shapes=[pltpu.VMEM((rows, length, BLK), F32)],
        compiler_params=pltpu.CompilerParams(vmem_limit_bytes=40 << 20),
        cost_estimate=pl.CostEstimate(flops=10**7, bytes_accessed=9 * 10**6, transcendentals=10**6),
        name="adjoint",
    )(do, h, ypre, a)


def gates_back_kernel(lam_ref, c_ref, inc, h_ref, h_in, u_ref, weights, cp, starts, du_ref, dw_ref, sums_ref):
    rows, length = u_ref.shape[0], u_ref.shape[1]
    tokens = rows * length
    p = cp[...]
    u = u_ref[...]
    uf = u.astype(F32)
    start = starts[...]
    start = jnp.concatenate([start, start], axis=2)
    w = weights[...]
    r, ig, decayed, rest = gates_of(u, w, p, start)
    mult = jnp.where(start > 0.5, 1.0, jnp.sqrt(rest))
    lam = lam_ref[...] + c_ref[...] * inc[...]
    before = jnp.stack([jnp.concatenate([h_in[row], h_ref[row][: length - 1]], axis=0) for row in range(rows)])
    keep = 1.0 - start
    d_la = lam * before * decayed * keep - jnp.where(
        start > 0.5, 0.0, lam * ig * uf * decayed * decayed * lax.rsqrt(jnp.where(start > 0.5, 1.0, rest))
    )
    dpa = d_la * (-8.0 * p[7:8][None]) * r * (1.0 - r)
    direct = lam * mult
    dpi = direct * uf * ig * (1.0 - ig)
    d_decay = d_la * (8.0 * p[8:9][None]) * r
    dz = jnp.concatenate(
        [dpa.reshape(tokens, BLK).astype(BF16), dpi.reshape(tokens, BLK).astype(BF16)], axis=1
    )
    back = lax.dot_general(dz, w, (((1,), (1,)), ((), ())), preferred_element_type=F32)
    du_ref[...] = (direct * ig + back.reshape(u.shape)).astype(BF16)
    dw_ref[...] = lax.dot_general(
        u.reshape(tokens, BLK), dz, (((0,), (0,)), ((), ())), preferred_element_type=F32
    )
    zero = jnp.zeros((5, BLK), F32)
    sums_ref[...] = jnp.concatenate(
        [jnp.sum(v.reshape(tokens, BLK), axis=0, keepdims=True) for v in (dpa, dpi, d_decay)] + [zero], axis=0
    )


def gates_back(lam, coef, inc, h, h_in, u, weights, cp, starts):
    rows, length, channels = u.shape
    wide = pl.BlockSpec((rows, length, BLK), lambda i: (0, 0, i))
    line = pl.BlockSpec((rows, 1, BLK), lambda i: (0, 0, i))
    square = pl.BlockSpec((BLK, 2 * BLK), lambda i: (i, 0))
    return pl.pallas_call(
        gates_back_kernel,
        grid=(channels // BLK,),
        in_specs=[
            wide, wide, line, wide, line, wide, square,
            pl.BlockSpec((cp.shape[0], BLK), lambda i: (0, i)),
            pl.BlockSpec(starts.shape, lambda i: (0, 0, 0)),
        ],
        out_specs=[wide, square, pl.BlockSpec((8, BLK), lambda i: (0, i))],
        out_shape=[
            jax.ShapeDtypeStruct(u.shape, BF16),
            jax.ShapeDtypeStruct((channels, 2 * BLK), F32),
            jax.ShapeDtypeStruct((8, channels), F32),
        ],
        compiler_params=pltpu.CompilerParams(vmem_limit_bytes=40 << 20),
        cost_estimate=pl.CostEstimate(flops=12 * 10**8, bytes_accessed=9 * 10**6, transcendentals=2 * 10**6),
        name="gates_back",
    )(lam, coef, inc, h, h_in, u, weights, cp, starts)


def log1p_small(e):
    series = jnp.ones_like(e) * (1.0 / 14)
    for k in range(13, 0, -1):
        series = 1.0 / k - e * series
    return jnp.where(e < 0.25, e * series, jnp.log(1.0 + e))


def front_kernel(n, *refs):
    (
        wx, wy, wo, gs, wg, wu, wd, rows_in, cot, starts, spread_r, pick_r, spread_d, pick_d,
        o_xy, o_out, o_gates, o_cp, o_gains, o_gu, o_d, o_cot, o_starts, o_ypre, o_u, o_a, o_h, o_hin, o_xb, o_before,
        o_x1, o_n2, o_n1t, o_ot, o_hidden, o_gate, o_up, o_pd,
        v_xy, v_out, v_gs, v_gates, v_rows, v_cot, v_starts, v_cp, v_gains, v_n1, v_n1t, v_xb, v_ypre, v_halo, v_u, v_a,
        v_b, v_h, v_c, v_carry, v_o, v_osib, v_ot, v_part, v_theirs, v_psib, v_x1, v_n2, v_w, v_hidden, v_gu, v_pd,
        local_sem, send_sem, recv_sem, load_sem, store_sem, pd_sem,
    ) = refs
    dp, x = lax.axis_index("dp"), lax.axis_index("tp")
    chip, core = dp // 2, dp % 2
    other = 1 - core
    pos = place_of(chip, n)
    half = n // 2
    nxt = (chip_at((pos + 1) % n, n) * 2 + core, x)
    prv = (chip_at((pos + n - 1) % n, n) * 2 + core, x)
    sib = (chip * 2 + other, x)
    over = (dp, 1 - x)
    greet([nxt, prv, sib, over])
    copies = Copies(local_sem, send_sem, recv_sem)
    send, stay = copies.send, copies.stay
    tokens, width = rows_in.shape
    rec = wx.shape[1]
    rh = rec // 2
    own, own_d = wo.shape[0], wx.shape[0]
    fh = wg.shape[1] // 2
    kept, every = [], []

    def put(src, dst):
        kept.append(stay(src, dst))

    def give(src, dst, device):
        copy = send(src, dst, device)
        every.append(copy)
        return copy

    def land(group):
        for copy in group:
            copy.wait_recv()

    class Chain:
        def __init__(self, pieces, arrived=None):
            self.pieces, self.arrived, self.hop = pieces, arrived, 0
            self.ways = ((nxt, n - 1), (prv, 1))
            self.moving = ([], [])

        def start(self, part):
            self.hop = 1
            for ref, own_core in self.pieces(pos):
                if own_core == part:
                    for way, (device, _) in enumerate(self.ways):
                        self.moving[way].append(give(ref, ref, device))
                    if self.arrived:
                        self.arrived(ref)

        def advance(self):
            self.hop += 1
            fresh = ([], [])
            blocks = [self.pieces((pos + back * (self.hop - 1)) % n) for _, back in self.ways]
            for i in range(len(blocks[0])):
                for way, (device, _) in enumerate(self.ways):
                    ref, own_core = blocks[way][i]
                    self.moving[way][i].wait_recv()
                    if self.hop < half or own_core == (way == 0):
                        fresh[way].append(give(ref, ref, device))
                    if self.arrived:
                        self.arrived(ref)
            self.moving = fresh

        def to_last(self):
            while self.hop < half:
                self.advance()

        def finish(self):
            block = self.pieces((pos + half) % n)
            for way in (0, 1):
                refs = [ref for ref, own_core in block if own_core == (way == 0)]
                for copy, ref in zip(self.moving[way], refs):
                    copy.wait_recv()
                    if self.arrived:
                        self.arrived(ref)

    parts = [(wx, v_xy.at[chip, core, x, :, pl.ds(0, rh)]), (wy, v_xy.at[chip, core, x, :, pl.ds(rh, rh)])]
    mine = [stay(half_cols(src, core), slot) for src, slot in parts]
    mine.append(stay(half_cols(wo, core), v_out.at[heads_first(chip, core, n), core, x]))
    mine.append(stay(gs, v_gs.at[core, chip, x]))
    pair = [give(half_cols(src, other), slot, sib) for src, slot in parts]
    pair.append(give(half_cols(wo, other), v_out.at[heads_first(chip, other, n), core, x], sib))

    crossed, held = [], []

    def rec_pieces(place):
        c = chip_at(place, n)
        at = heads_first(c, core, n)
        return [
            (v_xy.at[c, core, x], True), (v_gs.at[core, c, x], True), (v_out.at[at, core, x], True),
            (v_xy.at[c, other, x], False), (v_out.at[at, other, x], False),
        ]

    def rec_arrived(ref):
        if len(ref.shape) == 2 and ref.shape[1] == width // 2:
            held.append(ref)
        else:
            crossed.append(give(ref, ref, over))

    rec_chain = Chain(rec_pieces, rec_arrived)
    gu = Chain(lambda place: [
        (o_gu.at[chip_at(place, n), core], True), (o_gu.at[chip_at(place, n), other], False)
    ])
    down = Chain(lambda place: [(o_d.at[place, core], True), (o_d.at[place, other], False)])
    for copy in mine:
        copy.wait()
    rec_chain.start(True)
    land(pair)
    rec_chain.start(False)
    parts = [
        (wg, o_gu.at[chip, core, :, pl.ds(0, fh)]),
        (wu, o_gu.at[chip, core, :, pl.ds(fh, fh)]),
        (wd, o_d.at[pos, core]),
    ]
    late = [give(half_cols(src, other), slot, sib) for src, slot in parts]
    plain = [stay(half_cols(src, core), slot) for src, slot in parts]
    late += [give(rows_in, v_rows.at[1], sib), give(starts, v_starts.at[1], sib), give(cot, v_cot.at[2], sib)]
    plain += [stay(rows_in, v_rows.at[0]), stay(starts, v_starts.at[0]), stay(cot, v_cot.at[0])]
    rec_chain.to_last()
    land(late)
    for copy in plain:
        copy.wait()
    gu.start(True)
    gu.start(False)
    rec_chain.finish()
    swap = [give(v_gs.at[core, :, x], v_gs.at[core, :, x], sib)]
    put(v_starts, o_starts)
    if half > 3:
        gu.advance()
    land(crossed)
    swap.append(give(v_gs.at[core, :, 1 - x], v_gs.at[core, :, 1 - x], sib))
    outs = []

    def cross_held(count):
        for _ in range(min(count, len(held))):
            ref = held.pop(0)
            outs.append(give(ref, ref, over))

    cross_held(4)
    put(v_xy, o_xy)
    land(swap)

    small = v_gs[:, :, :, own : own + PAD, :128].reshape(4 * n * PAD, 128)
    spread = jnp.dot(small, spread_r[...], preferred_element_type=F32).reshape(4 * n, PAD, rh)
    heads = pick_r[:, pl.ds(pl.multiple_of(core * rh, 128), rh)]
    lines = jnp.sum(spread[:, :8] * heads[:, None, :], axis=0)
    decay = lines[7:8]
    e = jnp.exp(-jnp.abs(decay))
    v_cp[0:8, :] = lines
    v_cp[7:8, :] = jnp.maximum(-decay, 0.0) + log1p_small(e)
    v_cp[8:16, :] = jnp.broadcast_to(jax.nn.sigmoid(-decay), (8, rh))
    for i in range(width // WIDE):
        at = pl.ds(i * WIDE, WIDE)
        wide = jnp.dot(small, spread_d[:, at], preferred_element_type=F32).reshape(4 * n, PAD, WIDE)
        v_gains[:, at] = jnp.sum(wide[:, 8:] * pick_d[:, at][:, None, :], axis=0)
    for i in range(2 * n):
        v_gates[i * own : (i + 1) * own, :] = v_gs[(i // 2) % 2, core * half + i // 4, i % 2, 0:own, :]
    put(v_cp, o_cp)
    put(v_gains, o_gains)
    put(v_gates, o_gates)

    values = v_rows[...].astype(F32)
    scale = lax.rsqrt(jnp.mean(values * values, axis=-1, keepdims=True) + EPS)
    v_n1[...] = (values * scale * v_gains[0:1, :]).astype(BF16).reshape(2 * tokens, width)

    def project_x(i, _):
        at = pl.ds(pl.multiple_of(i * BLK, BLK), BLK)
        w = v_xy[:, :, :, :, at].reshape(width, BLK)
        v_xb[:, :, at] = jnp.dot(v_n1[...], w, preferred_element_type=F32).astype(BF16).reshape(2, tokens, BLK)
        return 0

    def project_y(i, _):
        at = pl.ds(pl.multiple_of(i * BLK, BLK), BLK)
        w = v_xy[:, :, :, :, pl.ds(pl.multiple_of(rh + i * BLK, BLK), BLK)].reshape(width, BLK)
        v_ypre[:, :, at] = jnp.dot(v_n1[...], w, preferred_element_type=F32).reshape(2, tokens, BLK)
        return 0

    lax.fori_loop(0, rh // BLK, project_x, 0)
    halo = give(v_xb.at[:, pl.ds(tokens - 16, 16)], v_halo, over)
    cross_held(4)
    put(v_xb, o_xb)
    if half > 3:
        gu.advance()
    lax.fori_loop(0, rh // BLK, project_y, 0)
    put(v_ypre, o_ypre)
    chips_n = BLK // (4 * own_d)

    def turn_n1(i, _):
        at = pl.ds(pl.multiple_of(i * BLK, BLK), BLK)
        turned = v_n1[:, at].astype(F32).T.astype(BF16)
        v_n1t[pl.ds(i * chips_n, chips_n)] = turned.reshape(chips_n, 2, 2, own_d, 2 * tokens)
        return 0

    lax.fori_loop(0, width // BLK, turn_n1, 0)
    halo.wait_recv()
    v_halo[...] = jnp.where(x == 0, jnp.zeros_like(v_halo), v_halo[...])
    put(v_halo, o_before)
    put(v_n1t.at[:, :, x], o_n1t.at[:, :, :, pl.ds(0, 2 * tokens)])

    def head(i, _):
        at = pl.ds(pl.multiple_of(i * BLK, BLK), BLK)
        p = v_cp[:, at]
        us = []
        for row in range(2):
            padded = jnp.concatenate([v_halo[row, :, at].astype(F32)[8:], v_xb[row, :, at].astype(F32)], axis=0)
            total = p[4:5] + p[0:1] * padded[8 : 8 + tokens]
            for k in range(1, 4):
                total = total + p[k : k + 1] * padded[8 - k : 8 - k + tokens]
            us.append(total.astype(BF16))
        u = jnp.stack(us)
        v_u[:, :, at] = u
        start = v_starts[...]
        start = jnp.concatenate([start, start], axis=2)
        _, ig, decayed, rest = gates_of(u, v_gates[at, :], p, start)
        v_a[:, :, at] = decayed * (1.0 - start)
        v_b[...] = jnp.where(start > 0.5, 1.0, jnp.sqrt(rest)) * ig * u.astype(F32)

        def eight(j, carry):
            rows8 = pl.ds(pl.multiple_of(j * 8, 8), 8)
            out = []
            for row in range(2):
                h, c = carry[row]
                a, b = v_a[row, rows8, at], v_b[row, rows8, :]
                hs, cs = [], []
                for k in range(8):
                    h = a[k : k + 1] * h + b[k : k + 1]
                    c = a[k : k + 1] * c
                    hs.append(h)
                    cs.append(c)
                v_h[row, rows8, at] = jnp.concatenate(hs, axis=0)
                v_c[row, rows8, at] = jnp.concatenate(cs, axis=0)
                out.append((h, c))
            return tuple(out)

        zero, one = jnp.zeros((1, BLK), F32), jnp.ones((1, BLK), F32)
        lax.fori_loop(0, tokens // 8, eight, ((zero, one),) * 2)
        return 0

    lax.fori_loop(0, rh // BLK, head, 0)
    carry = give(v_h.at[:, pl.ds(tokens - 8, 8)], v_carry, over)
    put(v_u, o_u)
    put(v_a, o_a)
    carry.wait_recv()
    carry.wait_send()
    cross_held(len(held))
    v_carry[...] = jnp.where(x == 0, jnp.zeros_like(v_carry), v_carry[...])
    put(v_carry, o_hin)

    def output(i, _):
        at = pl.ds(pl.multiple_of(i * BLK, BLK), BLK)
        h = v_h[:, :, at] + v_c[:, :, at] * v_carry[:, 7:8, at]
        v_h[:, :, at] = h
        value, _ = gelu_parts(v_ypre[:, :, at])
        v_o[:, :, at] = (h * value).astype(BF16)
        return 0

    lax.fori_loop(0, rh // BLK, output, 0)
    o_pair = give(v_o, v_osib, sib)
    put(v_h, o_h)
    gu.to_last()
    down.start(True)
    down.start(False)
    o_pair.wait_recv()
    land(outs)
    put(v_out, o_out)

    def project_row(row, ref):
        def tile(i, _):
            at = pl.ds(pl.multiple_of(i * BLK, BLK), BLK)
            w0 = v_out[0:half, :, :, :, at].reshape(rh, BLK)
            w1 = v_out[half:n, :, :, :, at].reshape(rh, BLK)
            ref[:, at] = jnp.dot(v_o[row], w0, preferred_element_type=F32) + jnp.dot(
                v_osib[1 - row], w1, preferred_element_type=F32
            )
            return 0

        lax.fori_loop(0, width // 2 // BLK, tile, 0)

    project_row(1, v_theirs)
    x1_pair = give(v_theirs, v_psib, sib)
    project_row(0, v_part)
    x1_pair.wait_recv()
    at_mine = pl.ds(pl.multiple_of(core * (width // 2), 128), width // 2)
    at_theirs = pl.ds(pl.multiple_of(other * (width // 2), 128), width // 2)
    v_x1[:, at_mine] = v_rows[0, :, at_mine].astype(F32) + v_part[...]
    v_x1[:, at_theirs] = v_rows[0, :, at_theirs].astype(F32) + v_psib[...]
    put(v_x1, o_x1)
    x1 = v_x1[...]
    scale = lax.rsqrt(jnp.mean(x1 * x1, axis=-1, keepdims=True) + EPS)
    v_n2[0] = (x1 * scale * v_gains[1:2, :]).astype(BF16)
    n2_over = give(v_n2.at[0], v_n2.at[1], over)
    n2_pair = give(v_n2.at[0], v_n2.at[2], sib)
    cot_over = give(v_cot.at[0], v_cot.at[1], over)
    n1_over = give(v_n1t.at[:, :, 1 - x], o_n1t.at[:, :, :, pl.ds(2 * tokens, 2 * tokens)], over)

    chips_o = 640 // (4 * own)

    def turn_o(i, _):
        at = pl.ds(pl.multiple_of(i * 640, 128), 640)
        here = v_o[:, :, at].astype(F32).reshape(2 * tokens, 640).T.astype(BF16)
        v_ot[pl.ds(i * chips_o, chips_o)] = here.reshape(chips_o, 2, 2, own, 2 * tokens)
        there = jnp.concatenate([v_osib[1, :, at], v_osib[0, :, at]], axis=0).astype(F32).T.astype(BF16)
        v_ot[pl.ds(half + i * chips_o, chips_o)] = there.reshape(chips_o, 2, 2, own, 2 * tokens)
        return 0

    lax.fori_loop(0, rh // 640, turn_o, 0)
    o_over = give(v_ot.at[:, :, 1 - x], o_ot.at[:, :, :, pl.ds(2 * tokens, 2 * tokens)], over)
    put(v_ot.at[:, :, x], o_ot.at[:, :, :, pl.ds(0, 2 * tokens)])

    tile = 128
    steps = fh // tile

    def loads(t, slot):
        first = pl.ds(pl.multiple_of(t * tile, tile), tile)
        second = pl.ds(pl.multiple_of(fh + t * tile, tile), tile)
        return [
            pltpu.make_async_copy(o_gu.at[:, :, :, first], v_w.at[slot, :, :, :, pl.ds(0, tile)], load_sem.at[slot, 0]),
            pltpu.make_async_copy(
                o_gu.at[:, :, :, second], v_w.at[slot, :, :, :, pl.ds(tile, tile)], load_sem.at[slot, 1]
            ),
        ]

    def stores(t, slot):
        at = pl.ds(pl.multiple_of(t * tile, tile), tile)
        return [
            pltpu.make_async_copy(v_gu.at[slot, :, pl.ds(0, tile)], o_gate.at[:, at], store_sem.at[slot, 0]),
            pltpu.make_async_copy(v_gu.at[slot, :, pl.ds(tile, tile)], o_up.at[:, at], store_sem.at[slot, 1]),
        ]

    gu.finish()
    for copy in loads(0, 0):
        copy.start()
    n2_pair.wait_recv()
    n2_over.wait_recv()
    n2_last = give(v_n2.at[1], v_n2.at[3], sib)
    n2_last.wait_recv()
    if half > 3:
        down.advance()
    put(v_n2, o_n2)

    def hidden_tile(t, _):
        slot = t % 2
        for copy in loads(t, slot):
            copy.wait()

        @pl.when(t + 1 < steps)
        def _():
            for copy in loads(t + 1, 1 - slot):
                copy.start()

        @pl.when(t >= 2)
        def _():
            for copy in stores(t - 2, slot):
                copy.wait()

        w = v_w[slot].reshape(width, 2 * tile)
        v_gu[slot] = jnp.dot(v_n2[...].reshape(4 * tokens, width), w, preferred_element_type=F32)
        for copy in stores(t, slot):
            copy.start()
        value, _ = gelu_parts(v_gu[slot, :, 0:tile])
        v_hidden[:, pl.ds(pl.multiple_of(t * tile, tile), tile)] = (value * v_gu[slot, :, tile:]).astype(BF16)
        return 0

    lax.fori_loop(0, steps, hidden_tile, 0)
    put(v_hidden, o_hidden)
    cot_over.wait_recv()
    cot_last = give(v_cot.at[1], v_cot.at[3], sib)
    if half > 3:
        down.advance()
    cot_last.wait_recv()
    put(v_cot, o_cot)

    def pd_store(t, slot):
        return pltpu.make_async_copy(v_pd.at[slot], o_pd.at[pl.ds(pl.multiple_of(t * BLK, BLK), BLK)], pd_sem.at[slot])

    def down_tile(t, _):
        slot = t % 2

        @pl.when(t >= 2)
        def _():
            pd_store(t - 2, slot).wait()

        left = v_cot[:, :, pl.ds(pl.multiple_of(t * BLK, BLK), BLK)].reshape(4 * tokens, BLK)
        v_pd[slot] = lax.dot_general(
            left, v_hidden[...], (((0,), (0,)), ((), ())), preferred_element_type=F32
        ).astype(BF16)
        pd_store(t, slot).start()
        return 0

    lax.fori_loop(0, width // BLK, down_tile, 0)
    down.to_last()
    for t in (steps - 2, steps - 1):
        for copy in stores(t, t % 2):
            copy.wait()
    for t in (width // BLK - 2, width // BLK - 1):
        pd_store(t, t % 2).wait()
    down.finish()
    land([n1_over, o_over])
    for copy in kept:
        copy.wait()
    for copy in every:
        if copy is not carry:
            copy.wait_send()


def front(n, wx, wy, wo, gs, wg, wu, wd, rows_in, cot, starts):
    rec, f = wx.shape[1], wg.shape[1]
    own, own_d, rows_f = wo.shape[0], wx.shape[0], wg.shape[0]
    rh, fh = rec // 2, f // 2
    tokens, width = rows_in.shape
    half = n // 2
    row = np.arange(4 * n)
    index = (row // 2) % n * 4 + row // (2 * n) * 2 + row % 2
    lane_r, lane_d, short = np.arange(rec), np.arange(width), np.arange(128)[:, None]
    spread_r = (lane_r[None, :rh] % own == short).astype(jnp.bfloat16)
    spread_d = (lane_d[None] % own_d == short).astype(jnp.bfloat16)
    pick_r = (index[:, None] == lane_r[None] // own).astype(np.float32)
    pick_d = (index[:, None] == lane_d[None] // own_d).astype(np.float32)
    outs = dict(
        w_xy=((n, 2, 2, own_d, rec), BF16),
        w_o=((n, 2, 2, own, width // 2), BF16),
        gates=((rh, WIDE), BF16),
        cp=((16, rh), F32),
        gains=((8, width), F32),
        w_gu=((n, 2, rows_f, f), BF16),
        w_d=((n, 2, rows_f, fh), BF16),
        cot=((4, tokens, width), BF16),
        starts=((2, tokens, 128), F32),
        ypre=((2, tokens, rh), F32),
        u=((2, tokens, rh), BF16),
        a=((2, tokens, rh), F32),
        h=((2, tokens, rh), F32),
        h_in=((2, 8, rh), F32),
        xb=((2, tokens, rh), BF16),
        before=((2, 16, rh), BF16),
        x1=((tokens, width), F32),
        n2=((4, tokens, width), BF16),
        n1_t=((n, 2, own_d, 4 * tokens), BF16),
        o_t=((n, 2, own, 4 * tokens), BF16),
        hidden=((4 * tokens, fh), BF16),
        gate=((4 * tokens, fh), F32),
        up=((4 * tokens, fh), F32),
        part_d=((width, fh), BF16),
    )
    state = (2, tokens, rh)
    scratch = [
        ((n, 2, 2, own_d, rec), BF16), ((n, 2, 2, own, width // 2), BF16), ((2, n, 2) + gs.shape, BF16),
        ((rh, WIDE), BF16), ((2, tokens, width), BF16), ((4, tokens, width), BF16), ((2, tokens, 128), F32),
        ((16, rh), F32), ((8, width), F32), ((2 * tokens, width), BF16), ((n, 2, 2, own_d, 2 * tokens), BF16),
        (state, BF16), (state, F32), ((2, 16, rh), BF16), (state, BF16), (state, F32),
        ((2, tokens, BLK), F32), (state, F32), (state, F32), ((2, 8, rh), F32), (state, BF16), (state, BF16),
        ((n, 2, 2, own, 2 * tokens), BF16), ((tokens, width // 2), F32), ((tokens, width // 2), F32),
        ((tokens, width // 2), F32), ((tokens, width), F32), ((4, tokens, width), BF16),
        ((2, n, 2, rows_f, BLK), BF16), ((4 * tokens, fh), BF16), ((2, 4 * tokens, BLK), F32), ((2, BLK, fh), BF16),
    ]
    count = 9 + (5 * n - 5) + 2 * (2 * n - 2) + 5 * n + 2 + 12
    dma = pltpu.SemaphoreType.DMA
    result = pl.pallas_call(
        functools.partial(front_kernel, n),
        out_shape=[jax.ShapeDtypeStruct(shape, kind) for shape, kind in outs.values()],
        in_specs=[pl.BlockSpec(memory_space=pl.ANY)] * 10 + [pl.BlockSpec(memory_space=pltpu.VMEM)] * 4,
        out_specs=[pl.BlockSpec(memory_space=pl.ANY)] * len(outs),
        scratch_shapes=[pltpu.VMEM(shape, kind) for shape, kind in scratch]
        + [dma((32,)), dma((count,)), dma((count,)), dma((2, 2)), dma((2, 2)), dma((2,))],
        compiler_params=pltpu.CompilerParams(
            collective_id=2, has_side_effects=True, vmem_limit_bytes=60 << 20
        ),
        name="front",
    )(wx, wy, wo, gs, wg, wu, wd, rows_in, cot, starts, spread_r, pick_r, spread_d, pick_d)
    return dict(zip(outs, result))


def finish_kernel(
    sums, x_sum, y_sum, out_sum, gates, vec,
    gate_ref, up_ref, x_ref, y_ref, out_ref, a_ref, i_ref, taps_ref, *lines,
):
    core = lax.axis_index("dp") % 2
    half = gate_ref.shape[1] // 2
    for first in (0, 1):

        @pl.when(core == first)
        def _():
            for i in (0, 1):
                start = (i != first) * 2 * half
                at = pl.ds(i * half, half)
                gate_ref[:, at] = sums[:, start : start + half].astype(F32)
                up_ref[:, at] = sums[:, start + half : start + 2 * half].astype(F32)

    x_ref[...] = x_sum[...]
    y_ref[...] = y_sum[...]
    out_ref[...] = out_sum[...]
    a_ref[...] = gates[:, :BLK]
    i_ref[...] = gates[:, BLK:]
    taps, own = taps_ref.shape
    taps_ref[...] = vec[0:taps, 0:own]
    for k, ref in enumerate(lines):
        ref[...] = vec[taps + k : taps + k + 1, 0 : ref.shape[1]]


def finish(sums, x_sum, y_sum, out_sum, gates, vec, taps):
    rows, cols = sums.shape
    own, own_d = out_sum.shape[0], x_sum.shape[0]
    steps = 2 if rows % 16 == 0 and own % 16 == 0 and own_d % 16 == 0 else 1

    def tiled(shape):
        return pl.BlockSpec((shape[0] // steps, shape[1]), lambda i: (i, 0))

    def fixed(shape):
        return pl.BlockSpec(shape, lambda i: (0, 0))

    big = [(rows, cols // 2)] * 2 + [x_sum.shape, y_sum.shape, out_sum.shape] + [(own, BLK)] * 2
    small = [(taps, own)] + [(1, own)] * 4 + [(1, own_d)] * 2
    return pl.pallas_call(
        finish_kernel,
        grid=(steps,),
        in_specs=[tiled(v.shape) for v in (sums, x_sum, y_sum, out_sum, gates)] + [fixed(vec.shape)],
        out_specs=[tiled(shape) for shape in big] + [fixed(shape) for shape in small],
        out_shape=[jax.ShapeDtypeStruct(shape, F32) for shape in big + small],
        compiler_params=pltpu.CompilerParams(vmem_limit_bytes=60 << 20),
        name="finish",
    )(sums, x_sum, y_sum, out_sum, gates, vec)


def nt(left, right):
    return lax.dot_general(left, right, (((1,), (1,)), ((), ())), preferred_element_type=F32)


def nn(left, right):
    return jnp.dot(left, right, preferred_element_type=F32)


def body(
    dp_size,
    layer_input, grad_out, lengths, resets, norm_gain, w_x, w_y, conv_w, conv_b, gate_a_w, gate_a_b,
    gate_i_w, gate_i_b, decay_param, w_out, mlp_gain, w_gate, w_up, w_down,
):
    n = dp_size // 2
    half = n // 2
    dp, x = lax.axis_index("dp"), lax.axis_index("tp")
    chip, core = dp // 2, dp % 2
    pos = place_of(chip, n)
    tokens, width = layer_input.shape[1], layer_input.shape[2]
    rec = w_x.shape[1]
    rh = rec // 2
    taps = conv_w.shape[0]
    own = rec // (2 * dp_size)
    own_d = width // (2 * dp_size)

    ring = [chip_at(i, n) for i in range(n)]
    up = [(ring[i] * 2 + c, ring[(i + 1) % n] * 2 + c) for i in range(n) for c in range(2)]
    down = [(b, a) for a, b in up]
    lanes = [[chip_id * 2 + c for chip_id in ring] for c in range(2)]
    pairs = [(d, d + 1 - 2 * (d % 2)) for d in range(dp_size)]

    def sibling(v):
        return lax.ppermute(v, "dp", pairs)

    def across(v):
        return lax.ppermute(v, "tp", [(0, 1), (1, 0)])

    def swapped(v):
        return jnp.concatenate([v[1:], v[:1]], axis=0)

    def by_core(mine, theirs, axis):
        return jnp.where(
            core == 0, jnp.concatenate([mine, theirs], axis), jnp.concatenate([theirs, mine], axis)
        )

    def ring_order(array, axis):
        size = array.shape[axis] // n
        return jnp.concatenate([lax.slice_in_dim(array, i * size, (i + 1) * size, axis=axis) for i in ring], axis)

    def chip_order(array, axis):
        size = array.shape[axis] // n
        return jnp.concatenate(
            [lax.slice_in_dim(array, ring.index(i) * size, (ring.index(i) + 1) * size, axis=axis) for i in range(n)],
            axis,
        )

    def after(value, *others):
        return lax.optimization_barrier((value,) + others)[0]

    rows_own = layer_input.reshape(tokens, width)
    place = x * tokens + jnp.arange(tokens, dtype=jnp.int32)
    starts = jnp.where((resets.reshape(tokens) > 0) | (place == 0), 1.0, 0.0).astype(F32)
    starts = jnp.broadcast_to(starts[:, None], (tokens, 128))
    valid = (place < lengths[0]).astype(F32)[:, None]
    cot = grad_out.reshape(tokens, width).astype(F32) * valid

    def lane_sum(array):
        return lax.psum_scatter(array, "dp", scatter_dimension=0, tiled=True, axis_index_groups=lanes)

    def plane(array, which):
        return lax.dynamic_index_in_dim(array, which, 2, keepdims=False)

    def both(mine, axis):
        return jnp.concatenate([mine, across(mine)], axis)

    def tn(left, right):
        return lax.dot_general(left, right, (((0,), (0,)), ((), ())), preferred_element_type=F32)

    fh = w_gate.shape[1] // 2
    cot_ring = ring_order(cot.astype(BF16), 1)
    if own % 16 == 0 and own_d % 16 == 0:
        vectors = jnp.concatenate([conv_w, jnp.stack([conv_b, gate_a_b, gate_i_b, decay_param])], axis=0)
        vectors = jnp.pad(vectors, ((0, 0), (0, WIDE - own)))
        gains = jnp.pad(jnp.stack([norm_gain, mlp_gain]), ((0, PAD - taps - 6), (0, WIDE - own_d)))
        gs = jnp.concatenate([jnp.concatenate([gate_a_w, gate_i_w], axis=1), vectors, gains], axis=0)
        got = front(n, w_x, w_y, w_out, gs, w_gate, w_up, w_down.T, rows_own, cot_ring, starts)
        w_xy, w_o = got["w_xy"].reshape(width, rec), got["w_o"].reshape(rec, width // 2)
        w_gu, w_d = got["w_gu"].reshape(width, 2 * fh), got["w_d"].reshape(width, fh)
        cot_all, n2_all = got["cot"].reshape(4 * tokens, width), got["n2"].reshape(4 * tokens, width)
        gain_one, gain_two, cp, gates = got["gains"][0], got["gains"][1], got["cp"], got["gates"]
        starts_two, ypre, u, a, h, xb, x1 = (got[key] for key in ("starts", "ypre", "u", "a", "h", "xb", "x1"))
        h_in, before = got["h_in"][:, 7:8], got["before"][:, PAD - taps + 1 :]
        n1_t, o_t = got["n1_t"].reshape(width // 2, 4 * tokens), got["o_t"].reshape(rh, 4 * tokens)
        hidden, gate, upv, part_d = got["hidden"], got["gate"], got["up"], got["part_d"]
        rs2 = lax.rsqrt(jnp.mean(x1 * x1, axis=-1, keepdims=True) + EPS)
    else:
        small = jnp.concatenate(
            [norm_gain, mlp_gain, conv_w.reshape(-1), conv_b, gate_a_b, gate_i_b, decay_param]
        )
        small = jnp.pad(small, (0, PAD * WIDE - small.shape[0])).reshape(PAD, WIDE)
        gs = jnp.concatenate([jnp.concatenate([gate_a_w, gate_i_w], axis=1), small], axis=0)
        w_xy, w_o, all_gs, w_gu, d_block, rows_two, cot_all, starts_two = gather_weights(
            n, w_x, w_y, w_out, gs, w_gate, w_up, w_down.T, rows_own, cot_ring, starts
        )
        w_d = lax.all_gather(
            d_block.reshape(-1, d_block.shape[2]), "dp", axis=0, tiled=True, axis_index_groups=lanes
        )
        w_gu = w_gu.reshape(width, w_gate.shape[1])
        w_xy = w_xy.reshape(width, rec)
        w_o = w_o.reshape(rec, width // 2)
        cot_all = cot_all.reshape(4 * tokens, width)

        vectors = all_gs[:, :, :, own:].transpose(1, 0, 2, 3, 4).reshape(2 * dp_size, PAD * WIDE)
        gain_one = vectors[:, :own_d].reshape(width).astype(F32)
        gain_two = vectors[:, own_d : 2 * own_d].reshape(width).astype(F32)
        lines = vectors[:, 2 * own_d : 2 * own_d + (taps + 4) * own].reshape(2 * dp_size, taps + 4, own)
        lines = lax.dynamic_slice_in_dim(lines, core * dp_size, dp_size, 0)
        lines = lines.transpose(1, 0, 2).reshape(taps + 4, rh).astype(F32)
        decay = lines[taps + 3 :]
        cp = jnp.concatenate(
            [lines[: taps + 3], jax.nn.softplus(-decay), jax.nn.sigmoid(-decay), jnp.zeros((7, rh), F32)], axis=0
        )
        gates = lax.dynamic_slice_in_dim(all_gs[:, :, :, :own], core * half, half, 1)
        gates = gates.transpose(1, 0, 2, 3, 4).reshape(rh, WIDE)

        n1, xb, ypre = project(rows_two, gain_one[None], w_xy)
        before = lax.ppermute(xb[:, tokens - (taps - 1) :], "tp", [(0, 1)])
        halo = jnp.concatenate([jnp.zeros((2, 8 - (taps - 1), rh), F32), before.astype(F32)], axis=1)
        u, a, h_local, coef = recurrence(xb, halo, gates, cp, starts_two)
        h_in = lax.ppermute(h_local[:, tokens - 1 :], "tp", [(0, 1)])
        h = h_local + coef * h_in
        ybr, _ = gelu_parts(ypre)
        o = (h * ybr).astype(BF16)
        o_sib = sibling(o)
        part_mine, part_theirs = project_out(o, o_sib, w_o)
        x1 = rows_own.astype(F32) + by_core(part_mine, sibling(part_theirs), 1)
        rs2 = lax.rsqrt(jnp.mean(x1 * x1, axis=-1, keepdims=True) + EPS)
        n2 = (x1 * rs2 * gain_two).astype(BF16)
        n2_x = across(n2)

        def plane_rows(values, rows):
            grouped = after(values, n2_x).T.reshape(n, 2, 2, rows, 2 * tokens)
            return plane(grouped, x), plane(grouped, 1 - x)

        o_here, o_send = plane_rows(jnp.concatenate([o, swapped(o_sib)], axis=2).reshape(2 * tokens, rec), own)
        n1_here, n1_send = plane_rows(n1, own_d)
        two = jnp.concatenate([n2, n2_x], axis=0)
        n2_all = jnp.concatenate([two, sibling(two)], axis=0)
        o_t = jnp.concatenate([o_here, across(o_send)], axis=3).reshape(rh, 4 * tokens)
        n1_t = jnp.concatenate([n1_here, across(n1_send)], axis=3).reshape(width // 2, 4 * tokens)

        gu = nn(n2_all, w_gu)
        gate, upv = gu[:, :fh], gu[:, fh:]
        act, _ = gelu_parts(gate)
        hidden = (act * upv).astype(BF16)

        part_d = tn(cot_all, hidden).astype(BF16)
    sum_d = lane_sum(part_d)
    act, slope = gelu_parts(gate)
    d_hidden = nn(after(cot_all, part_d), w_d)
    d_gu = jnp.concatenate([(d_hidden * upv * slope).astype(BF16), (d_hidden * act).astype(BF16)], axis=1)

    def pair_sum(partial):
        return (partial[: 2 * tokens].astype(F32) + sibling(partial[2 * tokens :]).astype(F32)).astype(BF16)

    d_n2_pair = pair_sum(nt(d_gu, w_gu).astype(BF16))
    d_n2_send = d_n2_pair[tokens:]
    d_n2 = d_n2_pair[:tokens].astype(F32) + across(d_n2_send).astype(F32)
    n2_rows = ring_order(after(n2_all, d_n2_send), 1).reshape(4 * tokens, n, 2, width // dp_size)
    n2_rows = plane(n2_rows, core).reshape(4 * tokens, width // 2)
    d_gu_sib = sibling(d_gu)
    d_gu_sib = jnp.concatenate([d_gu_sib[2 * tokens :], d_gu_sib[: 2 * tokens]], axis=0)
    part_gu = tn(n2_rows, after(jnp.concatenate([d_gu, d_gu_sib], axis=1), d_n2_send)).astype(BF16)
    sum_gu = lane_sum(part_gu)
    ff_pair = pair_sum(nt(after(hidden, part_gu), w_d).astype(BF16))
    ff_out = ff_pair[:tokens].astype(F32) + across(ff_pair[tokens:]).astype(F32)

    q2 = gain_two * d_n2
    d_gain_two = jnp.sum(d_n2 * x1 * rs2, axis=0)
    d_x1 = cot + rs2 * q2 - x1 * (rs2 * rs2 * rs2) * jnp.mean(x1 * q2, axis=-1, keepdims=True)
    dbr = d_x1.astype(BF16)
    dbr_mine = lax.dynamic_slice_in_dim(dbr, core * (width // 2), width // 2, 1)
    dbr_theirs = lax.dynamic_slice_in_dim(dbr, (1 - core) * (width // 2), width // 2, 1)
    dbr_half = jnp.concatenate([dbr_mine, sibling(dbr_theirs)], axis=0)
    do_part = nt(dbr_half, w_o)
    do = do_part[:, :rh].reshape(2, tokens, rh) + swapped(sibling(do_part[:, rh:].reshape(2, tokens, rh)))
    dbr_x = across(dbr_half)

    d_ypre, lam_local, coef_back = adjoint(do, h, ypre, a)
    d_ypre_x = both(d_ypre.reshape(2 * tokens, rh), 0)
    inc = lax.ppermute(a[:, :1] * lam_local[:, :1], "tp", [(1, 0)])
    du, d_gates, sums = gates_back(lam_local, coef_back, inc, h, h_in, u, gates, cp, starts_two)
    du_next = lax.ppermute(du[:, : taps - 1], "tp", [(1, 0)])
    du_pad = jnp.concatenate([du, du_next], axis=1).astype(F32)
    xb_pad = jnp.concatenate([before, xb], axis=1).astype(F32)
    d_taps = jnp.stack(
        [jnp.sum(du_pad[:, :tokens] * xb_pad[:, taps - 1 - k : taps - 1 - k + tokens], axis=(0, 1)) for k in range(taps)]
    )
    d_bias = jnp.sum(du_pad[:, :tokens], axis=(0, 1))[None]
    d_xb = sum(cp[k] * du_pad[:, k : k + tokens] for k in range(taps)).astype(BF16)
    d_xy = jnp.concatenate([d_xb, d_ypre], axis=2).reshape(2 * tokens, rec)
    result = (after(x1, d_xb) + chip_order(ff_out, 1)).astype(BF16).reshape(1, tokens, width)
    d_n1_part = nt(d_xy, w_xy).reshape(2, tokens, width)
    d_n1 = d_n1_part[0] + sibling(d_n1_part[1])
    q1 = gain_one * d_n1
    own_f = rows_own.astype(F32)
    own_rs = lax.rsqrt(jnp.mean(own_f * own_f, axis=-1, keepdims=True) + EPS)
    d_gain_one = jnp.sum(d_n1 * own_f * own_rs, axis=0)
    grad_x = d_x1 + own_rs * q1 - own_f * (own_rs * own_rs * own_rs) * jnp.mean(own_f * q1, axis=-1, keepdims=True)

    c_out = nn(after(o_t, d_xb), jnp.concatenate([dbr_half, dbr_x], axis=0)).astype(BF16).reshape(n, 2, own, width // 2)
    c_x = nn(n1_t, both(d_xb.reshape(2 * tokens, rh), 0)).astype(BF16).reshape(n, 2, own_d, rh)
    c_y = nn(n1_t, d_ypre_x).astype(BF16).reshape(n, 2, own_d, rh)

    def placed(part):
        zero = jnp.zeros_like(part)
        return by_core_rows(part, zero)

    def by_core_rows(mine, theirs):
        return jnp.where(
            core == 0, jnp.concatenate([mine, theirs], 0), jnp.concatenate([theirs, mine], 0)
        )

    g = d_gates.reshape(half, 2, 2, own, WIDE)
    g = plane(g, x) + across(plane(g, 1 - x).astype(BF16)).astype(F32)
    g_mine = lax.dynamic_index_in_dim(g, core, 1, keepdims=False)
    g_theirs = lax.dynamic_index_in_dim(g, 1 - core, 1, keepdims=False)
    g_lane = by_core_rows(g_mine, sibling(g_theirs))

    lines_back = jnp.concatenate([d_taps, d_bias, sums[:3]], axis=0)
    lines_back = lines_back.reshape(taps + 4, half, 2, 2, own).transpose(1, 2, 3, 0, 4)
    lines_back = placed(jnp.pad(lines_back, ((0, 0),) * 4 + ((0, 128 - own),)))
    gains = jnp.stack([d_gain_one.reshape(n, 2, 2, own_d), d_gain_two.reshape(n, 2, 2, own_d)], axis=3)
    gains = jnp.pad(gains, ((0, 0),) * 3 + ((0, PAD - taps - 6), (0, 128 - own_d)))
    vec = jnp.concatenate([lines_back, gains], axis=3)
    vec = plane(vec, x) + across(plane(vec, 1 - x))
    vec = lax.dynamic_index_in_dim(vec, core, 1, keepdims=False) + sibling(
        lax.dynamic_index_in_dim(vec, 1 - core, 1, keepdims=False)
    )

    def whole(block):
        rows = block.shape[0] // 2
        block = block.reshape(2, rows, block.shape[1])
        mine = lax.dynamic_index_in_dim(block, core, 0, keepdims=False)
        theirs = lax.dynamic_index_in_dim(block, 1 - core, 0, keepdims=False)
        return mine, sibling(theirs)

    def halves(pair):
        return by_core(pair[0], pair[1], 1).astype(F32)

    grad_down = halves(whole(sum_d)).T
    x_sum, y_sum, out_sum, sum_gates, sum_vec = scatter_sums(
        n, after(c_x, grad_down, result, grad_x), c_y, c_out, g_lane.astype(BF16), vec
    )
    done = finish(after(sum_gu, sum_vec), x_sum, y_sum, out_sum, sum_gates, sum_vec, taps)
    grad_gate, grad_up, grad_w_x, grad_w_y, grad_w_out, grad_a_w, grad_i_w, grad_taps = done[:8]
    grad_bias, grad_a_b, grad_i_b, grad_decay, grad_gain_one, grad_gain_two = (v.reshape(-1) for v in done[8:])
    return (
        result,
        grad_x.reshape(1, tokens, width),
        grad_gain_one,
        grad_w_x,
        grad_w_y,
        grad_taps,
        grad_bias,
        grad_a_w,
        grad_a_b,
        grad_i_w,
        grad_i_b,
        grad_decay,
        grad_w_out,
        grad_gain_two,
        grad_gate,
        grad_up,
        grad_down,
    )


def solution(mesh):
    every = ("dp", "tp")
    return jax.shard_map(
        functools.partial(body, mesh.shape["dp"]),
        mesh=mesh,
        in_specs=(
            P("dp", "tp", None),
            P("dp", "tp", None),
            P("dp"),
            P("dp", "tp"),
            P(every),
            P(every, None),
            P(every, None),
            P(None, every),
            P(every),
            P(every, None),
            P(every),
            P(every, None),
            P(every),
            P(every),
            P(every, None),
            P(every),
            P("dp", "tp"),
            P("dp", "tp"),
            P("tp", "dp"),
        ),
        out_specs=(
            P("dp", "tp", None),
            P("dp", "tp", None),
            P(every),
            P(every, None),
            P(every, None),
            P(None, every),
            P(every),
            P(every, None),
            P(every),
            P(every, None),
            P(every),
            P(every),
            P(every, None),
            P(every),
            P("dp", "tp"),
            P("dp", "tp"),
            P("tp", "dp"),
        ),
        check_vma=False,
    )
```

```python
import functools

import jax
import jax.numpy as jnp
import numpy as np
from jax import lax
from jax.experimental import pallas as pl
from jax.experimental.pallas import tpu as pltpu
from jax.sharding import PartitionSpec as P

BLK = 256
PAD = 16
WIDE = 512
EPS = 1e-06
MESH = pl.DeviceIdType.MESH
F32 = jnp.float32
BF16 = jnp.bfloat16


def chip_at(pos, n):
    back = pos // (n // 2)
    return (1 - back) * (2 * pos) + back * (2 * (n - 1 - pos) + 1)


def place_of(chip, n):
    odd = chip % 2
    return (1 - odd) * (chip // 2) + odd * (n - 1 - chip // 2)


def heads_first(chip, core, n):
    return (chip + n - core * (n // 2)) % n


class Copies:
    def __init__(self, local, sends, recvs):
        self.local, self.sends, self.recvs = local, sends, recvs
        self.locals_used = self.used = 0

    def stay(self, src, dst):
        copy = pltpu.make_async_copy(src, dst, self.local.at[self.locals_used])
        self.locals_used += 1
        copy.start()
        return copy

    def send(self, src, dst, device):
        copy = pltpu.make_async_remote_copy(
            src_ref=src, dst_ref=dst, send_sem=self.sends.at[self.used], recv_sem=self.recvs.at[self.used],
            device_id=device, device_id_type=MESH,
        )
        self.used += 1
        copy.start()
        return copy


def greet(devices):
    barrier = pltpu.get_barrier_semaphore()
    for device in devices:
        pl.semaphore_signal(barrier, inc=1, device_id=device, device_id_type=MESH)
    pl.semaphore_wait(barrier, len(devices))


def half_cols(ref, which):
    width = ref.shape[1] // 2
    return ref.at[:, pl.ds(pl.multiple_of(which * width, 128), width)]


def gather_kernel(
    n,
    wx, wy, wo, gs, wg, wu, wd, rows_in, cot, starts,
    o_xy, o_out, o_gs, o_gu, o_d, o_rows, o_cot, o_starts,
    local_sem, send_sem, recv_sem,
):
    dp, x = lax.axis_index("dp"), lax.axis_index("tp")
    chip, core = dp // 2, dp % 2
    other = 1 - core
    pos = place_of(chip, n)
    half = n // 2
    nxt = (chip_at((pos + 1) % n, n) * 2 + core, x)
    prv = (chip_at((pos + n - 1) % n, n) * 2 + core, x)
    sib = (chip * 2 + other, x)
    over = (dp, 1 - x)
    greet([nxt, prv, sib, over])
    copies = Copies(local_sem, send_sem, recv_sem)
    send, stay = copies.send, copies.stay

    def by_heads(chip_id, which):
        return heads_first(chip_id, which, n)

    rhalf = wx.shape[1] // 2
    fhalf = wg.shape[1] // 2
    rec_parts = [
        (wx, o_xy.at[chip, core, x, :, pl.ds(0, rhalf)]),
        (wy, o_xy.at[chip, core, x, :, pl.ds(rhalf, rhalf)]),
    ]
    ff_parts = [
        (wg, o_gu.at[chip, core, :, pl.ds(0, fhalf)]),
        (wu, o_gu.at[chip, core, :, pl.ds(fhalf, fhalf)]),
        (wd, o_d.at[core]),
    ]
    pair = [send(half_cols(src, other), slot, sib) for src, slot in rec_parts]
    pair.append(send(half_cols(wo, other), o_out.at[by_heads(chip, other), core, x], sib))
    mine = [stay(half_cols(src, core), slot) for src, slot in rec_parts] + [stay(gs, o_gs.at[core, chip, x])]
    mine.append(stay(half_cols(wo, core), o_out.at[by_heads(chip, core), core, x]))
    late = [send(half_cols(src, other), slot, sib) for src, slot in ff_parts]
    plain = [stay(half_cols(src, core), slot) for src, slot in ff_parts]
    late += [send(rows_in, o_rows.at[1], sib), send(starts, o_starts.at[1], sib), send(cot, o_cot.at[2], sib)]
    plain += [stay(rows_in, o_rows.at[0]), stay(starts, o_starts.at[0]), stay(cot, o_cot.at[0])]

    def rec_block(chip_id):
        return [o_xy.at[chip_id, :, x], o_out.at[by_heads(chip_id, core), :, x], o_gs.at[core, chip_id, x]]

    def rec_piece(chip_id, which):
        refs = [o_xy.at[chip_id, which, x], o_out.at[by_heads(chip_id, core), which, x]]
        return refs + ([o_gs.at[core, chip_id, x]] if which == 0 else [])

    def ff_block(chip_id):
        return [o_gu.at[chip_id]]

    def ff_piece(chip_id, which):
        return [o_gu.at[chip_id, which]]

    def send_all(refs, device):
        return [send(ref, ref, device) for ref in refs]

    def hop(s, block, piece):
        ahead = chip_at((pos + n - (s - 1)) % n, n)
        behind = chip_at((pos + s - 1) % n, n)
        if s < half:
            return send_all(block(ahead), nxt) + send_all(block(behind), prv)
        return send_all(piece(ahead, 0), nxt) + send_all(piece(behind, 1), prv)

    for copy in pair:
        copy.wait_recv()
    for copy in mine:
        copy.wait()
    done, crossed, moving = [], send_all(rec_block(chip), over), []
    for s in range(1, half + 1):
        for copy in moving:
            copy.wait_recv()
        done.extend(moving)
        moving = hop(s, rec_block, rec_piece)
        if s > 1:
            crossed.extend(send_all(rec_block(chip_at((pos + n - (s - 1)) % n, n)), over))
            crossed.extend(send_all(rec_block(chip_at((pos + s - 1) % n, n)), over))
    last_rec = moving
    for copy in late:
        copy.wait_recv()
    for copy in plain:
        copy.wait()
    moving = hop(1, ff_block, ff_piece)
    for copy in last_rec:
        copy.wait_recv()
    done.extend(last_rec)
    crossed.extend(send_all(rec_block(chip_at((pos + half) % n, n)), over))
    cot_over = send(cot, o_cot.at[1], over)
    for s in range(2, half + 1):
        for copy in moving:
            copy.wait_recv()
        done.extend(moving)
        moving = hop(s, ff_block, ff_piece)
    for copy in crossed:
        copy.wait_recv()
    swap = send(o_gs.at[core], o_gs.at[core], sib)
    cot_over.wait_recv()
    last = send(o_cot.at[1], o_cot.at[3], sib)
    for copy in moving:
        copy.wait_recv()
    done.extend(moving)
    swap.wait_recv()
    last.wait_recv()
    for copy in pair + late + done + crossed + [cot_over, swap, last]:
        copy.wait_send()


def gather_weights(n, wx, wy, wo, gs, wg, wu, wd, rows_in, cot, starts):
    r, d, (rows_f, f) = wx.shape[1], wo.shape[1], wg.shape
    tokens = rows_in.shape[0]
    shapes = [
        jax.ShapeDtypeStruct((n, 2, 2, wx.shape[0], r), BF16),
        jax.ShapeDtypeStruct((n, 2, 2, wo.shape[0], d // 2), BF16),
        jax.ShapeDtypeStruct((2, n, 2) + gs.shape, BF16),
        jax.ShapeDtypeStruct((n, 2, rows_f, f), BF16),
        jax.ShapeDtypeStruct((2, rows_f, f // 2), BF16),
        jax.ShapeDtypeStruct((2, tokens, d), BF16),
        jax.ShapeDtypeStruct((4, tokens, d), BF16),
        jax.ShapeDtypeStruct((2,) + starts.shape, F32),
    ]
    count = 9 + (3 * n - 1) + n + 3 * n + 3
    dma = pltpu.SemaphoreType.DMA
    return pl.pallas_call(
        functools.partial(gather_kernel, n),
        out_shape=shapes,
        in_specs=[pl.BlockSpec(memory_space=pltpu.VMEM)] * 10,
        out_specs=[pl.BlockSpec(memory_space=pl.ANY)] * 8,
        scratch_shapes=[dma((10,)), dma((count,)), dma((count,))],
        compiler_params=pltpu.CompilerParams(
            collective_id=0, has_side_effects=True, vmem_limit_bytes=24 << 20
        ),
        name="gather_weights",
    )(wx, wy, wo, gs, wg, wu, wd, rows_in, cot, starts)


def scatter_kernel(
    n,
    c_x, c_y, c_out, c_g, c_v,
    g_x, g_y, g_out, g_gates, g_vec,
    r_x, r_y, r_out, r_g, r_v, s_x, s_y, s_out,
    send_sem, recv_sem,
):
    dp, x = lax.axis_index("dp"), lax.axis_index("tp")
    chip, core = dp // 2, dp % 2
    pos = place_of(chip, n)
    half = n // 2
    nxt = (chip_at((pos + 1) % n, n) * 2 + core, x)
    prv = (chip_at((pos + n - 1) % n, n) * 2 + core, x)
    sib = (dp + 1 - 2 * core, x)
    greet([nxt, prv, sib])
    copies = Copies(None, send_sem, recv_sem)

    pieces = []
    for part in (0, 1):
        for terms, slots, first in ((c_out, r_out, core), (c_y, r_y, 0), (c_x, r_x, 0)):
            pieces.append((
                lambda c, terms=terms, part=part, first=first: terms.at[heads_first(c, first, n), part],
                lambda w, k, slots=slots, part=part: slots.at[part, w, k],
                part,
            ))
    pieces.append((lambda c: c_g.at[c], lambda w, k: r_g.at[w, k], 0))
    pieces.append((lambda c: c_v.at[c], lambda w, k: r_v.at[w, k], 1))

    def add(a, b):
        return a[...].astype(F32) + b[...].astype(F32)

    sent, coming = [], {}
    for k in range(half, -1, -1):
        for i, (term, slot, far) in enumerate(pieces):
            for way, (device, sign) in enumerate(((nxt, 1), (prv, n - 1))):
                first = half if way == far else half - 1
                if k > first or k == 0:
                    continue
                source = term(chip_at((pos + sign * k) % n, n))
                if k < first:
                    coming[i, way].wait_recv()
                    got = slot(way, k)
                    got[...] = add(got, source).astype(got.dtype)
                    source = got
                copy = copies.send(source, slot(way, k - 1), device)
                coming[i, way] = copy
                sent.append(copy)

    def total(i):
        term, slot, _ = pieces[i]
        for way in (0, 1):
            coming[i, way].wait_recv()
        return add(term(chip), slot(0, 0)) + slot(1, 0)[...].astype(F32)

    def cols(ref):
        width = ref.shape[1] // 2
        return pl.ds(pl.multiple_of(core * width, 128), width)

    final = []
    for i, (ref, handed) in enumerate(((g_out, s_out), (g_y, s_y), (g_x, s_x))):
        sums = [total(3 * part + i) for part in (0, 1)]
        for part in (0, 1):

            @pl.when(core == part)
            def _():
                ref[:, cols(ref)] = sums[part]
                handed[...] = sums[1 - part]

        final.append(copies.send(handed, ref.at[:, cols(ref)], sib))
    g_gates[...] = total(6)
    g_vec[...] = total(7)
    for copy in final:
        copy.wait_recv()
    for copy in sent + final:
        copy.wait_send()


def scatter_sums(n, c_x, c_y, c_out, c_g, c_v):
    _, _, rows_d, rhalf = c_x.shape
    _, _, rows_r, dhalf = c_out.shape
    half = n // 2
    count = 8 * (2 * half - 1) + 3
    dma = pltpu.SemaphoreType.DMA
    vmem = pl.BlockSpec(memory_space=pltpu.VMEM)
    return pl.pallas_call(
        functools.partial(scatter_kernel, n),
        out_shape=[
            jax.ShapeDtypeStruct((rows_d, 2 * rhalf), F32),
            jax.ShapeDtypeStruct((rows_d, 2 * rhalf), F32),
            jax.ShapeDtypeStruct((rows_r, 2 * dhalf), F32),
            jax.ShapeDtypeStruct(c_g.shape[1:], F32),
            jax.ShapeDtypeStruct(c_v.shape[1:], F32),
        ],
        in_specs=[vmem] * 5,
        out_specs=[vmem] * 5,
        scratch_shapes=[
            pltpu.VMEM((2, 2, half, rows_d, rhalf), BF16),
            pltpu.VMEM((2, 2, half, rows_d, rhalf), BF16),
            pltpu.VMEM((2, 2, half, rows_r, dhalf), BF16),
            pltpu.VMEM((2, half) + c_g.shape[1:], BF16),
            pltpu.VMEM((2, half) + c_v.shape[1:], F32),
            pltpu.VMEM((rows_d, rhalf), F32),
            pltpu.VMEM((rows_d, rhalf), F32),
            pltpu.VMEM((rows_r, dhalf), F32),
            dma((count,)), dma((count,)),
        ],
        compiler_params=pltpu.CompilerParams(
            collective_id=1, has_side_effects=True, vmem_limit_bytes=56 << 20
        ),
        name="scatter_sums",
    )(c_x, c_y, c_out, c_g, c_v)


def project_kernel(steps, rows, gain, w, n1_ref, x_ref, y_ref):
    i = pl.program_id(0)

    @pl.when(i == 0)
    def _():
        values = rows[...].astype(F32)
        scale = lax.rsqrt(jnp.mean(values * values, axis=-1, keepdims=True) + EPS)
        n1_ref[...] = (values * scale * gain[...]).astype(BF16).reshape(n1_ref.shape)

    result = jnp.dot(n1_ref[...], w[...], preferred_element_type=F32).reshape(y_ref.shape)

    @pl.when(i < steps)
    def _():
        x_ref[...] = result.astype(BF16)

    @pl.when(i >= steps)
    def _():
        y_ref[...] = result


def project(rows, gain, w):
    _, tokens, width = rows.shape
    rh = w.shape[1] // 2
    steps = rh // BLK
    return pl.pallas_call(
        functools.partial(project_kernel, steps),
        grid=(2 * steps,),
        in_specs=[
            pl.BlockSpec(rows.shape, lambda i: (0, 0, 0)),
            pl.BlockSpec((1, width), lambda i: (0, 0)),
            pl.BlockSpec((width, BLK), lambda i: (0, i)),
        ],
        out_specs=[
            pl.BlockSpec((2 * tokens, width), lambda i: (0, 0)),
            pl.BlockSpec((2, tokens, BLK), lambda i: (0, 0, jnp.minimum(i, steps - 1))),
            pl.BlockSpec((2, tokens, BLK), lambda i: (0, 0, jnp.maximum(i - steps, 0))),
        ],
        out_shape=[
            jax.ShapeDtypeStruct((2 * tokens, width), BF16),
            jax.ShapeDtypeStruct((2, tokens, rh), BF16),
            jax.ShapeDtypeStruct((2, tokens, rh), F32),
        ],
        compiler_params=pltpu.CompilerParams(vmem_limit_bytes=40 << 20),
        cost_estimate=pl.CostEstimate(flops=27 * 10**8, bytes_accessed=15 * 10**6, transcendentals=0),
        name="project",
    )(rows, gain, w)


def project_out_kernel(o, o_sib, w, mine_ref, theirs_ref):
    rh = o.shape[2]
    for row, ref in ((0, mine_ref), (1, theirs_ref)):
        ref[...] = jnp.dot(o[row], w[:rh], preferred_element_type=F32) + jnp.dot(
            o_sib[1 - row], w[rh:], preferred_element_type=F32
        )


def project_out(o, o_sib, w):
    _, tokens, rh = o.shape
    cols = w.shape[1]
    tile = min(BLK, cols)
    whole = pl.BlockSpec(o.shape, lambda i: (0, 0, 0))
    part = pl.BlockSpec((tokens, tile), lambda i: (0, i))
    return pl.pallas_call(
        project_out_kernel,
        grid=(cols // tile,),
        in_specs=[whole, whole, pl.BlockSpec((2 * rh, tile), lambda i: (0, i))],
        out_specs=[part, part],
        out_shape=[jax.ShapeDtypeStruct((tokens, cols), F32)] * 2,
        compiler_params=pltpu.CompilerParams(vmem_limit_bytes=40 << 20),
        cost_estimate=pl.CostEstimate(flops=14 * 10**8, bytes_accessed=8 * 10**6, transcendentals=0),
        name="project_out",
    )(o, o_sib, w)


def minus_expm1(v):
    series = jnp.ones_like(v)
    for k in range(9, 1, -1):
        series = 1.0 + series * v * (1.0 / k)
    return jnp.where(v > -0.5, -v * series, 1.0 - jnp.exp(v))


def gates_of(u, weights, cp, start):
    tokens = u.shape[0] * u.shape[1]
    flat = u.reshape(tokens, BLK)
    z = jnp.dot(flat, weights, preferred_element_type=F32)
    r = jax.nn.sigmoid(z[:, :BLK] + cp[5:6]).reshape(u.shape)
    ig = jax.nn.sigmoid(z[:, BLK:] + cp[6:7]).reshape(u.shape)
    la = -8.0 * r * cp[7:8][None]
    decayed = jnp.exp(la)
    rest = minus_expm1(2.0 * la)
    return r, ig, decayed, rest


def recurrence_kernel(xb, halo, weights, cp, starts, u_ref, a_ref, h_ref, c_ref, b_ref):
    rows, length = xb.shape[0], xb.shape[1]
    p = cp[...]
    us = []
    for row in range(rows):
        padded = jnp.concatenate([halo[row], xb[row].astype(F32)], axis=0)
        total = p[4:5] + p[0:1] * padded[8 : 8 + length]
        for k in range(1, 4):
            total = total + p[k : k + 1] * padded[8 - k : 8 - k + length]
        us.append(total.astype(BF16))
    u = jnp.stack(us)
    u_ref[...] = u
    start = starts[...]
    start = jnp.concatenate([start, start], axis=2)
    r, ig, decayed, rest = gates_of(u, weights[...], p, start)
    a_ref[...] = decayed * (1.0 - start)
    b_ref[...] = jnp.where(start > 0.5, 1.0, jnp.sqrt(rest)) * ig * u.astype(F32)

    def eight(i, carry):
        at = pl.ds(pl.multiple_of(i * 8, 8), 8)
        out = []
        for row in range(rows):
            h, c = carry[row]
            a, b = a_ref[row, at, :], b_ref[row, at, :]
            hs, cs = [], []
            for j in range(8):
                h = a[j : j + 1] * h + b[j : j + 1]
                c = a[j : j + 1] * c
                hs.append(h)
                cs.append(c)
            h_ref[row, at, :] = jnp.concatenate(hs, axis=0)
            c_ref[row, at, :] = jnp.concatenate(cs, axis=0)
            out.append((h, c))
        return tuple(out)

    zero, one = jnp.zeros((1, BLK), F32), jnp.ones((1, BLK), F32)
    lax.fori_loop(0, length // 8, eight, ((zero, one),) * rows)


def recurrence(xb, halo, weights, cp, starts):
    rows, length, channels = xb.shape
    wide = pl.BlockSpec((rows, length, BLK), lambda h: (0, 0, h))
    return pl.pallas_call(
        recurrence_kernel,
        grid=(channels // BLK,),
        in_specs=[
            wide,
            pl.BlockSpec((rows, 8, BLK), lambda h: (0, 0, h)),
            pl.BlockSpec((BLK, 2 * BLK), lambda h: (h, 0)),
            pl.BlockSpec((cp.shape[0], BLK), lambda h: (0, h)),
            pl.BlockSpec(starts.shape, lambda h: (0, 0, 0)),
        ],
        out_specs=[wide] * 4,
        out_shape=[jax.ShapeDtypeStruct(xb.shape, BF16)] + [jax.ShapeDtypeStruct(xb.shape, F32)] * 3,
        scratch_shapes=[pltpu.VMEM((rows, length, BLK), F32)],
        compiler_params=pltpu.CompilerParams(vmem_limit_bytes=40 << 20),
        cost_estimate=pl.CostEstimate(flops=4 * 10**8, bytes_accessed=6 * 10**6, transcendentals=2 * 10**6),
        name="recurrence",
    )(xb, halo, weights, cp, starts)


def gelu_parts(v):
    inner = 0.7978845608028654 * (v + 0.044715 * v * v * v)
    t = jnp.tanh(inner)
    value = 0.5 * v * (1.0 + t)
    slope = 0.5 * (1.0 + t) + 0.5 * v * (1.0 - t * t) * 0.7978845608028654 * (1.0 + 3.0 * 0.044715 * v * v)
    return value, slope


def adjoint_kernel(do, h_ref, y_ref, a_ref, dy_ref, lam_ref, c_ref, dh_ref):
    rows, length = do.shape[0], do.shape[1]
    value, slope = gelu_parts(y_ref[...])
    dy_ref[...] = (do[...] * h_ref[...] * slope).astype(BF16)
    dh_ref[...] = do[...] * value

    def eight(step, carry):
        i = length // 8 - 1 - step
        at = pl.ds(pl.multiple_of(i * 8, 8), 8)
        out = []
        for row in range(rows):
            ahead, c = carry[row]
            a, d = a_ref[row, at, :], dh_ref[row, at, :]
            ls, cs = [None] * 8, [None] * 8
            for j in range(7, -1, -1):
                lam = d[j : j + 1] + ahead
                ls[j], cs[j] = lam, c
                ahead = a[j : j + 1] * lam
                c = a[j : j + 1] * c
            lam_ref[row, at, :] = jnp.concatenate(ls, axis=0)
            c_ref[row, at, :] = jnp.concatenate(cs, axis=0)
            out.append((ahead, c))
        return tuple(out)

    zero, one = jnp.zeros((1, BLK), F32), jnp.ones((1, BLK), F32)
    lax.fori_loop(0, length // 8, eight, ((zero, one),) * rows)


def adjoint(do, h, ypre, a):
    rows, length, channels = do.shape
    wide = pl.BlockSpec((rows, length, BLK), lambda i: (0, 0, i))
    return pl.pallas_call(
        adjoint_kernel,
        grid=(channels // BLK,),
        in_specs=[wide] * 4,
        out_specs=[wide] * 3,
        out_shape=[jax.ShapeDtypeStruct(do.shape, BF16)] + [jax.ShapeDtypeStruct(do.shape, F32)] * 2,
        scratch_shapes=[pltpu.VMEM((rows, length, BLK), F32)],
        compiler_params=pltpu.CompilerParams(vmem_limit_bytes=40 << 20),
        cost_estimate=pl.CostEstimate(flops=10**7, bytes_accessed=9 * 10**6, transcendentals=10**6),
        name="adjoint",
    )(do, h, ypre, a)


def gates_back_kernel(lam_ref, c_ref, inc, h_ref, h_in, u_ref, weights, cp, starts, du_ref, dw_ref, sums_ref):
    rows, length = u_ref.shape[0], u_ref.shape[1]
    tokens = rows * length
    p = cp[...]
    u = u_ref[...]
    uf = u.astype(F32)
    start = starts[...]
    start = jnp.concatenate([start, start], axis=2)
    w = weights[...]
    r, ig, decayed, rest = gates_of(u, w, p, start)
    mult = jnp.where(start > 0.5, 1.0, jnp.sqrt(rest))
    lam = lam_ref[...] + c_ref[...] * inc[...]
    before = jnp.stack([jnp.concatenate([h_in[row], h_ref[row][: length - 1]], axis=0) for row in range(rows)])
    keep = 1.0 - start
    d_la = lam * before * decayed * keep - jnp.where(
        start > 0.5, 0.0, lam * ig * uf * decayed * decayed * lax.rsqrt(jnp.where(start > 0.5, 1.0, rest))
    )
    dpa = d_la * (-8.0 * p[7:8][None]) * r * (1.0 - r)
    direct = lam * mult
    dpi = direct * uf * ig * (1.0 - ig)
    d_decay = d_la * (8.0 * p[8:9][None]) * r
    dz = jnp.concatenate(
        [dpa.reshape(tokens, BLK).astype(BF16), dpi.reshape(tokens, BLK).astype(BF16)], axis=1
    )
    back = lax.dot_general(dz, w, (((1,), (1,)), ((), ())), preferred_element_type=F32)
    du_ref[...] = (direct * ig + back.reshape(u.shape)).astype(BF16)
    dw_ref[...] = lax.dot_general(
        u.reshape(tokens, BLK), dz, (((0,), (0,)), ((), ())), preferred_element_type=F32
    )
    zero = jnp.zeros((5, BLK), F32)
    sums_ref[...] = jnp.concatenate(
        [jnp.sum(v.reshape(tokens, BLK), axis=0, keepdims=True) for v in (dpa, dpi, d_decay)] + [zero], axis=0
    )


def gates_back(lam, coef, inc, h, h_in, u, weights, cp, starts):
    rows, length, channels = u.shape
    wide = pl.BlockSpec((rows, length, BLK), lambda i: (0, 0, i))
    line = pl.BlockSpec((rows, 1, BLK), lambda i: (0, 0, i))
    square = pl.BlockSpec((BLK, 2 * BLK), lambda i: (i, 0))
    return pl.pallas_call(
        gates_back_kernel,
        grid=(channels // BLK,),
        in_specs=[
            wide, wide, line, wide, line, wide, square,
            pl.BlockSpec((cp.shape[0], BLK), lambda i: (0, i)),
            pl.BlockSpec(starts.shape, lambda i: (0, 0, 0)),
        ],
        out_specs=[wide, square, pl.BlockSpec((8, BLK), lambda i: (0, i))],
        out_shape=[
            jax.ShapeDtypeStruct(u.shape, BF16),
            jax.ShapeDtypeStruct((channels, 2 * BLK), F32),
            jax.ShapeDtypeStruct((8, channels), F32),
        ],
        compiler_params=pltpu.CompilerParams(vmem_limit_bytes=40 << 20),
        cost_estimate=pl.CostEstimate(flops=12 * 10**8, bytes_accessed=9 * 10**6, transcendentals=2 * 10**6),
        name="gates_back",
    )(lam, coef, inc, h, h_in, u, weights, cp, starts)


def log1p_small(e):
    series = jnp.ones_like(e) * (1.0 / 14)
    for k in range(13, 0, -1):
        series = 1.0 / k - e * series
    return jnp.where(e < 0.25, e * series, jnp.log(1.0 + e))


def front_kernel(n, *refs):
    (
        wx, wy, wo, gs, wg, wu, wd, rows_in, grad, lengths, resets, spread_r, pick_r, spread_d, pick_d,
        o_xy, o_out, o_gates, o_cp, o_gains, o_gu, o_d, o_cot, o_starts, o_ypre, o_u, o_a, o_h, o_hin, o_xb, o_before,
        o_x1, o_n2, o_n1t, o_ot, o_hidden, o_gate, o_up, o_pd,
        v_xy, v_out, v_gs, v_gates, v_rows, v_cot, v_starts, v_cp, v_gains, v_n1, v_n1t, v_xb, v_ypre, v_halo, v_u, v_a,
        v_b, v_h, v_c, v_carry, v_o, v_osib, v_ot, v_part, v_theirs, v_psib, v_x1, v_n2, v_w, v_hidden, v_gu, v_pd, v_wd,
        local_sem, send_sem, recv_sem, load_sem, store_sem, pd_sem,
    ) = refs
    dp, x = lax.axis_index("dp"), lax.axis_index("tp")
    chip, core = dp // 2, dp % 2
    other = 1 - core
    pos = place_of(chip, n)
    half = n // 2
    nxt = (chip_at((pos + 1) % n, n) * 2 + core, x)
    prv = (chip_at((pos + n - 1) % n, n) * 2 + core, x)
    sib = (chip * 2 + other, x)
    over = (dp, 1 - x)
    copies = Copies(local_sem, send_sem, recv_sem)
    send, stay = copies.send, copies.stay
    tokens, width = rows_in.shape
    rec = wx.shape[1]
    rh = rec // 2
    own, own_d = wo.shape[0], wx.shape[0]
    fh = wg.shape[1] // 2
    own_f = wg.shape[0]
    kept, every = [], []

    def put(src, dst):
        kept.append(stay(src, dst))

    def give(src, dst, device):
        copy = send(src, dst, device)
        every.append(copy)
        return copy

    def land(group):
        for copy in group:
            copy.wait_recv()

    class Chain:
        def __init__(self, pieces, arrived=None):
            self.pieces, self.arrived, self.hop = pieces, arrived, 0
            self.ways = ((nxt, n - 1), (prv, 1))
            self.moving = ([], [])

        def start(self, part):
            self.hop = 1
            for ref, own_core in self.pieces(pos):
                if own_core == part:
                    for way, (device, _) in enumerate(self.ways):
                        self.moving[way].append(give(ref, ref, device))
                    if self.arrived:
                        self.arrived(ref)

        def advance(self):
            self.hop += 1
            fresh = ([], [])
            blocks = [self.pieces((pos + back * (self.hop - 1)) % n) for _, back in self.ways]
            for i in range(len(blocks[0])):
                for way, (device, _) in enumerate(self.ways):
                    ref, own_core = blocks[way][i]
                    self.moving[way][i].wait_recv()
                    if self.hop < half or own_core == (way == 0):
                        fresh[way].append(give(ref, ref, device))
                    if self.arrived:
                        self.arrived(ref)
            self.moving = fresh

        def to_last(self):
            while self.hop < half:
                self.advance()

        def finish(self):
            block = self.pieces((pos + half) % n)
            for way in (0, 1):
                refs = [ref for ref, own_core in block if own_core == (way == 0)]
                for copy, ref in zip(self.moving[way], refs):
                    copy.wait_recv()
                    if self.arrived:
                        self.arrived(ref)

    parts = [(wx, v_xy.at[chip, core, x, :, pl.ds(0, rh)]), (wy, v_xy.at[chip, core, x, :, pl.ds(rh, rh)])]
    mine = [stay(half_cols(src, core), slot) for src, slot in parts]
    mine.append(stay(half_cols(wo, core), v_out.at[heads_first(chip, core, n), core, x]))
    mine.append(stay(gs, v_gs.at[core, chip, x]))
    greet([nxt, prv, sib, over])
    pair = [give(half_cols(src, other), slot, sib) for src, slot in parts]
    pair.append(give(half_cols(wo, other), v_out.at[heads_first(chip, other, n), core, x], sib))

    crossed, held = [], []

    def rec_pieces(place):
        c = chip_at(place, n)
        at = heads_first(c, core, n)
        rows = (own + PAD) // 2
        return [
            (v_xy.at[c, core, x], True), (v_gs.at[core, c, x, pl.ds(0, rows)], True), (v_out.at[at, core, x], True),
            (v_xy.at[c, other, x], False), (v_gs.at[core, c, x, pl.ds(rows, rows)], False),
            (v_out.at[at, other, x], False),
        ]

    def rec_arrived(ref):
        if ref.shape[1] == width // 2:
            held.append(ref)
        else:
            crossed.append(give(ref, ref, over))

    rec_chain = Chain(rec_pieces, rec_arrived)
    gu = Chain(lambda place: [
        (o_gu.at[chip_at(place, n), core], True), (o_gu.at[chip_at(place, n), other], False)
    ])
    down = Chain(lambda place: [(o_d.at[place, core], True), (o_d.at[place, other], False)])
    for copy in mine:
        copy.wait()
    rec_chain.start(True)
    land(pair)
    rec_chain.start(False)
    parts = [(wg, o_gu.at[chip, core, :, pl.ds(0, fh)]), (wu, o_gu.at[chip, core, :, pl.ds(fh, fh)])]
    late = [give(half_cols(src, other), slot, sib) for src, slot in parts]
    plain = [stay(half_cols(src, core), slot) for src, slot in parts]
    late += [give(wd.at[pl.ds(pl.multiple_of(other * fh, 128), fh)], v_wd.at[1], sib), give(rows_in, v_rows.at[1], sib)]
    plain += [stay(wd.at[pl.ds(pl.multiple_of(core * fh, 128), fh)], v_wd.at[0]), stay(rows_in, v_rows.at[0])]
    cotangent = stay(grad, v_n2.at[0])

    lane = lax.broadcasted_iota(jnp.int32, (1, tokens), 1) + x * tokens
    begins = jnp.where((resets[...] > 0) | (lane == 0), 1.0, 0.0)
    v_starts[0] = jnp.broadcast_to(begins, (tokens, tokens)).T
    late.append(give(v_starts.at[0], v_starts.at[1], sib))
    valid = lax.broadcasted_iota(jnp.int32, (tokens, 1), 0) + x * tokens < lengths[0]
    valid = jnp.where(valid, 1.0, 0.0)
    cotangent.wait()
    size = width // n
    for i in range(n):
        from_chip = chip_at(i, n) * size
        v_cot[0, :, i * size : (i + 1) * size] = (v_n2[0, :, from_chip : from_chip + size].astype(F32) * valid).astype(BF16)
    late.append(give(v_cot.at[0], v_cot.at[2], sib))
    rec_chain.to_last()
    land(late)
    for copy in plain:
        copy.wait()
    gu.start(True)
    gu.start(False)
    rec_chain.finish()
    for i in range(fh // 128):
        at = pl.ds(i * 128, 128)
        for which in (0, 1):
            v_pd[which, 0:own_f, at] = v_wd[which, at, :].astype(F32).T.astype(BF16)
    turned = [stay(v_pd.at[which, pl.ds(0, own_f)], o_d.at[pos, place]) for which, place in ((0, core), (1, other))]
    swap = [give(v_gs.at[core, :, x], v_gs.at[core, :, x], sib)]
    put(v_starts, o_starts)
    if half > 3:
        gu.advance()
    land(crossed)
    swap.append(give(v_gs.at[core, :, 1 - x], v_gs.at[core, :, 1 - x], sib))
    outs = []

    def cross_held(count):
        for _ in range(min(count, len(held))):
            ref = held.pop(0)
            outs.append(give(ref, ref, over))

    cross_held(4)
    put(v_xy, o_xy)
    land(swap)

    small = v_gs[:, :, :, own : own + PAD, :128].reshape(4 * n * PAD, 128)
    spread = jnp.dot(small, spread_r[...], preferred_element_type=F32).reshape(4 * n, PAD, rh)
    heads = pick_r[:, pl.ds(pl.multiple_of(core * rh, 128), rh)]
    lines = jnp.sum(spread[:, :8] * heads[:, None, :], axis=0)
    decay = lines[7:8]
    e = jnp.exp(-jnp.abs(decay))
    v_cp[0:8, :] = lines
    v_cp[7:8, :] = jnp.maximum(-decay, 0.0) + log1p_small(e)
    v_cp[8:16, :] = jnp.broadcast_to(jax.nn.sigmoid(-decay), (8, rh))
    for i in range(width // WIDE):
        at = pl.ds(i * WIDE, WIDE)
        wide = jnp.dot(small, spread_d[:, at], preferred_element_type=F32).reshape(4 * n, PAD, WIDE)
        v_gains[:, at] = jnp.sum(wide[:, 8:] * pick_d[:, at][:, None, :], axis=0)
    for i in range(2 * n):
        v_gates[i * own : (i + 1) * own, :] = v_gs[(i // 2) % 2, core * half + i // 4, i % 2, 0:own, :]
    put(v_cp, o_cp)
    put(v_gains, o_gains)
    put(v_gates, o_gates)

    values = v_rows[...].astype(F32)
    scale = lax.rsqrt(jnp.mean(values * values, axis=-1, keepdims=True) + EPS)
    v_n1[...] = (values * scale * v_gains[0:1, :]).astype(BF16).reshape(2 * tokens, width)

    def project_x(i, _):
        at = pl.ds(pl.multiple_of(i * BLK, BLK), BLK)
        w = v_xy[:, :, :, :, at].reshape(width, BLK)
        v_xb[:, :, at] = jnp.dot(v_n1[...], w, preferred_element_type=F32).astype(BF16).reshape(2, tokens, BLK)
        return 0

    def project_y(i, _):
        at = pl.ds(pl.multiple_of(i * BLK, BLK), BLK)
        w = v_xy[:, :, :, :, pl.ds(pl.multiple_of(rh + i * BLK, BLK), BLK)].reshape(width, BLK)
        v_ypre[:, :, at] = jnp.dot(v_n1[...], w, preferred_element_type=F32).reshape(2, tokens, BLK)
        return 0

    lax.fori_loop(0, rh // BLK, project_x, 0)
    halo = give(v_xb.at[:, pl.ds(tokens - 16, 16)], v_halo, over)
    cross_held(4)
    put(v_xb, o_xb)
    if half > 3:
        gu.advance()
    lax.fori_loop(0, rh // BLK, project_y, 0)
    put(v_ypre, o_ypre)
    chips_n = BLK // (4 * own_d)

    def turn_n1(i, _):
        at = pl.ds(pl.multiple_of(i * BLK, BLK), BLK)
        turned = v_n1[:, at].astype(F32).T.astype(BF16)
        v_n1t[pl.ds(i * chips_n, chips_n)] = turned.reshape(chips_n, 2, 2, own_d, 2 * tokens)
        return 0

    lax.fori_loop(0, width // BLK, turn_n1, 0)
    halo.wait_recv()
    v_halo[...] = jnp.where(x == 0, jnp.zeros_like(v_halo), v_halo[...])
    put(v_halo, o_before)
    put(v_n1t.at[:, :, x], o_n1t.at[:, :, :, pl.ds(0, 2 * tokens)])

    def head(i, _):
        at = pl.ds(pl.multiple_of(i * BLK, BLK), BLK)
        p = v_cp[:, at]
        us = []
        for row in range(2):
            padded = jnp.concatenate([v_halo[row, :, at].astype(F32)[8:], v_xb[row, :, at].astype(F32)], axis=0)
            total = p[4:5] + p[0:1] * padded[8 : 8 + tokens]
            for k in range(1, 4):
                total = total + p[k : k + 1] * padded[8 - k : 8 - k + tokens]
            us.append(total.astype(BF16))
        u = jnp.stack(us)
        v_u[:, :, at] = u
        start = v_starts[...]
        start = jnp.concatenate([start, start], axis=2)
        _, ig, decayed, rest = gates_of(u, v_gates[at, :], p, start)
        v_a[:, :, at] = decayed * (1.0 - start)
        v_b[...] = jnp.where(start > 0.5, 1.0, jnp.sqrt(rest)) * ig * u.astype(F32)

        def eight(j, carry):
            rows8 = pl.ds(pl.multiple_of(j * 8, 8), 8)
            out = []
            for row in range(2):
                h, c = carry[row]
                a, b = v_a[row, rows8, at], v_b[row, rows8, :]
                hs, cs = [], []
                for k in range(8):
                    h = a[k : k + 1] * h + b[k : k + 1]
                    c = a[k : k + 1] * c
                    hs.append(h)
                    cs.append(c)
                v_h[row, rows8, at] = jnp.concatenate(hs, axis=0)
                v_c[row, rows8, at] = jnp.concatenate(cs, axis=0)
                out.append((h, c))
            return tuple(out)

        zero, one = jnp.zeros((1, BLK), F32), jnp.ones((1, BLK), F32)
        lax.fori_loop(0, tokens // 8, eight, ((zero, one),) * 2)
        return 0

    lax.fori_loop(0, rh // BLK, head, 0)
    carry = give(v_h.at[:, pl.ds(tokens - 8, 8)], v_carry, over)
    put(v_u, o_u)
    put(v_a, o_a)
    carry.wait_recv()
    carry.wait_send()
    cross_held(len(held))
    v_carry[...] = jnp.where(x == 0, jnp.zeros_like(v_carry), v_carry[...])
    put(v_carry, o_hin)

    def output(i, _):
        at = pl.ds(pl.multiple_of(i * BLK, BLK), BLK)
        h = v_h[:, :, at] + v_c[:, :, at] * v_carry[:, 7:8, at]
        v_h[:, :, at] = h
        value, _ = gelu_parts(v_ypre[:, :, at])
        v_o[:, :, at] = (h * value).astype(BF16)
        return 0

    lax.fori_loop(0, rh // BLK, output, 0)
    o_pair = give(v_o, v_osib, sib)
    put(v_h, o_h)
    gu.to_last()
    for copy in turned:
        copy.wait()
    down.start(True)
    down.start(False)
    o_pair.wait_recv()
    land(outs)
    put(v_out, o_out)

    def project_row(row, ref):
        def tile(i, _):
            at = pl.ds(pl.multiple_of(i * BLK, BLK), BLK)
            w0 = v_out[0:half, :, :, :, at].reshape(rh, BLK)
            w1 = v_out[half:n, :, :, :, at].reshape(rh, BLK)
            ref[:, at] = jnp.dot(v_o[row], w0, preferred_element_type=F32) + jnp.dot(
                v_osib[1 - row], w1, preferred_element_type=F32
            )
            return 0

        lax.fori_loop(0, width // 2 // BLK, tile, 0)

    project_row(1, v_theirs)
    x1_pair = give(v_theirs, v_psib, sib)
    project_row(0, v_part)
    x1_pair.wait_recv()
    at_mine = pl.ds(pl.multiple_of(core * (width // 2), 128), width // 2)
    at_theirs = pl.ds(pl.multiple_of(other * (width // 2), 128), width // 2)
    v_x1[:, at_mine] = v_rows[0, :, at_mine].astype(F32) + v_part[...]
    v_x1[:, at_theirs] = v_rows[0, :, at_theirs].astype(F32) + v_psib[...]
    put(v_x1, o_x1)
    x1 = v_x1[...]
    scale = lax.rsqrt(jnp.mean(x1 * x1, axis=-1, keepdims=True) + EPS)
    v_n2[0] = (x1 * scale * v_gains[1:2, :]).astype(BF16)
    n2_over = give(v_n2.at[0], v_n2.at[1], over)
    n2_pair = give(v_n2.at[0], v_n2.at[2], sib)
    cot_over = give(v_cot.at[0], v_cot.at[1], over)
    n1_over = give(v_n1t.at[:, :, 1 - x], o_n1t.at[:, :, :, pl.ds(2 * tokens, 2 * tokens)], over)

    chips_o = 640 // (4 * own)

    def turn_o(i, _):
        at = pl.ds(pl.multiple_of(i * 640, 128), 640)
        here = v_o[:, :, at].astype(F32).reshape(2 * tokens, 640).T.astype(BF16)
        v_ot[pl.ds(i * chips_o, chips_o)] = here.reshape(chips_o, 2, 2, own, 2 * tokens)
        there = jnp.concatenate([v_osib[1, :, at], v_osib[0, :, at]], axis=0).astype(F32).T.astype(BF16)
        v_ot[pl.ds(half + i * chips_o, chips_o)] = there.reshape(chips_o, 2, 2, own, 2 * tokens)
        return 0

    lax.fori_loop(0, rh // 640, turn_o, 0)
    o_over = give(v_ot.at[:, :, 1 - x], o_ot.at[:, :, :, pl.ds(2 * tokens, 2 * tokens)], over)
    put(v_ot.at[:, :, x], o_ot.at[:, :, :, pl.ds(0, 2 * tokens)])

    tile = 128
    steps = fh // tile

    def loads(t, slot):
        first = pl.ds(pl.multiple_of(t * tile, tile), tile)
        second = pl.ds(pl.multiple_of(fh + t * tile, tile), tile)
        return [
            pltpu.make_async_copy(o_gu.at[:, :, :, first], v_w.at[slot, :, :, :, pl.ds(0, tile)], load_sem.at[slot, 0]),
            pltpu.make_async_copy(
                o_gu.at[:, :, :, second], v_w.at[slot, :, :, :, pl.ds(tile, tile)], load_sem.at[slot, 1]
            ),
        ]

    def stores(t, slot):
        at = pl.ds(pl.multiple_of(t * tile, tile), tile)
        return [
            pltpu.make_async_copy(v_gu.at[slot, :, pl.ds(0, tile)], o_gate.at[:, at], store_sem.at[slot, 0]),
            pltpu.make_async_copy(v_gu.at[slot, :, pl.ds(tile, tile)], o_up.at[:, at], store_sem.at[slot, 1]),
        ]

    gu.finish()
    for copy in loads(0, 0):
        copy.start()
    n2_pair.wait_recv()
    n2_over.wait_recv()
    n2_last = give(v_n2.at[1], v_n2.at[3], sib)
    n2_last.wait_recv()
    if half > 3:
        down.advance()
    put(v_n2, o_n2)

    def hidden_tile(t, _):
        slot = t % 2
        for copy in loads(t, slot):
            copy.wait()

        @pl.when(t + 1 < steps)
        def _():
            for copy in loads(t + 1, 1 - slot):
                copy.start()

        @pl.when(t >= 2)
        def _():
            for copy in stores(t - 2, slot):
                copy.wait()

        w = v_w[slot].reshape(width, 2 * tile)
        v_gu[slot] = jnp.dot(v_n2[...].reshape(4 * tokens, width), w, preferred_element_type=F32)
        for copy in stores(t, slot):
            copy.start()
        value, _ = gelu_parts(v_gu[slot, :, 0:tile])
        v_hidden[:, pl.ds(pl.multiple_of(t * tile, tile), tile)] = (value * v_gu[slot, :, tile:]).astype(BF16)
        return 0

    lax.fori_loop(0, steps, hidden_tile, 0)
    put(v_hidden, o_hidden)
    cot_over.wait_recv()
    cot_last = give(v_cot.at[1], v_cot.at[3], sib)
    if half > 3:
        down.advance()
    cot_last.wait_recv()
    put(v_cot, o_cot)

    def pd_store(t, slot):
        return pltpu.make_async_copy(v_pd.at[slot], o_pd.at[pl.ds(pl.multiple_of(t * BLK, BLK), BLK)], pd_sem.at[slot])

    def down_tile(t, _):
        slot = t % 2

        @pl.when(t >= 2)
        def _():
            pd_store(t - 2, slot).wait()

        left = v_cot[:, :, pl.ds(pl.multiple_of(t * BLK, BLK), BLK)].reshape(4 * tokens, BLK)
        v_pd[slot] = lax.dot_general(
            left, v_hidden[...], (((0,), (0,)), ((), ())), preferred_element_type=F32
        ).astype(BF16)
        pd_store(t, slot).start()
        return 0

    lax.fori_loop(0, width // BLK, down_tile, 0)
    down.to_last()
    for t in (steps - 2, steps - 1):
        for copy in stores(t, t % 2):
            copy.wait()
    for t in (width // BLK - 2, width // BLK - 1):
        pd_store(t, t % 2).wait()
    down.finish()
    land([n1_over, o_over])
    for copy in kept:
        copy.wait()
    for copy in every:
        if copy is not carry:
            copy.wait_send()


def front(n, wx, wy, wo, gs, wg, wu, wd, rows_in, grad, lengths, resets):
    rec, f = wx.shape[1], wg.shape[1]
    own, own_d, rows_f = wo.shape[0], wx.shape[0], wg.shape[0]
    rh, fh = rec // 2, f // 2
    tokens, width = rows_in.shape
    half = n // 2
    row = np.arange(4 * n)
    index = (row // 2) % n * 4 + row // (2 * n) * 2 + row % 2
    lane_r, lane_d, short = np.arange(rec), np.arange(width), np.arange(128)[:, None]
    spread_r = (lane_r[None, :rh] % own == short).astype(jnp.bfloat16)
    spread_d = (lane_d[None] % own_d == short).astype(jnp.bfloat16)
    pick_r = (index[:, None] == lane_r[None] // own).astype(np.float32)
    pick_d = (index[:, None] == lane_d[None] // own_d).astype(np.float32)
    outs = dict(
        w_xy=((n, 2, 2, own_d, rec), BF16),
        w_o=((n, 2, 2, own, width // 2), BF16),
        gates=((rh, WIDE), BF16),
        cp=((16, rh), F32),
        gains=((8, width), F32),
        w_gu=((n, 2, rows_f, f), BF16),
        w_d=((n, 2, rows_f, fh), BF16),
        cot=((4, tokens, width), BF16),
        starts=((2, tokens, 128), F32),
        ypre=((2, tokens, rh), F32),
        u=((2, tokens, rh), BF16),
        a=((2, tokens, rh), F32),
        h=((2, tokens, rh), F32),
        h_in=((2, 8, rh), F32),
        xb=((2, tokens, rh), BF16),
        before=((2, 16, rh), BF16),
        x1=((tokens, width), F32),
        n2=((4, tokens, width), BF16),
        n1_t=((n, 2, own_d, 4 * tokens), BF16),
        o_t=((n, 2, own, 4 * tokens), BF16),
        hidden=((4 * tokens, fh), BF16),
        gate=((4 * tokens, fh), F32),
        up=((4 * tokens, fh), F32),
        part_d=((width, fh), BF16),
    )
    state = (2, tokens, rh)
    scratch = [
        ((n, 2, 2, own_d, rec), BF16), ((n, 2, 2, own, width // 2), BF16), ((2, n, 2) + gs.shape, BF16),
        ((rh, WIDE), BF16), ((2, tokens, width), BF16), ((4, tokens, width), BF16), ((2, tokens, 128), F32),
        ((16, rh), F32), ((8, width), F32), ((2 * tokens, width), BF16), ((n, 2, 2, own_d, 2 * tokens), BF16),
        (state, BF16), (state, F32), ((2, 16, rh), BF16), (state, BF16), (state, F32),
        ((2, tokens, BLK), F32), (state, F32), (state, F32), ((2, 8, rh), F32), (state, BF16), (state, BF16),
        ((n, 2, 2, own, 2 * tokens), BF16), ((tokens, width // 2), F32), ((tokens, width // 2), F32),
        ((tokens, width // 2), F32), ((tokens, width), F32), ((4, tokens, width), BF16),
        ((2, n, 2, rows_f, BLK), BF16), ((4 * tokens, fh), BF16), ((2, 4 * tokens, BLK), F32), ((2, BLK, fh), BF16), ((2, fh, own_d * 2), BF16),
    ]
    count = 9 + (6 * n - 6) + 2 * (2 * n - 2) + 6 * n + 2 + 12
    dma = pltpu.SemaphoreType.DMA
    result = pl.pallas_call(
        functools.partial(front_kernel, n),
        out_shape=[jax.ShapeDtypeStruct(shape, kind) for shape, kind in outs.values()],
        in_specs=[pl.BlockSpec(memory_space=pl.ANY)] * 9
        + [pl.BlockSpec(memory_space=pltpu.SMEM)]
        + [pl.BlockSpec(memory_space=pltpu.VMEM)] * 5,
        out_specs=[pl.BlockSpec(memory_space=pl.ANY)] * len(outs),
        scratch_shapes=[pltpu.VMEM(shape, kind) for shape, kind in scratch]
        + [dma((32,)), dma((count,)), dma((count,)), dma((2, 2)), dma((2, 2)), dma((2,))],
        compiler_params=pltpu.CompilerParams(
            collective_id=2, has_side_effects=True, vmem_limit_bytes=60 << 20
        ),
        name="front",
    )(wx, wy, wo, gs, wg, wu, wd, rows_in, grad, lengths, resets, spread_r, pick_r, spread_d, pick_d)
    return dict(zip(outs, result))


def finish_kernel(
    sums, x_sum, y_sum, out_sum, gates, vec,
    gate_ref, up_ref, x_ref, y_ref, out_ref, a_ref, i_ref, taps_ref, *lines,
):
    core = lax.axis_index("dp") % 2
    half = gate_ref.shape[1] // 2
    for first in (0, 1):

        @pl.when(core == first)
        def _():
            for i in (0, 1):
                start = (i != first) * 2 * half
                at = pl.ds(i * half, half)
                gate_ref[:, at] = sums[:, start : start + half].astype(F32)
                up_ref[:, at] = sums[:, start + half : start + 2 * half].astype(F32)

    x_ref[...] = x_sum[...]
    y_ref[...] = y_sum[...]
    out_ref[...] = out_sum[...]
    a_ref[...] = gates[:, :BLK]
    i_ref[...] = gates[:, BLK:]
    taps, own = taps_ref.shape
    taps_ref[...] = vec[0:taps, 0:own]
    for k, ref in enumerate(lines):
        ref[...] = vec[taps + k : taps + k + 1, 0 : ref.shape[1]]


def finish(sums, x_sum, y_sum, out_sum, gates, vec, taps):
    rows, cols = sums.shape
    own, own_d = out_sum.shape[0], x_sum.shape[0]
    steps = 2 if rows % 16 == 0 and own % 16 == 0 and own_d % 16 == 0 else 1

    def tiled(shape):
        return pl.BlockSpec((shape[0] // steps, shape[1]), lambda i: (i, 0))

    def fixed(shape):
        return pl.BlockSpec(shape, lambda i: (0, 0))

    big = [(rows, cols // 2)] * 2 + [x_sum.shape, y_sum.shape, out_sum.shape] + [(own, BLK)] * 2
    small = [(taps, own)] + [(1, own)] * 4 + [(1, own_d)] * 2
    return pl.pallas_call(
        finish_kernel,
        grid=(steps,),
        in_specs=[tiled(v.shape) for v in (sums, x_sum, y_sum, out_sum, gates)] + [fixed(vec.shape)],
        out_specs=[tiled(shape) for shape in big] + [fixed(shape) for shape in small],
        out_shape=[jax.ShapeDtypeStruct(shape, F32) for shape in big + small],
        compiler_params=pltpu.CompilerParams(vmem_limit_bytes=60 << 20),
        name="finish",
    )(sums, x_sum, y_sum, out_sum, gates, vec)


def nt(left, right):
    return lax.dot_general(left, right, (((1,), (1,)), ((), ())), preferred_element_type=F32)


def nn(left, right):
    return jnp.dot(left, right, preferred_element_type=F32)


def body(
    dp_size,
    layer_input, grad_out, lengths, resets, norm_gain, w_x, w_y, conv_w, conv_b, gate_a_w, gate_a_b,
    gate_i_w, gate_i_b, decay_param, w_out, mlp_gain, w_gate, w_up, w_down,
):
    n = dp_size // 2
    half = n // 2
    dp, x = lax.axis_index("dp"), lax.axis_index("tp")
    chip, core = dp // 2, dp % 2
    pos = place_of(chip, n)
    tokens, width = layer_input.shape[1], layer_input.shape[2]
    rec = w_x.shape[1]
    rh = rec // 2
    taps = conv_w.shape[0]
    own = rec // (2 * dp_size)
    own_d = width // (2 * dp_size)

    ring = [chip_at(i, n) for i in range(n)]
    up = [(ring[i] * 2 + c, ring[(i + 1) % n] * 2 + c) for i in range(n) for c in range(2)]
    down = [(b, a) for a, b in up]
    lanes = [[chip_id * 2 + c for chip_id in ring] for c in range(2)]
    pairs = [(d, d + 1 - 2 * (d % 2)) for d in range(dp_size)]

    def sibling(v):
        return lax.ppermute(v, "dp", pairs)

    def across(v):
        return lax.ppermute(v, "tp", [(0, 1), (1, 0)])

    def swapped(v):
        return jnp.concatenate([v[1:], v[:1]], axis=0)

    def by_core(mine, theirs, axis):
        return jnp.where(
            core == 0, jnp.concatenate([mine, theirs], axis), jnp.concatenate([theirs, mine], axis)
        )

    def ring_order(array, axis):
        size = array.shape[axis] // n
        return jnp.concatenate([lax.slice_in_dim(array, i * size, (i + 1) * size, axis=axis) for i in ring], axis)

    def chip_order(array, axis):
        size = array.shape[axis] // n
        return jnp.concatenate(
            [lax.slice_in_dim(array, ring.index(i) * size, (ring.index(i) + 1) * size, axis=axis) for i in range(n)],
            axis,
        )

    def after(value, *others):
        return lax.optimization_barrier((value,) + others)[0]

    rows_own = layer_input.reshape(tokens, width)
    place = x * tokens + jnp.arange(tokens, dtype=jnp.int32)
    starts = jnp.where((resets.reshape(tokens) > 0) | (place == 0), 1.0, 0.0).astype(F32)
    starts = jnp.broadcast_to(starts[:, None], (tokens, 128))
    valid = (place < lengths[0]).astype(F32)[:, None]
    cot = grad_out.reshape(tokens, width).astype(F32) * valid

    def lane_sum(array):
        return lax.psum_scatter(array, "dp", scatter_dimension=0, tiled=True, axis_index_groups=lanes)

    def plane(array, which):
        return lax.dynamic_index_in_dim(array, which, 2, keepdims=False)

    def both(mine, axis):
        return jnp.concatenate([mine, across(mine)], axis)

    def tn(left, right):
        return lax.dot_general(left, right, (((0,), (0,)), ((), ())), preferred_element_type=F32)

    fh = w_gate.shape[1] // 2
    if own % 16 == 0 and own_d % 16 == 0:
        vectors = jnp.concatenate([conv_w, jnp.stack([conv_b, gate_a_b, gate_i_b, decay_param])], axis=0)
        vectors = jnp.pad(vectors, ((0, 0), (0, WIDE - own)))
        gains = jnp.pad(jnp.stack([norm_gain, mlp_gain]), ((0, PAD - taps - 6), (0, WIDE - own_d)))
        gs = jnp.concatenate([jnp.concatenate([gate_a_w, gate_i_w], axis=1), vectors, gains], axis=0)
        got = front(
            n, w_x, w_y, w_out, gs, w_gate, w_up, w_down, rows_own, grad_out.reshape(tokens, width), lengths, resets
        )
        w_xy, w_o = got["w_xy"].reshape(width, rec), got["w_o"].reshape(rec, width // 2)
        w_gu, w_d = got["w_gu"].reshape(width, 2 * fh), got["w_d"].reshape(width, fh)
        cot_all, n2_all = got["cot"].reshape(4 * tokens, width), got["n2"].reshape(4 * tokens, width)
        gain_one, gain_two, cp, gates = got["gains"][0], got["gains"][1], got["cp"], got["gates"]
        starts_two, ypre, u, a, h, xb, x1 = (got[key] for key in ("starts", "ypre", "u", "a", "h", "xb", "x1"))
        h_in, before = got["h_in"][:, 7:8], got["before"][:, PAD - taps + 1 :]
        n1_t, o_t = got["n1_t"].reshape(width // 2, 4 * tokens), got["o_t"].reshape(rh, 4 * tokens)
        hidden, gate, upv, part_d = got["hidden"], got["gate"], got["up"], got["part_d"]
        rs2 = lax.rsqrt(jnp.mean(x1 * x1, axis=-1, keepdims=True) + EPS)
    else:
        small = jnp.concatenate(
            [norm_gain, mlp_gain, conv_w.reshape(-1), conv_b, gate_a_b, gate_i_b, decay_param]
        )
        small = jnp.pad(small, (0, PAD * WIDE - small.shape[0])).reshape(PAD, WIDE)
        gs = jnp.concatenate([jnp.concatenate([gate_a_w, gate_i_w], axis=1), small], axis=0)
        w_xy, w_o, all_gs, w_gu, d_block, rows_two, cot_all, starts_two = gather_weights(
            n, w_x, w_y, w_out, gs, w_gate, w_up, w_down.T, rows_own, ring_order(cot.astype(BF16), 1), starts
        )
        w_d = lax.all_gather(
            d_block.reshape(-1, d_block.shape[2]), "dp", axis=0, tiled=True, axis_index_groups=lanes
        )
        w_gu = w_gu.reshape(width, w_gate.shape[1])
        w_xy = w_xy.reshape(width, rec)
        w_o = w_o.reshape(rec, width // 2)
        cot_all = cot_all.reshape(4 * tokens, width)

        vectors = all_gs[:, :, :, own:].transpose(1, 0, 2, 3, 4).reshape(2 * dp_size, PAD * WIDE)
        gain_one = vectors[:, :own_d].reshape(width).astype(F32)
        gain_two = vectors[:, own_d : 2 * own_d].reshape(width).astype(F32)
        lines = vectors[:, 2 * own_d : 2 * own_d + (taps + 4) * own].reshape(2 * dp_size, taps + 4, own)
        lines = lax.dynamic_slice_in_dim(lines, core * dp_size, dp_size, 0)
        lines = lines.transpose(1, 0, 2).reshape(taps + 4, rh).astype(F32)
        decay = lines[taps + 3 :]
        cp = jnp.concatenate(
            [lines[: taps + 3], jax.nn.softplus(-decay), jax.nn.sigmoid(-decay), jnp.zeros((7, rh), F32)], axis=0
        )
        gates = lax.dynamic_slice_in_dim(all_gs[:, :, :, :own], core * half, half, 1)
        gates = gates.transpose(1, 0, 2, 3, 4).reshape(rh, WIDE)

        n1, xb, ypre = project(rows_two, gain_one[None], w_xy)
        before = lax.ppermute(xb[:, tokens - (taps - 1) :], "tp", [(0, 1)])
        halo = jnp.concatenate([jnp.zeros((2, 8 - (taps - 1), rh), F32), before.astype(F32)], axis=1)
        u, a, h_local, coef = recurrence(xb, halo, gates, cp, starts_two)
        h_in = lax.ppermute(h_local[:, tokens - 1 :], "tp", [(0, 1)])
        h = h_local + coef * h_in
        ybr, _ = gelu_parts(ypre)
        o = (h * ybr).astype(BF16)
        o_sib = sibling(o)
        part_mine, part_theirs = project_out(o, o_sib, w_o)
        x1 = rows_own.astype(F32) + by_core(part_mine, sibling(part_theirs), 1)
        rs2 = lax.rsqrt(jnp.mean(x1 * x1, axis=-1, keepdims=True) + EPS)
        n2 = (x1 * rs2 * gain_two).astype(BF16)
        n2_x = across(n2)

        def plane_rows(values, rows):
            grouped = after(values, n2_x).T.reshape(n, 2, 2, rows, 2 * tokens)
            return plane(grouped, x), plane(grouped, 1 - x)

        o_here, o_send = plane_rows(jnp.concatenate([o, swapped(o_sib)], axis=2).reshape(2 * tokens, rec), own)
        n1_here, n1_send = plane_rows(n1, own_d)
        two = jnp.concatenate([n2, n2_x], axis=0)
        n2_all = jnp.concatenate([two, sibling(two)], axis=0)
        o_t = jnp.concatenate([o_here, across(o_send)], axis=3).reshape(rh, 4 * tokens)
        n1_t = jnp.concatenate([n1_here, across(n1_send)], axis=3).reshape(width // 2, 4 * tokens)

        gu = nn(n2_all, w_gu)
        gate, upv = gu[:, :fh], gu[:, fh:]
        act, _ = gelu_parts(gate)
        hidden = (act * upv).astype(BF16)

        part_d = tn(cot_all, hidden).astype(BF16)
    sum_d = lane_sum(part_d)
    act, slope = gelu_parts(gate)
    d_hidden = nn(after(cot_all, part_d), w_d)
    d_gu = jnp.concatenate([(d_hidden * upv * slope).astype(BF16), (d_hidden * act).astype(BF16)], axis=1)

    def pair_sum(partial):
        return (partial[: 2 * tokens].astype(F32) + sibling(partial[2 * tokens :]).astype(F32)).astype(BF16)

    d_n2_pair = pair_sum(nt(d_gu, w_gu).astype(BF16))
    d_n2_send = d_n2_pair[tokens:]
    d_n2 = d_n2_pair[:tokens].astype(F32) + across(d_n2_send).astype(F32)
    n2_rows = ring_order(after(n2_all, d_n2_send), 1).reshape(4 * tokens, n, 2, width // dp_size)
    n2_rows = plane(n2_rows, core).reshape(4 * tokens, width // 2)
    d_gu_sib = sibling(d_gu)
    d_gu_sib = jnp.concatenate([d_gu_sib[2 * tokens :], d_gu_sib[: 2 * tokens]], axis=0)
    part_gu = tn(n2_rows, after(jnp.concatenate([d_gu, d_gu_sib], axis=1), d_n2_send)).astype(BF16)
    sum_gu = lane_sum(part_gu)
    ff_pair = pair_sum(nt(after(hidden, part_gu), w_d).astype(BF16))
    ff_out = ff_pair[:tokens].astype(F32) + across(ff_pair[tokens:]).astype(F32)

    q2 = gain_two * d_n2
    d_gain_two = jnp.sum(d_n2 * x1 * rs2, axis=0)
    d_x1 = cot + rs2 * q2 - x1 * (rs2 * rs2 * rs2) * jnp.mean(x1 * q2, axis=-1, keepdims=True)
    dbr = d_x1.astype(BF16)
    dbr_mine = lax.dynamic_slice_in_dim(dbr, core * (width // 2), width // 2, 1)
    dbr_theirs = lax.dynamic_slice_in_dim(dbr, (1 - core) * (width // 2), width // 2, 1)
    dbr_half = jnp.concatenate([dbr_mine, sibling(dbr_theirs)], axis=0)
    do_part = nt(dbr_half, w_o)
    do = do_part[:, :rh].reshape(2, tokens, rh) + swapped(sibling(do_part[:, rh:].reshape(2, tokens, rh)))
    dbr_x = across(dbr_half)

    d_ypre, lam_local, coef_back = adjoint(do, h, ypre, a)
    d_ypre_x = both(d_ypre.reshape(2 * tokens, rh), 0)
    inc = lax.ppermute(a[:, :1] * lam_local[:, :1], "tp", [(1, 0)])
    du, d_gates, sums = gates_back(lam_local, coef_back, inc, h, h_in, u, gates, cp, starts_two)
    du_next = lax.ppermute(du[:, : taps - 1], "tp", [(1, 0)])
    du_pad = jnp.concatenate([du, du_next], axis=1).astype(F32)
    xb_pad = jnp.concatenate([before, xb], axis=1).astype(F32)
    d_taps = jnp.stack(
        [jnp.sum(du_pad[:, :tokens] * xb_pad[:, taps - 1 - k : taps - 1 - k + tokens], axis=(0, 1)) for k in range(taps)]
    )
    d_bias = jnp.sum(du_pad[:, :tokens], axis=(0, 1))[None]
    d_xb = sum(cp[k] * du_pad[:, k : k + tokens] for k in range(taps)).astype(BF16)
    d_xy = jnp.concatenate([d_xb, d_ypre], axis=2).reshape(2 * tokens, rec)
    result = (after(x1, d_xb) + chip_order(ff_out, 1)).astype(BF16).reshape(1, tokens, width)
    d_n1_part = nt(d_xy, w_xy).reshape(2, tokens, width)
    d_n1 = d_n1_part[0] + sibling(d_n1_part[1])
    q1 = gain_one * d_n1
    own_f = rows_own.astype(F32)
    own_rs = lax.rsqrt(jnp.mean(own_f * own_f, axis=-1, keepdims=True) + EPS)
    d_gain_one = jnp.sum(d_n1 * own_f * own_rs, axis=0)
    grad_x = d_x1 + own_rs * q1 - own_f * (own_rs * own_rs * own_rs) * jnp.mean(own_f * q1, axis=-1, keepdims=True)

    c_out = nn(after(o_t, d_xb), jnp.concatenate([dbr_half, dbr_x], axis=0)).astype(BF16).reshape(n, 2, own, width // 2)
    c_x = nn(n1_t, both(d_xb.reshape(2 * tokens, rh), 0)).astype(BF16).reshape(n, 2, own_d, rh)
    c_y = nn(n1_t, d_ypre_x).astype(BF16).reshape(n, 2, own_d, rh)

    def placed(part):
        zero = jnp.zeros_like(part)
        return by_core_rows(part, zero)

    def by_core_rows(mine, theirs):
        return jnp.where(
            core == 0, jnp.concatenate([mine, theirs], 0), jnp.concatenate([theirs, mine], 0)
        )

    g = d_gates.reshape(half, 2, 2, own, WIDE)
    g = plane(g, x) + across(plane(g, 1 - x).astype(BF16)).astype(F32)
    g_mine = lax.dynamic_index_in_dim(g, core, 1, keepdims=False)
    g_theirs = lax.dynamic_index_in_dim(g, 1 - core, 1, keepdims=False)
    g_lane = by_core_rows(g_mine, sibling(g_theirs))

    lines_back = jnp.concatenate([d_taps, d_bias, sums[:3]], axis=0)
    lines_back = lines_back.reshape(taps + 4, half, 2, 2, own).transpose(1, 2, 3, 0, 4)
    lines_back = placed(jnp.pad(lines_back, ((0, 0),) * 4 + ((0, 128 - own),)))
    gains = jnp.stack([d_gain_one.reshape(n, 2, 2, own_d), d_gain_two.reshape(n, 2, 2, own_d)], axis=3)
    gains = jnp.pad(gains, ((0, 0),) * 3 + ((0, PAD - taps - 6), (0, 128 - own_d)))
    vec = jnp.concatenate([lines_back, gains], axis=3)
    vec = plane(vec, x) + across(plane(vec, 1 - x))
    vec = lax.dynamic_index_in_dim(vec, core, 1, keepdims=False) + sibling(
        lax.dynamic_index_in_dim(vec, 1 - core, 1, keepdims=False)
    )

    def whole(block):
        rows = block.shape[0] // 2
        block = block.reshape(2, rows, block.shape[1])
        mine = lax.dynamic_index_in_dim(block, core, 0, keepdims=False)
        theirs = lax.dynamic_index_in_dim(block, 1 - core, 0, keepdims=False)
        return mine, sibling(theirs)

    def halves(pair):
        return by_core(pair[0], pair[1], 1).astype(F32)

    grad_down = halves(whole(sum_d)).T
    x_sum, y_sum, out_sum, sum_gates, sum_vec = scatter_sums(
        n, after(c_x, grad_down, result, grad_x), c_y, c_out, g_lane.astype(BF16), vec
    )
    done = finish(after(sum_gu, sum_vec), x_sum, y_sum, out_sum, sum_gates, sum_vec, taps)
    grad_gate, grad_up, grad_w_x, grad_w_y, grad_w_out, grad_a_w, grad_i_w, grad_taps = done[:8]
    grad_bias, grad_a_b, grad_i_b, grad_decay, grad_gain_one, grad_gain_two = (v.reshape(-1) for v in done[8:])
    return (
        result,
        grad_x.reshape(1, tokens, width),
        grad_gain_one,
        grad_w_x,
        grad_w_y,
        grad_taps,
        grad_bias,
        grad_a_w,
        grad_a_b,
        grad_i_w,
        grad_i_b,
        grad_decay,
        grad_w_out,
        grad_gain_two,
        grad_gate,
        grad_up,
        grad_down,
    )


def solution(mesh):
    every = ("dp", "tp")
    return jax.shard_map(
        functools.partial(body, mesh.shape["dp"]),
        mesh=mesh,
        in_specs=(
            P("dp", "tp", None),
            P("dp", "tp", None),
            P("dp"),
            P("dp", "tp"),
            P(every),
            P(every, None),
            P(every, None),
            P(None, every),
            P(every),
            P(every, None),
            P(every),
            P(every, None),
            P(every),
            P(every),
            P(every, None),
            P(every),
            P("dp", "tp"),
            P("dp", "tp"),
            P("tp", "dp"),
        ),
        out_specs=(
            P("dp", "tp", None),
            P("dp", "tp", None),
            P(every),
            P(every, None),
            P(every, None),
            P(None, every),
            P(every),
            P(every, None),
            P(every),
            P(every, None),
            P(every),
            P(every),
            P(every, None),
            P(every),
            P("dp", "tp"),
            P("dp", "tp"),
            P("tp", "dp"),
        ),
        check_vma=False,
    )
```

```python
import functools

import jax
import jax.numpy as jnp
import numpy as np
from jax import lax
from jax.experimental import pallas as pl
from jax.experimental.pallas import tpu as pltpu
from jax.sharding import PartitionSpec as P

BLK = 256
PAD = 16
WIDE = 512
EPS = 1e-06
MESH = pl.DeviceIdType.MESH
F32 = jnp.float32
BF16 = jnp.bfloat16


def chip_at(pos, n):
    back = pos // (n // 2)
    return (1 - back) * (2 * pos) + back * (2 * (n - 1 - pos) + 1)


def place_of(chip, n):
    odd = chip % 2
    return (1 - odd) * (chip // 2) + odd * (n - 1 - chip // 2)


def heads_first(chip, core, n):
    return (chip + n - core * (n // 2)) % n


class Copies:
    def __init__(self, local, sends, recvs):
        self.local, self.sends, self.recvs = local, sends, recvs
        self.locals_used = self.used = 0

    def stay(self, src, dst):
        copy = pltpu.make_async_copy(src, dst, self.local.at[self.locals_used])
        self.locals_used += 1
        copy.start()
        return copy

    def send(self, src, dst, device):
        copy = pltpu.make_async_remote_copy(
            src_ref=src, dst_ref=dst, send_sem=self.sends.at[self.used], recv_sem=self.recvs.at[self.used],
            device_id=device, device_id_type=MESH,
        )
        self.used += 1
        copy.start()
        return copy


def greet(devices):
    barrier = pltpu.get_barrier_semaphore()
    for device in devices:
        pl.semaphore_signal(barrier, inc=1, device_id=device, device_id_type=MESH)
    pl.semaphore_wait(barrier, len(devices))


def half_cols(ref, which):
    width = ref.shape[1] // 2
    return ref.at[:, pl.ds(pl.multiple_of(which * width, 128), width)]


def gather_kernel(
    n,
    wx, wy, wo, gs, wg, wu, wd, rows_in, cot, starts,
    o_xy, o_out, o_gs, o_gu, o_d, o_rows, o_cot, o_starts,
    local_sem, send_sem, recv_sem,
):
    dp, x = lax.axis_index("dp"), lax.axis_index("tp")
    chip, core = dp // 2, dp % 2
    other = 1 - core
    pos = place_of(chip, n)
    half = n // 2
    nxt = (chip_at((pos + 1) % n, n) * 2 + core, x)
    prv = (chip_at((pos + n - 1) % n, n) * 2 + core, x)
    sib = (chip * 2 + other, x)
    over = (dp, 1 - x)
    greet([nxt, prv, sib, over])
    copies = Copies(local_sem, send_sem, recv_sem)
    send, stay = copies.send, copies.stay

    def by_heads(chip_id, which):
        return heads_first(chip_id, which, n)

    rhalf = wx.shape[1] // 2
    fhalf = wg.shape[1] // 2
    rec_parts = [
        (wx, o_xy.at[chip, core, x, :, pl.ds(0, rhalf)]),
        (wy, o_xy.at[chip, core, x, :, pl.ds(rhalf, rhalf)]),
    ]
    ff_parts = [
        (wg, o_gu.at[chip, core, :, pl.ds(0, fhalf)]),
        (wu, o_gu.at[chip, core, :, pl.ds(fhalf, fhalf)]),
        (wd, o_d.at[core]),
    ]
    pair = [send(half_cols(src, other), slot, sib) for src, slot in rec_parts]
    pair.append(send(half_cols(wo, other), o_out.at[by_heads(chip, other), core, x], sib))
    mine = [stay(half_cols(src, core), slot) for src, slot in rec_parts] + [stay(gs, o_gs.at[core, chip, x])]
    mine.append(stay(half_cols(wo, core), o_out.at[by_heads(chip, core), core, x]))
    late = [send(half_cols(src, other), slot, sib) for src, slot in ff_parts]
    plain = [stay(half_cols(src, core), slot) for src, slot in ff_parts]
    late += [send(rows_in, o_rows.at[1], sib), send(starts, o_starts.at[1], sib), send(cot, o_cot.at[2], sib)]
    plain += [stay(rows_in, o_rows.at[0]), stay(starts, o_starts.at[0]), stay(cot, o_cot.at[0])]

    def rec_block(chip_id):
        return [o_xy.at[chip_id, :, x], o_out.at[by_heads(chip_id, core), :, x], o_gs.at[core, chip_id, x]]

    def rec_piece(chip_id, which):
        refs = [o_xy.at[chip_id, which, x], o_out.at[by_heads(chip_id, core), which, x]]
        return refs + ([o_gs.at[core, chip_id, x]] if which == 0 else [])

    def ff_block(chip_id):
        return [o_gu.at[chip_id]]

    def ff_piece(chip_id, which):
        return [o_gu.at[chip_id, which]]

    def send_all(refs, device):
        return [send(ref, ref, device) for ref in refs]

    def hop(s, block, piece):
        ahead = chip_at((pos + n - (s - 1)) % n, n)
        behind = chip_at((pos + s - 1) % n, n)
        if s < half:
            return send_all(block(ahead), nxt) + send_all(block(behind), prv)
        return send_all(piece(ahead, 0), nxt) + send_all(piece(behind, 1), prv)

    for copy in pair:
        copy.wait_recv()
    for copy in mine:
        copy.wait()
    done, crossed, moving = [], send_all(rec_block(chip), over), []
    for s in range(1, half + 1):
        for copy in moving:
            copy.wait_recv()
        done.extend(moving)
        moving = hop(s, rec_block, rec_piece)
        if s > 1:
            crossed.extend(send_all(rec_block(chip_at((pos + n - (s - 1)) % n, n)), over))
            crossed.extend(send_all(rec_block(chip_at((pos + s - 1) % n, n)), over))
    last_rec = moving
    for copy in late:
        copy.wait_recv()
    for copy in plain:
        copy.wait()
    moving = hop(1, ff_block, ff_piece)
    for copy in last_rec:
        copy.wait_recv()
    done.extend(last_rec)
    crossed.extend(send_all(rec_block(chip_at((pos + half) % n, n)), over))
    cot_over = send(cot, o_cot.at[1], over)
    for s in range(2, half + 1):
        for copy in moving:
            copy.wait_recv()
        done.extend(moving)
        moving = hop(s, ff_block, ff_piece)
    for copy in crossed:
        copy.wait_recv()
    swap = send(o_gs.at[core], o_gs.at[core], sib)
    cot_over.wait_recv()
    last = send(o_cot.at[1], o_cot.at[3], sib)
    for copy in moving:
        copy.wait_recv()
    done.extend(moving)
    swap.wait_recv()
    last.wait_recv()
    for copy in pair + late + done + crossed + [cot_over, swap, last]:
        copy.wait_send()


def gather_weights(n, wx, wy, wo, gs, wg, wu, wd, rows_in, cot, starts):
    r, d, (rows_f, f) = wx.shape[1], wo.shape[1], wg.shape
    tokens = rows_in.shape[0]
    shapes = [
        jax.ShapeDtypeStruct((n, 2, 2, wx.shape[0], r), BF16),
        jax.ShapeDtypeStruct((n, 2, 2, wo.shape[0], d // 2), BF16),
        jax.ShapeDtypeStruct((2, n, 2) + gs.shape, BF16),
        jax.ShapeDtypeStruct((n, 2, rows_f, f), BF16),
        jax.ShapeDtypeStruct((2, rows_f, f // 2), BF16),
        jax.ShapeDtypeStruct((2, tokens, d), BF16),
        jax.ShapeDtypeStruct((4, tokens, d), BF16),
        jax.ShapeDtypeStruct((2,) + starts.shape, F32),
    ]
    count = 9 + (3 * n - 1) + n + 3 * n + 3
    dma = pltpu.SemaphoreType.DMA
    return pl.pallas_call(
        functools.partial(gather_kernel, n),
        out_shape=shapes,
        in_specs=[pl.BlockSpec(memory_space=pltpu.VMEM)] * 10,
        out_specs=[pl.BlockSpec(memory_space=pl.ANY)] * 8,
        scratch_shapes=[dma((10,)), dma((count,)), dma((count,))],
        compiler_params=pltpu.CompilerParams(
            collective_id=0, has_side_effects=True, vmem_limit_bytes=24 << 20
        ),
        name="gather_weights",
    )(wx, wy, wo, gs, wg, wu, wd, rows_in, cot, starts)


def scatter_kernel(
    n,
    c_x, c_y, c_out, c_g, c_v,
    g_x, g_y, g_out, g_gates, g_vec,
    r_x, r_y, r_out, r_g, r_v, s_x, s_y, s_out,
    send_sem, recv_sem,
):
    dp, x = lax.axis_index("dp"), lax.axis_index("tp")
    chip, core = dp // 2, dp % 2
    pos = place_of(chip, n)
    half = n // 2
    nxt = (chip_at((pos + 1) % n, n) * 2 + core, x)
    prv = (chip_at((pos + n - 1) % n, n) * 2 + core, x)
    sib = (dp + 1 - 2 * core, x)
    greet([nxt, prv, sib])
    copies = Copies(None, send_sem, recv_sem)

    pieces = []
    for part in (0, 1):
        for terms, slots, first in ((c_out, r_out, core), (c_y, r_y, 0), (c_x, r_x, 0)):
            pieces.append((
                lambda c, terms=terms, part=part, first=first: terms.at[heads_first(c, first, n), part],
                lambda w, k, slots=slots, part=part: slots.at[part, w, k],
                part,
            ))
    pieces.append((lambda c: c_g.at[c], lambda w, k: r_g.at[w, k], 0))
    pieces.append((lambda c: c_v.at[c], lambda w, k: r_v.at[w, k], 1))

    def add(a, b):
        return a[...].astype(F32) + b[...].astype(F32)

    sent, coming = [], {}
    for k in range(half, -1, -1):
        for i, (term, slot, far) in enumerate(pieces):
            for way, (device, sign) in enumerate(((nxt, 1), (prv, n - 1))):
                first = half if way == far else half - 1
                if k > first or k == 0:
                    continue
                source = term(chip_at((pos + sign * k) % n, n))
                if k < first:
                    coming[i, way].wait_recv()
                    got = slot(way, k)
                    got[...] = add(got, source).astype(got.dtype)
                    source = got
                copy = copies.send(source, slot(way, k - 1), device)
                coming[i, way] = copy
                sent.append(copy)

    def total(i):
        term, slot, _ = pieces[i]
        for way in (0, 1):
            coming[i, way].wait_recv()
        return add(term(chip), slot(0, 0)) + slot(1, 0)[...].astype(F32)

    def cols(ref):
        width = ref.shape[1] // 2
        return pl.ds(pl.multiple_of(core * width, 128), width)

    final = []
    for i, (ref, handed) in enumerate(((g_out, s_out), (g_y, s_y), (g_x, s_x))):
        sums = [total(3 * part + i) for part in (0, 1)]
        for part in (0, 1):

            @pl.when(core == part)
            def _():
                ref[:, cols(ref)] = sums[part]
                handed[...] = sums[1 - part]

        final.append(copies.send(handed, ref.at[:, cols(ref)], sib))
    g_gates[...] = total(6)
    g_vec[...] = total(7)
    for copy in final:
        copy.wait_recv()
    for copy in sent + final:
        copy.wait_send()


def scatter_sums(n, c_x, c_y, c_out, c_g, c_v):
    _, _, rows_d, rhalf = c_x.shape
    _, _, rows_r, dhalf = c_out.shape
    half = n // 2
    count = 8 * (2 * half - 1) + 3
    dma = pltpu.SemaphoreType.DMA
    vmem = pl.BlockSpec(memory_space=pltpu.VMEM)
    return pl.pallas_call(
        functools.partial(scatter_kernel, n),
        out_shape=[
            jax.ShapeDtypeStruct((rows_d, 2 * rhalf), F32),
            jax.ShapeDtypeStruct((rows_d, 2 * rhalf), F32),
            jax.ShapeDtypeStruct((rows_r, 2 * dhalf), F32),
            jax.ShapeDtypeStruct(c_g.shape[1:], F32),
            jax.ShapeDtypeStruct(c_v.shape[1:], F32),
        ],
        in_specs=[vmem] * 5,
        out_specs=[vmem] * 5,
        scratch_shapes=[
            pltpu.VMEM((2, 2, half, rows_d, rhalf), BF16),
            pltpu.VMEM((2, 2, half, rows_d, rhalf), BF16),
            pltpu.VMEM((2, 2, half, rows_r, dhalf), BF16),
            pltpu.VMEM((2, half) + c_g.shape[1:], BF16),
            pltpu.VMEM((2, half) + c_v.shape[1:], F32),
            pltpu.VMEM((rows_d, rhalf), F32),
            pltpu.VMEM((rows_d, rhalf), F32),
            pltpu.VMEM((rows_r, dhalf), F32),
            dma((count,)), dma((count,)),
        ],
        compiler_params=pltpu.CompilerParams(
            collective_id=1, has_side_effects=True, vmem_limit_bytes=56 << 20
        ),
        name="scatter_sums",
    )(c_x, c_y, c_out, c_g, c_v)


def project_kernel(steps, rows, gain, w, n1_ref, x_ref, y_ref):
    i = pl.program_id(0)

    @pl.when(i == 0)
    def _():
        values = rows[...].astype(F32)
        scale = lax.rsqrt(jnp.mean(values * values, axis=-1, keepdims=True) + EPS)
        n1_ref[...] = (values * scale * gain[...]).astype(BF16).reshape(n1_ref.shape)

    result = jnp.dot(n1_ref[...], w[...], preferred_element_type=F32).reshape(y_ref.shape)

    @pl.when(i < steps)
    def _():
        x_ref[...] = result.astype(BF16)

    @pl.when(i >= steps)
    def _():
        y_ref[...] = result


def project(rows, gain, w):
    _, tokens, width = rows.shape
    rh = w.shape[1] // 2
    steps = rh // BLK
    return pl.pallas_call(
        functools.partial(project_kernel, steps),
        grid=(2 * steps,),
        in_specs=[
            pl.BlockSpec(rows.shape, lambda i: (0, 0, 0)),
            pl.BlockSpec((1, width), lambda i: (0, 0)),
            pl.BlockSpec((width, BLK), lambda i: (0, i)),
        ],
        out_specs=[
            pl.BlockSpec((2 * tokens, width), lambda i: (0, 0)),
            pl.BlockSpec((2, tokens, BLK), lambda i: (0, 0, jnp.minimum(i, steps - 1))),
            pl.BlockSpec((2, tokens, BLK), lambda i: (0, 0, jnp.maximum(i - steps, 0))),
        ],
        out_shape=[
            jax.ShapeDtypeStruct((2 * tokens, width), BF16),
            jax.ShapeDtypeStruct((2, tokens, rh), BF16),
            jax.ShapeDtypeStruct((2, tokens, rh), F32),
        ],
        compiler_params=pltpu.CompilerParams(vmem_limit_bytes=40 << 20),
        cost_estimate=pl.CostEstimate(flops=27 * 10**8, bytes_accessed=15 * 10**6, transcendentals=0),
        name="project",
    )(rows, gain, w)


def project_out_kernel(o, o_sib, w, mine_ref, theirs_ref):
    rh = o.shape[2]
    for row, ref in ((0, mine_ref), (1, theirs_ref)):
        ref[...] = jnp.dot(o[row], w[:rh], preferred_element_type=F32) + jnp.dot(
            o_sib[1 - row], w[rh:], preferred_element_type=F32
        )


def project_out(o, o_sib, w):
    _, tokens, rh = o.shape
    cols = w.shape[1]
    tile = min(BLK, cols)
    whole = pl.BlockSpec(o.shape, lambda i: (0, 0, 0))
    part = pl.BlockSpec((tokens, tile), lambda i: (0, i))
    return pl.pallas_call(
        project_out_kernel,
        grid=(cols // tile,),
        in_specs=[whole, whole, pl.BlockSpec((2 * rh, tile), lambda i: (0, i))],
        out_specs=[part, part],
        out_shape=[jax.ShapeDtypeStruct((tokens, cols), F32)] * 2,
        compiler_params=pltpu.CompilerParams(vmem_limit_bytes=40 << 20),
        cost_estimate=pl.CostEstimate(flops=14 * 10**8, bytes_accessed=8 * 10**6, transcendentals=0),
        name="project_out",
    )(o, o_sib, w)


def minus_expm1(v):
    series = jnp.ones_like(v)
    for k in range(9, 1, -1):
        series = 1.0 + series * v * (1.0 / k)
    return jnp.where(v > -0.5, -v * series, 1.0 - jnp.exp(v))


def gates_of(u, weights, cp, start):
    tokens = u.shape[0] * u.shape[1]
    flat = u.reshape(tokens, BLK)
    z = jnp.dot(flat, weights, preferred_element_type=F32)
    r = jax.nn.sigmoid(z[:, :BLK] + cp[5:6]).reshape(u.shape)
    ig = jax.nn.sigmoid(z[:, BLK:] + cp[6:7]).reshape(u.shape)
    la = -8.0 * r * cp[7:8][None]
    decayed = jnp.exp(la)
    rest = minus_expm1(2.0 * la)
    return r, ig, decayed, rest


def recurrence_kernel(xb, halo, weights, cp, starts, u_ref, a_ref, h_ref, c_ref, b_ref):
    rows, length = xb.shape[0], xb.shape[1]
    p = cp[...]
    us = []
    for row in range(rows):
        padded = jnp.concatenate([halo[row], xb[row].astype(F32)], axis=0)
        total = p[4:5] + p[0:1] * padded[8 : 8 + length]
        for k in range(1, 4):
            total = total + p[k : k + 1] * padded[8 - k : 8 - k + length]
        us.append(total.astype(BF16))
    u = jnp.stack(us)
    u_ref[...] = u
    start = starts[...]
    start = jnp.concatenate([start, start], axis=2)
    r, ig, decayed, rest = gates_of(u, weights[...], p, start)
    a_ref[...] = decayed * (1.0 - start)
    b_ref[...] = jnp.where(start > 0.5, 1.0, jnp.sqrt(rest)) * ig * u.astype(F32)

    def eight(i, carry):
        at = pl.ds(pl.multiple_of(i * 8, 8), 8)
        out = []
        for row in range(rows):
            h, c = carry[row]
            a, b = a_ref[row, at, :], b_ref[row, at, :]
            hs, cs = [], []
            for j in range(8):
                h = a[j : j + 1] * h + b[j : j + 1]
                c = a[j : j + 1] * c
                hs.append(h)
                cs.append(c)
            h_ref[row, at, :] = jnp.concatenate(hs, axis=0)
            c_ref[row, at, :] = jnp.concatenate(cs, axis=0)
            out.append((h, c))
        return tuple(out)

    zero, one = jnp.zeros((1, BLK), F32), jnp.ones((1, BLK), F32)
    lax.fori_loop(0, length // 8, eight, ((zero, one),) * rows)


def recurrence(xb, halo, weights, cp, starts):
    rows, length, channels = xb.shape
    wide = pl.BlockSpec((rows, length, BLK), lambda h: (0, 0, h))
    return pl.pallas_call(
        recurrence_kernel,
        grid=(channels // BLK,),
        in_specs=[
            wide,
            pl.BlockSpec((rows, 8, BLK), lambda h: (0, 0, h)),
            pl.BlockSpec((BLK, 2 * BLK), lambda h: (h, 0)),
            pl.BlockSpec((cp.shape[0], BLK), lambda h: (0, h)),
            pl.BlockSpec(starts.shape, lambda h: (0, 0, 0)),
        ],
        out_specs=[wide] * 4,
        out_shape=[jax.ShapeDtypeStruct(xb.shape, BF16)] + [jax.ShapeDtypeStruct(xb.shape, F32)] * 3,
        scratch_shapes=[pltpu.VMEM((rows, length, BLK), F32)],
        compiler_params=pltpu.CompilerParams(vmem_limit_bytes=40 << 20),
        cost_estimate=pl.CostEstimate(flops=4 * 10**8, bytes_accessed=6 * 10**6, transcendentals=2 * 10**6),
        name="recurrence",
    )(xb, halo, weights, cp, starts)


def gelu_parts(v):
    inner = 0.7978845608028654 * (v + 0.044715 * v * v * v)
    t = jnp.tanh(inner)
    value = 0.5 * v * (1.0 + t)
    slope = 0.5 * (1.0 + t) + 0.5 * v * (1.0 - t * t) * 0.7978845608028654 * (1.0 + 3.0 * 0.044715 * v * v)
    return value, slope


def adjoint_kernel(do, h_ref, y_ref, a_ref, dy_ref, lam_ref, c_ref, dh_ref):
    rows, length = do.shape[0], do.shape[1]
    value, slope = gelu_parts(y_ref[...])
    dy_ref[...] = (do[...] * h_ref[...] * slope).astype(BF16)
    dh_ref[...] = do[...] * value

    def eight(step, carry):
        i = length // 8 - 1 - step
        at = pl.ds(pl.multiple_of(i * 8, 8), 8)
        out = []
        for row in range(rows):
            ahead, c = carry[row]
            a, d = a_ref[row, at, :], dh_ref[row, at, :]
            ls, cs = [None] * 8, [None] * 8
            for j in range(7, -1, -1):
                lam = d[j : j + 1] + ahead
                ls[j], cs[j] = lam, c
                ahead = a[j : j + 1] * lam
                c = a[j : j + 1] * c
            lam_ref[row, at, :] = jnp.concatenate(ls, axis=0)
            c_ref[row, at, :] = jnp.concatenate(cs, axis=0)
            out.append((ahead, c))
        return tuple(out)

    zero, one = jnp.zeros((1, BLK), F32), jnp.ones((1, BLK), F32)
    lax.fori_loop(0, length // 8, eight, ((zero, one),) * rows)


def adjoint(do, h, ypre, a):
    rows, length, channels = do.shape
    wide = pl.BlockSpec((rows, length, BLK), lambda i: (0, 0, i))
    return pl.pallas_call(
        adjoint_kernel,
        grid=(channels // BLK,),
        in_specs=[wide] * 4,
        out_specs=[wide] * 3,
        out_shape=[jax.ShapeDtypeStruct(do.shape, BF16)] + [jax.ShapeDtypeStruct(do.shape, F32)] * 2,
        scratch_shapes=[pltpu.VMEM((rows, length, BLK), F32)],
        compiler_params=pltpu.CompilerParams(vmem_limit_bytes=40 << 20),
        cost_estimate=pl.CostEstimate(flops=10**7, bytes_accessed=9 * 10**6, transcendentals=10**6),
        name="adjoint",
    )(do, h, ypre, a)


def gates_back_kernel(lam_ref, c_ref, inc, h_ref, h_in, u_ref, weights, cp, starts, du_ref, dw_ref, sums_ref):
    rows, length = u_ref.shape[0], u_ref.shape[1]
    tokens = rows * length
    p = cp[...]
    u = u_ref[...]
    uf = u.astype(F32)
    start = starts[...]
    start = jnp.concatenate([start, start], axis=2)
    w = weights[...]
    r, ig, decayed, rest = gates_of(u, w, p, start)
    mult = jnp.where(start > 0.5, 1.0, jnp.sqrt(rest))
    lam = lam_ref[...] + c_ref[...] * inc[...]
    before = jnp.stack([jnp.concatenate([h_in[row], h_ref[row][: length - 1]], axis=0) for row in range(rows)])
    keep = 1.0 - start
    d_la = lam * before * decayed * keep - jnp.where(
        start > 0.5, 0.0, lam * ig * uf * decayed * decayed * lax.rsqrt(jnp.where(start > 0.5, 1.0, rest))
    )
    dpa = d_la * (-8.0 * p[7:8][None]) * r * (1.0 - r)
    direct = lam * mult
    dpi = direct * uf * ig * (1.0 - ig)
    d_decay = d_la * (8.0 * p[8:9][None]) * r
    dz = jnp.concatenate(
        [dpa.reshape(tokens, BLK).astype(BF16), dpi.reshape(tokens, BLK).astype(BF16)], axis=1
    )
    back = lax.dot_general(dz, w, (((1,), (1,)), ((), ())), preferred_element_type=F32)
    du_ref[...] = (direct * ig + back.reshape(u.shape)).astype(BF16)
    dw_ref[...] = lax.dot_general(
        u.reshape(tokens, BLK), dz, (((0,), (0,)), ((), ())), preferred_element_type=F32
    )
    zero = jnp.zeros((5, BLK), F32)
    sums_ref[...] = jnp.concatenate(
        [jnp.sum(v.reshape(tokens, BLK), axis=0, keepdims=True) for v in (dpa, dpi, d_decay)] + [zero], axis=0
    )


def gates_back(lam, coef, inc, h, h_in, u, weights, cp, starts):
    rows, length, channels = u.shape
    wide = pl.BlockSpec((rows, length, BLK), lambda i: (0, 0, i))
    line = pl.BlockSpec((rows, 1, BLK), lambda i: (0, 0, i))
    square = pl.BlockSpec((BLK, 2 * BLK), lambda i: (i, 0))
    return pl.pallas_call(
        gates_back_kernel,
        grid=(channels // BLK,),
        in_specs=[
            wide, wide, line, wide, line, wide, square,
            pl.BlockSpec((cp.shape[0], BLK), lambda i: (0, i)),
            pl.BlockSpec(starts.shape, lambda i: (0, 0, 0)),
        ],
        out_specs=[wide, square, pl.BlockSpec((8, BLK), lambda i: (0, i))],
        out_shape=[
            jax.ShapeDtypeStruct(u.shape, BF16),
            jax.ShapeDtypeStruct((channels, 2 * BLK), F32),
            jax.ShapeDtypeStruct((8, channels), F32),
        ],
        compiler_params=pltpu.CompilerParams(vmem_limit_bytes=40 << 20),
        cost_estimate=pl.CostEstimate(flops=12 * 10**8, bytes_accessed=9 * 10**6, transcendentals=2 * 10**6),
        name="gates_back",
    )(lam, coef, inc, h, h_in, u, weights, cp, starts)


def log1p_small(e):
    series = jnp.ones_like(e) * (1.0 / 14)
    for k in range(13, 0, -1):
        series = 1.0 / k - e * series
    return jnp.where(e < 0.25, e * series, jnp.log(1.0 + e))


def front_kernel(n, *refs):
    (
        wx, wy, wo, gs, wg, wu, wd, rows_in, grad, lengths, resets, spread_r, pick_r, spread_d, pick_d,
        o_xy, o_out, o_gates, o_cp, o_gains, o_gu, o_d, o_cot, o_starts, o_ypre, o_u, o_a, o_h, o_hin, o_xb, o_before,
        o_x1, o_n2, o_n1t, o_ot, o_hidden, o_gate, o_up, o_pd,
        v_xy, v_out, v_gs, v_gates, v_rows, v_cot, v_starts, v_cp, v_gains, v_n1, v_n1t, v_xb, v_ypre, v_halo, v_u, v_a,
        v_b, v_h, v_c, v_carry, v_o, v_osib, v_ot, v_part, v_theirs, v_psib, v_x1, v_n2, v_w, v_hidden, v_gu, v_pd, v_wd,
        local_sem, send_sem, recv_sem, load_sem, store_sem, pd_sem,
    ) = refs
    dp, x = lax.axis_index("dp"), lax.axis_index("tp")
    chip, core = dp // 2, dp % 2
    other = 1 - core
    pos = place_of(chip, n)
    half = n // 2
    nxt = (chip_at((pos + 1) % n, n) * 2 + core, x)
    prv = (chip_at((pos + n - 1) % n, n) * 2 + core, x)
    sib = (chip * 2 + other, x)
    over = (dp, 1 - x)
    copies = Copies(local_sem, send_sem, recv_sem)
    send, stay = copies.send, copies.stay
    tokens, width = rows_in.shape
    rec = wx.shape[1]
    rh = rec // 2
    own, own_d = wo.shape[0], wx.shape[0]
    fh = wg.shape[1] // 2
    own_f = wg.shape[0]
    kept, every = [], []

    def put(src, dst):
        kept.append(stay(src, dst))

    def give(src, dst, device):
        copy = send(src, dst, device)
        every.append(copy)
        return copy

    def land(group):
        for copy in group:
            copy.wait_recv()

    class Chain:
        def __init__(self, pieces, arrived=None):
            self.pieces, self.arrived, self.hop = pieces, arrived, 0
            self.ways = ((nxt, n - 1), (prv, 1))
            self.moving = ([], [])

        def start(self, part):
            self.hop = 1
            for ref, own_core in self.pieces(pos):
                if own_core == part:
                    for way, (device, _) in enumerate(self.ways):
                        self.moving[way].append(give(ref, ref, device))
                    if self.arrived:
                        self.arrived(ref)

        def advance(self):
            self.hop += 1
            fresh = ([], [])
            blocks = [self.pieces((pos + back * (self.hop - 1)) % n) for _, back in self.ways]
            for i in range(len(blocks[0])):
                for way, (device, _) in enumerate(self.ways):
                    ref, own_core = blocks[way][i]
                    self.moving[way][i].wait_recv()
                    if self.hop < half or own_core == (way == 0):
                        fresh[way].append(give(ref, ref, device))
                    if self.arrived:
                        self.arrived(ref)
            self.moving = fresh

        def to_last(self):
            while self.hop < half:
                self.advance()

        def finish(self):
            block = self.pieces((pos + half) % n)
            for way in (0, 1):
                refs = [ref for ref, own_core in block if own_core == (way == 0)]
                for copy, ref in zip(self.moving[way], refs):
                    copy.wait_recv()
                    if self.arrived:
                        self.arrived(ref)

    parts = [(wx, v_xy.at[chip, core, x, :, pl.ds(0, rh)]), (wy, v_xy.at[chip, core, x, :, pl.ds(rh, rh)])]
    mine = [stay(half_cols(src, core), slot) for src, slot in parts]
    mine.append(stay(half_cols(wo, core), v_out.at[heads_first(chip, core, n), core, x]))
    mine.append(stay(gs, v_gs.at[core, chip, x]))
    greet([nxt, prv, sib, over])
    pair = [give(half_cols(src, other), slot, sib) for src, slot in parts]
    pair.append(give(half_cols(wo, other), v_out.at[heads_first(chip, other, n), core, x], sib))

    crossed, held = [], []

    def rec_pieces(place):
        c = chip_at(place, n)
        at = heads_first(c, core, n)
        rows = (own + PAD) // 2
        return [
            (v_xy.at[c, core, x], True), (v_gs.at[core, c, x, pl.ds(0, rows)], True), (v_out.at[at, core, x], True),
            (v_xy.at[c, other, x], False), (v_gs.at[core, c, x, pl.ds(rows, rows)], False),
            (v_out.at[at, other, x], False),
        ]

    def rec_arrived(ref):
        if ref.shape[1] == width // 2:
            held.append(ref)
        else:
            crossed.append(give(ref, ref, over))

    rec_chain = Chain(rec_pieces, rec_arrived)
    gu = Chain(lambda place: [
        (o_gu.at[chip_at(place, n), core], True), (o_gu.at[chip_at(place, n), other], False)
    ])
    down = Chain(lambda place: [(o_d.at[place, core], True), (o_d.at[place, other], False)])
    for copy in mine:
        copy.wait()
    rec_chain.start(True)
    land(pair)
    rec_chain.start(False)
    parts = [(wg, o_gu.at[chip, core, :, pl.ds(0, fh)]), (wu, o_gu.at[chip, core, :, pl.ds(fh, fh)])]
    late = [give(half_cols(src, other), slot, sib) for src, slot in parts]
    plain = [stay(half_cols(src, core), slot) for src, slot in parts]
    late += [give(wd.at[pl.ds(pl.multiple_of(other * fh, 128), fh)], v_wd.at[1], sib), give(rows_in, v_rows.at[1], sib)]
    plain += [stay(wd.at[pl.ds(pl.multiple_of(core * fh, 128), fh)], v_wd.at[0]), stay(rows_in, v_rows.at[0])]
    cotangent = stay(grad, v_n2.at[0])

    lane = lax.broadcasted_iota(jnp.int32, (1, tokens), 1) + x * tokens
    begins = jnp.where((resets[...] > 0) | (lane == 0), 1.0, 0.0)
    v_starts[0] = jnp.broadcast_to(begins, (tokens, tokens)).T
    late.append(give(v_starts.at[0], v_starts.at[1], sib))
    valid = lax.broadcasted_iota(jnp.int32, (tokens, 1), 0) + x * tokens < lengths[0]
    valid = jnp.where(valid, 1.0, 0.0)
    cotangent.wait()
    size = width // n
    for i in range(n):
        from_chip = chip_at(i, n) * size
        v_cot[0, :, i * size : (i + 1) * size] = (v_n2[0, :, from_chip : from_chip + size].astype(F32) * valid).astype(BF16)
    late.append(give(v_cot.at[0], v_cot.at[2], sib))
    rec_chain.to_last()
    land(late)
    for copy in plain:
        copy.wait()
    gu.start(True)
    gu.start(False)
    rec_chain.finish()
    for i in range(fh // 128):
        at = pl.ds(i * 128, 128)
        for which in (0, 1):
            v_pd[which, 0:own_f, at] = v_wd[which, at, :].astype(F32).T.astype(BF16)
    turned = [stay(v_pd.at[which, pl.ds(0, own_f)], o_d.at[pos, place]) for which, place in ((0, core), (1, other))]
    swap = [give(v_gs.at[core, :, x], v_gs.at[core, :, x], sib)]
    put(v_starts, o_starts)
    if half > 3:
        gu.advance()
    land(crossed)
    swap.append(give(v_gs.at[core, :, 1 - x], v_gs.at[core, :, 1 - x], sib))
    outs = []

    def cross_held(count):
        for _ in range(min(count, len(held))):
            ref = held.pop(0)
            outs.append(give(ref, ref, over))

    cross_held(4)
    put(v_xy, o_xy)
    land(swap)

    small = v_gs[:, :, :, own : own + PAD, :128].reshape(4 * n * PAD, 128)
    spread = jnp.dot(small, spread_r[...], preferred_element_type=F32).reshape(4 * n, PAD, rh)
    heads = pick_r[:, pl.ds(pl.multiple_of(core * rh, 128), rh)]
    lines = jnp.sum(spread[:, :8] * heads[:, None, :], axis=0)
    decay = lines[7:8]
    e = jnp.exp(-jnp.abs(decay))
    v_cp[0:8, :] = lines
    v_cp[7:8, :] = jnp.maximum(-decay, 0.0) + log1p_small(e)
    v_cp[8:16, :] = jnp.broadcast_to(jax.nn.sigmoid(-decay), (8, rh))
    for i in range(width // WIDE):
        at = pl.ds(i * WIDE, WIDE)
        wide = jnp.dot(small, spread_d[:, at], preferred_element_type=F32).reshape(4 * n, PAD, WIDE)
        v_gains[:, at] = jnp.sum(wide[:, 8:] * pick_d[:, at][:, None, :], axis=0)
    for i in range(2 * n):
        v_gates[i * own : (i + 1) * own, :] = v_gs[(i // 2) % 2, core * half + i // 4, i % 2, 0:own, :]
    put(v_cp, o_cp)
    put(v_gains, o_gains)
    put(v_gates, o_gates)

    values = v_rows[...].astype(F32)
    scale = lax.rsqrt(jnp.mean(values * values, axis=-1, keepdims=True) + EPS)
    v_n1[...] = (values * scale * v_gains[0:1, :]).astype(BF16).reshape(2 * tokens, width)

    def project_x(i, _):
        at = pl.ds(pl.multiple_of(i * BLK, BLK), BLK)
        w = v_xy[:, :, :, :, at].reshape(width, BLK)
        v_xb[:, :, at] = jnp.dot(v_n1[...], w, preferred_element_type=F32).astype(BF16).reshape(2, tokens, BLK)
        return 0

    def project_y(i, _):
        at = pl.ds(pl.multiple_of(i * BLK, BLK), BLK)
        w = v_xy[:, :, :, :, pl.ds(pl.multiple_of(rh + i * BLK, BLK), BLK)].reshape(width, BLK)
        v_ypre[:, :, at] = jnp.dot(v_n1[...], w, preferred_element_type=F32).reshape(2, tokens, BLK)
        return 0

    lax.fori_loop(0, rh // BLK, project_x, 0)
    halo = give(v_xb.at[:, pl.ds(tokens - 16, 16)], v_halo, over)
    cross_held(4)
    put(v_xb, o_xb)
    if half > 3:
        gu.advance()
    lax.fori_loop(0, rh // BLK, project_y, 0)
    put(v_ypre, o_ypre)
    chips_n = BLK // (4 * own_d)

    def turn_n1(i, _):
        at = pl.ds(pl.multiple_of(i * BLK, BLK), BLK)
        turned = v_n1[:, at].astype(F32).T.astype(BF16)
        v_n1t[pl.ds(i * chips_n, chips_n)] = turned.reshape(chips_n, 2, 2, own_d, 2 * tokens)
        return 0

    lax.fori_loop(0, width // BLK, turn_n1, 0)
    halo.wait_recv()
    v_halo[...] = jnp.where(x == 0, jnp.zeros_like(v_halo), v_halo[...])
    put(v_halo, o_before)
    put(v_n1t.at[:, :, x], o_n1t.at[:, :, :, pl.ds(0, 2 * tokens)])

    def head(i, _):
        at = pl.ds(pl.multiple_of(i * BLK, BLK), BLK)
        p = v_cp[:, at]
        us = []
        for row in range(2):
            padded = jnp.concatenate([v_halo[row, :, at].astype(F32)[8:], v_xb[row, :, at].astype(F32)], axis=0)
            total = p[4:5] + p[0:1] * padded[8 : 8 + tokens]
            for k in range(1, 4):
                total = total + p[k : k + 1] * padded[8 - k : 8 - k + tokens]
            us.append(total.astype(BF16))
        u = jnp.stack(us)
        v_u[:, :, at] = u
        start = v_starts[...]
        start = jnp.concatenate([start, start], axis=2)
        _, ig, decayed, rest = gates_of(u, v_gates[at, :], p, start)
        v_a[:, :, at] = decayed * (1.0 - start)
        v_b[...] = jnp.where(start > 0.5, 1.0, jnp.sqrt(rest)) * ig * u.astype(F32)

        def eight(j, carry):
            rows8 = pl.ds(pl.multiple_of(j * 8, 8), 8)
            out = []
            for row in range(2):
                h, c = carry[row]
                a, b = v_a[row, rows8, at], v_b[row, rows8, :]
                hs, cs = [], []
                for k in range(8):
                    h = a[k : k + 1] * h + b[k : k + 1]
                    c = a[k : k + 1] * c
                    hs.append(h)
                    cs.append(c)
                v_h[row, rows8, at] = jnp.concatenate(hs, axis=0)
                v_c[row, rows8, at] = jnp.concatenate(cs, axis=0)
                out.append((h, c))
            return tuple(out)

        zero, one = jnp.zeros((1, BLK), F32), jnp.ones((1, BLK), F32)
        lax.fori_loop(0, tokens // 8, eight, ((zero, one),) * 2)
        return 0

    lax.fori_loop(0, rh // BLK, head, 0)
    carry = give(v_h.at[:, pl.ds(tokens - 8, 8)], v_carry, over)
    put(v_u, o_u)
    put(v_a, o_a)
    carry.wait_recv()
    carry.wait_send()
    cross_held(len(held))
    v_carry[...] = jnp.where(x == 0, jnp.zeros_like(v_carry), v_carry[...])
    put(v_carry, o_hin)

    def output(i, _):
        at = pl.ds(pl.multiple_of(i * BLK, BLK), BLK)
        h = v_h[:, :, at] + v_c[:, :, at] * v_carry[:, 7:8, at]
        v_h[:, :, at] = h
        value, _ = gelu_parts(v_ypre[:, :, at])
        v_o[:, :, at] = (h * value).astype(BF16)
        return 0

    lax.fori_loop(0, rh // BLK, output, 0)
    o_pair = give(v_o, v_osib, sib)
    put(v_h, o_h)
    gu.to_last()
    for copy in turned:
        copy.wait()
    down.start(True)
    down.start(False)
    o_pair.wait_recv()
    land(outs)
    put(v_out, o_out)

    def project_row(row, ref):
        def tile(i, _):
            at = pl.ds(pl.multiple_of(i * BLK, BLK), BLK)
            w0 = v_out[0:half, :, :, :, at].reshape(rh, BLK)
            w1 = v_out[half:n, :, :, :, at].reshape(rh, BLK)
            ref[:, at] = jnp.dot(v_o[row], w0, preferred_element_type=F32) + jnp.dot(
                v_osib[1 - row], w1, preferred_element_type=F32
            )
            return 0

        lax.fori_loop(0, width // 2 // BLK, tile, 0)

    project_row(1, v_theirs)
    x1_pair = give(v_theirs, v_psib, sib)
    project_row(0, v_part)
    x1_pair.wait_recv()
    at_mine = pl.ds(pl.multiple_of(core * (width // 2), 128), width // 2)
    at_theirs = pl.ds(pl.multiple_of(other * (width // 2), 128), width // 2)
    v_x1[:, at_mine] = v_rows[0, :, at_mine].astype(F32) + v_part[...]
    v_x1[:, at_theirs] = v_rows[0, :, at_theirs].astype(F32) + v_psib[...]
    put(v_x1, o_x1)
    x1 = v_x1[...]
    scale = lax.rsqrt(jnp.mean(x1 * x1, axis=-1, keepdims=True) + EPS)
    v_n2[0] = (x1 * scale * v_gains[1:2, :]).astype(BF16)
    n2_over = give(v_n2.at[0], v_n2.at[1], over)
    n2_pair = give(v_n2.at[0], v_n2.at[2], sib)
    cot_over = give(v_cot.at[0], v_cot.at[1], over)
    n1_over = give(v_n1t.at[:, :, 1 - x], o_n1t.at[:, :, :, pl.ds(2 * tokens, 2 * tokens)], over)

    chips_o = 640 // (4 * own)

    def turn_o(i, _):
        at = pl.ds(pl.multiple_of(i * 640, 128), 640)
        here = v_o[:, :, at].astype(F32).reshape(2 * tokens, 640).T.astype(BF16)
        v_ot[pl.ds(i * chips_o, chips_o)] = here.reshape(chips_o, 2, 2, own, 2 * tokens)
        there = jnp.concatenate([v_osib[1, :, at], v_osib[0, :, at]], axis=0).astype(F32).T.astype(BF16)
        v_ot[pl.ds(half + i * chips_o, chips_o)] = there.reshape(chips_o, 2, 2, own, 2 * tokens)
        return 0

    lax.fori_loop(0, rh // 640, turn_o, 0)
    o_over = give(v_ot.at[:, :, 1 - x], o_ot.at[:, :, :, pl.ds(2 * tokens, 2 * tokens)], over)
    put(v_ot.at[:, :, x], o_ot.at[:, :, :, pl.ds(0, 2 * tokens)])

    tile = 128
    steps = fh // tile

    def loads(t, slot):
        first = pl.ds(pl.multiple_of(t * tile, tile), tile)
        second = pl.ds(pl.multiple_of(fh + t * tile, tile), tile)
        return [
            pltpu.make_async_copy(o_gu.at[:, :, :, first], v_w.at[slot, :, :, :, pl.ds(0, tile)], load_sem.at[slot, 0]),
            pltpu.make_async_copy(
                o_gu.at[:, :, :, second], v_w.at[slot, :, :, :, pl.ds(tile, tile)], load_sem.at[slot, 1]
            ),
        ]

    def stores(t, slot):
        at = pl.ds(pl.multiple_of(t * tile, tile), tile)
        return [
            pltpu.make_async_copy(v_gu.at[slot, :, pl.ds(0, tile)], o_gate.at[:, at], store_sem.at[slot, 0]),
            pltpu.make_async_copy(v_gu.at[slot, :, pl.ds(tile, tile)], o_up.at[:, at], store_sem.at[slot, 1]),
        ]

    gu.finish()
    for copy in loads(0, 0):
        copy.start()
    n2_pair.wait_recv()
    n2_over.wait_recv()
    n2_last = give(v_n2.at[1], v_n2.at[3], sib)
    n2_last.wait_recv()
    if half > 3:
        down.advance()
    put(v_n2, o_n2)

    def hidden_tile(t, _):
        slot = t % 2
        for copy in loads(t, slot):
            copy.wait()

        @pl.when(t + 1 < steps)
        def _():
            for copy in loads(t + 1, 1 - slot):
                copy.start()

        @pl.when(t >= 2)
        def _():
            for copy in stores(t - 2, slot):
                copy.wait()

        w = v_w[slot].reshape(width, 2 * tile)
        v_gu[slot] = jnp.dot(v_n2[...].reshape(4 * tokens, width), w, preferred_element_type=F32)
        for copy in stores(t, slot):
            copy.start()
        value, _ = gelu_parts(v_gu[slot, :, 0:tile])
        v_hidden[:, pl.ds(pl.multiple_of(t * tile, tile), tile)] = (value * v_gu[slot, :, tile:]).astype(BF16)
        return 0

    lax.fori_loop(0, steps, hidden_tile, 0)
    put(v_hidden, o_hidden)
    cot_over.wait_recv()
    cot_last = give(v_cot.at[1], v_cot.at[3], sib)
    if half > 3:
        down.advance()
    cot_last.wait_recv()
    put(v_cot, o_cot)

    def pd_store(t, slot):
        return pltpu.make_async_copy(v_pd.at[slot], o_pd.at[pl.ds(pl.multiple_of(t * BLK, BLK), BLK)], pd_sem.at[slot])

    def down_tile(t, _):
        slot = t % 2

        @pl.when(t >= 2)
        def _():
            pd_store(t - 2, slot).wait()

        left = v_cot[:, :, pl.ds(pl.multiple_of(t * BLK, BLK), BLK)].reshape(4 * tokens, BLK)
        v_pd[slot] = lax.dot_general(
            left, v_hidden[...], (((0,), (0,)), ((), ())), preferred_element_type=F32
        ).astype(BF16)
        pd_store(t, slot).start()
        return 0

    lax.fori_loop(0, width // BLK, down_tile, 0)
    down.to_last()
    for t in (steps - 2, steps - 1):
        for copy in stores(t, t % 2):
            copy.wait()
    for t in (width // BLK - 2, width // BLK - 1):
        pd_store(t, t % 2).wait()
    down.finish()
    land([n1_over, o_over])
    for copy in kept:
        copy.wait()
    for copy in every:
        if copy is not carry:
            copy.wait_send()


def front(n, wx, wy, wo, gs, wg, wu, wd, rows_in, grad, lengths, resets):
    rec, f = wx.shape[1], wg.shape[1]
    own, own_d, rows_f = wo.shape[0], wx.shape[0], wg.shape[0]
    rh, fh = rec // 2, f // 2
    tokens, width = rows_in.shape
    half = n // 2
    row = np.arange(4 * n)
    index = (row // 2) % n * 4 + row // (2 * n) * 2 + row % 2
    lane_r, lane_d, short = np.arange(rec), np.arange(width), np.arange(128)[:, None]
    spread_r = (lane_r[None, :rh] % own == short).astype(jnp.bfloat16)
    spread_d = (lane_d[None] % own_d == short).astype(jnp.bfloat16)
    pick_r = (index[:, None] == lane_r[None] // own).astype(np.float32)
    pick_d = (index[:, None] == lane_d[None] // own_d).astype(np.float32)
    outs = dict(
        w_xy=((n, 2, 2, own_d, rec), BF16),
        w_o=((n, 2, 2, own, width // 2), BF16),
        gates=((rh, WIDE), BF16),
        cp=((16, rh), F32),
        gains=((8, width), F32),
        w_gu=((n, 2, rows_f, f), BF16),
        w_d=((n, 2, rows_f, fh), BF16),
        cot=((4, tokens, width), BF16),
        starts=((2, tokens, 128), F32),
        ypre=((2, tokens, rh), F32),
        u=((2, tokens, rh), BF16),
        a=((2, tokens, rh), F32),
        h=((2, tokens, rh), F32),
        h_in=((2, 8, rh), F32),
        xb=((2, tokens, rh), BF16),
        before=((2, 16, rh), BF16),
        x1=((tokens, width), F32),
        n2=((4, tokens, width), BF16),
        n1_t=((n, 2, own_d, 4 * tokens), BF16),
        o_t=((n, 2, own, 4 * tokens), BF16),
        hidden=((4 * tokens, fh), BF16),
        gate=((4 * tokens, fh), F32),
        up=((4 * tokens, fh), F32),
        part_d=((width, fh), BF16),
    )
    state = (2, tokens, rh)
    scratch = [
        ((n, 2, 2, own_d, rec), BF16), ((n, 2, 2, own, width // 2), BF16), ((2, n, 2) + gs.shape, BF16),
        ((rh, WIDE), BF16), ((2, tokens, width), BF16), ((4, tokens, width), BF16), ((2, tokens, 128), F32),
        ((16, rh), F32), ((8, width), F32), ((2 * tokens, width), BF16), ((n, 2, 2, own_d, 2 * tokens), BF16),
        (state, BF16), (state, F32), ((2, 16, rh), BF16), (state, BF16), (state, F32),
        ((2, tokens, BLK), F32), (state, F32), (state, F32), ((2, 8, rh), F32), (state, BF16), (state, BF16),
        ((n, 2, 2, own, 2 * tokens), BF16), ((tokens, width // 2), F32), ((tokens, width // 2), F32),
        ((tokens, width // 2), F32), ((tokens, width), F32), ((4, tokens, width), BF16),
        ((2, n, 2, rows_f, BLK), BF16), ((4 * tokens, fh), BF16), ((2, 4 * tokens, BLK), F32), ((2, BLK, fh), BF16), ((2, fh, own_d * 2), BF16),
    ]
    count = 9 + (6 * n - 6) + 2 * (2 * n - 2) + 6 * n + 2 + 12
    dma = pltpu.SemaphoreType.DMA
    result = pl.pallas_call(
        functools.partial(front_kernel, n),
        out_shape=[jax.ShapeDtypeStruct(shape, kind) for shape, kind in outs.values()],
        in_specs=[pl.BlockSpec(memory_space=pl.ANY)] * 9
        + [pl.BlockSpec(memory_space=pltpu.SMEM)]
        + [pl.BlockSpec(memory_space=pltpu.VMEM)] * 5,
        out_specs=[pl.BlockSpec(memory_space=pl.ANY)] * len(outs),
        scratch_shapes=[pltpu.VMEM(shape, kind) for shape, kind in scratch]
        + [dma((32,)), dma((count,)), dma((count,)), dma((2, 2)), dma((2, 2)), dma((2,))],
        compiler_params=pltpu.CompilerParams(
            collective_id=2, has_side_effects=True, vmem_limit_bytes=60 << 20
        ),
        name="front",
    )(wx, wy, wo, gs, wg, wu, wd, rows_in, grad, lengths, resets, spread_r, pick_r, spread_d, pick_d)
    return dict(zip(outs, result))


def ff_back_kernel(n, *refs):
    (
        part_d, cot, w_d, gate, up, n2, w_gu,
        g_d, d_n2, o_part,
        v_pd, v_cot, v_n2, v_wd, v_gate, v_up, v_dgu, v_sib, v_wgu, v_dn2, v_pair, v_plane, v_part, r_d, handed,
        local_sem, send_sem, recv_sem, down_sem, up_sem, part_sem,
    ) = refs
    dp, x = lax.axis_index("dp"), lax.axis_index("tp")
    chip, core = dp // 2, dp % 2
    pos = place_of(chip, n)
    half = n // 2
    nxt = (chip_at((pos + 1) % n, n) * 2 + core, x)
    prv = (chip_at((pos + n - 1) % n, n) * 2 + core, x)
    sib = (dp + 1 - 2 * core, x)
    over = (dp, 1 - x)
    copies = Copies(local_sem, send_sem, recv_sem)
    send, stay = copies.send, copies.stay
    rows, fh = v_pd.shape[2], v_pd.shape[3]
    count, width = v_cot.shape
    tokens = count // 4
    products = stay(part_d, v_pd)
    rest = [stay(cot, v_cot), stay(n2, v_n2)]
    greet([nxt, prv, sib, over])

    chains = [(part, way) for part in (0, 1) for way in (0, 1)]
    coming, sent, left = {}, [], {}

    def forward():
        for part, way in chains:
            first = half if way == part else half - 1
            k = left.get((part, way), first)
            if k == 0:
                continue
            device, sign = ((nxt, 1), (prv, n - 1))[way]
            source = (part_d if k == first else v_pd).at[(pos + sign * k) % n, part]
            if k < first:
                coming[part, way].wait_recv()
                got = r_d.at[part, way, k]
                got[...] = (got[...].astype(F32) + source[...].astype(F32)).astype(BF16)
                source = got
            copy = send(source, r_d.at[part, way, k - 1], device)
            coming[part, way] = copy
            sent.append(copy)
            left[part, way] = k - 1

    forward()

    def down_loads(t, slot):
        at = pl.ds(pl.multiple_of(t * BLK, BLK), BLK)
        pairs = ((w_d, v_wd), (gate, v_gate), (up, v_up))
        return [
            pltpu.make_async_copy(src.at[:, at], dst.at[slot], down_sem.at[slot, i])
            for i, (src, dst) in enumerate(pairs)
        ]

    steps = fh // BLK
    for copy in down_loads(0, 0):
        copy.start()
    for copy in rest + [products]:
        copy.wait()

    def cotangent_tile(t, _):
        slot = t % 2
        for copy in down_loads(t, slot):
            copy.wait()

        @pl.when(t + 1 < steps)
        def _():
            for copy in down_loads(t + 1, 1 - slot):
                copy.start()

        d_hidden = jnp.dot(v_cot[...], v_wd[slot], preferred_element_type=F32)
        act, slope = gelu_parts(v_gate[slot])
        v_dgu[:, pl.ds(pl.multiple_of(t * BLK, BLK), BLK)] = (d_hidden * v_up[slot] * slope).astype(BF16)
        v_dgu[:, pl.ds(pl.multiple_of(fh + t * BLK, BLK), BLK)] = (d_hidden * act).astype(BF16)
        return 0

    def up_loads(t, slot):
        at = pl.ds(pl.multiple_of(t * BLK, BLK), BLK)
        return pltpu.make_async_copy(w_gu.at[at], v_wgu.at[slot], up_sem.at[slot])

    up_loads(0, 0).start()
    lax.fori_loop(0, steps, cotangent_tile, 0)
    swap = [
        send(v_dgu.at[pl.ds(0, 2 * tokens)], v_sib.at[pl.ds(2 * tokens, 2 * tokens)], sib),
        send(v_dgu.at[pl.ds(2 * tokens, 2 * tokens)], v_sib.at[pl.ds(0, 2 * tokens)], sib),
    ]

    def norm_tile(t, _):
        slot = t % 2
        up_loads(t, slot).wait()

        @pl.when(t + 1 < width // BLK)
        def _():
            up_loads(t + 1, 1 - slot).start()

        product = nt(v_dgu[...], v_wgu[slot]).astype(BF16)
        v_dn2[:, :, pl.ds(pl.multiple_of(t * BLK, BLK), BLK)] = product.reshape(4, tokens, BLK)
        return 0

    lax.fori_loop(0, width // BLK // 2, norm_tile, 0)
    forward()
    lax.fori_loop(width // BLK // 2, width // BLK, norm_tile, 0)
    pair = send(v_dn2.at[pl.ds(2, 2)], v_pair, sib)
    for copy in swap:
        copy.wait_recv()

    def part_store(i, slot):
        return pltpu.make_async_copy(
            v_part.at[slot], o_part.at[pl.ds(pl.multiple_of(i * rows, 8), rows)], part_sem.at[slot]
        )

    def part_tile(i, _):
        slot = i % 2

        @pl.when(i >= 2)
        def _():
            part_store(i - 2, slot).wait()

        at = pl.ds(pl.multiple_of(chip_at(i, n) * 2 * rows + core * rows, 128), rows)
        columns = v_n2[:, at]
        for j, ref in enumerate((v_dgu, v_sib)):
            product = lax.dot_general(columns, ref[...], (((0,), (0,)), ((), ())), preferred_element_type=F32)
            v_part[slot, :, 2 * fh * j : 2 * fh * (j + 1)] = product.astype(BF16)
        part_store(i, slot).start()
        return 0

    lax.fori_loop(0, n // 4, part_tile, 0)
    pair.wait_recv()
    for i in (1, 0):
        v_pair[i] = (v_dn2[i].astype(F32) + v_pair[i].astype(F32)).astype(BF16)
        if i == 1:
            plane = send(v_pair.at[1], v_plane, over)
    lax.fori_loop(n // 4, n // 2, part_tile, 0)
    forward()
    lax.fori_loop(n // 2, n, part_tile, 0)
    plane.wait_recv()
    d_n2[...] = v_pair[0].astype(F32) + v_plane[...].astype(F32)
    while any(left.values()):
        forward()
    for i in (n - 2, n - 1):
        part_store(i, i % 2).wait()

    at = pl.ds(pl.multiple_of(core * fh, 128), fh)
    totals = []
    for part in (0, 1):
        for way in (0, 1):
            coming[part, way].wait_recv()
        totals.append(v_pd[pos, part].astype(F32) + r_d[part, 0, 0].astype(F32) + r_d[part, 1, 0].astype(F32))
    for part in (0, 1):

        @pl.when(core == part)
        def _():
            g_d[:, at] = totals[part]
            handed[...] = totals[1 - part]

    last = send(handed, g_d.at[:, at], sib)
    last.wait_recv()
    for copy in sent + swap + [pair, plane, last]:
        copy.wait_send()


def ff_back(n, part_d, cot, w_d, gate, up, n2, w_gu):
    width, fh = part_d.shape
    count = cot.shape[0]
    tokens = count // 4
    rows = width // (2 * n)
    half = n // 2
    dma = pltpu.SemaphoreType.DMA
    scratch = [
        ((n, 2, rows, fh), BF16), ((count, width), BF16), ((count, width), BF16), ((2, width, BLK), BF16),
        ((2, count, BLK), F32), ((2, count, BLK), F32), ((count, 2 * fh), BF16), ((count, 2 * fh), BF16),
        ((2, BLK, 2 * fh), BF16), ((4, tokens, width), BF16), ((2, tokens, width), BF16), ((tokens, width), BF16),
        ((2, rows, 4 * fh), BF16), ((2, 2, half, rows, fh), BF16), ((rows, fh), F32),
    ]
    copies = 2 * (2 * half - 1) + 5
    return pl.pallas_call(
        functools.partial(ff_back_kernel, n),
        out_shape=[
            jax.ShapeDtypeStruct((rows, 2 * fh), F32),
            jax.ShapeDtypeStruct((tokens, width), F32),
            jax.ShapeDtypeStruct((n * rows, 4 * fh), BF16),
        ],
        in_specs=[pl.BlockSpec(memory_space=pl.ANY)] * 7,
        out_specs=[pl.BlockSpec(memory_space=pltpu.VMEM)] * 2 + [pl.BlockSpec(memory_space=pl.ANY)],
        scratch_shapes=[pltpu.VMEM(shape, kind) for shape, kind in scratch]
        + [dma((3,)), dma((copies,)), dma((copies,)), dma((2, 3)), dma((2,)), dma((2,))],
        compiler_params=pltpu.CompilerParams(
            collective_id=3, has_side_effects=True, vmem_limit_bytes=60 << 20
        ),
        name="ff_back",
    )(part_d.reshape(n, 2, rows, fh), cot, w_d, gate, up, n2, w_gu)


def finish_kernel(
    sums, x_sum, y_sum, out_sum, gates, vec,
    gate_ref, up_ref, x_ref, y_ref, out_ref, a_ref, i_ref, taps_ref, *lines,
):
    core = lax.axis_index("dp") % 2
    half = gate_ref.shape[1] // 2
    for first in (0, 1):

        @pl.when(core == first)
        def _():
            for i in (0, 1):
                start = (i != first) * 2 * half
                at = pl.ds(i * half, half)
                gate_ref[:, at] = sums[:, start : start + half].astype(F32)
                up_ref[:, at] = sums[:, start + half : start + 2 * half].astype(F32)

    x_ref[...] = x_sum[...]
    y_ref[...] = y_sum[...]
    out_ref[...] = out_sum[...]
    a_ref[...] = gates[:, :BLK]
    i_ref[...] = gates[:, BLK:]
    taps, own = taps_ref.shape
    taps_ref[...] = vec[0:taps, 0:own]
    for k, ref in enumerate(lines):
        ref[...] = vec[taps + k : taps + k + 1, 0 : ref.shape[1]]


def finish(sums, x_sum, y_sum, out_sum, gates, vec, taps):
    rows, cols = sums.shape
    own, own_d = out_sum.shape[0], x_sum.shape[0]
    steps = 2 if rows % 16 == 0 and own % 16 == 0 and own_d % 16 == 0 else 1

    def tiled(shape):
        return pl.BlockSpec((shape[0] // steps, shape[1]), lambda i: (i, 0))

    def fixed(shape):
        return pl.BlockSpec(shape, lambda i: (0, 0))

    big = [(rows, cols // 2)] * 2 + [x_sum.shape, y_sum.shape, out_sum.shape] + [(own, BLK)] * 2
    small = [(taps, own)] + [(1, own)] * 4 + [(1, own_d)] * 2
    return pl.pallas_call(
        finish_kernel,
        grid=(steps,),
        in_specs=[tiled(v.shape) for v in (sums, x_sum, y_sum, out_sum, gates)] + [fixed(vec.shape)],
        out_specs=[tiled(shape) for shape in big] + [fixed(shape) for shape in small],
        out_shape=[jax.ShapeDtypeStruct(shape, F32) for shape in big + small],
        compiler_params=pltpu.CompilerParams(vmem_limit_bytes=60 << 20),
        name="finish",
    )(sums, x_sum, y_sum, out_sum, gates, vec)


def nt(left, right):
    return lax.dot_general(left, right, (((1,), (1,)), ((), ())), preferred_element_type=F32)


def nn(left, right):
    return jnp.dot(left, right, preferred_element_type=F32)


def body(
    dp_size,
    layer_input, grad_out, lengths, resets, norm_gain, w_x, w_y, conv_w, conv_b, gate_a_w, gate_a_b,
    gate_i_w, gate_i_b, decay_param, w_out, mlp_gain, w_gate, w_up, w_down,
):
    n = dp_size // 2
    half = n // 2
    dp, x = lax.axis_index("dp"), lax.axis_index("tp")
    chip, core = dp // 2, dp % 2
    pos = place_of(chip, n)
    tokens, width = layer_input.shape[1], layer_input.shape[2]
    rec = w_x.shape[1]
    rh = rec // 2
    taps = conv_w.shape[0]
    own = rec // (2 * dp_size)
    own_d = width // (2 * dp_size)

    ring = [chip_at(i, n) for i in range(n)]
    up = [(ring[i] * 2 + c, ring[(i + 1) % n] * 2 + c) for i in range(n) for c in range(2)]
    down = [(b, a) for a, b in up]
    lanes = [[chip_id * 2 + c for chip_id in ring] for c in range(2)]
    pairs = [(d, d + 1 - 2 * (d % 2)) for d in range(dp_size)]

    def sibling(v):
        return lax.ppermute(v, "dp", pairs)

    def across(v):
        return lax.ppermute(v, "tp", [(0, 1), (1, 0)])

    def swapped(v):
        return jnp.concatenate([v[1:], v[:1]], axis=0)

    def by_core(mine, theirs, axis):
        return jnp.where(
            core == 0, jnp.concatenate([mine, theirs], axis), jnp.concatenate([theirs, mine], axis)
        )

    def ring_order(array, axis):
        size = array.shape[axis] // n
        return jnp.concatenate([lax.slice_in_dim(array, i * size, (i + 1) * size, axis=axis) for i in ring], axis)

    def chip_order(array, axis):
        size = array.shape[axis] // n
        return jnp.concatenate(
            [lax.slice_in_dim(array, ring.index(i) * size, (ring.index(i) + 1) * size, axis=axis) for i in range(n)],
            axis,
        )

    def after(value, *others):
        return lax.optimization_barrier((value,) + others)[0]

    rows_own = layer_input.reshape(tokens, width)
    place = x * tokens + jnp.arange(tokens, dtype=jnp.int32)
    starts = jnp.where((resets.reshape(tokens) > 0) | (place == 0), 1.0, 0.0).astype(F32)
    starts = jnp.broadcast_to(starts[:, None], (tokens, 128))
    valid = (place < lengths[0]).astype(F32)[:, None]
    cot = grad_out.reshape(tokens, width).astype(F32) * valid

    def lane_sum(array):
        return lax.psum_scatter(array, "dp", scatter_dimension=0, tiled=True, axis_index_groups=lanes)

    def plane(array, which):
        return lax.dynamic_index_in_dim(array, which, 2, keepdims=False)

    def both(mine, axis):
        return jnp.concatenate([mine, across(mine)], axis)

    def tn(left, right):
        return lax.dot_general(left, right, (((0,), (0,)), ((), ())), preferred_element_type=F32)

    fh = w_gate.shape[1] // 2
    if own % 16 == 0 and own_d % 16 == 0:
        vectors = jnp.concatenate([conv_w, jnp.stack([conv_b, gate_a_b, gate_i_b, decay_param])], axis=0)
        vectors = jnp.pad(vectors, ((0, 0), (0, WIDE - own)))
        gains = jnp.pad(jnp.stack([norm_gain, mlp_gain]), ((0, PAD - taps - 6), (0, WIDE - own_d)))
        gs = jnp.concatenate([jnp.concatenate([gate_a_w, gate_i_w], axis=1), vectors, gains], axis=0)
        got = front(
            n, w_x, w_y, w_out, gs, w_gate, w_up, w_down, rows_own, grad_out.reshape(tokens, width), lengths, resets
        )
        w_xy, w_o = got["w_xy"].reshape(width, rec), got["w_o"].reshape(rec, width // 2)
        w_gu, w_d = got["w_gu"].reshape(width, 2 * fh), got["w_d"].reshape(width, fh)
        cot_all, n2_all = got["cot"].reshape(4 * tokens, width), got["n2"].reshape(4 * tokens, width)
        gain_one, gain_two, cp, gates = got["gains"][0], got["gains"][1], got["cp"], got["gates"]
        starts_two, ypre, u, a, h, xb, x1 = (got[key] for key in ("starts", "ypre", "u", "a", "h", "xb", "x1"))
        h_in, before = got["h_in"][:, 7:8], got["before"][:, PAD - taps + 1 :]
        n1_t, o_t = got["n1_t"].reshape(width // 2, 4 * tokens), got["o_t"].reshape(rh, 4 * tokens)
        hidden, gate, upv, part_d = got["hidden"], got["gate"], got["up"], got["part_d"]
        rs2 = lax.rsqrt(jnp.mean(x1 * x1, axis=-1, keepdims=True) + EPS)
    else:
        small = jnp.concatenate(
            [norm_gain, mlp_gain, conv_w.reshape(-1), conv_b, gate_a_b, gate_i_b, decay_param]
        )
        small = jnp.pad(small, (0, PAD * WIDE - small.shape[0])).reshape(PAD, WIDE)
        gs = jnp.concatenate([jnp.concatenate([gate_a_w, gate_i_w], axis=1), small], axis=0)
        w_xy, w_o, all_gs, w_gu, d_block, rows_two, cot_all, starts_two = gather_weights(
            n, w_x, w_y, w_out, gs, w_gate, w_up, w_down.T, rows_own, ring_order(cot.astype(BF16), 1), starts
        )
        w_d = lax.all_gather(
            d_block.reshape(-1, d_block.shape[2]), "dp", axis=0, tiled=True, axis_index_groups=lanes
        )
        w_gu = w_gu.reshape(width, w_gate.shape[1])
        w_xy = w_xy.reshape(width, rec)
        w_o = w_o.reshape(rec, width // 2)
        cot_all = cot_all.reshape(4 * tokens, width)

        vectors = all_gs[:, :, :, own:].transpose(1, 0, 2, 3, 4).reshape(2 * dp_size, PAD * WIDE)
        gain_one = vectors[:, :own_d].reshape(width).astype(F32)
        gain_two = vectors[:, own_d : 2 * own_d].reshape(width).astype(F32)
        lines = vectors[:, 2 * own_d : 2 * own_d + (taps + 4) * own].reshape(2 * dp_size, taps + 4, own)
        lines = lax.dynamic_slice_in_dim(lines, core * dp_size, dp_size, 0)
        lines = lines.transpose(1, 0, 2).reshape(taps + 4, rh).astype(F32)
        decay = lines[taps + 3 :]
        cp = jnp.concatenate(
            [lines[: taps + 3], jax.nn.softplus(-decay), jax.nn.sigmoid(-decay), jnp.zeros((7, rh), F32)], axis=0
        )
        gates = lax.dynamic_slice_in_dim(all_gs[:, :, :, :own], core * half, half, 1)
        gates = gates.transpose(1, 0, 2, 3, 4).reshape(rh, WIDE)

        n1, xb, ypre = project(rows_two, gain_one[None], w_xy)
        before = lax.ppermute(xb[:, tokens - (taps - 1) :], "tp", [(0, 1)])
        halo = jnp.concatenate([jnp.zeros((2, 8 - (taps - 1), rh), F32), before.astype(F32)], axis=1)
        u, a, h_local, coef = recurrence(xb, halo, gates, cp, starts_two)
        h_in = lax.ppermute(h_local[:, tokens - 1 :], "tp", [(0, 1)])
        h = h_local + coef * h_in
        ybr, _ = gelu_parts(ypre)
        o = (h * ybr).astype(BF16)
        o_sib = sibling(o)
        part_mine, part_theirs = project_out(o, o_sib, w_o)
        x1 = rows_own.astype(F32) + by_core(part_mine, sibling(part_theirs), 1)
        rs2 = lax.rsqrt(jnp.mean(x1 * x1, axis=-1, keepdims=True) + EPS)
        n2 = (x1 * rs2 * gain_two).astype(BF16)
        n2_x = across(n2)

        def plane_rows(values, rows):
            grouped = after(values, n2_x).T.reshape(n, 2, 2, rows, 2 * tokens)
            return plane(grouped, x), plane(grouped, 1 - x)

        o_here, o_send = plane_rows(jnp.concatenate([o, swapped(o_sib)], axis=2).reshape(2 * tokens, rec), own)
        n1_here, n1_send = plane_rows(n1, own_d)
        two = jnp.concatenate([n2, n2_x], axis=0)
        n2_all = jnp.concatenate([two, sibling(two)], axis=0)
        o_t = jnp.concatenate([o_here, across(o_send)], axis=3).reshape(rh, 4 * tokens)
        n1_t = jnp.concatenate([n1_here, across(n1_send)], axis=3).reshape(width // 2, 4 * tokens)

        gu = nn(n2_all, w_gu)
        gate, upv = gu[:, :fh], gu[:, fh:]
        act, _ = gelu_parts(gate)
        hidden = (act * upv).astype(BF16)

        part_d = tn(cot_all, hidden).astype(BF16)
    def pair_sum(partial):
        return (partial[: 2 * tokens].astype(F32) + sibling(partial[2 * tokens :]).astype(F32)).astype(BF16)

    if own % 16 == 0 and own_d % 16 == 0:
        grad_d, d_n2, part_gu = ff_back(n, part_d, cot_all, w_d, gate, upv, n2_all, w_gu)
    else:
        sum_d = lane_sum(part_d)
        act, slope = gelu_parts(gate)
        d_hidden = nn(after(cot_all, part_d), w_d)
        d_gu = jnp.concatenate([(d_hidden * upv * slope).astype(BF16), (d_hidden * act).astype(BF16)], axis=1)

        d_n2_pair = pair_sum(nt(d_gu, w_gu).astype(BF16))
        d_n2_send = d_n2_pair[tokens:]
        d_n2 = d_n2_pair[:tokens].astype(F32) + across(d_n2_send).astype(F32)
        n2_rows = ring_order(after(n2_all, d_n2_send), 1).reshape(4 * tokens, n, 2, width // dp_size)
        n2_rows = plane(n2_rows, core).reshape(4 * tokens, width // 2)
        d_gu_sib = sibling(d_gu)
        d_gu_sib = jnp.concatenate([d_gu_sib[2 * tokens :], d_gu_sib[: 2 * tokens]], axis=0)
        part_gu = tn(n2_rows, after(jnp.concatenate([d_gu, d_gu_sib], axis=1), d_n2_send)).astype(BF16)
        grad_d = None
    sum_gu = lane_sum(part_gu)
    ff_pair = pair_sum(nt(after(hidden, part_gu), w_d).astype(BF16))
    ff_out = ff_pair[:tokens].astype(F32) + across(ff_pair[tokens:]).astype(F32)

    q2 = gain_two * d_n2
    d_gain_two = jnp.sum(d_n2 * x1 * rs2, axis=0)
    d_x1 = cot + rs2 * q2 - x1 * (rs2 * rs2 * rs2) * jnp.mean(x1 * q2, axis=-1, keepdims=True)
    dbr = d_x1.astype(BF16)
    dbr_mine = lax.dynamic_slice_in_dim(dbr, core * (width // 2), width // 2, 1)
    dbr_theirs = lax.dynamic_slice_in_dim(dbr, (1 - core) * (width // 2), width // 2, 1)
    dbr_half = jnp.concatenate([dbr_mine, sibling(dbr_theirs)], axis=0)
    do_part = nt(dbr_half, w_o)
    do = do_part[:, :rh].reshape(2, tokens, rh) + swapped(sibling(do_part[:, rh:].reshape(2, tokens, rh)))
    dbr_x = across(dbr_half)

    d_ypre, lam_local, coef_back = adjoint(do, h, ypre, a)
    d_ypre_x = both(d_ypre.reshape(2 * tokens, rh), 0)
    inc = lax.ppermute(a[:, :1] * lam_local[:, :1], "tp", [(1, 0)])
    du, d_gates, sums = gates_back(lam_local, coef_back, inc, h, h_in, u, gates, cp, starts_two)
    du_next = lax.ppermute(du[:, : taps - 1], "tp", [(1, 0)])
    du_pad = jnp.concatenate([du, du_next], axis=1).astype(F32)
    xb_pad = jnp.concatenate([before, xb], axis=1).astype(F32)
    d_taps = jnp.stack(
        [jnp.sum(du_pad[:, :tokens] * xb_pad[:, taps - 1 - k : taps - 1 - k + tokens], axis=(0, 1)) for k in range(taps)]
    )
    d_bias = jnp.sum(du_pad[:, :tokens], axis=(0, 1))[None]
    d_xb = sum(cp[k] * du_pad[:, k : k + tokens] for k in range(taps)).astype(BF16)
    d_xy = jnp.concatenate([d_xb, d_ypre], axis=2).reshape(2 * tokens, rec)
    result = (after(x1, d_xb) + chip_order(ff_out, 1)).astype(BF16).reshape(1, tokens, width)
    d_n1_part = nt(d_xy, w_xy).reshape(2, tokens, width)
    d_n1 = d_n1_part[0] + sibling(d_n1_part[1])
    q1 = gain_one * d_n1
    own_f = rows_own.astype(F32)
    own_rs = lax.rsqrt(jnp.mean(own_f * own_f, axis=-1, keepdims=True) + EPS)
    d_gain_one = jnp.sum(d_n1 * own_f * own_rs, axis=0)
    grad_x = d_x1 + own_rs * q1 - own_f * (own_rs * own_rs * own_rs) * jnp.mean(own_f * q1, axis=-1, keepdims=True)

    c_out = nn(after(o_t, d_xb), jnp.concatenate([dbr_half, dbr_x], axis=0)).astype(BF16).reshape(n, 2, own, width // 2)
    c_x = nn(n1_t, both(d_xb.reshape(2 * tokens, rh), 0)).astype(BF16).reshape(n, 2, own_d, rh)
    c_y = nn(n1_t, d_ypre_x).astype(BF16).reshape(n, 2, own_d, rh)

    def placed(part):
        zero = jnp.zeros_like(part)
        return by_core_rows(part, zero)

    def by_core_rows(mine, theirs):
        return jnp.where(
            core == 0, jnp.concatenate([mine, theirs], 0), jnp.concatenate([theirs, mine], 0)
        )

    g = d_gates.reshape(half, 2, 2, own, WIDE)
    g = plane(g, x) + across(plane(g, 1 - x).astype(BF16)).astype(F32)
    g_mine = lax.dynamic_index_in_dim(g, core, 1, keepdims=False)
    g_theirs = lax.dynamic_index_in_dim(g, 1 - core, 1, keepdims=False)
    g_lane = by_core_rows(g_mine, sibling(g_theirs))

    lines_back = jnp.concatenate([d_taps, d_bias, sums[:3]], axis=0)
    lines_back = lines_back.reshape(taps + 4, half, 2, 2, own).transpose(1, 2, 3, 0, 4)
    lines_back = placed(jnp.pad(lines_back, ((0, 0),) * 4 + ((0, 128 - own),)))
    gains = jnp.stack([d_gain_one.reshape(n, 2, 2, own_d), d_gain_two.reshape(n, 2, 2, own_d)], axis=3)
    gains = jnp.pad(gains, ((0, 0),) * 3 + ((0, PAD - taps - 6), (0, 128 - own_d)))
    vec = jnp.concatenate([lines_back, gains], axis=3)
    vec = plane(vec, x) + across(plane(vec, 1 - x))
    vec = lax.dynamic_index_in_dim(vec, core, 1, keepdims=False) + sibling(
        lax.dynamic_index_in_dim(vec, 1 - core, 1, keepdims=False)
    )

    def whole(block):
        rows = block.shape[0] // 2
        block = block.reshape(2, rows, block.shape[1])
        mine = lax.dynamic_index_in_dim(block, core, 0, keepdims=False)
        theirs = lax.dynamic_index_in_dim(block, 1 - core, 0, keepdims=False)
        return mine, sibling(theirs)

    def halves(pair):
        return by_core(pair[0], pair[1], 1).astype(F32)

    grad_down = (halves(whole(sum_d)) if grad_d is None else grad_d).T
    x_sum, y_sum, out_sum, sum_gates, sum_vec = scatter_sums(
        n, after(c_x, grad_down, result, grad_x), c_y, c_out, g_lane.astype(BF16), vec
    )
    done = finish(after(sum_gu, sum_vec), x_sum, y_sum, out_sum, sum_gates, sum_vec, taps)
    grad_gate, grad_up, grad_w_x, grad_w_y, grad_w_out, grad_a_w, grad_i_w, grad_taps = done[:8]
    grad_bias, grad_a_b, grad_i_b, grad_decay, grad_gain_one, grad_gain_two = (v.reshape(-1) for v in done[8:])
    return (
        result,
        grad_x.reshape(1, tokens, width),
        grad_gain_one,
        grad_w_x,
        grad_w_y,
        grad_taps,
        grad_bias,
        grad_a_w,
        grad_a_b,
        grad_i_w,
        grad_i_b,
        grad_decay,
        grad_w_out,
        grad_gain_two,
        grad_gate,
        grad_up,
        grad_down,
    )


def solution(mesh):
    every = ("dp", "tp")
    return jax.shard_map(
        functools.partial(body, mesh.shape["dp"]),
        mesh=mesh,
        in_specs=(
            P("dp", "tp", None),
            P("dp", "tp", None),
            P("dp"),
            P("dp", "tp"),
            P(every),
            P(every, None),
            P(every, None),
            P(None, every),
            P(every),
            P(every, None),
            P(every),
            P(every, None),
            P(every),
            P(every),
            P(every, None),
            P(every),
            P("dp", "tp"),
            P("dp", "tp"),
            P("tp", "dp"),
        ),
        out_specs=(
            P("dp", "tp", None),
            P("dp", "tp", None),
            P(every),
            P(every, None),
            P(every, None),
            P(None, every),
            P(every),
            P(every, None),
            P(every),
            P(every, None),
            P(every),
            P(every),
            P(every, None),
            P(every),
            P("dp", "tp"),
            P("dp", "tp"),
            P("tp", "dp"),
        ),
        check_vma=False,
    )
```

```python
import functools

import jax
import jax.numpy as jnp
import numpy as np
from jax import lax
from jax.experimental import pallas as pl
from jax.experimental.pallas import tpu as pltpu
from jax.sharding import PartitionSpec as P

BLK = 256
PAD = 16
WIDE = 512
EPS = 1e-06
MESH = pl.DeviceIdType.MESH
F32 = jnp.float32
BF16 = jnp.bfloat16


def chip_at(pos, n):
    back = pos // (n // 2)
    return (1 - back) * (2 * pos) + back * (2 * (n - 1 - pos) + 1)


def place_of(chip, n):
    odd = chip % 2
    return (1 - odd) * (chip // 2) + odd * (n - 1 - chip // 2)


def heads_first(chip, core, n):
    return (chip + n - core * (n // 2)) % n


class Copies:
    def __init__(self, local, sends, recvs):
        self.local, self.sends, self.recvs = local, sends, recvs
        self.locals_used = self.used = 0

    def stay(self, src, dst):
        copy = pltpu.make_async_copy(src, dst, self.local.at[self.locals_used])
        self.locals_used += 1
        copy.start()
        return copy

    def send(self, src, dst, device):
        copy = pltpu.make_async_remote_copy(
            src_ref=src, dst_ref=dst, send_sem=self.sends.at[self.used], recv_sem=self.recvs.at[self.used],
            device_id=device, device_id_type=MESH,
        )
        self.used += 1
        copy.start()
        return copy


def greet(devices):
    barrier = pltpu.get_barrier_semaphore()
    for device in devices:
        pl.semaphore_signal(barrier, inc=1, device_id=device, device_id_type=MESH)
    pl.semaphore_wait(barrier, len(devices))


def half_cols(ref, which):
    width = ref.shape[1] // 2
    return ref.at[:, pl.ds(pl.multiple_of(which * width, 128), width)]


def gather_kernel(
    n,
    wx, wy, wo, gs, wg, wu, wd, rows_in, cot, starts,
    o_xy, o_out, o_gs, o_gu, o_d, o_rows, o_cot, o_starts,
    local_sem, send_sem, recv_sem,
):
    dp, x = lax.axis_index("dp"), lax.axis_index("tp")
    chip, core = dp // 2, dp % 2
    other = 1 - core
    pos = place_of(chip, n)
    half = n // 2
    nxt = (chip_at((pos + 1) % n, n) * 2 + core, x)
    prv = (chip_at((pos + n - 1) % n, n) * 2 + core, x)
    sib = (chip * 2 + other, x)
    over = (dp, 1 - x)
    greet([nxt, prv, sib, over])
    copies = Copies(local_sem, send_sem, recv_sem)
    send, stay = copies.send, copies.stay

    def by_heads(chip_id, which):
        return heads_first(chip_id, which, n)

    rhalf = wx.shape[1] // 2
    fhalf = wg.shape[1] // 2
    rec_parts = [
        (wx, o_xy.at[chip, core, x, :, pl.ds(0, rhalf)]),
        (wy, o_xy.at[chip, core, x, :, pl.ds(rhalf, rhalf)]),
    ]
    ff_parts = [
        (wg, o_gu.at[chip, core, :, pl.ds(0, fhalf)]),
        (wu, o_gu.at[chip, core, :, pl.ds(fhalf, fhalf)]),
        (wd, o_d.at[core]),
    ]
    pair = [send(half_cols(src, other), slot, sib) for src, slot in rec_parts]
    pair.append(send(half_cols(wo, other), o_out.at[by_heads(chip, other), core, x], sib))
    mine = [stay(half_cols(src, core), slot) for src, slot in rec_parts] + [stay(gs, o_gs.at[core, chip, x])]
    mine.append(stay(half_cols(wo, core), o_out.at[by_heads(chip, core), core, x]))
    late = [send(half_cols(src, other), slot, sib) for src, slot in ff_parts]
    plain = [stay(half_cols(src, core), slot) for src, slot in ff_parts]
    late += [send(rows_in, o_rows.at[1], sib), send(starts, o_starts.at[1], sib), send(cot, o_cot.at[2], sib)]
    plain += [stay(rows_in, o_rows.at[0]), stay(starts, o_starts.at[0]), stay(cot, o_cot.at[0])]

    def rec_block(chip_id):
        return [o_xy.at[chip_id, :, x], o_out.at[by_heads(chip_id, core), :, x], o_gs.at[core, chip_id, x]]

    def rec_piece(chip_id, which):
        refs = [o_xy.at[chip_id, which, x], o_out.at[by_heads(chip_id, core), which, x]]
        return refs + ([o_gs.at[core, chip_id, x]] if which == 0 else [])

    def ff_block(chip_id):
        return [o_gu.at[chip_id]]

    def ff_piece(chip_id, which):
        return [o_gu.at[chip_id, which]]

    def send_all(refs, device):
        return [send(ref, ref, device) for ref in refs]

    def hop(s, block, piece):
        ahead = chip_at((pos + n - (s - 1)) % n, n)
        behind = chip_at((pos + s - 1) % n, n)
        if s < half:
            return send_all(block(ahead), nxt) + send_all(block(behind), prv)
        return send_all(piece(ahead, 0), nxt) + send_all(piece(behind, 1), prv)

    for copy in pair:
        copy.wait_recv()
    for copy in mine:
        copy.wait()
    done, crossed, moving = [], send_all(rec_block(chip), over), []
    for s in range(1, half + 1):
        for copy in moving:
            copy.wait_recv()
        done.extend(moving)
        moving = hop(s, rec_block, rec_piece)
        if s > 1:
            crossed.extend(send_all(rec_block(chip_at((pos + n - (s - 1)) % n, n)), over))
            crossed.extend(send_all(rec_block(chip_at((pos + s - 1) % n, n)), over))
    last_rec = moving
    for copy in late:
        copy.wait_recv()
    for copy in plain:
        copy.wait()
    moving = hop(1, ff_block, ff_piece)
    for copy in last_rec:
        copy.wait_recv()
    done.extend(last_rec)
    crossed.extend(send_all(rec_block(chip_at((pos + half) % n, n)), over))
    cot_over = send(cot, o_cot.at[1], over)
    for s in range(2, half + 1):
        for copy in moving:
            copy.wait_recv()
        done.extend(moving)
        moving = hop(s, ff_block, ff_piece)
    for copy in crossed:
        copy.wait_recv()
    swap = send(o_gs.at[core], o_gs.at[core], sib)
    cot_over.wait_recv()
    last = send(o_cot.at[1], o_cot.at[3], sib)
    for copy in moving:
        copy.wait_recv()
    done.extend(moving)
    swap.wait_recv()
    last.wait_recv()
    for copy in pair + late + done + crossed + [cot_over, swap, last]:
        copy.wait_send()


def gather_weights(n, wx, wy, wo, gs, wg, wu, wd, rows_in, cot, starts):
    r, d, (rows_f, f) = wx.shape[1], wo.shape[1], wg.shape
    tokens = rows_in.shape[0]
    shapes = [
        jax.ShapeDtypeStruct((n, 2, 2, wx.shape[0], r), BF16),
        jax.ShapeDtypeStruct((n, 2, 2, wo.shape[0], d // 2), BF16),
        jax.ShapeDtypeStruct((2, n, 2) + gs.shape, BF16),
        jax.ShapeDtypeStruct((n, 2, rows_f, f), BF16),
        jax.ShapeDtypeStruct((2, rows_f, f // 2), BF16),
        jax.ShapeDtypeStruct((2, tokens, d), BF16),
        jax.ShapeDtypeStruct((4, tokens, d), BF16),
        jax.ShapeDtypeStruct((2,) + starts.shape, F32),
    ]
    count = 9 + (3 * n - 1) + n + 3 * n + 3
    dma = pltpu.SemaphoreType.DMA
    return pl.pallas_call(
        functools.partial(gather_kernel, n),
        out_shape=shapes,
        in_specs=[pl.BlockSpec(memory_space=pltpu.VMEM)] * 10,
        out_specs=[pl.BlockSpec(memory_space=pl.ANY)] * 8,
        scratch_shapes=[dma((10,)), dma((count,)), dma((count,))],
        compiler_params=pltpu.CompilerParams(
            collective_id=0, has_side_effects=True, vmem_limit_bytes=24 << 20
        ),
        name="gather_weights",
    )(wx, wy, wo, gs, wg, wu, wd, rows_in, cot, starts)


def scatter_kernel(
    n,
    h_x, h_y, h_out, h_g, h_v,
    g_x, g_y, g_out, g_gates, g_vec,
    r_x, r_y, r_out, r_g, r_v, s_x, s_y, s_out, c_x, c_y, c_out, c_g, c_v,
    send_sem, recv_sem, local_sem,
):
    dp, x = lax.axis_index("dp"), lax.axis_index("tp")
    chip, core = dp // 2, dp % 2
    pos = place_of(chip, n)
    half = n // 2
    nxt = (chip_at((pos + 1) % n, n) * 2 + core, x)
    prv = (chip_at((pos + n - 1) % n, n) * 2 + core, x)
    sib = (dp + 1 - 2 * core, x)
    copies = Copies(local_sem, send_sem, recv_sem)
    loads = [
        copies.stay(src, dst) for src, dst in ((h_out, c_out), (h_y, c_y), (h_x, c_x), (h_g, c_g), (h_v, c_v))
    ]
    greet([nxt, prv, sib])

    pieces = []
    for part in (0, 1):
        for far_terms, terms, slots, first in ((h_out, c_out, r_out, core), (h_y, c_y, r_y, 0), (h_x, c_x, r_x, 0)):
            pieces.append((
                lambda c, terms=terms, part=part, first=first: terms.at[heads_first(c, first, n), part],
                lambda w, k, slots=slots, part=part: slots.at[part, w, k],
                part,
                lambda c, terms=far_terms, part=part, first=first: terms.at[heads_first(c, first, n), part],
            ))
    pieces.append((lambda c: c_g.at[c], lambda w, k: r_g.at[w, k], 0, lambda c: h_g.at[c]))
    pieces.append((lambda c: c_v.at[c], lambda w, k: r_v.at[w, k], 1, lambda c: h_v.at[c]))

    def add(a, b):
        return a[...].astype(F32) + b[...].astype(F32)

    sent, coming = [], {}
    for k in range(half, -1, -1):
        if k == half - 1:
            for copy in loads:
                copy.wait()
        for i, (term, slot, far, raw) in enumerate(pieces):
            for way, (device, sign) in enumerate(((nxt, 1), (prv, n - 1))):
                first = half if way == far else half - 1
                if k > first or k == 0:
                    continue
                source = (raw if k == half else term)(chip_at((pos + sign * k) % n, n))
                if k < first:
                    coming[i, way].wait_recv()
                    got = slot(way, k)
                    got[...] = add(got, source).astype(got.dtype)
                    source = got
                copy = copies.send(source, slot(way, k - 1), device)
                coming[i, way] = copy
                sent.append(copy)

    def total(i):
        term, slot = pieces[i][:2]
        for way in (0, 1):
            coming[i, way].wait_recv()
        return add(term(chip), slot(0, 0)) + slot(1, 0)[...].astype(F32)

    def cols(ref):
        width = ref.shape[1] // 2
        return pl.ds(pl.multiple_of(core * width, 128), width)

    final = []
    for i, (ref, handed) in enumerate(((g_out, s_out), (g_y, s_y), (g_x, s_x))):
        sums = [total(3 * part + i) for part in (0, 1)]
        for part in (0, 1):

            @pl.when(core == part)
            def _():
                ref[:, cols(ref)] = sums[part]
                handed[...] = sums[1 - part]

        final.append(copies.send(handed, ref.at[:, cols(ref)], sib))
    g_gates[...] = total(6)
    g_vec[...] = total(7)
    for copy in final:
        copy.wait_recv()
    for copy in sent + final:
        copy.wait_send()


def scatter_sums(n, c_x, c_y, c_out, c_g, c_v):
    _, _, rows_d, rhalf = c_x.shape
    _, _, rows_r, dhalf = c_out.shape
    half = n // 2
    count = 8 * (2 * half - 1) + 3
    dma = pltpu.SemaphoreType.DMA
    vmem = pl.BlockSpec(memory_space=pltpu.VMEM)
    return pl.pallas_call(
        functools.partial(scatter_kernel, n),
        out_shape=[
            jax.ShapeDtypeStruct((rows_d, 2 * rhalf), F32),
            jax.ShapeDtypeStruct((rows_d, 2 * rhalf), F32),
            jax.ShapeDtypeStruct((rows_r, 2 * dhalf), F32),
            jax.ShapeDtypeStruct(c_g.shape[1:], F32),
            jax.ShapeDtypeStruct(c_v.shape[1:], F32),
        ],
        in_specs=[pl.BlockSpec(memory_space=pl.ANY)] * 5,
        out_specs=[vmem] * 5,
        scratch_shapes=[
            pltpu.VMEM((2, 2, half, rows_d, rhalf), BF16),
            pltpu.VMEM((2, 2, half, rows_d, rhalf), BF16),
            pltpu.VMEM((2, 2, half, rows_r, dhalf), BF16),
            pltpu.VMEM((2, half) + c_g.shape[1:], BF16),
            pltpu.VMEM((2, half) + c_v.shape[1:], F32),
            pltpu.VMEM((rows_d, rhalf), F32),
            pltpu.VMEM((rows_d, rhalf), F32),
            pltpu.VMEM((rows_r, dhalf), F32),
        ]
        + [pltpu.VMEM(v.shape, v.dtype) for v in (c_x, c_y, c_out, c_g, c_v)]
        + [
            dma((count,)), dma((count,)), dma((5,)),
        ],
        compiler_params=pltpu.CompilerParams(
            collective_id=1, has_side_effects=True, vmem_limit_bytes=56 << 20
        ),
        name="scatter_sums",
    )(c_x, c_y, c_out, c_g, c_v)


def project_kernel(steps, rows, gain, w, n1_ref, x_ref, y_ref):
    i = pl.program_id(0)

    @pl.when(i == 0)
    def _():
        values = rows[...].astype(F32)
        scale = lax.rsqrt(jnp.mean(values * values, axis=-1, keepdims=True) + EPS)
        n1_ref[...] = (values * scale * gain[...]).astype(BF16).reshape(n1_ref.shape)

    result = jnp.dot(n1_ref[...], w[...], preferred_element_type=F32).reshape(y_ref.shape)

    @pl.when(i < steps)
    def _():
        x_ref[...] = result.astype(BF16)

    @pl.when(i >= steps)
    def _():
        y_ref[...] = result


def project(rows, gain, w):
    _, tokens, width = rows.shape
    rh = w.shape[1] // 2
    steps = rh // BLK
    return pl.pallas_call(
        functools.partial(project_kernel, steps),
        grid=(2 * steps,),
        in_specs=[
            pl.BlockSpec(rows.shape, lambda i: (0, 0, 0)),
            pl.BlockSpec((1, width), lambda i: (0, 0)),
            pl.BlockSpec((width, BLK), lambda i: (0, i)),
        ],
        out_specs=[
            pl.BlockSpec((2 * tokens, width), lambda i: (0, 0)),
            pl.BlockSpec((2, tokens, BLK), lambda i: (0, 0, jnp.minimum(i, steps - 1))),
            pl.BlockSpec((2, tokens, BLK), lambda i: (0, 0, jnp.maximum(i - steps, 0))),
        ],
        out_shape=[
            jax.ShapeDtypeStruct((2 * tokens, width), BF16),
            jax.ShapeDtypeStruct((2, tokens, rh), BF16),
            jax.ShapeDtypeStruct((2, tokens, rh), F32),
        ],
        compiler_params=pltpu.CompilerParams(vmem_limit_bytes=40 << 20),
        cost_estimate=pl.CostEstimate(flops=27 * 10**8, bytes_accessed=15 * 10**6, transcendentals=0),
        name="project",
    )(rows, gain, w)


def project_out_kernel(o, o_sib, w, mine_ref, theirs_ref):
    rh = o.shape[2]
    for row, ref in ((0, mine_ref), (1, theirs_ref)):
        ref[...] = jnp.dot(o[row], w[:rh], preferred_element_type=F32) + jnp.dot(
            o_sib[1 - row], w[rh:], preferred_element_type=F32
        )


def project_out(o, o_sib, w):
    _, tokens, rh = o.shape
    cols = w.shape[1]
    tile = min(BLK, cols)
    whole = pl.BlockSpec(o.shape, lambda i: (0, 0, 0))
    part = pl.BlockSpec((tokens, tile), lambda i: (0, i))
    return pl.pallas_call(
        project_out_kernel,
        grid=(cols // tile,),
        in_specs=[whole, whole, pl.BlockSpec((2 * rh, tile), lambda i: (0, i))],
        out_specs=[part, part],
        out_shape=[jax.ShapeDtypeStruct((tokens, cols), F32)] * 2,
        compiler_params=pltpu.CompilerParams(vmem_limit_bytes=40 << 20),
        cost_estimate=pl.CostEstimate(flops=14 * 10**8, bytes_accessed=8 * 10**6, transcendentals=0),
        name="project_out",
    )(o, o_sib, w)


def minus_expm1(v):
    series = jnp.ones_like(v)
    for k in range(9, 1, -1):
        series = 1.0 + series * v * (1.0 / k)
    return jnp.where(v > -0.5, -v * series, 1.0 - jnp.exp(v))


def gates_of(u, weights, cp, start):
    tokens = u.shape[0] * u.shape[1]
    flat = u.reshape(tokens, BLK)
    z = jnp.dot(flat, weights, preferred_element_type=F32)
    r = jax.nn.sigmoid(z[:, :BLK] + cp[5:6]).reshape(u.shape)
    ig = jax.nn.sigmoid(z[:, BLK:] + cp[6:7]).reshape(u.shape)
    la = -8.0 * r * cp[7:8][None]
    decayed = jnp.exp(la)
    rest = minus_expm1(2.0 * la)
    return r, ig, decayed, rest


def recurrence_kernel(xb, halo, weights, cp, starts, u_ref, a_ref, h_ref, c_ref, b_ref):
    rows, length = xb.shape[0], xb.shape[1]
    p = cp[...]
    us = []
    for row in range(rows):
        padded = jnp.concatenate([halo[row], xb[row].astype(F32)], axis=0)
        total = p[4:5] + p[0:1] * padded[8 : 8 + length]
        for k in range(1, 4):
            total = total + p[k : k + 1] * padded[8 - k : 8 - k + length]
        us.append(total.astype(BF16))
    u = jnp.stack(us)
    u_ref[...] = u
    start = starts[...]
    start = jnp.concatenate([start, start], axis=2)
    r, ig, decayed, rest = gates_of(u, weights[...], p, start)
    a_ref[...] = decayed * (1.0 - start)
    b_ref[...] = jnp.where(start > 0.5, 1.0, jnp.sqrt(rest)) * ig * u.astype(F32)

    def eight(i, carry):
        at = pl.ds(pl.multiple_of(i * 8, 8), 8)
        out = []
        for row in range(rows):
            h, c = carry[row]
            a, b = a_ref[row, at, :], b_ref[row, at, :]
            hs, cs = [], []
            for j in range(8):
                h = a[j : j + 1] * h + b[j : j + 1]
                c = a[j : j + 1] * c
                hs.append(h)
                cs.append(c)
            h_ref[row, at, :] = jnp.concatenate(hs, axis=0)
            c_ref[row, at, :] = jnp.concatenate(cs, axis=0)
            out.append((h, c))
        return tuple(out)

    zero, one = jnp.zeros((1, BLK), F32), jnp.ones((1, BLK), F32)
    lax.fori_loop(0, length // 8, eight, ((zero, one),) * rows)


def recurrence(xb, halo, weights, cp, starts):
    rows, length, channels = xb.shape
    wide = pl.BlockSpec((rows, length, BLK), lambda h: (0, 0, h))
    return pl.pallas_call(
        recurrence_kernel,
        grid=(channels // BLK,),
        in_specs=[
            wide,
            pl.BlockSpec((rows, 8, BLK), lambda h: (0, 0, h)),
            pl.BlockSpec((BLK, 2 * BLK), lambda h: (h, 0)),
            pl.BlockSpec((cp.shape[0], BLK), lambda h: (0, h)),
            pl.BlockSpec(starts.shape, lambda h: (0, 0, 0)),
        ],
        out_specs=[wide] * 4,
        out_shape=[jax.ShapeDtypeStruct(xb.shape, BF16)] + [jax.ShapeDtypeStruct(xb.shape, F32)] * 3,
        scratch_shapes=[pltpu.VMEM((rows, length, BLK), F32)],
        compiler_params=pltpu.CompilerParams(vmem_limit_bytes=40 << 20),
        cost_estimate=pl.CostEstimate(flops=4 * 10**8, bytes_accessed=6 * 10**6, transcendentals=2 * 10**6),
        name="recurrence",
    )(xb, halo, weights, cp, starts)


def gelu_parts(v):
    inner = 0.7978845608028654 * (v + 0.044715 * v * v * v)
    t = jnp.tanh(inner)
    value = 0.5 * v * (1.0 + t)
    slope = 0.5 * (1.0 + t) + 0.5 * v * (1.0 - t * t) * 0.7978845608028654 * (1.0 + 3.0 * 0.044715 * v * v)
    return value, slope


def adjoint_kernel(do, h_ref, y_ref, a_ref, dy_ref, lam_ref, c_ref, dh_ref):
    rows, length = do.shape[0], do.shape[1]
    value, slope = gelu_parts(y_ref[...])
    dy_ref[...] = (do[...] * h_ref[...] * slope).astype(BF16)
    dh_ref[...] = do[...] * value

    def eight(step, carry):
        i = length // 8 - 1 - step
        at = pl.ds(pl.multiple_of(i * 8, 8), 8)
        out = []
        for row in range(rows):
            ahead, c = carry[row]
            a, d = a_ref[row, at, :], dh_ref[row, at, :]
            ls, cs = [None] * 8, [None] * 8
            for j in range(7, -1, -1):
                lam = d[j : j + 1] + ahead
                ls[j], cs[j] = lam, c
                ahead = a[j : j + 1] * lam
                c = a[j : j + 1] * c
            lam_ref[row, at, :] = jnp.concatenate(ls, axis=0)
            c_ref[row, at, :] = jnp.concatenate(cs, axis=0)
            out.append((ahead, c))
        return tuple(out)

    zero, one = jnp.zeros((1, BLK), F32), jnp.ones((1, BLK), F32)
    lax.fori_loop(0, length // 8, eight, ((zero, one),) * rows)


def adjoint(do, h, ypre, a):
    rows, length, channels = do.shape
    wide = pl.BlockSpec((rows, length, BLK), lambda i: (0, 0, i))
    return pl.pallas_call(
        adjoint_kernel,
        grid=(channels // BLK,),
        in_specs=[wide] * 4,
        out_specs=[wide] * 3,
        out_shape=[jax.ShapeDtypeStruct(do.shape, BF16)] + [jax.ShapeDtypeStruct(do.shape, F32)] * 2,
        scratch_shapes=[pltpu.VMEM((rows, length, BLK), F32)],
        compiler_params=pltpu.CompilerParams(vmem_limit_bytes=40 << 20),
        cost_estimate=pl.CostEstimate(flops=10**7, bytes_accessed=9 * 10**6, transcendentals=10**6),
        name="adjoint",
    )(do, h, ypre, a)


def gates_back_kernel(lam_ref, c_ref, inc, h_ref, h_in, u_ref, weights, cp, starts, du_ref, dw_ref, sums_ref):
    rows, length = u_ref.shape[0], u_ref.shape[1]
    tokens = rows * length
    p = cp[...]
    u = u_ref[...]
    uf = u.astype(F32)
    start = starts[...]
    start = jnp.concatenate([start, start], axis=2)
    w = weights[...]
    r, ig, decayed, rest = gates_of(u, w, p, start)
    mult = jnp.where(start > 0.5, 1.0, jnp.sqrt(rest))
    lam = lam_ref[...] + c_ref[...] * inc[...]
    before = jnp.stack([jnp.concatenate([h_in[row], h_ref[row][: length - 1]], axis=0) for row in range(rows)])
    keep = 1.0 - start
    d_la = lam * before * decayed * keep - jnp.where(
        start > 0.5, 0.0, lam * ig * uf * decayed * decayed * lax.rsqrt(jnp.where(start > 0.5, 1.0, rest))
    )
    dpa = d_la * (-8.0 * p[7:8][None]) * r * (1.0 - r)
    direct = lam * mult
    dpi = direct * uf * ig * (1.0 - ig)
    d_decay = d_la * (8.0 * p[8:9][None]) * r
    dz = jnp.concatenate(
        [dpa.reshape(tokens, BLK).astype(BF16), dpi.reshape(tokens, BLK).astype(BF16)], axis=1
    )
    back = lax.dot_general(dz, w, (((1,), (1,)), ((), ())), preferred_element_type=F32)
    du_ref[...] = (direct * ig + back.reshape(u.shape)).astype(BF16)
    dw_ref[...] = lax.dot_general(
        u.reshape(tokens, BLK), dz, (((0,), (0,)), ((), ())), preferred_element_type=F32
    )
    zero = jnp.zeros((5, BLK), F32)
    sums_ref[...] = jnp.concatenate(
        [jnp.sum(v.reshape(tokens, BLK), axis=0, keepdims=True) for v in (dpa, dpi, d_decay)] + [zero], axis=0
    )


def gates_back(lam, coef, inc, h, h_in, u, weights, cp, starts):
    rows, length, channels = u.shape
    wide = pl.BlockSpec((rows, length, BLK), lambda i: (0, 0, i))
    line = pl.BlockSpec((rows, 1, BLK), lambda i: (0, 0, i))
    square = pl.BlockSpec((BLK, 2 * BLK), lambda i: (i, 0))
    return pl.pallas_call(
        gates_back_kernel,
        grid=(channels // BLK,),
        in_specs=[
            wide, wide, line, wide, line, wide, square,
            pl.BlockSpec((cp.shape[0], BLK), lambda i: (0, i)),
            pl.BlockSpec(starts.shape, lambda i: (0, 0, 0)),
        ],
        out_specs=[wide, square, pl.BlockSpec((8, BLK), lambda i: (0, i))],
        out_shape=[
            jax.ShapeDtypeStruct(u.shape, BF16),
            jax.ShapeDtypeStruct((channels, 2 * BLK), F32),
            jax.ShapeDtypeStruct((8, channels), F32),
        ],
        compiler_params=pltpu.CompilerParams(vmem_limit_bytes=40 << 20),
        cost_estimate=pl.CostEstimate(flops=12 * 10**8, bytes_accessed=9 * 10**6, transcendentals=2 * 10**6),
        name="gates_back",
    )(lam, coef, inc, h, h_in, u, weights, cp, starts)


def log1p_small(e):
    series = jnp.ones_like(e) * (1.0 / 14)
    for k in range(13, 0, -1):
        series = 1.0 / k - e * series
    return jnp.where(e < 0.25, e * series, jnp.log(1.0 + e))


def front_kernel(n, *refs):
    (
        wx, wy, wo, gs, wg, wu, wd, rows_in, grad, lengths, resets, spread_r, pick_r, spread_d, pick_d,
        o_xy, o_out, o_gates, o_cp, o_gains, o_gu, o_d, o_cot, o_starts, o_ypre, o_u, o_a, o_h, o_hin, o_xb, o_before,
        o_x1, o_n2, o_n1t, o_ot, o_hidden, o_gate, o_up, o_pd,
        v_xy, v_out, v_gs, v_gates, v_rows, v_cot, v_starts, v_cp, v_gains, v_n1, v_n1t, v_xb, v_ypre, v_halo, v_u, v_a,
        v_b, v_h, v_c, v_carry, v_o, v_osib, v_ot, v_part, v_theirs, v_psib, v_x1, v_n2, v_w, v_hidden, v_gu, v_pd, v_wd,
        local_sem, send_sem, recv_sem, load_sem, store_sem, pd_sem,
    ) = refs
    dp, x = lax.axis_index("dp"), lax.axis_index("tp")
    chip, core = dp // 2, dp % 2
    other = 1 - core
    pos = place_of(chip, n)
    half = n // 2
    nxt = (chip_at((pos + 1) % n, n) * 2 + core, x)
    prv = (chip_at((pos + n - 1) % n, n) * 2 + core, x)
    sib = (chip * 2 + other, x)
    over = (dp, 1 - x)
    copies = Copies(local_sem, send_sem, recv_sem)
    send, stay = copies.send, copies.stay
    tokens, width = rows_in.shape
    rec = wx.shape[1]
    rh = rec // 2
    own, own_d = wo.shape[0], wx.shape[0]
    fh = wg.shape[1] // 2
    own_f = wg.shape[0]
    kept, every = [], []

    def put(src, dst):
        kept.append(stay(src, dst))

    def give(src, dst, device):
        copy = send(src, dst, device)
        every.append(copy)
        return copy

    def land(group):
        for copy in group:
            copy.wait_recv()

    class Chain:
        def __init__(self, pieces, arrived=None):
            self.pieces, self.arrived, self.hop = pieces, arrived, 0
            self.ways = ((nxt, n - 1), (prv, 1))
            self.moving = ([], [])

        def start(self, part):
            self.hop = 1
            for ref, own_core in self.pieces(pos):
                if own_core == part:
                    for way, (device, _) in enumerate(self.ways):
                        self.moving[way].append(give(ref, ref, device))
                    if self.arrived:
                        self.arrived(ref)

        def advance(self):
            self.hop += 1
            fresh = ([], [])
            blocks = [self.pieces((pos + back * (self.hop - 1)) % n) for _, back in self.ways]
            for i in range(len(blocks[0])):
                for way, (device, _) in enumerate(self.ways):
                    ref, own_core = blocks[way][i]
                    self.moving[way][i].wait_recv()
                    if self.hop < half or own_core == (way == 0):
                        fresh[way].append(give(ref, ref, device))
                    if self.arrived:
                        self.arrived(ref)
            self.moving = fresh

        def to_last(self):
            while self.hop < half:
                self.advance()

        def finish(self):
            block = self.pieces((pos + half) % n)
            for way in (0, 1):
                refs = [ref for ref, own_core in block if own_core == (way == 0)]
                for copy, ref in zip(self.moving[way], refs):
                    copy.wait_recv()
                    if self.arrived:
                        self.arrived(ref)

    parts = [(wx, v_xy.at[chip, core, x, :, pl.ds(0, rh)]), (wy, v_xy.at[chip, core, x, :, pl.ds(rh, rh)])]
    mine = [stay(half_cols(src, core), slot) for src, slot in parts]
    mine.append(stay(half_cols(wo, core), v_out.at[heads_first(chip, core, n), core, x]))
    mine.append(stay(gs, v_gs.at[core, chip, x]))
    greet([nxt, prv, sib, over])
    pair = [give(half_cols(src, other), slot, sib) for src, slot in parts]
    pair.append(give(half_cols(wo, other), v_out.at[heads_first(chip, other, n), core, x], sib))

    crossed, held = [], []

    def rec_pieces(place):
        c = chip_at(place, n)
        at = heads_first(c, core, n)
        rows = (own + PAD) // 2
        return [
            (v_xy.at[c, core, x], True), (v_gs.at[core, c, x, pl.ds(0, rows)], True), (v_out.at[at, core, x], True),
            (v_xy.at[c, other, x], False), (v_gs.at[core, c, x, pl.ds(rows, rows)], False),
            (v_out.at[at, other, x], False),
        ]

    def rec_arrived(ref):
        if ref.shape[1] == width // 2:
            held.append(ref)
        else:
            crossed.append(give(ref, ref, over))

    rec_chain = Chain(rec_pieces, rec_arrived)
    gu = Chain(lambda place: [
        (o_gu.at[chip_at(place, n), core], True), (o_gu.at[chip_at(place, n), other], False)
    ])
    down = Chain(lambda place: [(o_d.at[place, core], True), (o_d.at[place, other], False)])
    for copy in mine:
        copy.wait()
    rec_chain.start(True)
    land(pair)
    rec_chain.start(False)
    parts = [(wg, o_gu.at[chip, core, :, pl.ds(0, fh)]), (wu, o_gu.at[chip, core, :, pl.ds(fh, fh)])]
    late = [give(half_cols(src, other), slot, sib) for src, slot in parts]
    plain = [stay(half_cols(src, core), slot) for src, slot in parts]
    late += [give(wd.at[pl.ds(pl.multiple_of(other * fh, 128), fh)], v_wd.at[1], sib), give(rows_in, v_rows.at[1], sib)]
    plain += [stay(wd.at[pl.ds(pl.multiple_of(core * fh, 128), fh)], v_wd.at[0]), stay(rows_in, v_rows.at[0])]
    cotangent = stay(grad, v_n2.at[0])

    lane = lax.broadcasted_iota(jnp.int32, (1, tokens), 1) + x * tokens
    begins = jnp.where((resets[...] > 0) | (lane == 0), 1.0, 0.0)
    v_starts[0] = jnp.broadcast_to(begins, (tokens, tokens)).T
    late.append(give(v_starts.at[0], v_starts.at[1], sib))
    valid = lax.broadcasted_iota(jnp.int32, (tokens, 1), 0) + x * tokens < lengths[0]
    valid = jnp.where(valid, 1.0, 0.0)
    cotangent.wait()
    size = width // n
    for i in range(n):
        from_chip = chip_at(i, n) * size
        v_cot[0, :, i * size : (i + 1) * size] = (v_n2[0, :, from_chip : from_chip + size].astype(F32) * valid).astype(BF16)
    late.append(give(v_cot.at[0], v_cot.at[2], sib))
    rec_chain.to_last()
    land(late)
    for copy in plain:
        copy.wait()
    gu.start(True)
    gu.start(False)
    rec_chain.finish()
    for i in range(fh // 128):
        at = pl.ds(i * 128, 128)
        for which in (0, 1):
            v_pd[which, 0:own_f, at] = v_wd[which, at, :].astype(F32).T.astype(BF16)
    turned = [stay(v_pd.at[which, pl.ds(0, own_f)], o_d.at[pos, place]) for which, place in ((0, core), (1, other))]
    swap = [give(v_gs.at[core, :, x], v_gs.at[core, :, x], sib)]
    put(v_starts, o_starts)
    if half > 3:
        gu.advance()
    land(crossed)
    swap.append(give(v_gs.at[core, :, 1 - x], v_gs.at[core, :, 1 - x], sib))
    outs = []

    def cross_held(count):
        for _ in range(min(count, len(held))):
            ref = held.pop(0)
            outs.append(give(ref, ref, over))

    cross_held(4)
    put(v_xy, o_xy)
    land(swap)

    small = v_gs[:, :, :, own : own + PAD, :128].reshape(4 * n * PAD, 128)
    spread = jnp.dot(small, spread_r[...], preferred_element_type=F32).reshape(4 * n, PAD, rh)
    heads = pick_r[:, pl.ds(pl.multiple_of(core * rh, 128), rh)]
    lines = jnp.sum(spread[:, :8] * heads[:, None, :], axis=0)
    decay = lines[7:8]
    e = jnp.exp(-jnp.abs(decay))
    v_cp[0:8, :] = lines
    v_cp[7:8, :] = jnp.maximum(-decay, 0.0) + log1p_small(e)
    v_cp[8:16, :] = jnp.broadcast_to(jax.nn.sigmoid(-decay), (8, rh))
    for i in range(width // WIDE):
        at = pl.ds(i * WIDE, WIDE)
        wide = jnp.dot(small, spread_d[:, at], preferred_element_type=F32).reshape(4 * n, PAD, WIDE)
        v_gains[:, at] = jnp.sum(wide[:, 8:] * pick_d[:, at][:, None, :], axis=0)
    for i in range(2 * n):
        v_gates[i * own : (i + 1) * own, :] = v_gs[(i // 2) % 2, core * half + i // 4, i % 2, 0:own, :]
    put(v_cp, o_cp)
    put(v_gains, o_gains)
    put(v_gates, o_gates)

    values = v_rows[...].astype(F32)
    scale = lax.rsqrt(jnp.mean(values * values, axis=-1, keepdims=True) + EPS)
    v_n1[...] = (values * scale * v_gains[0:1, :]).astype(BF16).reshape(2 * tokens, width)

    def project_x(i, _):
        at = pl.ds(pl.multiple_of(i * BLK, BLK), BLK)
        w = v_xy[:, :, :, :, at].reshape(width, BLK)
        v_xb[:, :, at] = jnp.dot(v_n1[...], w, preferred_element_type=F32).astype(BF16).reshape(2, tokens, BLK)
        return 0

    def project_y(i, _):
        at = pl.ds(pl.multiple_of(i * BLK, BLK), BLK)
        w = v_xy[:, :, :, :, pl.ds(pl.multiple_of(rh + i * BLK, BLK), BLK)].reshape(width, BLK)
        v_ypre[:, :, at] = jnp.dot(v_n1[...], w, preferred_element_type=F32).reshape(2, tokens, BLK)
        return 0

    lax.fori_loop(0, rh // BLK, project_x, 0)
    halo = give(v_xb.at[:, pl.ds(tokens - 16, 16)], v_halo, over)
    cross_held(4)
    put(v_xb, o_xb)
    if half > 3:
        gu.advance()
    lax.fori_loop(0, rh // BLK, project_y, 0)
    put(v_ypre, o_ypre)
    chips_n = BLK // (4 * own_d)

    def turn_n1(i, _):
        at = pl.ds(pl.multiple_of(i * BLK, BLK), BLK)
        turned = v_n1[:, at].astype(F32).T.astype(BF16)
        v_n1t[pl.ds(i * chips_n, chips_n)] = turned.reshape(chips_n, 2, 2, own_d, 2 * tokens)
        return 0

    lax.fori_loop(0, width // BLK, turn_n1, 0)
    halo.wait_recv()
    v_halo[...] = jnp.where(x == 0, jnp.zeros_like(v_halo), v_halo[...])
    put(v_halo, o_before)
    put(v_n1t.at[:, :, x], o_n1t.at[:, :, :, pl.ds(0, 2 * tokens)])

    def head(i, _):
        at = pl.ds(pl.multiple_of(i * BLK, BLK), BLK)
        p = v_cp[:, at]
        us = []
        for row in range(2):
            padded = jnp.concatenate([v_halo[row, :, at].astype(F32)[8:], v_xb[row, :, at].astype(F32)], axis=0)
            total = p[4:5] + p[0:1] * padded[8 : 8 + tokens]
            for k in range(1, 4):
                total = total + p[k : k + 1] * padded[8 - k : 8 - k + tokens]
            us.append(total.astype(BF16))
        u = jnp.stack(us)
        v_u[:, :, at] = u
        start = v_starts[...]
        start = jnp.concatenate([start, start], axis=2)
        _, ig, decayed, rest = gates_of(u, v_gates[at, :], p, start)
        v_a[:, :, at] = decayed * (1.0 - start)
        v_b[...] = jnp.where(start > 0.5, 1.0, jnp.sqrt(rest)) * ig * u.astype(F32)

        def eight(j, carry):
            rows8 = pl.ds(pl.multiple_of(j * 8, 8), 8)
            out = []
            for row in range(2):
                h, c = carry[row]
                a, b = v_a[row, rows8, at], v_b[row, rows8, :]
                hs, cs = [], []
                for k in range(8):
                    h = a[k : k + 1] * h + b[k : k + 1]
                    c = a[k : k + 1] * c
                    hs.append(h)
                    cs.append(c)
                v_h[row, rows8, at] = jnp.concatenate(hs, axis=0)
                v_c[row, rows8, at] = jnp.concatenate(cs, axis=0)
                out.append((h, c))
            return tuple(out)

        zero, one = jnp.zeros((1, BLK), F32), jnp.ones((1, BLK), F32)
        lax.fori_loop(0, tokens // 8, eight, ((zero, one),) * 2)
        return 0

    lax.fori_loop(0, rh // BLK, head, 0)
    carry = give(v_h.at[:, pl.ds(tokens - 8, 8)], v_carry, over)
    put(v_u, o_u)
    put(v_a, o_a)
    carry.wait_recv()
    carry.wait_send()
    cross_held(len(held))
    v_carry[...] = jnp.where(x == 0, jnp.zeros_like(v_carry), v_carry[...])
    put(v_carry, o_hin)

    def output(i, _):
        at = pl.ds(pl.multiple_of(i * BLK, BLK), BLK)
        h = v_h[:, :, at] + v_c[:, :, at] * v_carry[:, 7:8, at]
        v_h[:, :, at] = h
        value, _ = gelu_parts(v_ypre[:, :, at])
        v_o[:, :, at] = (h * value).astype(BF16)
        return 0

    lax.fori_loop(0, rh // BLK, output, 0)
    o_pair = give(v_o, v_osib, sib)
    put(v_h, o_h)
    gu.to_last()
    for copy in turned:
        copy.wait()
    down.start(True)
    down.start(False)
    o_pair.wait_recv()
    land(outs)
    put(v_out, o_out)

    def project_row(row, ref):
        def tile(i, _):
            at = pl.ds(pl.multiple_of(i * BLK, BLK), BLK)
            w0 = v_out[0:half, :, :, :, at].reshape(rh, BLK)
            w1 = v_out[half:n, :, :, :, at].reshape(rh, BLK)
            ref[:, at] = jnp.dot(v_o[row], w0, preferred_element_type=F32) + jnp.dot(
                v_osib[1 - row], w1, preferred_element_type=F32
            )
            return 0

        lax.fori_loop(0, width // 2 // BLK, tile, 0)

    project_row(1, v_theirs)
    x1_pair = give(v_theirs, v_psib, sib)
    project_row(0, v_part)
    x1_pair.wait_recv()
    at_mine = pl.ds(pl.multiple_of(core * (width // 2), 128), width // 2)
    at_theirs = pl.ds(pl.multiple_of(other * (width // 2), 128), width // 2)
    v_x1[:, at_mine] = v_rows[0, :, at_mine].astype(F32) + v_part[...]
    v_x1[:, at_theirs] = v_rows[0, :, at_theirs].astype(F32) + v_psib[...]
    put(v_x1, o_x1)
    x1 = v_x1[...]
    scale = lax.rsqrt(jnp.mean(x1 * x1, axis=-1, keepdims=True) + EPS)
    v_n2[0] = (x1 * scale * v_gains[1:2, :]).astype(BF16)
    n2_over = give(v_n2.at[0], v_n2.at[1], over)
    n2_pair = give(v_n2.at[0], v_n2.at[2], sib)
    cot_over = give(v_cot.at[0], v_cot.at[1], over)
    n1_over = give(v_n1t.at[:, :, 1 - x], o_n1t.at[:, :, :, pl.ds(2 * tokens, 2 * tokens)], over)

    chips_o = 640 // (4 * own)

    def turn_o(i, _):
        at = pl.ds(pl.multiple_of(i * 640, 128), 640)
        here = v_o[:, :, at].astype(F32).reshape(2 * tokens, 640).T.astype(BF16)
        v_ot[pl.ds(i * chips_o, chips_o)] = here.reshape(chips_o, 2, 2, own, 2 * tokens)
        there = jnp.concatenate([v_osib[1, :, at], v_osib[0, :, at]], axis=0).astype(F32).T.astype(BF16)
        v_ot[pl.ds(half + i * chips_o, chips_o)] = there.reshape(chips_o, 2, 2, own, 2 * tokens)
        return 0

    lax.fori_loop(0, rh // 640, turn_o, 0)
    o_over = give(v_ot.at[:, :, 1 - x], o_ot.at[:, :, :, pl.ds(2 * tokens, 2 * tokens)], over)
    put(v_ot.at[:, :, x], o_ot.at[:, :, :, pl.ds(0, 2 * tokens)])

    tile = 128
    steps = fh // tile

    def loads(t, slot):
        first = pl.ds(pl.multiple_of(t * tile, tile), tile)
        second = pl.ds(pl.multiple_of(fh + t * tile, tile), tile)
        return [
            pltpu.make_async_copy(o_gu.at[:, :, :, first], v_w.at[slot, :, :, :, pl.ds(0, tile)], load_sem.at[slot, 0]),
            pltpu.make_async_copy(
                o_gu.at[:, :, :, second], v_w.at[slot, :, :, :, pl.ds(tile, tile)], load_sem.at[slot, 1]
            ),
        ]

    def stores(t, slot):
        at = pl.ds(pl.multiple_of(t * tile, tile), tile)
        return [
            pltpu.make_async_copy(v_gu.at[slot, :, pl.ds(0, tile)], o_gate.at[:, at], store_sem.at[slot, 0]),
            pltpu.make_async_copy(v_gu.at[slot, :, pl.ds(tile, tile)], o_up.at[:, at], store_sem.at[slot, 1]),
        ]

    gu.finish()
    for copy in loads(0, 0):
        copy.start()
    n2_pair.wait_recv()
    n2_over.wait_recv()
    n2_last = give(v_n2.at[1], v_n2.at[3], sib)
    n2_last.wait_recv()
    if half > 3:
        down.advance()
    put(v_n2, o_n2)

    def hidden_tile(t, _):
        slot = t % 2
        for copy in loads(t, slot):
            copy.wait()

        @pl.when(t + 1 < steps)
        def _():
            for copy in loads(t + 1, 1 - slot):
                copy.start()

        @pl.when(t >= 2)
        def _():
            for copy in stores(t - 2, slot):
                copy.wait()

        w = v_w[slot].reshape(width, 2 * tile)
        v_gu[slot] = jnp.dot(v_n2[...].reshape(4 * tokens, width), w, preferred_element_type=F32)
        for copy in stores(t, slot):
            copy.start()
        value, _ = gelu_parts(v_gu[slot, :, 0:tile])
        v_hidden[:, pl.ds(pl.multiple_of(t * tile, tile), tile)] = (value * v_gu[slot, :, tile:]).astype(BF16)
        return 0

    lax.fori_loop(0, steps, hidden_tile, 0)
    put(v_hidden, o_hidden)
    cot_over.wait_recv()
    cot_last = give(v_cot.at[1], v_cot.at[3], sib)
    if half > 3:
        down.advance()
    cot_last.wait_recv()
    put(v_cot, o_cot)

    def pd_store(t, slot):
        return pltpu.make_async_copy(v_pd.at[slot], o_pd.at[pl.ds(pl.multiple_of(t * BLK, BLK), BLK)], pd_sem.at[slot])

    def down_tile(t, _):
        slot = t % 2

        @pl.when(t >= 2)
        def _():
            pd_store(t - 2, slot).wait()

        left = v_cot[:, :, pl.ds(pl.multiple_of(t * BLK, BLK), BLK)].reshape(4 * tokens, BLK)
        v_pd[slot] = lax.dot_general(
            left, v_hidden[...], (((0,), (0,)), ((), ())), preferred_element_type=F32
        ).astype(BF16)
        pd_store(t, slot).start()
        return 0

    lax.fori_loop(0, width // BLK, down_tile, 0)
    down.to_last()
    for t in (steps - 2, steps - 1):
        for copy in stores(t, t % 2):
            copy.wait()
    for t in (width // BLK - 2, width // BLK - 1):
        pd_store(t, t % 2).wait()
    down.finish()
    land([n1_over, o_over])
    for copy in kept:
        copy.wait()
    for copy in every:
        if copy is not carry:
            copy.wait_send()


def front(n, wx, wy, wo, gs, wg, wu, wd, rows_in, grad, lengths, resets):
    rec, f = wx.shape[1], wg.shape[1]
    own, own_d, rows_f = wo.shape[0], wx.shape[0], wg.shape[0]
    rh, fh = rec // 2, f // 2
    tokens, width = rows_in.shape
    half = n // 2
    row = np.arange(4 * n)
    index = (row // 2) % n * 4 + row // (2 * n) * 2 + row % 2
    lane_r, lane_d, short = np.arange(rec), np.arange(width), np.arange(128)[:, None]
    spread_r = (lane_r[None, :rh] % own == short).astype(jnp.bfloat16)
    spread_d = (lane_d[None] % own_d == short).astype(jnp.bfloat16)
    pick_r = (index[:, None] == lane_r[None] // own).astype(np.float32)
    pick_d = (index[:, None] == lane_d[None] // own_d).astype(np.float32)
    outs = dict(
        w_xy=((n, 2, 2, own_d, rec), BF16),
        w_o=((n, 2, 2, own, width // 2), BF16),
        gates=((rh, WIDE), BF16),
        cp=((16, rh), F32),
        gains=((8, width), F32),
        w_gu=((n, 2, rows_f, f), BF16),
        w_d=((n, 2, rows_f, fh), BF16),
        cot=((4, tokens, width), BF16),
        starts=((2, tokens, 128), F32),
        ypre=((2, tokens, rh), F32),
        u=((2, tokens, rh), BF16),
        a=((2, tokens, rh), F32),
        h=((2, tokens, rh), F32),
        h_in=((2, 8, rh), F32),
        xb=((2, tokens, rh), BF16),
        before=((2, 16, rh), BF16),
        x1=((tokens, width), F32),
        n2=((4, tokens, width), BF16),
        n1_t=((n, 2, own_d, 4 * tokens), BF16),
        o_t=((n, 2, own, 4 * tokens), BF16),
        hidden=((4 * tokens, fh), BF16),
        gate=((4 * tokens, fh), F32),
        up=((4 * tokens, fh), F32),
        part_d=((width, fh), BF16),
    )
    state = (2, tokens, rh)
    scratch = [
        ((n, 2, 2, own_d, rec), BF16), ((n, 2, 2, own, width // 2), BF16), ((2, n, 2) + gs.shape, BF16),
        ((rh, WIDE), BF16), ((2, tokens, width), BF16), ((4, tokens, width), BF16), ((2, tokens, 128), F32),
        ((16, rh), F32), ((8, width), F32), ((2 * tokens, width), BF16), ((n, 2, 2, own_d, 2 * tokens), BF16),
        (state, BF16), (state, F32), ((2, 16, rh), BF16), (state, BF16), (state, F32),
        ((2, tokens, BLK), F32), (state, F32), (state, F32), ((2, 8, rh), F32), (state, BF16), (state, BF16),
        ((n, 2, 2, own, 2 * tokens), BF16), ((tokens, width // 2), F32), ((tokens, width // 2), F32),
        ((tokens, width // 2), F32), ((tokens, width), F32), ((4, tokens, width), BF16),
        ((2, n, 2, rows_f, BLK), BF16), ((4 * tokens, fh), BF16), ((2, 4 * tokens, BLK), F32), ((2, BLK, fh), BF16), ((2, fh, own_d * 2), BF16),
    ]
    count = 9 + (6 * n - 6) + 2 * (2 * n - 2) + 6 * n + 2 + 12
    dma = pltpu.SemaphoreType.DMA
    result = pl.pallas_call(
        functools.partial(front_kernel, n),
        out_shape=[jax.ShapeDtypeStruct(shape, kind) for shape, kind in outs.values()],
        in_specs=[pl.BlockSpec(memory_space=pl.ANY)] * 9
        + [pl.BlockSpec(memory_space=pltpu.SMEM)]
        + [pl.BlockSpec(memory_space=pltpu.VMEM)] * 5,
        out_specs=[pl.BlockSpec(memory_space=pl.ANY)] * len(outs),
        scratch_shapes=[pltpu.VMEM(shape, kind) for shape, kind in scratch]
        + [dma((32,)), dma((count,)), dma((count,)), dma((2, 2)), dma((2, 2)), dma((2,))],
        compiler_params=pltpu.CompilerParams(
            collective_id=2, has_side_effects=True, vmem_limit_bytes=60 << 20
        ),
        name="front",
    )(wx, wy, wo, gs, wg, wu, wd, rows_in, grad, lengths, resets, spread_r, pick_r, spread_d, pick_d)
    return dict(zip(outs, result))


def ff_back_kernel(n, *refs):
    (
        part_d, cot, w_d, gate, up, n2, w_gu,
        g_d, d_n2, o_part,
        v_pd, v_cot, v_n2, v_wd, v_gate, v_up, v_dgu, v_sib, v_wgu, v_dn2, v_pair, v_plane, v_part, r_d, handed,
        local_sem, send_sem, recv_sem, down_sem, up_sem, part_sem,
    ) = refs
    dp, x = lax.axis_index("dp"), lax.axis_index("tp")
    chip, core = dp // 2, dp % 2
    pos = place_of(chip, n)
    half = n // 2
    nxt = (chip_at((pos + 1) % n, n) * 2 + core, x)
    prv = (chip_at((pos + n - 1) % n, n) * 2 + core, x)
    sib = (dp + 1 - 2 * core, x)
    over = (dp, 1 - x)
    copies = Copies(local_sem, send_sem, recv_sem)
    send, stay = copies.send, copies.stay
    rows, fh = v_pd.shape[2], v_pd.shape[3]
    count, width = v_cot.shape
    tokens = count // 4
    products = stay(part_d, v_pd)
    rest = [stay(cot, v_cot), stay(n2, v_n2)]
    greet([nxt, prv, sib, over])

    chains = [(part, way) for part in (0, 1) for way in (0, 1)]
    coming, sent, left = {}, [], {}

    def forward():
        for part, way in chains:
            first = half if way == part else half - 1
            k = left.get((part, way), first)
            if k == 0:
                continue
            device, sign = ((nxt, 1), (prv, n - 1))[way]
            source = (part_d if k == first else v_pd).at[(pos + sign * k) % n, part]
            if k < first:
                coming[part, way].wait_recv()
                got = r_d.at[part, way, k]
                got[...] = (got[...].astype(F32) + source[...].astype(F32)).astype(BF16)
                source = got
            copy = send(source, r_d.at[part, way, k - 1], device)
            coming[part, way] = copy
            sent.append(copy)
            left[part, way] = k - 1

    forward()

    def down_loads(t, slot):
        at = pl.ds(pl.multiple_of(t * BLK, BLK), BLK)
        pairs = ((w_d, v_wd), (gate, v_gate), (up, v_up))
        return [
            pltpu.make_async_copy(src.at[:, at], dst.at[slot], down_sem.at[slot, i])
            for i, (src, dst) in enumerate(pairs)
        ]

    steps = fh // BLK
    for copy in down_loads(0, 0):
        copy.start()
    for copy in rest + [products]:
        copy.wait()

    def cotangent_tile(t, _):
        slot = t % 2
        for copy in down_loads(t, slot):
            copy.wait()

        @pl.when(t + 1 < steps)
        def _():
            for copy in down_loads(t + 1, 1 - slot):
                copy.start()

        d_hidden = jnp.dot(v_cot[...], v_wd[slot], preferred_element_type=F32)
        act, slope = gelu_parts(v_gate[slot])
        v_dgu[:, pl.ds(pl.multiple_of(t * BLK, BLK), BLK)] = (d_hidden * v_up[slot] * slope).astype(BF16)
        v_dgu[:, pl.ds(pl.multiple_of(fh + t * BLK, BLK), BLK)] = (d_hidden * act).astype(BF16)
        return 0

    def up_loads(t, slot):
        at = pl.ds(pl.multiple_of(t * BLK, BLK), BLK)
        return pltpu.make_async_copy(w_gu.at[at], v_wgu.at[slot], up_sem.at[slot])

    up_loads(0, 0).start()
    lax.fori_loop(0, steps, cotangent_tile, 0)
    swap = [
        send(v_dgu.at[pl.ds(0, 2 * tokens)], v_sib.at[pl.ds(2 * tokens, 2 * tokens)], sib),
        send(v_dgu.at[pl.ds(2 * tokens, 2 * tokens)], v_sib.at[pl.ds(0, 2 * tokens)], sib),
    ]

    def norm_tile(t, _):
        slot = t % 2
        up_loads(t, slot).wait()

        @pl.when(t + 1 < width // BLK)
        def _():
            up_loads(t + 1, 1 - slot).start()

        product = nt(v_dgu[...], v_wgu[slot]).astype(BF16)
        v_dn2[:, :, pl.ds(pl.multiple_of(t * BLK, BLK), BLK)] = product.reshape(4, tokens, BLK)
        return 0

    lax.fori_loop(0, width // BLK // 2, norm_tile, 0)
    forward()
    lax.fori_loop(width // BLK // 2, width // BLK, norm_tile, 0)
    pair = send(v_dn2.at[pl.ds(2, 2)], v_pair, sib)
    for copy in swap:
        copy.wait_recv()

    def part_store(i, slot):
        return pltpu.make_async_copy(
            v_part.at[slot], o_part.at[pl.ds(pl.multiple_of(i * rows, 8), rows)], part_sem.at[slot]
        )

    def part_tile(i, _):
        slot = i % 2

        @pl.when(i >= 2)
        def _():
            part_store(i - 2, slot).wait()

        at = pl.ds(pl.multiple_of(chip_at(i, n) * 2 * rows + core * rows, 128), rows)
        columns = v_n2[:, at]
        for j, ref in enumerate((v_dgu, v_sib)):
            product = lax.dot_general(columns, ref[...], (((0,), (0,)), ((), ())), preferred_element_type=F32)
            v_part[slot, :, 2 * fh * j : 2 * fh * (j + 1)] = product.astype(BF16)
        part_store(i, slot).start()
        return 0

    lax.fori_loop(0, n // 4, part_tile, 0)
    pair.wait_recv()
    for i in (1, 0):
        v_pair[i] = (v_dn2[i].astype(F32) + v_pair[i].astype(F32)).astype(BF16)
        if i == 1:
            plane = send(v_pair.at[1], v_plane, over)
    lax.fori_loop(n // 4, n // 2, part_tile, 0)
    forward()
    lax.fori_loop(n // 2, n, part_tile, 0)
    plane.wait_recv()
    d_n2[...] = v_pair[0].astype(F32) + v_plane[...].astype(F32)
    while any(left.values()):
        forward()
    for i in (n - 2, n - 1):
        part_store(i, i % 2).wait()

    at = pl.ds(pl.multiple_of(core * fh, 128), fh)
    totals = []
    for part in (0, 1):
        for way in (0, 1):
            coming[part, way].wait_recv()
        totals.append(v_pd[pos, part].astype(F32) + r_d[part, 0, 0].astype(F32) + r_d[part, 1, 0].astype(F32))
    for part in (0, 1):

        @pl.when(core == part)
        def _():
            g_d[:, at] = totals[part]
            handed[...] = totals[1 - part]

    last = send(handed, g_d.at[:, at], sib)
    last.wait_recv()
    for copy in sent + swap + [pair, plane, last]:
        copy.wait_send()


def ff_back(n, part_d, cot, w_d, gate, up, n2, w_gu):
    width, fh = part_d.shape
    count = cot.shape[0]
    tokens = count // 4
    rows = width // (2 * n)
    half = n // 2
    dma = pltpu.SemaphoreType.DMA
    scratch = [
        ((n, 2, rows, fh), BF16), ((count, width), BF16), ((count, width), BF16), ((2, width, BLK), BF16),
        ((2, count, BLK), F32), ((2, count, BLK), F32), ((count, 2 * fh), BF16), ((count, 2 * fh), BF16),
        ((2, BLK, 2 * fh), BF16), ((4, tokens, width), BF16), ((2, tokens, width), BF16), ((tokens, width), BF16),
        ((2, rows, 4 * fh), BF16), ((2, 2, half, rows, fh), BF16), ((rows, fh), F32),
    ]
    copies = 2 * (2 * half - 1) + 5
    return pl.pallas_call(
        functools.partial(ff_back_kernel, n),
        out_shape=[
            jax.ShapeDtypeStruct((rows, 2 * fh), F32),
            jax.ShapeDtypeStruct((tokens, width), F32),
            jax.ShapeDtypeStruct((n * rows, 4 * fh), BF16),
        ],
        in_specs=[pl.BlockSpec(memory_space=pl.ANY)] * 7,
        out_specs=[pl.BlockSpec(memory_space=pltpu.VMEM)] * 2 + [pl.BlockSpec(memory_space=pl.ANY)],
        scratch_shapes=[pltpu.VMEM(shape, kind) for shape, kind in scratch]
        + [dma((3,)), dma((copies,)), dma((copies,)), dma((2, 3)), dma((2,)), dma((2,))],
        compiler_params=pltpu.CompilerParams(
            collective_id=3, has_side_effects=True, vmem_limit_bytes=60 << 20
        ),
        name="ff_back",
    )(part_d.reshape(n, 2, rows, fh), cot, w_d, gate, up, n2, w_gu)


def finish_kernel(
    sums, x_sum, y_sum, out_sum, gates, vec,
    gate_ref, up_ref, x_ref, y_ref, out_ref, a_ref, i_ref, taps_ref, *lines,
):
    core = lax.axis_index("dp") % 2
    half = gate_ref.shape[1] // 2
    for first in (0, 1):

        @pl.when(core == first)
        def _():
            for i in (0, 1):
                start = (i != first) * 2 * half
                at = pl.ds(i * half, half)
                gate_ref[:, at] = sums[:, start : start + half].astype(F32)
                up_ref[:, at] = sums[:, start + half : start + 2 * half].astype(F32)

    x_ref[...] = x_sum[...]
    y_ref[...] = y_sum[...]
    out_ref[...] = out_sum[...]
    a_ref[...] = gates[:, :BLK]
    i_ref[...] = gates[:, BLK:]
    taps, own = taps_ref.shape
    taps_ref[...] = vec[0:taps, 0:own]
    for k, ref in enumerate(lines):
        ref[...] = vec[taps + k : taps + k + 1, 0 : ref.shape[1]]


def finish(sums, x_sum, y_sum, out_sum, gates, vec, taps):
    rows, cols = sums.shape
    own, own_d = out_sum.shape[0], x_sum.shape[0]
    steps = 2 if rows % 16 == 0 and own % 16 == 0 and own_d % 16 == 0 else 1

    def tiled(shape):
        return pl.BlockSpec((shape[0] // steps, shape[1]), lambda i: (i, 0))

    def fixed(shape):
        return pl.BlockSpec(shape, lambda i: (0, 0))

    big = [(rows, cols // 2)] * 2 + [x_sum.shape, y_sum.shape, out_sum.shape] + [(own, BLK)] * 2
    small = [(taps, own)] + [(1, own)] * 4 + [(1, own_d)] * 2
    return pl.pallas_call(
        finish_kernel,
        grid=(steps,),
        in_specs=[tiled(v.shape) for v in (sums, x_sum, y_sum, out_sum, gates)] + [fixed(vec.shape)],
        out_specs=[tiled(shape) for shape in big] + [fixed(shape) for shape in small],
        out_shape=[jax.ShapeDtypeStruct(shape, F32) for shape in big + small],
        compiler_params=pltpu.CompilerParams(vmem_limit_bytes=60 << 20),
        name="finish",
    )(sums, x_sum, y_sum, out_sum, gates, vec)


def nt(left, right):
    return lax.dot_general(left, right, (((1,), (1,)), ((), ())), preferred_element_type=F32)


def nn(left, right):
    return jnp.dot(left, right, preferred_element_type=F32)


def body(
    dp_size,
    layer_input, grad_out, lengths, resets, norm_gain, w_x, w_y, conv_w, conv_b, gate_a_w, gate_a_b,
    gate_i_w, gate_i_b, decay_param, w_out, mlp_gain, w_gate, w_up, w_down,
):
    n = dp_size // 2
    half = n // 2
    dp, x = lax.axis_index("dp"), lax.axis_index("tp")
    chip, core = dp // 2, dp % 2
    pos = place_of(chip, n)
    tokens, width = layer_input.shape[1], layer_input.shape[2]
    rec = w_x.shape[1]
    rh = rec // 2
    taps = conv_w.shape[0]
    own = rec // (2 * dp_size)
    own_d = width // (2 * dp_size)

    ring = [chip_at(i, n) for i in range(n)]
    up = [(ring[i] * 2 + c, ring[(i + 1) % n] * 2 + c) for i in range(n) for c in range(2)]
    down = [(b, a) for a, b in up]
    lanes = [[chip_id * 2 + c for chip_id in ring] for c in range(2)]
    pairs = [(d, d + 1 - 2 * (d % 2)) for d in range(dp_size)]

    def sibling(v):
        return lax.ppermute(v, "dp", pairs)

    def across(v):
        return lax.ppermute(v, "tp", [(0, 1), (1, 0)])

    def swapped(v):
        return jnp.concatenate([v[1:], v[:1]], axis=0)

    def by_core(mine, theirs, axis):
        return jnp.where(
            core == 0, jnp.concatenate([mine, theirs], axis), jnp.concatenate([theirs, mine], axis)
        )

    def ring_order(array, axis):
        size = array.shape[axis] // n
        return jnp.concatenate([lax.slice_in_dim(array, i * size, (i + 1) * size, axis=axis) for i in ring], axis)

    def chip_order(array, axis):
        size = array.shape[axis] // n
        return jnp.concatenate(
            [lax.slice_in_dim(array, ring.index(i) * size, (ring.index(i) + 1) * size, axis=axis) for i in range(n)],
            axis,
        )

    def after(value, *others):
        return lax.optimization_barrier((value,) + others)[0]

    rows_own = layer_input.reshape(tokens, width)
    place = x * tokens + jnp.arange(tokens, dtype=jnp.int32)
    starts = jnp.where((resets.reshape(tokens) > 0) | (place == 0), 1.0, 0.0).astype(F32)
    starts = jnp.broadcast_to(starts[:, None], (tokens, 128))
    valid = (place < lengths[0]).astype(F32)[:, None]
    cot = grad_out.reshape(tokens, width).astype(F32) * valid

    def lane_sum(array):
        return lax.psum_scatter(array, "dp", scatter_dimension=0, tiled=True, axis_index_groups=lanes)

    def plane(array, which):
        return lax.dynamic_index_in_dim(array, which, 2, keepdims=False)

    def both(mine, axis):
        return jnp.concatenate([mine, across(mine)], axis)

    def tn(left, right):
        return lax.dot_general(left, right, (((0,), (0,)), ((), ())), preferred_element_type=F32)

    fh = w_gate.shape[1] // 2
    if own % 16 == 0 and own_d % 16 == 0:
        vectors = jnp.concatenate([conv_w, jnp.stack([conv_b, gate_a_b, gate_i_b, decay_param])], axis=0)
        vectors = jnp.pad(vectors, ((0, 0), (0, WIDE - own)))
        gains = jnp.pad(jnp.stack([norm_gain, mlp_gain]), ((0, PAD - taps - 6), (0, WIDE - own_d)))
        gs = jnp.concatenate([jnp.concatenate([gate_a_w, gate_i_w], axis=1), vectors, gains], axis=0)
        got = front(
            n, w_x, w_y, w_out, gs, w_gate, w_up, w_down, rows_own, grad_out.reshape(tokens, width), lengths, resets
        )
        w_xy, w_o = got["w_xy"].reshape(width, rec), got["w_o"].reshape(rec, width // 2)
        w_gu, w_d = got["w_gu"].reshape(width, 2 * fh), got["w_d"].reshape(width, fh)
        cot_all, n2_all = got["cot"].reshape(4 * tokens, width), got["n2"].reshape(4 * tokens, width)
        gain_one, gain_two, cp, gates = got["gains"][0], got["gains"][1], got["cp"], got["gates"]
        starts_two, ypre, u, a, h, xb, x1 = (got[key] for key in ("starts", "ypre", "u", "a", "h", "xb", "x1"))
        h_in, before = got["h_in"][:, 7:8], got["before"][:, PAD - taps + 1 :]
        n1_t, o_t = got["n1_t"].reshape(width // 2, 4 * tokens), got["o_t"].reshape(rh, 4 * tokens)
        hidden, gate, upv, part_d = got["hidden"], got["gate"], got["up"], got["part_d"]
        rs2 = lax.rsqrt(jnp.mean(x1 * x1, axis=-1, keepdims=True) + EPS)
    else:
        small = jnp.concatenate(
            [norm_gain, mlp_gain, conv_w.reshape(-1), conv_b, gate_a_b, gate_i_b, decay_param]
        )
        small = jnp.pad(small, (0, PAD * WIDE - small.shape[0])).reshape(PAD, WIDE)
        gs = jnp.concatenate([jnp.concatenate([gate_a_w, gate_i_w], axis=1), small], axis=0)
        w_xy, w_o, all_gs, w_gu, d_block, rows_two, cot_all, starts_two = gather_weights(
            n, w_x, w_y, w_out, gs, w_gate, w_up, w_down.T, rows_own, ring_order(cot.astype(BF16), 1), starts
        )
        w_d = lax.all_gather(
            d_block.reshape(-1, d_block.shape[2]), "dp", axis=0, tiled=True, axis_index_groups=lanes
        )
        w_gu = w_gu.reshape(width, w_gate.shape[1])
        w_xy = w_xy.reshape(width, rec)
        w_o = w_o.reshape(rec, width // 2)
        cot_all = cot_all.reshape(4 * tokens, width)

        vectors = all_gs[:, :, :, own:].transpose(1, 0, 2, 3, 4).reshape(2 * dp_size, PAD * WIDE)
        gain_one = vectors[:, :own_d].reshape(width).astype(F32)
        gain_two = vectors[:, own_d : 2 * own_d].reshape(width).astype(F32)
        lines = vectors[:, 2 * own_d : 2 * own_d + (taps + 4) * own].reshape(2 * dp_size, taps + 4, own)
        lines = lax.dynamic_slice_in_dim(lines, core * dp_size, dp_size, 0)
        lines = lines.transpose(1, 0, 2).reshape(taps + 4, rh).astype(F32)
        decay = lines[taps + 3 :]
        cp = jnp.concatenate(
            [lines[: taps + 3], jax.nn.softplus(-decay), jax.nn.sigmoid(-decay), jnp.zeros((7, rh), F32)], axis=0
        )
        gates = lax.dynamic_slice_in_dim(all_gs[:, :, :, :own], core * half, half, 1)
        gates = gates.transpose(1, 0, 2, 3, 4).reshape(rh, WIDE)

        n1, xb, ypre = project(rows_two, gain_one[None], w_xy)
        before = lax.ppermute(xb[:, tokens - (taps - 1) :], "tp", [(0, 1)])
        halo = jnp.concatenate([jnp.zeros((2, 8 - (taps - 1), rh), F32), before.astype(F32)], axis=1)
        u, a, h_local, coef = recurrence(xb, halo, gates, cp, starts_two)
        h_in = lax.ppermute(h_local[:, tokens - 1 :], "tp", [(0, 1)])
        h = h_local + coef * h_in
        ybr, _ = gelu_parts(ypre)
        o = (h * ybr).astype(BF16)
        o_sib = sibling(o)
        part_mine, part_theirs = project_out(o, o_sib, w_o)
        x1 = rows_own.astype(F32) + by_core(part_mine, sibling(part_theirs), 1)
        rs2 = lax.rsqrt(jnp.mean(x1 * x1, axis=-1, keepdims=True) + EPS)
        n2 = (x1 * rs2 * gain_two).astype(BF16)
        n2_x = across(n2)

        def plane_rows(values, rows):
            grouped = after(values, n2_x).T.reshape(n, 2, 2, rows, 2 * tokens)
            return plane(grouped, x), plane(grouped, 1 - x)

        o_here, o_send = plane_rows(jnp.concatenate([o, swapped(o_sib)], axis=2).reshape(2 * tokens, rec), own)
        n1_here, n1_send = plane_rows(n1, own_d)
        two = jnp.concatenate([n2, n2_x], axis=0)
        n2_all = jnp.concatenate([two, sibling(two)], axis=0)
        o_t = jnp.concatenate([o_here, across(o_send)], axis=3).reshape(rh, 4 * tokens)
        n1_t = jnp.concatenate([n1_here, across(n1_send)], axis=3).reshape(width // 2, 4 * tokens)

        gu = nn(n2_all, w_gu)
        gate, upv = gu[:, :fh], gu[:, fh:]
        act, _ = gelu_parts(gate)
        hidden = (act * upv).astype(BF16)

        part_d = tn(cot_all, hidden).astype(BF16)
    def pair_sum(partial):
        return (partial[: 2 * tokens].astype(F32) + sibling(partial[2 * tokens :]).astype(F32)).astype(BF16)

    if own % 16 == 0 and own_d % 16 == 0:
        grad_d, d_n2, part_gu = ff_back(n, part_d, cot_all, w_d, gate, upv, n2_all, w_gu)
    else:
        sum_d = lane_sum(part_d)
        act, slope = gelu_parts(gate)
        d_hidden = nn(after(cot_all, part_d), w_d)
        d_gu = jnp.concatenate([(d_hidden * upv * slope).astype(BF16), (d_hidden * act).astype(BF16)], axis=1)

        d_n2_pair = pair_sum(nt(d_gu, w_gu).astype(BF16))
        d_n2_send = d_n2_pair[tokens:]
        d_n2 = d_n2_pair[:tokens].astype(F32) + across(d_n2_send).astype(F32)
        n2_rows = ring_order(after(n2_all, d_n2_send), 1).reshape(4 * tokens, n, 2, width // dp_size)
        n2_rows = plane(n2_rows, core).reshape(4 * tokens, width // 2)
        d_gu_sib = sibling(d_gu)
        d_gu_sib = jnp.concatenate([d_gu_sib[2 * tokens :], d_gu_sib[: 2 * tokens]], axis=0)
        part_gu = tn(n2_rows, after(jnp.concatenate([d_gu, d_gu_sib], axis=1), d_n2_send)).astype(BF16)
        grad_d = None
    sum_gu = lane_sum(part_gu)

    q2 = gain_two * d_n2
    d_gain_two = jnp.sum(d_n2 * x1 * rs2, axis=0)
    d_x1 = cot + rs2 * q2 - x1 * (rs2 * rs2 * rs2) * jnp.mean(x1 * q2, axis=-1, keepdims=True)
    dbr = d_x1.astype(BF16)
    dbr_mine = lax.dynamic_slice_in_dim(dbr, core * (width // 2), width // 2, 1)
    dbr_theirs = lax.dynamic_slice_in_dim(dbr, (1 - core) * (width // 2), width // 2, 1)
    dbr_half = jnp.concatenate([dbr_mine, sibling(dbr_theirs)], axis=0)
    do_part = nt(dbr_half, w_o)
    do = do_part[:, :rh].reshape(2, tokens, rh) + swapped(sibling(do_part[:, rh:].reshape(2, tokens, rh)))
    dbr_x = across(dbr_half)

    d_ypre, lam_local, coef_back = adjoint(do, h, ypre, a)
    d_ypre_x = both(d_ypre.reshape(2 * tokens, rh), 0)
    ff_pair = pair_sum(nt(after(hidden, part_gu, d_ypre), w_d).astype(BF16))
    ff_out = ff_pair[:tokens].astype(F32) + across(ff_pair[tokens:]).astype(F32)
    inc = lax.ppermute(a[:, :1] * lam_local[:, :1], "tp", [(1, 0)])
    du, d_gates, sums = gates_back(lam_local, coef_back, inc, h, h_in, u, gates, cp, starts_two)
    du_next = lax.ppermute(du[:, : taps - 1], "tp", [(1, 0)])
    du_pad = jnp.concatenate([du, du_next], axis=1).astype(F32)
    xb_pad = jnp.concatenate([before, xb], axis=1).astype(F32)
    d_taps = jnp.stack(
        [jnp.sum(du_pad[:, :tokens] * xb_pad[:, taps - 1 - k : taps - 1 - k + tokens], axis=(0, 1)) for k in range(taps)]
    )
    d_bias = jnp.sum(du_pad[:, :tokens], axis=(0, 1))[None]
    d_xb = sum(cp[k] * du_pad[:, k : k + tokens] for k in range(taps)).astype(BF16)
    d_xy = jnp.concatenate([d_xb, d_ypre], axis=2).reshape(2 * tokens, rec)
    result = (after(x1, d_xb) + chip_order(ff_out, 1)).astype(BF16).reshape(1, tokens, width)
    d_n1_part = nt(d_xy, w_xy).reshape(2, tokens, width)
    d_n1 = d_n1_part[0] + sibling(d_n1_part[1])
    q1 = gain_one * d_n1
    own_f = rows_own.astype(F32)
    own_rs = lax.rsqrt(jnp.mean(own_f * own_f, axis=-1, keepdims=True) + EPS)
    d_gain_one = jnp.sum(d_n1 * own_f * own_rs, axis=0)
    grad_x = d_x1 + own_rs * q1 - own_f * (own_rs * own_rs * own_rs) * jnp.mean(own_f * q1, axis=-1, keepdims=True)

    c_out = nn(after(o_t, d_xb), jnp.concatenate([dbr_half, dbr_x], axis=0)).astype(BF16).reshape(n, 2, own, width // 2)
    c_x = nn(n1_t, both(d_xb.reshape(2 * tokens, rh), 0)).astype(BF16).reshape(n, 2, own_d, rh)
    c_y = nn(n1_t, d_ypre_x).astype(BF16).reshape(n, 2, own_d, rh)

    def placed(part):
        zero = jnp.zeros_like(part)
        return by_core_rows(part, zero)

    def by_core_rows(mine, theirs):
        return jnp.where(
            core == 0, jnp.concatenate([mine, theirs], 0), jnp.concatenate([theirs, mine], 0)
        )

    g = d_gates.reshape(half, 2, 2, own, WIDE)
    g = plane(g, x) + across(plane(g, 1 - x).astype(BF16)).astype(F32)
    g_mine = lax.dynamic_index_in_dim(g, core, 1, keepdims=False)
    g_theirs = lax.dynamic_index_in_dim(g, 1 - core, 1, keepdims=False)
    g_lane = by_core_rows(g_mine, sibling(g_theirs))

    lines_back = jnp.concatenate([d_taps, d_bias, sums[:3]], axis=0)
    lines_back = lines_back.reshape(taps + 4, half, 2, 2, own).transpose(1, 2, 3, 0, 4)
    lines_back = placed(jnp.pad(lines_back, ((0, 0),) * 4 + ((0, 128 - own),)))
    gains = jnp.stack([d_gain_one.reshape(n, 2, 2, own_d), d_gain_two.reshape(n, 2, 2, own_d)], axis=3)
    gains = jnp.pad(gains, ((0, 0),) * 3 + ((0, PAD - taps - 6), (0, 128 - own_d)))
    vec = jnp.concatenate([lines_back, gains], axis=3)
    vec = plane(vec, x) + across(plane(vec, 1 - x))
    vec = lax.dynamic_index_in_dim(vec, core, 1, keepdims=False) + sibling(
        lax.dynamic_index_in_dim(vec, 1 - core, 1, keepdims=False)
    )

    def whole(block):
        rows = block.shape[0] // 2
        block = block.reshape(2, rows, block.shape[1])
        mine = lax.dynamic_index_in_dim(block, core, 0, keepdims=False)
        theirs = lax.dynamic_index_in_dim(block, 1 - core, 0, keepdims=False)
        return mine, sibling(theirs)

    def halves(pair):
        return by_core(pair[0], pair[1], 1).astype(F32)

    grad_down = (halves(whole(sum_d)) if grad_d is None else grad_d).T
    x_sum, y_sum, out_sum, sum_gates, sum_vec = scatter_sums(
        n, after(c_x, grad_down, result, grad_x), c_y, c_out, g_lane.astype(BF16), vec
    )
    done = finish(after(sum_gu, sum_vec), x_sum, y_sum, out_sum, sum_gates, sum_vec, taps)
    grad_gate, grad_up, grad_w_x, grad_w_y, grad_w_out, grad_a_w, grad_i_w, grad_taps = done[:8]
    grad_bias, grad_a_b, grad_i_b, grad_decay, grad_gain_one, grad_gain_two = (v.reshape(-1) for v in done[8:])
    return (
        result,
        grad_x.reshape(1, tokens, width),
        grad_gain_one,
        grad_w_x,
        grad_w_y,
        grad_taps,
        grad_bias,
        grad_a_w,
        grad_a_b,
        grad_i_w,
        grad_i_b,
        grad_decay,
        grad_w_out,
        grad_gain_two,
        grad_gate,
        grad_up,
        grad_down,
    )


def solution(mesh):
    every = ("dp", "tp")
    return jax.shard_map(
        functools.partial(body, mesh.shape["dp"]),
        mesh=mesh,
        in_specs=(
            P("dp", "tp", None),
            P("dp", "tp", None),
            P("dp"),
            P("dp", "tp"),
            P(every),
            P(every, None),
            P(every, None),
            P(None, every),
            P(every),
            P(every, None),
            P(every),
            P(every, None),
            P(every),
            P(every),
            P(every, None),
            P(every),
            P("dp", "tp"),
            P("dp", "tp"),
            P("tp", "dp"),
        ),
        out_specs=(
            P("dp", "tp", None),
            P("dp", "tp", None),
            P(every),
            P(every, None),
            P(every, None),
            P(None, every),
            P(every),
            P(every, None),
            P(every),
            P(every, None),
            P(every),
            P(every),
            P(every, None),
            P(every),
            P("dp", "tp"),
            P("dp", "tp"),
            P("tp", "dp"),
        ),
        check_vma=False,
    )
```
